32 devices in a mesh: slide: 4 (over y, core), blk: 8 (over z, x).
Axes of the slice: x: 2, y: 2, z: 4, core: 2. Of those that a mesh axis runs over, the one named last changes fastest.
Arguments:
- counts: int32 [4, 1024, 1024], P('slide', 'blk'), may hold values from 0 to 39, as said below
- library: int32 [4, 1024], P('slide', 'blk'), may hold values from 2000 to 19999
- gene_ids: int32 [1024], replicated, may hold values from 0 to 16383, as said below
- positions: int32 [4, 2, 1024], P('slide', None, 'blk'), may hold values from 0 to 2047
- slide_of_cell: int32 [4, 1024], P('slide', 'blk'), may hold values from 0 to 3, as said below
- latent_noise: float32 [4, 1024, 512], P('slide', 'blk'), may hold values from -6 to 6
- decoded_grad: bfloat16 [4, 1024, 1024], P('slide', 'blk'), may hold values from -6 to 6
- gene_table: bfloat16 [16384, 1024], P('blk'), may hold values from -0.0625 to 0.0625
- first_gain: float32 [1024], replicated, may hold values from 0.5 to 1.5
- first_shift: float32 [1024], replicated, may hold values from -1.5 to 1.5
- query_weight: bfloat16 [1024, 1024], replicated, may hold values from -0.25 to 0.25
- key_weight: bfloat16 [1024, 1024], replicated, may hold values from -0.25 to 0.25
- value_weight: bfloat16 [1024, 1024], replicated, may hold values from -0.1875 to 0.1875
- output_weight: bfloat16 [1024, 1024], replicated, may hold values from -0.375 to 0.375
- second_gain: float32 [1024], replicated, may hold values from 0.5 to 1.5
- second_shift: float32 [1024], replicated, may hold values from -1.5 to 1.5
- hidden_weight: bfloat16 [1024, 4096], replicated, may hold values from -0.1875 to 0.1875
- hidden_bias: float32 [4096], replicated, may hold values from -3 to 3
- down_weight: bfloat16 [4096, 1024], replicated, may hold values from -0.09375 to 0.09375
- down_bias: float32 [1024], replicated, may hold values from -3 to 3
- mean_weight: bfloat16 [1024, 512], replicated, may hold values from -0.09375 to 0.09375
- logvar_weight: bfloat16 [1024, 512], replicated, may hold values from -0.046875 to 0.046875
- component_means: float32 [16, 512], replicated, may hold values from -5 to 5
- decoder_weight: bfloat16 [512, 1024], replicated, may hold values from -0.25 to 0.25
- divergence_weight: float32 [1], replicated, may hold values from 0.005 to 0.02
- free_floor: float32 [512], replicated, may hold values from 0.1 to 4
Outputs:
- decoded: float32 [4, 1024, 1024], P('slide', 'blk')
- divergence: float32 [1], replicated
- gene_table_grad: float32 [16384, 1024], P('blk')
- first_gain_grad: float32 [1024], P('blk')
- first_shift_grad: float32 [1024], P('blk')
- query_weight_grad: float32 [1024, 1024], P('blk')
- key_weight_grad: float32 [1024, 1024], P('blk')
- value_weight_grad: float32 [1024, 1024], P('blk')
- output_weight_grad: float32 [1024, 1024], P('blk')
- second_gain_grad: float32 [1024], P('blk')
- second_shift_grad: float32 [1024], P('blk')
- hidden_weight_grad: float32 [1024, 4096], P('blk')
- hidden_bias_grad: float32 [4096], P('blk')
- down_weight_grad: float32 [4096, 1024], P('blk')
- down_bias_grad: float32 [1024], P('blk')
- mean_weight_grad: float32 [1024, 512], P('blk')
- logvar_weight_grad: float32 [1024, 512], P('blk')
- component_means_grad: float32 [16, 512], P(None, 'blk')
- decoder_weight_grad: float32 [512, 1024], P('blk')
The draws below stay inside these ranges and needn't reach their ends.
Inputs may be any that keep to these rules, and one draw needn't show every extreme that they name: `counts`: most entries are zero, about four in five. `gene_ids`: distinct rows of the gene table. `slide_of_cell`: each of the 4 slides of a group holds about 1024/4 cells, at any positions of the group.
All inputs are finite; a program needn't handle non-finite values.
Results may differ from the reference program's by a relative error of at most 0.019.
Values may be sent and summed in bfloat16 or wider, within the bound.
A program may use at most 256 MiB of HBM per device.

```python
import math
import jax
import jax.numpy as jnp
from jax import lax

D = 1024
HEADS = 16
HEAD_DIM = 64
FF = 4096
LATENT = 512
COMPS = 16
PANEL = 1024
VOCAB = 16384
SLIDES = 4
GROUP = 1024
GROUPS = 4


def draw_counts(key, part):
    key = jax.random.fold_in(key, 31)
    key_present, key_amount = jax.random.split(key)
    shape = (GROUPS, GROUP, PANEL)
    present = jax.random.randint(key_present, shape, 0, 5) == 0
    amount = jax.random.randint(key_amount, shape, 1, 40)
    return jnp.where(present, amount, 0).astype(jnp.int32)


def draw_gene_ids(key, part):
    key = jax.random.fold_in(key, 11)
    key_inner, key_order = jax.random.split(key)
    inner_rows = jax.random.permutation(key_inner, jnp.arange(1, VOCAB - 1, dtype=jnp.int32))[:PANEL - 2]
    ends = jnp.array([0, VOCAB - 1], dtype=jnp.int32)
    rows = jnp.concatenate([ends, inner_rows.astype(jnp.int32)])
    return jax.random.permutation(key_order, rows).astype(jnp.int32)


def draw_slide_of_cell(key, part):
    key = jax.random.fold_in(key, 23)
    group_keys = jax.random.split(key, GROUPS)
    jitter = GROUP // (4 * SLIDES)

    def one_group(group_key):
        key_cuts, key_order = jax.random.split(group_key)
        cuts = jnp.arange(1, SLIDES, dtype=jnp.int32) * (GROUP // SLIDES) + jax.random.randint(key_cuts, (SLIDES - 1,), -jitter, jitter + 1)
        places = jnp.arange(GROUP, dtype=jnp.int32)
        ordered = jnp.sum((places[:, None] >= cuts[None, :]).astype(jnp.int32), axis=1)
        return jax.random.permutation(key_order, ordered).astype(jnp.int32)
    return jax.vmap(one_group)(group_keys)


def with_ends(drawn, stream_key, least, high):
    spot = [jax.random.randint(jax.random.fold_in(stream_key, axis), (), 0, length) for axis, length in enumerate(drawn.shape)]
    widest = drawn.shape.index(max(drawn.shape))
    next_to = spot[:widest] + [(spot[widest] + 1) % drawn.shape[widest]] + spot[widest + 1:]
    return drawn.at[tuple(spot)].set(least).at[tuple(next_to)].set(high)


def block_levels(own_key, dims, cuts, least, top_value):
    factor_of, own = 1.0, jax.random.fold_in(own_key, 6)
    for axis_at, parts in cuts:
        heights = jnp.exp(jax.random.uniform(jax.random.fold_in(own, axis_at), (parts,), jnp.float32, least / len(cuts), top_value / len(cuts)))
        factor_of = factor_of * jnp.repeat(heights, dims[axis_at] // parts).reshape([-1 if axis == axis_at else 1 for axis in range(len(dims))])
    return factor_of


def centred(stream_key, dims, deviation, most, cuts=(), kind=jnp.bfloat16):
    level = block_levels(stream_key, dims, cuts, -0.22, 0.18) if cuts else 1.0
    values = jax.random.normal(stream_key, dims, jnp.float32) * deviation * level
    return jnp.minimum(jnp.maximum(values, -most), most).astype(kind)


def setup_inputs(seed: int = 0) -> dict:
    splits = jax.random.split(jax.random.key(seed), 27)
    counts = draw_counts(jax.random.fold_in(splits[26], 71), 0)
    library = with_ends(jax.random.randint(splits[1], (GROUPS, GROUP), 2000, 20000), jax.random.fold_in(splits[1], 1), 2000, 19999).astype(jnp.int32)
    gene_ids = draw_gene_ids(jax.random.fold_in(splits[26], 71), 0)
    positions = with_ends(jax.random.randint(splits[3], (GROUPS, 2, GROUP), 0, 2048), jax.random.fold_in(splits[3], 1), 0, 2047).astype(jnp.int32)
    slide_of_cell = draw_slide_of_cell(jax.random.fold_in(splits[26], 71), 0)
    latent_noise = centred(splits[5], (GROUPS, GROUP, LATENT), 1.0, 6.0, ((0, 4), (1, 8)), jnp.float32)
    decoded_grad = centred(splits[6], (GROUPS, GROUP, PANEL), 1.0, 6.0, ((0, 4), (1, 8)))
    gene_table = centred(splits[7], (VOCAB, D), (PANEL * 9) ** -0.5, 0.0625, ((0, 8),))
    first_gain = jnp.clip(1.0 + 0.1 * jax.random.normal(splits[8], (D,), jnp.float32), 0.5, 1.5)
    first_shift = centred(splits[9], (D,), 0.3, 1.5, (), jnp.float32)
    query_weight = centred(splits[10], (D, D), (D // 2) ** -0.5, 0.25)
    key_weight = centred(splits[11], (D, D), (D // 2) ** -0.5, 0.25)
    value_weight = centred(splits[12], (D, D), D ** -0.5, 0.1875)
    output_weight = centred(splits[13], (D, D), (D // 4) ** -0.5, 0.375)
    second_gain = jnp.clip(1.0 + 0.1 * jax.random.normal(splits[14], (D,), jnp.float32), 0.5, 1.5)
    second_shift = centred(splits[15], (D,), 0.3, 1.5, (), jnp.float32)
    hidden_weight = centred(splits[16], (D, FF), D ** -0.5, 0.1875)
    hidden_bias = centred(splits[17], (FF,), 0.5, 3.0, (), jnp.float32)
    down_weight = centred(splits[18], (FF, D), FF ** -0.5, 0.09375)
    down_bias = centred(splits[19], (D,), 0.5, 3.0, (), jnp.float32)
    mean_weight = centred(splits[20], (D, LATENT), (D * 4) ** -0.5, 0.09375)
    logvar_weight = centred(splits[21], (D, LATENT), (D * 16) ** -0.5, 0.046875)
    component_means = centred(splits[22], (COMPS, LATENT), 1.0, 5.0, (), jnp.float32)
    decoder_weight = centred(splits[23], (LATENT, PANEL), LATENT ** -0.5, 0.25)
    divergence_weight = jnp.clip(jnp.exp(jax.random.uniform(splits[24], (1,), jnp.float32, math.log(0.005), math.log(0.02))), 0.005, 0.02)
    free_floor = jnp.clip(jnp.exp(jax.random.uniform(splits[25], (LATENT,), jnp.float32, math.log(0.1), math.log(4.0))), 0.1, 4.0)
    return dict(counts=counts, library=library, gene_ids=gene_ids, positions=positions, slide_of_cell=slide_of_cell, latent_noise=latent_noise, decoded_grad=decoded_grad, gene_table=gene_table, first_gain=first_gain, first_shift=first_shift, query_weight=query_weight, key_weight=key_weight, value_weight=value_weight, output_weight=output_weight, second_gain=second_gain, second_shift=second_shift, hidden_weight=hidden_weight, hidden_bias=hidden_bias, down_weight=down_weight, down_bias=down_bias, mean_weight=mean_weight, logvar_weight=logvar_weight, component_means=component_means, decoder_weight=decoder_weight, divergence_weight=divergence_weight, free_floor=free_floor)


@jax.custom_vjp
def low(v):
    return lax.optimization_barrier(v.astype(jnp.bfloat16)).astype(jnp.float32)

@jax.custom_vjp
def low_back(v):
    return v

def low_keep(v):
    return (low(v), None)

def low_pass(kept, grad):
    return (grad,)

def back_keep(v):
    return (v, None)

def back_low(kept, grad):
    return (low(grad),)
low.defvjp(low_keep, low_pass)
low_back.defvjp(back_keep, back_low)

def product(left, right):
    return jnp.dot(left, right, precision=lax.Precision.HIGHEST)

def normalized(counts, library):
    scaled = counts.astype(jnp.float32) * (10000.0 / library.astype(jnp.float32))[..., None]
    return jnp.log1p(scaled)

def position_code(coords, model_width):
    quarter = model_width // 4
    freqs = jnp.exp(-math.log(10000.0) * jnp.arange(quarter, dtype=jnp.float32) / quarter)
    along_x = coords[0].astype(jnp.float32)[:, None] * freqs[None, :]
    along_y = coords[1].astype(jnp.float32)[:, None] * freqs[None, :]
    return jnp.concatenate([jnp.sin(along_x), jnp.cos(along_x), jnp.sin(along_y), jnp.cos(along_y)], axis=1)

def layer_norm(inputs, scaling, offsets):
    centre = inputs - lax.optimization_barrier(jnp.mean(inputs, axis=-1, keepdims=True))
    spread = lax.optimization_barrier(jnp.mean(centre * centre, axis=-1, keepdims=True))
    return centre * lax.rsqrt(spread + 1e-05) * scaling + offsets

def gelu_tanh(inputs):
    return 0.5 * inputs * (1.0 + jnp.tanh(0.7978845608028654 * (inputs + 0.044715 * inputs * inputs * inputs)))

def divergence_cells(mean_part, logvar_part, centres):
    latent_width = mean_part.shape[-1]
    crossed = jnp.dot(mean_part, centres.T, precision=lax.Precision.HIGHEST)
    centre_square = lax.optimization_barrier(jnp.sum(centres * centres, axis=-1))
    logits = (crossed - 0.5 * centre_square[None, :]) / math.sqrt(latent_width)
    shifted = jnp.exp(logits - lax.optimization_barrier(jnp.max(logits, axis=-1, keepdims=True)))
    resp = shifted / lax.optimization_barrier(jnp.sum(shifted, axis=-1, keepdims=True))
    mixed = jnp.dot(resp, centres, precision=lax.Precision.HIGHEST)
    mixed_square = jnp.dot(resp, centres * centres, precision=lax.Precision.HIGHEST)
    return 0.5 * (jnp.exp(logvar_part) - 1.0 - logvar_part + mean_part * mean_part - 2.0 * mean_part * mixed + mixed_square)

def attention(query_all, keys_all, values_all, slide_labels):
    block_rows = min(512, GROUP)
    block_count = GROUP // block_rows
    query_blocks = query_all.reshape(GROUPS * block_count, block_rows, HEADS, HEAD_DIM)
    key_groups = keys_all.reshape(GROUPS, GROUP, HEADS, HEAD_DIM)
    value_groups = values_all.reshape(GROUPS, GROUP, HEADS, HEAD_DIM)
    label_blocks = slide_labels.reshape(GROUPS * block_count, block_rows)
    owners = jnp.arange(GROUPS * block_count, dtype=jnp.int32) // block_count

    def block_out(block_items):
        query_block, query_labels, owner = block_items
        key_group = key_groups[owner]
        value_group = value_groups[owner]
        key_labels = slide_labels[owner]
        scores = jnp.einsum('qhd,khd->hqk', query_block, key_group, precision=lax.Precision.HIGHEST) * HEAD_DIM ** (-0.5)
        same_slide = (query_labels[:, None] == key_labels[None, :])[None]
        scores = low_back(jnp.where(same_slide, scores, -1e+30))
        shifted = jnp.exp(scores - lax.optimization_barrier(jnp.max(scores, axis=-1, keepdims=True)))
        shares = shifted / lax.optimization_barrier(jnp.sum(shifted, axis=-1, keepdims=True))
        return jnp.einsum('hqk,khd->qhd', low(shares), value_group, precision=lax.Precision.HIGHEST)
    outputs = lax.map(jax.checkpoint(block_out), (query_blocks, label_blocks, owners))
    return outputs.reshape(GROUPS * GROUP, D)

def reference(counts, library, gene_ids, positions, slide_of_cell, latent_noise, decoded_grad, gene_table, first_gain, first_shift, query_weight, key_weight, value_weight, output_weight, second_gain, second_shift, hidden_weight, hidden_bias, down_weight, down_bias, mean_weight, logvar_weight, component_means, decoder_weight, divergence_weight, free_floor):
    cell_count = GROUPS * GROUP
    express = normalized(counts, library).reshape(cell_count, PANEL)
    coding = jax.vmap(position_code, in_axes=(0, None))(positions, D).reshape(cell_count, D)
    noise_flat = latent_noise.astype(jnp.float32).reshape(cell_count, LATENT)
    weight_floor = divergence_weight.astype(jnp.float32)
    floor_bits = free_floor.astype(jnp.float32)
    params = tuple((item.astype(jnp.float32) for item in (gene_table, first_gain, first_shift, query_weight, key_weight, value_weight, output_weight, second_gain, second_shift, hidden_weight, hidden_bias, down_weight, down_bias, mean_weight, logvar_weight, component_means, decoder_weight)))

    def forward(table, gain_one, shift_one, weight_query, weight_key, weight_value, weight_output, gain_two, shift_two, weight_hidden, bias_hidden, weight_down, bias_down, weight_mean, weight_logvar, centres, weight_decoder):
        panel_weight = table[gene_ids]
        hidden_start = low_back(product(low(express), panel_weight)) + coding
        normed_one = low(layer_norm(hidden_start, gain_one, shift_one))
        query_low = low(low_back(product(normed_one, weight_query)))
        key_low = low(low_back(product(normed_one, weight_key)))
        value_low = low(low_back(product(normed_one, weight_value)))
        attended = low(low_back(attention(query_low, key_low, value_low, slide_of_cell)))
        hidden_middle = hidden_start + low_back(product(attended, weight_output))
        normed_two = low(layer_norm(hidden_middle, gain_two, shift_two))
        inner_sum = low_back(product(normed_two, weight_hidden) + bias_hidden)
        act_low = low(gelu_tanh(inner_sum))
        hidden_final = hidden_middle + low_back(product(act_low, weight_down) + bias_down)
        base_low = low(hidden_final)
        mean_lat = low_back(product(base_low, weight_mean))
        log_var = low_back(product(base_low, weight_logvar))
        latent = low(mean_lat + jnp.exp(0.5 * log_var) * noise_flat)
        decoded = product(latent, weight_decoder)
        kl_mean = lax.optimization_barrier(jnp.sum(divergence_cells(mean_lat, log_var, centres), axis=0)) / cell_count
        divergence = weight_floor * jnp.mean(jnp.maximum(kl_mean, floor_bits))
        return (decoded.reshape(GROUPS, GROUP, PANEL), divergence)
    outputs, pull_back = jax.vjp(forward, *params)
    decoded, divergence = outputs
    grads = pull_back((decoded_grad.astype(jnp.float32), jnp.full((1,), cell_count * LATENT, jnp.float32)))
    return (decoded, divergence, grads[0], grads[1], grads[2], grads[3], grads[4], grads[5], grads[6], grads[7], grads[8], grads[9], grads[10], grads[11], grads[12], grads[13], grads[14], grads[15], grads[16])
```

```python
import functools
import math

import jax
import jax.numpy as jnp
from jax import lax
from jax.experimental import pallas as pl
from jax.experimental.pallas import tpu as pltpu
from jax.sharding import PartitionSpec as P

HEAD_DIM = 64
MESH = pl.DeviceIdType.MESH
F32 = jnp.float32
BF16 = jnp.bfloat16


def normalized(counts, library):
    scaled = counts.astype(jnp.float32) * (10000.0 / library.astype(jnp.float32))[..., None]
    return jnp.log1p(scaled)


def position_code(coords, model_width):
    quarter = model_width // 4
    freqs = jnp.exp(-math.log(10000.0) * jnp.arange(quarter, dtype=jnp.float32) / quarter)
    along_x = coords[0].astype(jnp.float32)[:, None] * freqs[None, :]
    along_y = coords[1].astype(jnp.float32)[:, None] * freqs[None, :]
    return jnp.concatenate(
        [jnp.sin(along_x), jnp.cos(along_x), jnp.sin(along_y), jnp.cos(along_y)], axis=1
    )


def layer_norm(inputs, scaling, offsets):
    centre = inputs - jnp.mean(inputs, axis=-1, keepdims=True)
    spread = jnp.mean(centre * centre, axis=-1, keepdims=True)
    return centre * lax.rsqrt(spread + 1e-05) * scaling + offsets


def gelu_tanh(inputs):
    return (
        0.5
        * inputs
        * (1.0 + jnp.tanh(0.7978845608028654 * (inputs + 0.044715 * inputs * inputs * inputs)))
    )


def divergence_cells(mean_part, logvar_part, centres):
    latent_width = mean_part.shape[-1]
    crossed = jnp.dot(mean_part, centres.T, precision=lax.Precision.HIGHEST)
    centre_square = jnp.sum(centres * centres, axis=-1)
    logits = (crossed - 0.5 * centre_square[None, :]) / math.sqrt(latent_width)
    shifted = jnp.exp(logits - jnp.max(logits, axis=-1, keepdims=True))
    resp = shifted / jnp.sum(shifted, axis=-1, keepdims=True)
    mixed = jnp.dot(resp, centres, precision=lax.Precision.HIGHEST)
    mixed_square = jnp.dot(resp, centres * centres, precision=lax.Precision.HIGHEST)
    return 0.5 * (
        jnp.exp(logvar_part)
        - 1.0
        - logvar_part
        + mean_part * mean_part
        - 2.0 * mean_part * mixed
        + mixed_square
    )


def to_heads(array, head_count):
    return array.reshape(array.shape[0], head_count, -1).transpose(1, 0, 2)


def from_heads(array):
    return array.transpose(1, 0, 2).reshape(array.shape[1], -1)


def matmul(left, right):
    return jnp.dot(left, right, preferred_element_type=jnp.float32)


def on_device_general(
    counts,
    library,
    gene_ids,
    positions,
    slide_of_cell,
    latent_noise,
    decoded_grad,
    gene_table,
    first_gain,
    first_shift,
    query_weight,
    key_weight,
    value_weight,
    output_weight,
    second_gain,
    second_shift,
    hidden_weight,
    hidden_bias,
    down_weight,
    down_bias,
    mean_weight,
    logvar_weight,
    component_means,
    decoder_weight,
    divergence_weight,
    free_floor,
):
    cell_count = counts.shape[1]
    model_width = gene_table.shape[1]
    head_count = model_width // HEAD_DIM
    score_scale = HEAD_DIM ** (-0.5)
    express = normalized(counts[0], library[0]).astype(jnp.bfloat16)
    table_rows = gene_table.shape[0]
    first_row = lax.axis_index("blk") * table_rows
    selector = (
        gene_ids[:, None] == first_row + jnp.arange(table_rows, dtype=jnp.int32)[None, :]
    ).astype(jnp.bfloat16)
    panel_part = matmul(selector, gene_table)
    panel_weight = lax.psum(panel_part, "blk").astype(jnp.bfloat16)
    hidden_start = matmul(express, panel_weight) + position_code(positions[0], model_width)
    normed_one = layer_norm(hidden_start, first_gain, first_shift).astype(jnp.bfloat16)
    query_low = matmul(normed_one, query_weight).astype(jnp.bfloat16)
    key_low = matmul(normed_one, key_weight).astype(jnp.bfloat16)
    value_low = matmul(normed_one, value_weight).astype(jnp.bfloat16)
    slide_labels = slide_of_cell[0].astype(jnp.bfloat16)
    keys_all, values_all, labels_all = (
        lax.all_gather(key_low, "blk", axis=0, tiled=True),
        lax.all_gather(value_low, "blk", axis=0, tiled=True),
        lax.all_gather(slide_labels, "blk", axis=0, tiled=True),
    )
    same_slide = slide_labels[:, None] == labels_all[None, :]
    query_heads = to_heads(query_low, head_count)
    key_heads = to_heads(keys_all, head_count)
    value_heads = to_heads(values_all, head_count)

    def head_forward(head_items):
        query_head, key_head, value_head = head_items
        scores = (
            jnp.einsum("qd,kd->qk", query_head, key_head, preferred_element_type=jnp.float32)
            * score_scale
        )
        scores = jnp.where(same_slide, scores, -1e30)
        row_max = jnp.max(scores, axis=1, keepdims=True)
        shifted = jnp.exp(scores - row_max)
        row_sum = jnp.sum(shifted, axis=1, keepdims=True)
        shares = shifted / row_sum
        attended_head = jnp.einsum(
            "qk,kd->qd", shares.astype(jnp.bfloat16), value_head, preferred_element_type=jnp.float32
        )
        return (attended_head, row_max[:, 0], row_sum[:, 0])

    attended_heads, row_maxes, row_sums = lax.map(
        head_forward, (query_heads, key_heads, value_heads)
    )
    attended = from_heads(attended_heads).astype(jnp.bfloat16)
    hidden_middle = hidden_start + matmul(attended, output_weight)
    normed_two = layer_norm(hidden_middle, second_gain, second_shift).astype(jnp.bfloat16)
    inner_sum = matmul(normed_two, hidden_weight) + hidden_bias
    act_low = gelu_tanh(inner_sum).astype(jnp.bfloat16)
    hidden_final = hidden_middle + matmul(act_low, down_weight) + down_bias
    base_low = hidden_final.astype(jnp.bfloat16)
    mean_lat = matmul(base_low, mean_weight)
    log_var = matmul(base_low, logvar_weight)
    noise_local = latent_noise[0]

    def bottleneck(mean_part, logvar_part, centres):
        return (
            mean_part + jnp.exp(0.5 * logvar_part) * noise_local,
            divergence_cells(mean_part, logvar_part, centres),
        )

    (latent, kl_cell), pull_latent = jax.vjp(bottleneck, mean_lat, log_var, component_means)
    latent_low = latent.astype(jnp.bfloat16)
    decoded = matmul(latent_low, decoder_weight)
    everyone = cell_count * lax.axis_size("blk") * lax.axis_size("slide")
    kl_sum = lax.psum(jnp.sum(kl_cell, axis=0), ("slide", "blk"))
    kl_mean = kl_sum / everyone
    divergence = divergence_weight * jnp.mean(jnp.maximum(kl_mean, free_floor))
    binding = (kl_mean > free_floor).astype(jnp.float32)
    grad_source = decoded_grad[0]
    grad_latent = matmul(grad_source, decoder_weight.T)
    decoder_grad = matmul(latent_low.T, grad_source)
    grad_kl = jnp.broadcast_to(divergence_weight * binding, kl_cell.shape)
    grad_mean, grad_logvar, centres_grad = pull_latent((grad_latent, grad_kl))
    grad_mean_low = grad_mean.astype(jnp.bfloat16)
    grad_logvar_low = grad_logvar.astype(jnp.bfloat16)
    mean_grad = matmul(base_low.T, grad_mean_low)
    logvar_grad = matmul(base_low.T, grad_logvar_low)
    grad_final = matmul(grad_mean_low, mean_weight.T) + matmul(grad_logvar_low, logvar_weight.T)
    grad_branch = grad_final.astype(jnp.bfloat16)
    down_grad = matmul(act_low.T, grad_branch)
    down_bias_grad = jnp.sum(grad_branch.astype(jnp.float32), axis=0)
    grad_act = matmul(grad_branch, down_weight.T)
    gelu_pull = jax.vjp(gelu_tanh, inner_sum)[1]
    grad_inner = gelu_pull(grad_act)[0].astype(jnp.bfloat16)
    hidden_grad = matmul(normed_two.T, grad_inner)
    hidden_bias_grad = jnp.sum(grad_inner.astype(jnp.float32), axis=0)
    norm_two_pull = jax.vjp(layer_norm, hidden_middle, second_gain, second_shift)[1]
    grad_norm_two, second_gain_grad, second_shift_grad = norm_two_pull(
        matmul(grad_inner, hidden_weight.T)
    )
    grad_middle = grad_final + grad_norm_two
    grad_out = grad_middle.astype(jnp.bfloat16)
    output_grad = matmul(attended.T, grad_out)
    grad_attended = matmul(grad_out, output_weight.T).astype(jnp.bfloat16)
    keys_again, values_again = (
        lax.all_gather(key_low, "blk", axis=0, tiled=True),
        lax.all_gather(value_low, "blk", axis=0, tiled=True),
    )
    key_heads_back = to_heads(keys_again, head_count)
    value_heads_back = to_heads(values_again, head_count)
    grad_heads_local = to_heads(grad_attended, head_count)

    def head_queries(head_items):
        query_head, key_head, value_head, grad_head, row_max, row_sum = head_items
        scores = (
            jnp.einsum("qd,kd->qk", query_head, key_head, preferred_element_type=jnp.float32)
            * score_scale
        )
        scores = jnp.where(same_slide, scores, -1e30)
        shares = jnp.exp(scores - row_max[:, None]) / row_sum[:, None]
        grad_shares = jnp.einsum(
            "qd,kd->qk", grad_head, value_head, preferred_element_type=jnp.float32
        )
        inner_dot = jnp.sum(shares * grad_shares, axis=1, keepdims=True)
        grad_scores = (shares * (grad_shares - inner_dot)).astype(jnp.bfloat16)
        grad_query_head = (
            jnp.einsum("qk,kd->qd", grad_scores, key_head, preferred_element_type=jnp.float32)
            * score_scale
        )
        return (grad_query_head, inner_dot[:, 0])

    grad_query_heads, inner_dots = lax.map(
        head_queries,
        (query_heads, key_heads_back, value_heads_back, grad_heads_local, row_maxes, row_sums),
    )
    queries_group, grads_group = (
        lax.all_gather(query_low, "blk", axis=0, tiled=True),
        lax.all_gather(grad_attended, "blk", axis=0, tiled=True),
    )
    maxes_group, totals_group, dots_group = (
        lax.all_gather(row_maxes, "blk", axis=1, tiled=True),
        lax.all_gather(row_sums, "blk", axis=1, tiled=True),
        lax.all_gather(inner_dots, "blk", axis=1, tiled=True),
    )
    mask_back = labels_all[:, None] == slide_labels[None, :]

    def head_keys(head_items):
        query_head, key_head, value_head, grad_head, row_max, row_sum, inner_dot = head_items
        scores = (
            jnp.einsum("qd,kd->qk", query_head, key_head, preferred_element_type=jnp.float32)
            * score_scale
        )
        scores = jnp.where(mask_back, scores, -1e30)
        shares = jnp.exp(scores - row_max[:, None]) / row_sum[:, None]
        grad_shares = jnp.einsum(
            "qd,kd->qk", grad_head, value_head, preferred_element_type=jnp.float32
        )
        grad_scores = (shares * (grad_shares - inner_dot[:, None])).astype(jnp.bfloat16)
        grad_key_head = (
            jnp.einsum("qk,qd->kd", grad_scores, query_head, preferred_element_type=jnp.float32)
            * score_scale
        )
        grad_value_head = jnp.einsum(
            "qk,qd->kd", shares.astype(jnp.bfloat16), grad_head, preferred_element_type=jnp.float32
        )
        return (grad_key_head, grad_value_head)

    grad_key_heads, grad_value_heads = lax.map(
        head_keys,
        (
            to_heads(queries_group, head_count),
            to_heads(key_low, head_count),
            to_heads(value_low, head_count),
            to_heads(grads_group, head_count),
            maxes_group,
            totals_group,
            dots_group,
        ),
    )
    grad_query_low = from_heads(grad_query_heads).astype(jnp.bfloat16)
    grad_key = from_heads(grad_key_heads)
    grad_value = from_heads(grad_value_heads)
    grad_key_low = grad_key.astype(jnp.bfloat16)
    grad_value_low = grad_value.astype(jnp.bfloat16)
    query_grad = matmul(normed_one.T, grad_query_low)
    key_grad = matmul(normed_one.T, grad_key_low)
    value_grad = matmul(normed_one.T, grad_value_low)
    grad_norm_input = (
        matmul(grad_query_low, query_weight.T)
        + matmul(grad_key_low, key_weight.T)
        + matmul(grad_value_low, value_weight.T)
    )
    norm_one_pull = jax.vjp(layer_norm, hidden_start, first_gain, first_shift)[1]
    grad_norm_one, first_gain_grad, first_shift_grad = norm_one_pull(grad_norm_input)
    grad_start = grad_middle + grad_norm_one
    grad_encoded = grad_start.astype(jnp.bfloat16)
    panel_grad = matmul(express.T, grad_encoded)
    panel_total = lax.psum(panel_grad, ("slide", "blk"))
    table_grad = jnp.dot(
        selector.astype(jnp.float32).T, panel_total, precision=lax.Precision.HIGHEST
    )
    shares_grads = (
        lax.psum_scatter(first_gain_grad, "blk", scatter_dimension=0, tiled=True),
        lax.psum_scatter(first_shift_grad, "blk", scatter_dimension=0, tiled=True),
        lax.psum_scatter(query_grad, "blk", scatter_dimension=0, tiled=True),
        lax.psum_scatter(key_grad, "blk", scatter_dimension=0, tiled=True),
        lax.psum_scatter(value_grad, "blk", scatter_dimension=0, tiled=True),
        lax.psum_scatter(output_grad, "blk", scatter_dimension=0, tiled=True),
        lax.psum_scatter(second_gain_grad, "blk", scatter_dimension=0, tiled=True),
        lax.psum_scatter(second_shift_grad, "blk", scatter_dimension=0, tiled=True),
        lax.psum_scatter(hidden_grad, "blk", scatter_dimension=0, tiled=True),
        lax.psum_scatter(hidden_bias_grad, "blk", scatter_dimension=0, tiled=True),
        lax.psum_scatter(down_grad, "blk", scatter_dimension=0, tiled=True),
        lax.psum_scatter(down_bias_grad, "blk", scatter_dimension=0, tiled=True),
        lax.psum_scatter(mean_grad, "blk", scatter_dimension=0, tiled=True),
        lax.psum_scatter(logvar_grad, "blk", scatter_dimension=0, tiled=True),
        lax.psum_scatter(centres_grad, "blk", scatter_dimension=1, tiled=True),
        lax.psum_scatter(decoder_grad, "blk", scatter_dimension=0, tiled=True),
    )
    summed = (
        lax.psum(shares_grads[0].astype(jnp.bfloat16), "slide").astype(jnp.float32),
        lax.psum(shares_grads[1].astype(jnp.bfloat16), "slide").astype(jnp.float32),
        lax.psum(shares_grads[2].astype(jnp.bfloat16), "slide").astype(jnp.float32),
        lax.psum(shares_grads[3].astype(jnp.bfloat16), "slide").astype(jnp.float32),
        lax.psum(shares_grads[4].astype(jnp.bfloat16), "slide").astype(jnp.float32),
        lax.psum(shares_grads[5].astype(jnp.bfloat16), "slide").astype(jnp.float32),
        lax.psum(shares_grads[6].astype(jnp.bfloat16), "slide").astype(jnp.float32),
        lax.psum(shares_grads[7].astype(jnp.bfloat16), "slide").astype(jnp.float32),
        lax.psum(shares_grads[8].astype(jnp.bfloat16), "slide").astype(jnp.float32),
        lax.psum(shares_grads[9].astype(jnp.bfloat16), "slide").astype(jnp.float32),
        lax.psum(shares_grads[10].astype(jnp.bfloat16), "slide").astype(jnp.float32),
        lax.psum(shares_grads[11].astype(jnp.bfloat16), "slide").astype(jnp.float32),
        lax.psum(shares_grads[12].astype(jnp.bfloat16), "slide").astype(jnp.float32),
        lax.psum(shares_grads[13].astype(jnp.bfloat16), "slide").astype(jnp.float32),
        lax.psum(shares_grads[14].astype(jnp.bfloat16), "slide").astype(jnp.float32),
        lax.psum(shares_grads[15].astype(jnp.bfloat16), "slide").astype(jnp.float32),
    )
    return (decoded[None], divergence, table_grad) + tuple(summed)


def fits(mesh):
    return mesh.shape["slide"] == 4 and mesh.shape["blk"] == 8


def flipped(index, mask):
    for bit in (1, 2, 4):
        if mask & bit:
            index = index + bit - 2 * bit * ((index // bit) % 2)
    return index


def greet(slide, blk, peers):
    barrier = pltpu.get_barrier_semaphore()
    for far_slide, far_blk in peers:
        pl.semaphore_signal(
            barrier,
            inc=1,
            device_id={"slide": flipped(slide, far_slide), "blk": flipped(blk, far_blk)},
            device_id_type=MESH,
        )
    pl.semaphore_wait(barrier, len(peers))


def gather_blocks(slide, blk, out_ref, send_sem, recv_sem):
    copies = {}

    def push(rel_slide, rel_blk, to_slide, to_blk):
        slot = flipped(slide, rel_slide) * 8 + flipped(blk, rel_blk)
        key = (rel_slide ^ to_slide) * 8 + (rel_blk ^ to_blk)
        copies[key] = pltpu.make_async_remote_copy(
            src_ref=out_ref.at[slot],
            dst_ref=out_ref.at[slot],
            send_sem=send_sem.at[key],
            recv_sem=recv_sem.at[key],
            device_id={"slide": flipped(slide, to_slide), "blk": flipped(blk, to_blk)},
            device_id_type=MESH,
        )
        copies[key].start()

    for far in (2, 4, 6):
        push(0, 0, 0, far)
    push(0, 0, 0, 1)
    push(0, 0, 2, 0)
    push(0, 0, 1, 0)
    for rel in (2, 4, 6):
        copies[rel].wait_recv()
        push(0, rel, 0, 1)
        push(0, rel, 2, 0)
        push(0, rel, 1, 0)
    for rel in (1, 3, 5, 7):
        copies[rel].wait_recv()
        push(0, rel, 2, 0)
        push(0, rel, 1, 0)
    for rel in (0, 2, 4, 6, 1, 3, 5, 7):
        copies[16 + rel].wait_recv()
        push(2, rel, 1, 0)
    for rel in (0, 2, 4, 6, 1, 3, 5, 7):
        copies[8 + rel].wait_recv()
    for rel in (0, 2, 4, 6, 1, 3, 5, 7):
        copies[24 + rel].wait_recv()
    for key in sorted(copies):
        copies[key].wait_send()


GATHER_PEERS = [(0, 1), (0, 2), (0, 4), (0, 6), (2, 0), (1, 0)]
BLK_PEERS = [(0, far) for far in range(1, 8)]
SLIDE_PEERS = [(far, 0) for far in range(1, 4)]


def panel_kernel(part_ref, out_ref, land, send_one, recv_one, send_sem, recv_sem):
    slide, blk = lax.axis_index("slide"), lax.axis_index("blk")
    greet(slide, blk, BLK_PEERS + [(2, 0), (1, 0)])
    copies = []
    for far in range(1, 8):
        target = flipped(blk, far)
        copies.append(
            pltpu.make_async_remote_copy(
                src_ref=part_ref.at[target],
                dst_ref=land.at[far],
                send_sem=send_one.at[far],
                recv_sem=recv_one.at[far],
                device_id={"slide": slide, "blk": target},
                device_id_type=MESH,
            )
        )
        copies[-1].start()
    total = part_ref[blk].astype(F32)
    for far in range(1, 8):
        copies[far - 1].wait_recv()
        total = total + land[far].astype(F32)
    out_ref[slide * 8 + blk] = total.astype(BF16)
    gather_blocks(slide, blk, out_ref, send_sem, recv_sem)
    for copy in copies:
        copy.wait_send()


def panel_rows(part):
    _, rows, width = part.shape
    return pl.pallas_call(
        panel_kernel,
        out_shape=jax.ShapeDtypeStruct((32, rows, width), BF16),
        in_specs=[pl.BlockSpec(memory_space=pltpu.VMEM)],
        out_specs=pl.BlockSpec(memory_space=pltpu.VMEM),
        scratch_shapes=[
            pltpu.VMEM((8, rows, width), BF16),
            pltpu.SemaphoreType.DMA((8,)),
            pltpu.SemaphoreType.DMA((8,)),
            pltpu.SemaphoreType.DMA((32,)),
            pltpu.SemaphoreType.DMA((32,)),
        ],
        compiler_params=pltpu.CompilerParams(
            collective_id=1, has_side_effects=True, vmem_limit_bytes=32 << 20
        ),
        name="panel_rows",
    )(part)


def gather_kernel(block_ref, out_ref, send_sem, recv_sem):
    slide, blk = lax.axis_index("slide"), lax.axis_index("blk")
    greet(slide, blk, GATHER_PEERS)
    out_ref[slide * 8 + blk] = block_ref[...]
    gather_blocks(slide, blk, out_ref, send_sem, recv_sem)


def gather_everywhere(block):
    return pl.pallas_call(
        gather_kernel,
        out_shape=jax.ShapeDtypeStruct((32,) + block.shape, block.dtype),
        in_specs=[pl.BlockSpec(memory_space=pltpu.VMEM)],
        out_specs=pl.BlockSpec(memory_space=pltpu.VMEM),
        scratch_shapes=[
            pltpu.SemaphoreType.DMA((32,)),
            pltpu.SemaphoreType.DMA((32,)),
        ],
        compiler_params=pltpu.CompilerParams(
            collective_id=2, has_side_effects=True, vmem_limit_bytes=32 << 20
        ),
        name="gather_everywhere",
    )(block)


def exchange(slide, blk, peers, source_of, land, place, send_sem, recv_sem):
    copies = []
    for number, (far_slide, far_blk) in enumerate(peers):
        to_slide, to_blk = flipped(slide, far_slide), flipped(blk, far_blk)
        copies.append(
            pltpu.make_async_remote_copy(
                src_ref=source_of(to_slide, to_blk),
                dst_ref=land.at[place],
                send_sem=send_sem.at[number],
                recv_sem=recv_sem.at[number],
                device_id={"slide": to_slide, "blk": to_blk},
                device_id_type=MESH,
            )
        )
        copies[-1].start()
    return copies


def sum_all_kernel(in_ref, out_ref, land_one, land_two, own, send_one, recv_one, send_two, recv_two):
    slide, blk = lax.axis_index("slide"), lax.axis_index("blk")
    greet(slide, blk, SLIDE_PEERS + BLK_PEERS)
    copies = exchange(slide, blk, SLIDE_PEERS, lambda *_: in_ref, land_one, slide, send_one, recv_one)
    land_one[slide] = in_ref[...]
    for copy in copies:
        copy.wait()
    own[...] = (land_one[0] + land_one[1]) + (land_one[2] + land_one[3])
    copies = exchange(slide, blk, BLK_PEERS, lambda *_: own, land_two, blk, send_two, recv_two)
    land_two[blk] = own[...]
    for copy in copies:
        copy.wait()
    total = land_two[0]
    for place in range(1, 8):
        total = total + land_two[place]
    out_ref[...] = total


def sum_all(block):
    return pl.pallas_call(
        sum_all_kernel,
        out_shape=jax.ShapeDtypeStruct(block.shape, F32),
        in_specs=[pl.BlockSpec(memory_space=pltpu.VMEM)],
        out_specs=pl.BlockSpec(memory_space=pltpu.VMEM),
        scratch_shapes=[
            pltpu.VMEM((4,) + block.shape, F32),
            pltpu.VMEM((8,) + block.shape, F32),
            pltpu.VMEM(block.shape, F32),
            pltpu.SemaphoreType.DMA((3,)),
            pltpu.SemaphoreType.DMA((3,)),
            pltpu.SemaphoreType.DMA((7,)),
            pltpu.SemaphoreType.DMA((7,)),
        ],
        compiler_params=pltpu.CompilerParams(collective_id=3, has_side_effects=True),
        name="sum_all",
    )(block)


def sum_parts_kernel(in_ref, out_ref, land_one, land_two, own, send_one, recv_one, send_two, recv_two):
    slide, blk = lax.axis_index("slide"), lax.axis_index("blk")
    greet(slide, blk, SLIDE_PEERS + BLK_PEERS)
    copies = exchange(
        slide, blk, BLK_PEERS, lambda _, to_blk: in_ref.at[to_blk], land_one, blk, send_two, recv_two
    )
    land_one[blk] = in_ref[blk]
    for copy in copies:
        copy.wait()
    total = land_one[0]
    for place in range(1, 8):
        total = total + land_one[place]
    own[...] = total
    copies = exchange(slide, blk, SLIDE_PEERS, lambda *_: own, land_two, slide, send_one, recv_one)
    land_two[slide] = total
    for copy in copies:
        copy.wait()
    out_ref[...] = (land_two[0] + land_two[1]) + (land_two[2] + land_two[3])


def sum_parts(parts):
    shape = parts.shape[1:]
    return pl.pallas_call(
        sum_parts_kernel,
        out_shape=jax.ShapeDtypeStruct(shape, F32),
        in_specs=[pl.BlockSpec(memory_space=pltpu.VMEM)],
        out_specs=pl.BlockSpec(memory_space=pltpu.VMEM),
        scratch_shapes=[
            pltpu.VMEM((8,) + shape, F32),
            pltpu.VMEM((4,) + shape, F32),
            pltpu.VMEM(shape, F32),
            pltpu.SemaphoreType.DMA((3,)),
            pltpu.SemaphoreType.DMA((3,)),
            pltpu.SemaphoreType.DMA((7,)),
            pltpu.SemaphoreType.DMA((7,)),
        ],
        compiler_params=pltpu.CompilerParams(collective_id=4, has_side_effects=True),
        name="sum_parts",
    )(parts)


def dot_nt(left, right):
    return lax.dot_general(left, right, (((1,), (1,)), ((), ())), preferred_element_type=F32)


def dot_tn(left, right):
    return lax.dot_general(left, right, (((0,), (0,)), ((), ())), preferred_element_type=F32)


def head_scores(query, key, same_slide):
    scores = jnp.where(same_slide, dot_nt(query, key) * (HEAD_DIM**-0.5), -1e30)
    shifted = jnp.exp(scores - jnp.max(scores, axis=1, keepdims=True))
    return shifted / jnp.sum(shifted, axis=1, keepdims=True)


def attend_kernel(q_ref, k_ref, v_ref, row_ref, col_ref, out_ref):
    same_slide = row_ref[...] == col_ref[...]
    lanes = lax.broadcasted_iota(jnp.int32, q_ref.shape, 1)
    query, key, value = q_ref[...], k_ref[...], v_ref[...]
    out = None
    for head in range(q_ref.shape[1] // HEAD_DIM):
        mine = lanes // HEAD_DIM == head
        shares = head_scores(jnp.where(mine, query, 0), key, same_slide)
        part = jnp.dot(shares.astype(BF16), value, preferred_element_type=F32)
        out = part if out is None else jnp.where(mine, part, out)
    out_ref[...] = out.astype(BF16)


def attend(query, key, value, row_labels, col_labels, rows=256):
    count, width = query.shape
    whole = pl.BlockSpec((count, width), lambda i: (0, 0))
    part = pl.BlockSpec((rows, width), lambda i: (i, 0))
    return pl.pallas_call(
        attend_kernel,
        grid=(count // rows,),
        out_shape=jax.ShapeDtypeStruct((count, width), BF16),
        in_specs=[
            part,
            whole,
            whole,
            pl.BlockSpec((rows, 1), lambda i: (i, 0)),
            pl.BlockSpec((1, count), lambda i: (0, 0)),
        ],
        out_specs=part,
        compiler_params=pltpu.CompilerParams(vmem_limit_bytes=48 << 20),
        cost_estimate=pl.CostEstimate(
            flops=8 * count * count * width, bytes_accessed=8 * count * width, transcendentals=0
        ),
        name="attend",
    )(query, key, value, row_labels, col_labels)


def attend_back_kernel(q_ref, g_ref, k_ref, v_ref, row_ref, col_ref, dq_ref, dk_ref, dv_ref, dk_sum, dv_sum):
    step = pl.program_id(0)

    @pl.when(step == 0)
    def _():
        dk_sum[...] = jnp.zeros_like(dk_sum)
        dv_sum[...] = jnp.zeros_like(dv_sum)

    scale = HEAD_DIM**-0.5
    same_slide = row_ref[...] == col_ref[...]
    lanes = lax.broadcasted_iota(jnp.int32, q_ref.shape, 1)
    query, grad, key, value = q_ref[...], g_ref[...], k_ref[...], v_ref[...]
    grad_query = None
    for head in range(q_ref.shape[1] // HEAD_DIM):
        mine = lanes // HEAD_DIM == head
        own_query = jnp.where(mine, query, 0)
        own_grad = jnp.where(mine, grad, 0)
        shares = head_scores(own_query, key, same_slide)
        grad_shares = dot_nt(own_grad, value)
        inner = jnp.sum(shares * grad_shares, axis=1, keepdims=True)
        grad_scores = (shares * (grad_shares - inner)).astype(BF16)
        part = jnp.dot(grad_scores, key, preferred_element_type=F32)
        grad_query = part if grad_query is None else jnp.where(mine, part, grad_query)
        dk_sum[...] += dot_tn(grad_scores, own_query)
        dv_sum[...] += dot_tn(shares.astype(BF16), own_grad)
    dq_ref[...] = (grad_query * scale).astype(BF16)

    @pl.when(step == pl.num_programs(0) - 1)
    def _():
        dk_ref[...] = (dk_sum[...] * scale).astype(BF16)
        dv_ref[...] = dv_sum[...].astype(BF16)


def attend_back(query, grad, key, value, row_labels, col_labels, rows=256):
    count, width = query.shape
    whole = pl.BlockSpec((count, width), lambda i: (0, 0))
    part = pl.BlockSpec((rows, width), lambda i: (i, 0))
    shape = jax.ShapeDtypeStruct((count, width), BF16)
    return pl.pallas_call(
        attend_back_kernel,
        grid=(count // rows,),
        out_shape=(shape, shape, shape),
        in_specs=[
            part,
            part,
            whole,
            whole,
            pl.BlockSpec((rows, 1), lambda i: (i, 0)),
            pl.BlockSpec((1, count), lambda i: (0, 0)),
        ],
        out_specs=(part, whole, whole),
        scratch_shapes=[pltpu.VMEM((count, width), F32), pltpu.VMEM((count, width), F32)],
        compiler_params=pltpu.CompilerParams(vmem_limit_bytes=48 << 20),
        cost_estimate=pl.CostEstimate(
            flops=20 * count * count * width, bytes_accessed=14 * count * width, transcendentals=0
        ),
        name="attend_back",
    )(query, grad, key, value, row_labels, col_labels)


def over_slide(array, mask):
    return lax.ppermute(array, "slide", [(place, place ^ mask) for place in range(4)])


def over_blk(array, mask):
    return lax.ppermute(array, "blk", [(place, place ^ mask) for place in range(8)])


def gather_slide(array):
    far = over_slide(array, 2)
    return [array, over_slide(array, 1), far, over_slide(far, 1)]


def swap_slide(pick, slide):
    return [pick(slide)] + [over_slide(pick(jnp.bitwise_xor(slide, far)), far) for far in (1, 2, 3)]


def in_order(parts, index):
    low = jnp.bitwise_and(index, 1) == 1
    high = jnp.bitwise_and(index, 2) == 2
    one = [jnp.where(low, parts[j ^ 1], parts[j]) for j in range(4)]
    return [jnp.where(high, one[j ^ 2], one[j]) for j in range(4)]


def reduce_blk(left, right, blk):
    cells, total_rows = left.shape
    rows = total_rows // 8
    shaped = left.reshape(cells, 4, 2, rows)
    along_x = blk % 2
    along_z = blk // 2

    def half(which):
        columns = lax.dynamic_index_in_dim(shaped, which, 2, keepdims=False).reshape(cells, 4 * rows)
        return dot_tn(columns, right)

    away = over_blk(half(1 - along_x).astype(BF16), 1)
    kept = (half(along_x) + away.astype(F32)).astype(BF16).reshape(4, rows, right.shape[1])

    def piece(which):
        return lax.dynamic_index_in_dim(kept, which, 0, keepdims=False)

    total = piece(along_z).astype(F32)
    for far in (1, 2, 3):
        total = total + over_blk(piece(jnp.bitwise_xor(along_z, far)), 2 * far).astype(F32)
    return total.astype(BF16)


def on_device_fast(
    counts,
    library,
    gene_ids,
    positions,
    slide_of_cell,
    latent_noise,
    decoded_grad,
    gene_table,
    first_gain,
    first_shift,
    query_weight,
    key_weight,
    value_weight,
    output_weight,
    second_gain,
    second_shift,
    hidden_weight,
    hidden_bias,
    down_weight,
    down_bias,
    mean_weight,
    logvar_weight,
    component_means,
    decoder_weight,
    divergence_weight,
    free_floor,
):
    cells = counts.shape[1]
    width = gene_table.shape[1]
    genes = gene_ids.shape[0]
    latents = mean_weight.shape[1]
    inner = hidden_weight.shape[1]
    slide, blk = lax.axis_index("slide"), lax.axis_index("blk")
    per = width // 8

    def columns(array, start, size):
        return lax.dynamic_slice_in_dim(array, start, size, 1)

    table_rows = gene_table.shape[0]
    first_row = blk * table_rows
    row_ids = first_row + jnp.arange(table_rows, dtype=jnp.int32)
    my_ids = lax.dynamic_slice_in_dim(gene_ids, slide * (genes // 4), genes // 4, 0)
    selector = (my_ids[:, None] == row_ids[None, :]).astype(BF16)
    part = matmul(selector, gene_table).astype(BF16).reshape(8, genes // 32, width)
    panel_weight = panel_rows(part).reshape(genes, width)

    express = normalized(counts[0], library[0]).astype(BF16)
    hidden_start = matmul(express, panel_weight) + position_code(positions[0], width)
    normed_one = layer_norm(hidden_start, first_gain, first_shift).astype(BF16)

    def to_blocks(array):
        return array.reshape(cells, 8, per).transpose(1, 0, 2)

    def from_blocks(array):
        return array.transpose(1, 0, 2).reshape(cells, 8 * per)

    labels = jnp.broadcast_to(
        jnp.pad(slide_of_cell[0].astype(BF16), (0, per - cells))[None, None, :], (8, 16, per)
    )
    qkv = jnp.concatenate(
        [to_blocks(matmul(normed_one, w).astype(BF16)) for w in (query_weight, key_weight, value_weight)]
        + [labels],
        axis=1,
    )
    qkv = lax.all_to_all(qkv, "blk", 0, 0)
    query, key, value = [
        qkv[:, i * cells : (i + 1) * cells].reshape(8 * cells, per) for i in range(3)
    ]
    labels_all = qkv[:, 3 * cells, :cells].reshape(8 * cells).astype(F32)
    row_labels, col_labels = labels_all[:, None], labels_all[None, :]
    attended = attend(query, key, value, row_labels, col_labels)
    attended = from_blocks(lax.all_to_all(attended.reshape(8, cells, per), "blk", 0, 0))

    hidden_middle = hidden_start + matmul(attended, output_weight)
    normed_two = layer_norm(hidden_middle, second_gain, second_shift).astype(BF16)
    inner_sum = matmul(normed_two, hidden_weight) + hidden_bias
    act_low = gelu_tanh(inner_sum).astype(BF16)
    hidden_final = hidden_middle + matmul(act_low, down_weight) + down_bias
    base_low = hidden_final.astype(BF16)
    mean_lat = matmul(base_low, mean_weight)
    log_var = matmul(base_low, logvar_weight)
    noise_local = latent_noise[0]

    def bottleneck(mean_part, logvar_part, centres):
        return (
            mean_part + jnp.exp(0.5 * logvar_part) * noise_local,
            divergence_cells(mean_part, logvar_part, centres),
        )

    (latent, kl_cell), pull_latent = jax.vjp(bottleneck, mean_lat, log_var, component_means)
    latent_low = latent.astype(BF16)
    decoded = matmul(latent_low, decoder_weight)
    everyone = cells * 32
    kl_rows = jnp.pad(jnp.sum(kl_cell, axis=0).reshape(-1, 128), ((0, 8 - latents // 128), (0, 0)))
    kl_mean = sum_all(kl_rows)[: latents // 128].reshape(latents) / everyone
    divergence = divergence_weight * jnp.mean(jnp.maximum(kl_mean, free_floor))
    binding = (kl_mean > free_floor).astype(F32)
    grad_source = decoded_grad[0]

    whole_fwd = jnp.concatenate([express, normed_one, attended, normed_two, base_low, latent_low], axis=1)
    whole_fwd = jnp.concatenate(gather_slide(whole_fwd), axis=0)
    express_all, normed_one_all, attended_all, normed_two_all, base_all = [
        whole_fwd[:, i * width : (i + 1) * width] for i in range(5)
    ]
    latent_all = whole_fwd[:, 5 * width :]
    act_parts = act_low.reshape(cells, 8, 4, inner // 32)

    def pick_fwd(which):
        act = lax.dynamic_index_in_dim(act_parts, which, 2, keepdims=False).reshape(cells, inner // 4)
        return jnp.concatenate([act, columns(grad_source, which * (genes // 4), genes // 4)], axis=1)

    quarter_fwd = jnp.concatenate(swap_slide(pick_fwd, slide), axis=0)
    act_all, source_all = quarter_fwd[:, : inner // 4], quarter_fwd[:, inner // 4 :]

    grad_latent = matmul(grad_source, decoder_weight.T)
    grad_kl = jnp.broadcast_to(divergence_weight * binding, kl_cell.shape)
    grad_mean, grad_logvar, centres_grad = pull_latent((grad_latent, grad_kl))
    grad_mean_low = grad_mean.astype(BF16)
    grad_logvar_low = grad_logvar.astype(BF16)
    grad_final = matmul(grad_mean_low, mean_weight.T) + matmul(grad_logvar_low, logvar_weight.T)
    grad_branch = grad_final.astype(BF16)
    down_bias_grad = jnp.sum(grad_branch.astype(F32), axis=0)
    branch_all = jnp.concatenate(gather_slide(grad_branch), axis=0)
    lat_quarter = latents // 4

    def pick_lat(which):
        return jnp.concatenate(
            [
                columns(grad_mean_low, which * lat_quarter, lat_quarter),
                columns(grad_logvar_low, which * lat_quarter, lat_quarter),
            ],
            axis=1,
        )

    lat_all = jnp.concatenate(swap_slide(pick_lat, slide), axis=0)
    down_sum = reduce_blk(act_all, branch_all, blk)
    lat_sum = reduce_blk(base_all, lat_all, blk)
    decoder_sum = reduce_blk(latent_all, source_all, blk)

    grad_act = matmul(grad_branch, down_weight.T)
    gelu_pull = jax.vjp(gelu_tanh, inner_sum)[1]
    grad_inner = gelu_pull(grad_act)[0].astype(BF16)
    hidden_bias_grad = jnp.sum(grad_inner.astype(F32), axis=0)
    norm_two_pull = jax.vjp(layer_norm, hidden_middle, second_gain, second_shift)[1]
    grad_norm_two, second_gain_grad, second_shift_grad = norm_two_pull(matmul(grad_inner, hidden_weight.T))
    grad_middle = grad_final + grad_norm_two
    grad_out = grad_middle.astype(BF16)
    inner_all = jnp.concatenate(
        swap_slide(lambda which: columns(grad_inner, which * (inner // 4), inner // 4), slide), axis=0
    )
    hidden_sum = reduce_blk(normed_two_all, inner_all, blk)
    out_all = jnp.concatenate(
        swap_slide(lambda which: columns(grad_out, which * (width // 4), width // 4), slide), axis=0
    )
    output_sum = reduce_blk(attended_all, out_all, blk)

    grad_attended = matmul(grad_out, output_weight.T).astype(BF16)
    grad_heads = lax.all_to_all(to_blocks(grad_attended), "blk", 0, 0).reshape(8 * cells, per)
    grads = attend_back(query, grad_heads, key, value, row_labels, col_labels)
    grads = jnp.concatenate([grad.reshape(8, cells, per) for grad in grads], axis=1)
    grads = lax.all_to_all(grads, "blk", 0, 0)
    grad_query, grad_key, grad_value = [
        from_blocks(grads[:, i * cells : (i + 1) * cells]) for i in range(3)
    ]
    grad_norm_input = (
        matmul(grad_query, query_weight.T) + matmul(grad_key, key_weight.T) + matmul(grad_value, value_weight.T)
    )
    norm_one_pull = jax.vjp(layer_norm, hidden_start, first_gain, first_shift)[1]
    grad_norm_one, first_gain_grad, first_shift_grad = norm_one_pull(grad_norm_input)
    grad_encoded = (grad_middle + grad_norm_one).astype(BF16)
    quarter = width // 4

    def pick_qkv(which):
        return jnp.concatenate(
            [columns(grad, which * quarter, quarter) for grad in (grad_query, grad_key, grad_value)], axis=1
        )

    qkv_all = jnp.concatenate(swap_slide(pick_qkv, slide), axis=0)
    encoded_all = jnp.concatenate(
        swap_slide(lambda which: columns(grad_encoded, which * quarter, quarter), slide), axis=0
    )
    panel_sum = reduce_blk(express_all, encoded_all, blk)
    qkv_sum = reduce_blk(normed_one_all, qkv_all, blk)

    panel_all = gather_everywhere(panel_sum).reshape(4, genes, quarter)
    spread = (row_ids[:, None] == gene_ids[None, :]).astype(BF16)
    table_grad = jnp.concatenate([matmul(spread, panel_all[i]) for i in range(4)], axis=1)

    small = jnp.concatenate(
        [
            item.reshape(8, -1, 128)
            for item in (
                first_gain_grad,
                first_shift_grad,
                second_gain_grad,
                second_shift_grad,
                hidden_bias_grad,
                down_bias_grad,
                centres_grad.reshape(16, 8, -1).transpose(1, 0, 2),
            )
        ],
        axis=1,
    )
    count = small.shape[1]
    small = sum_parts(jnp.pad(small, ((0, 0), (0, -count % 8), (0, 0))))
    bias_rows = inner // 8 // 128
    small_gain_one, small_shift_one, small_gain_two, small_shift_two = [
        small[i] for i in range(4)
    ]
    small_hidden = small[4 : 4 + bias_rows].reshape(-1)
    small_down = small[4 + bias_rows]
    small_centres = small[5 + bias_rows : count].reshape(16, -1)

    def wide(total):
        return jnp.concatenate(in_order([p.astype(F32) for p in gather_slide(total)], slide), axis=1)

    def tall(total):
        return jnp.concatenate(in_order([p.astype(F32) for p in gather_slide(total)], slide), axis=0)

    def split(total, sizes):
        parts = in_order([p.astype(F32) for p in gather_slide(total)], slide)
        outs, start = [], 0
        for size in sizes:
            outs.append(jnp.concatenate([p[:, start : start + size] for p in parts], axis=1))
            start += size
        return outs

    query_grad, key_grad, value_grad = split(qkv_sum, [quarter] * 3)
    mean_grad, logvar_grad = split(lat_sum, [lat_quarter] * 2)
    return (
        decoded[None],
        divergence,
        table_grad,
        small_gain_one,
        small_shift_one,
        query_grad,
        key_grad,
        value_grad,
        wide(output_sum),
        small_gain_two,
        small_shift_two,
        wide(hidden_sum),
        small_hidden,
        tall(down_sum),
        small_down,
        mean_grad,
        logvar_grad,
        small_centres,
        wide(decoder_sum),
    )


def solution(mesh):
    placed = (
        P("slide", "blk", None),
        P("slide", "blk"),
        P(),
        P("slide", None, "blk"),
        P("slide", "blk"),
        P("slide", "blk", None),
        P("slide", "blk", None),
        P("blk", None),
        P(),
        P(),
        P(),
        P(),
        P(),
        P(),
        P(),
        P(),
        P(),
        P(),
        P(),
        P(),
        P(),
        P(),
        P(),
        P(),
        P(),
        P(),
    )
    return jax.shard_map(
        on_device_fast if fits(mesh) else on_device_general,
        mesh=mesh,
        in_specs=placed,
        out_specs=(
            P("slide", "blk", None),
            P(),
            P("blk", None),
            P("blk"),
            P("blk"),
            P("blk", None),
            P("blk", None),
            P("blk", None),
            P("blk", None),
            P("blk"),
            P("blk"),
            P("blk", None),
            P("blk"),
            P("blk", None),
            P("blk"),
            P("blk", None),
            P("blk", None),
            P(None, "blk"),
            P("blk", None),
        ),
        check_vma=False,
    )
```

```python
import functools
import math

import jax
import jax.numpy as jnp
from jax import lax
from jax.experimental import pallas as pl
from jax.experimental.pallas import tpu as pltpu
from jax.sharding import PartitionSpec as P

HEAD_DIM = 64
MESH = pl.DeviceIdType.MESH
F32 = jnp.float32
BF16 = jnp.bfloat16


def normalized(counts, library):
    scaled = counts.astype(jnp.float32) * (10000.0 / library.astype(jnp.float32))[..., None]
    return jnp.log1p(scaled)


def position_code(coords, model_width):
    quarter = model_width // 4
    freqs = jnp.exp(-math.log(10000.0) * jnp.arange(quarter, dtype=jnp.float32) / quarter)
    along_x = coords[0].astype(jnp.float32)[:, None] * freqs[None, :]
    along_y = coords[1].astype(jnp.float32)[:, None] * freqs[None, :]
    return jnp.concatenate(
        [jnp.sin(along_x), jnp.cos(along_x), jnp.sin(along_y), jnp.cos(along_y)], axis=1
    )


def layer_norm(inputs, scaling, offsets):
    centre = inputs - jnp.mean(inputs, axis=-1, keepdims=True)
    spread = jnp.mean(centre * centre, axis=-1, keepdims=True)
    return centre * lax.rsqrt(spread + 1e-05) * scaling + offsets


def gelu_tanh(inputs):
    return (
        0.5
        * inputs
        * (1.0 + jnp.tanh(0.7978845608028654 * (inputs + 0.044715 * inputs * inputs * inputs)))
    )


def divergence_cells(mean_part, logvar_part, centres):
    latent_width = mean_part.shape[-1]
    crossed = jnp.dot(mean_part, centres.T, precision=lax.Precision.HIGHEST)
    centre_square = jnp.sum(centres * centres, axis=-1)
    logits = (crossed - 0.5 * centre_square[None, :]) / math.sqrt(latent_width)
    shifted = jnp.exp(logits - jnp.max(logits, axis=-1, keepdims=True))
    resp = shifted / jnp.sum(shifted, axis=-1, keepdims=True)
    mixed = jnp.dot(resp, centres, precision=lax.Precision.HIGHEST)
    mixed_square = jnp.dot(resp, centres * centres, precision=lax.Precision.HIGHEST)
    return 0.5 * (
        jnp.exp(logvar_part)
        - 1.0
        - logvar_part
        + mean_part * mean_part
        - 2.0 * mean_part * mixed
        + mixed_square
    )


def to_heads(array, head_count):
    return array.reshape(array.shape[0], head_count, -1).transpose(1, 0, 2)


def from_heads(array):
    return array.transpose(1, 0, 2).reshape(array.shape[1], -1)


def matmul(left, right):
    return jnp.dot(left, right, preferred_element_type=jnp.float32)


def on_device_general(
    counts,
    library,
    gene_ids,
    positions,
    slide_of_cell,
    latent_noise,
    decoded_grad,
    gene_table,
    first_gain,
    first_shift,
    query_weight,
    key_weight,
    value_weight,
    output_weight,
    second_gain,
    second_shift,
    hidden_weight,
    hidden_bias,
    down_weight,
    down_bias,
    mean_weight,
    logvar_weight,
    component_means,
    decoder_weight,
    divergence_weight,
    free_floor,
):
    cell_count = counts.shape[1]
    model_width = gene_table.shape[1]
    head_count = model_width // HEAD_DIM
    score_scale = HEAD_DIM ** (-0.5)
    express = normalized(counts[0], library[0]).astype(jnp.bfloat16)
    table_rows = gene_table.shape[0]
    first_row = lax.axis_index("blk") * table_rows
    selector = (
        gene_ids[:, None] == first_row + jnp.arange(table_rows, dtype=jnp.int32)[None, :]
    ).astype(jnp.bfloat16)
    panel_part = matmul(selector, gene_table)
    panel_weight = lax.psum(panel_part, "blk").astype(jnp.bfloat16)
    hidden_start = matmul(express, panel_weight) + position_code(positions[0], model_width)
    normed_one = layer_norm(hidden_start, first_gain, first_shift).astype(jnp.bfloat16)
    query_low = matmul(normed_one, query_weight).astype(jnp.bfloat16)
    key_low = matmul(normed_one, key_weight).astype(jnp.bfloat16)
    value_low = matmul(normed_one, value_weight).astype(jnp.bfloat16)
    slide_labels = slide_of_cell[0].astype(jnp.bfloat16)
    keys_all, values_all, labels_all = (
        lax.all_gather(key_low, "blk", axis=0, tiled=True),
        lax.all_gather(value_low, "blk", axis=0, tiled=True),
        lax.all_gather(slide_labels, "blk", axis=0, tiled=True),
    )
    same_slide = slide_labels[:, None] == labels_all[None, :]
    query_heads = to_heads(query_low, head_count)
    key_heads = to_heads(keys_all, head_count)
    value_heads = to_heads(values_all, head_count)

    def head_forward(head_items):
        query_head, key_head, value_head = head_items
        scores = (
            jnp.einsum("qd,kd->qk", query_head, key_head, preferred_element_type=jnp.float32)
            * score_scale
        )
        scores = jnp.where(same_slide, scores, -1e30)
        row_max = jnp.max(scores, axis=1, keepdims=True)
        shifted = jnp.exp(scores - row_max)
        row_sum = jnp.sum(shifted, axis=1, keepdims=True)
        shares = shifted / row_sum
        attended_head = jnp.einsum(
            "qk,kd->qd", shares.astype(jnp.bfloat16), value_head, preferred_element_type=jnp.float32
        )
        return (attended_head, row_max[:, 0], row_sum[:, 0])

    attended_heads, row_maxes, row_sums = lax.map(
        head_forward, (query_heads, key_heads, value_heads)
    )
    attended = from_heads(attended_heads).astype(jnp.bfloat16)
    hidden_middle = hidden_start + matmul(attended, output_weight)
    normed_two = layer_norm(hidden_middle, second_gain, second_shift).astype(jnp.bfloat16)
    inner_sum = matmul(normed_two, hidden_weight) + hidden_bias
    act_low = gelu_tanh(inner_sum).astype(jnp.bfloat16)
    hidden_final = hidden_middle + matmul(act_low, down_weight) + down_bias
    base_low = hidden_final.astype(jnp.bfloat16)
    mean_lat = matmul(base_low, mean_weight)
    log_var = matmul(base_low, logvar_weight)
    noise_local = latent_noise[0]

    def bottleneck(mean_part, logvar_part, centres):
        return (
            mean_part + jnp.exp(0.5 * logvar_part) * noise_local,
            divergence_cells(mean_part, logvar_part, centres),
        )

    (latent, kl_cell), pull_latent = jax.vjp(bottleneck, mean_lat, log_var, component_means)
    latent_low = latent.astype(jnp.bfloat16)
    decoded = matmul(latent_low, decoder_weight)
    everyone = cell_count * lax.axis_size("blk") * lax.axis_size("slide")
    kl_sum = lax.psum(jnp.sum(kl_cell, axis=0), ("slide", "blk"))
    kl_mean = kl_sum / everyone
    divergence = divergence_weight * jnp.mean(jnp.maximum(kl_mean, free_floor))
    binding = (kl_mean > free_floor).astype(jnp.float32)
    grad_source = decoded_grad[0]
    grad_latent = matmul(grad_source, decoder_weight.T)
    decoder_grad = matmul(latent_low.T, grad_source)
    grad_kl = jnp.broadcast_to(divergence_weight * binding, kl_cell.shape)
    grad_mean, grad_logvar, centres_grad = pull_latent((grad_latent, grad_kl))
    grad_mean_low = grad_mean.astype(jnp.bfloat16)
    grad_logvar_low = grad_logvar.astype(jnp.bfloat16)
    mean_grad = matmul(base_low.T, grad_mean_low)
    logvar_grad = matmul(base_low.T, grad_logvar_low)
    grad_final = matmul(grad_mean_low, mean_weight.T) + matmul(grad_logvar_low, logvar_weight.T)
    grad_branch = grad_final.astype(jnp.bfloat16)
    down_grad = matmul(act_low.T, grad_branch)
    down_bias_grad = jnp.sum(grad_branch.astype(jnp.float32), axis=0)
    grad_act = matmul(grad_branch, down_weight.T)
    gelu_pull = jax.vjp(gelu_tanh, inner_sum)[1]
    grad_inner = gelu_pull(grad_act)[0].astype(jnp.bfloat16)
    hidden_grad = matmul(normed_two.T, grad_inner)
    hidden_bias_grad = jnp.sum(grad_inner.astype(jnp.float32), axis=0)
    norm_two_pull = jax.vjp(layer_norm, hidden_middle, second_gain, second_shift)[1]
    grad_norm_two, second_gain_grad, second_shift_grad = norm_two_pull(
        matmul(grad_inner, hidden_weight.T)
    )
    grad_middle = grad_final + grad_norm_two
    grad_out = grad_middle.astype(jnp.bfloat16)
    output_grad = matmul(attended.T, grad_out)
    grad_attended = matmul(grad_out, output_weight.T).astype(jnp.bfloat16)
    keys_again, values_again = (
        lax.all_gather(key_low, "blk", axis=0, tiled=True),
        lax.all_gather(value_low, "blk", axis=0, tiled=True),
    )
    key_heads_back = to_heads(keys_again, head_count)
    value_heads_back = to_heads(values_again, head_count)
    grad_heads_local = to_heads(grad_attended, head_count)

    def head_queries(head_items):
        query_head, key_head, value_head, grad_head, row_max, row_sum = head_items
        scores = (
            jnp.einsum("qd,kd->qk", query_head, key_head, preferred_element_type=jnp.float32)
            * score_scale
        )
        scores = jnp.where(same_slide, scores, -1e30)
        shares = jnp.exp(scores - row_max[:, None]) / row_sum[:, None]
        grad_shares = jnp.einsum(
            "qd,kd->qk", grad_head, value_head, preferred_element_type=jnp.float32
        )
        inner_dot = jnp.sum(shares * grad_shares, axis=1, keepdims=True)
        grad_scores = (shares * (grad_shares - inner_dot)).astype(jnp.bfloat16)
        grad_query_head = (
            jnp.einsum("qk,kd->qd", grad_scores, key_head, preferred_element_type=jnp.float32)
            * score_scale
        )
        return (grad_query_head, inner_dot[:, 0])

    grad_query_heads, inner_dots = lax.map(
        head_queries,
        (query_heads, key_heads_back, value_heads_back, grad_heads_local, row_maxes, row_sums),
    )
    queries_group, grads_group = (
        lax.all_gather(query_low, "blk", axis=0, tiled=True),
        lax.all_gather(grad_attended, "blk", axis=0, tiled=True),
    )
    maxes_group, totals_group, dots_group = (
        lax.all_gather(row_maxes, "blk", axis=1, tiled=True),
        lax.all_gather(row_sums, "blk", axis=1, tiled=True),
        lax.all_gather(inner_dots, "blk", axis=1, tiled=True),
    )
    mask_back = labels_all[:, None] == slide_labels[None, :]

    def head_keys(head_items):
        query_head, key_head, value_head, grad_head, row_max, row_sum, inner_dot = head_items
        scores = (
            jnp.einsum("qd,kd->qk", query_head, key_head, preferred_element_type=jnp.float32)
            * score_scale
        )
        scores = jnp.where(mask_back, scores, -1e30)
        shares = jnp.exp(scores - row_max[:, None]) / row_sum[:, None]
        grad_shares = jnp.einsum(
            "qd,kd->qk", grad_head, value_head, preferred_element_type=jnp.float32
        )
        grad_scores = (shares * (grad_shares - inner_dot[:, None])).astype(jnp.bfloat16)
        grad_key_head = (
            jnp.einsum("qk,qd->kd", grad_scores, query_head, preferred_element_type=jnp.float32)
            * score_scale
        )
        grad_value_head = jnp.einsum(
            "qk,qd->kd", shares.astype(jnp.bfloat16), grad_head, preferred_element_type=jnp.float32
        )
        return (grad_key_head, grad_value_head)

    grad_key_heads, grad_value_heads = lax.map(
        head_keys,
        (
            to_heads(queries_group, head_count),
            to_heads(key_low, head_count),
            to_heads(value_low, head_count),
            to_heads(grads_group, head_count),
            maxes_group,
            totals_group,
            dots_group,
        ),
    )
    grad_query_low = from_heads(grad_query_heads).astype(jnp.bfloat16)
    grad_key = from_heads(grad_key_heads)
    grad_value = from_heads(grad_value_heads)
    grad_key_low = grad_key.astype(jnp.bfloat16)
    grad_value_low = grad_value.astype(jnp.bfloat16)
    query_grad = matmul(normed_one.T, grad_query_low)
    key_grad = matmul(normed_one.T, grad_key_low)
    value_grad = matmul(normed_one.T, grad_value_low)
    grad_norm_input = (
        matmul(grad_query_low, query_weight.T)
        + matmul(grad_key_low, key_weight.T)
        + matmul(grad_value_low, value_weight.T)
    )
    norm_one_pull = jax.vjp(layer_norm, hidden_start, first_gain, first_shift)[1]
    grad_norm_one, first_gain_grad, first_shift_grad = norm_one_pull(grad_norm_input)
    grad_start = grad_middle + grad_norm_one
    grad_encoded = grad_start.astype(jnp.bfloat16)
    panel_grad = matmul(express.T, grad_encoded)
    panel_total = lax.psum(panel_grad, ("slide", "blk"))
    table_grad = jnp.dot(
        selector.astype(jnp.float32).T, panel_total, precision=lax.Precision.HIGHEST
    )
    shares_grads = (
        lax.psum_scatter(first_gain_grad, "blk", scatter_dimension=0, tiled=True),
        lax.psum_scatter(first_shift_grad, "blk", scatter_dimension=0, tiled=True),
        lax.psum_scatter(query_grad, "blk", scatter_dimension=0, tiled=True),
        lax.psum_scatter(key_grad, "blk", scatter_dimension=0, tiled=True),
        lax.psum_scatter(value_grad, "blk", scatter_dimension=0, tiled=True),
        lax.psum_scatter(output_grad, "blk", scatter_dimension=0, tiled=True),
        lax.psum_scatter(second_gain_grad, "blk", scatter_dimension=0, tiled=True),
        lax.psum_scatter(second_shift_grad, "blk", scatter_dimension=0, tiled=True),
        lax.psum_scatter(hidden_grad, "blk", scatter_dimension=0, tiled=True),
        lax.psum_scatter(hidden_bias_grad, "blk", scatter_dimension=0, tiled=True),
        lax.psum_scatter(down_grad, "blk", scatter_dimension=0, tiled=True),
        lax.psum_scatter(down_bias_grad, "blk", scatter_dimension=0, tiled=True),
        lax.psum_scatter(mean_grad, "blk", scatter_dimension=0, tiled=True),
        lax.psum_scatter(logvar_grad, "blk", scatter_dimension=0, tiled=True),
        lax.psum_scatter(centres_grad, "blk", scatter_dimension=1, tiled=True),
        lax.psum_scatter(decoder_grad, "blk", scatter_dimension=0, tiled=True),
    )
    summed = (
        lax.psum(shares_grads[0].astype(jnp.bfloat16), "slide").astype(jnp.float32),
        lax.psum(shares_grads[1].astype(jnp.bfloat16), "slide").astype(jnp.float32),
        lax.psum(shares_grads[2].astype(jnp.bfloat16), "slide").astype(jnp.float32),
        lax.psum(shares_grads[3].astype(jnp.bfloat16), "slide").astype(jnp.float32),
        lax.psum(shares_grads[4].astype(jnp.bfloat16), "slide").astype(jnp.float32),
        lax.psum(shares_grads[5].astype(jnp.bfloat16), "slide").astype(jnp.float32),
        lax.psum(shares_grads[6].astype(jnp.bfloat16), "slide").astype(jnp.float32),
        lax.psum(shares_grads[7].astype(jnp.bfloat16), "slide").astype(jnp.float32),
        lax.psum(shares_grads[8].astype(jnp.bfloat16), "slide").astype(jnp.float32),
        lax.psum(shares_grads[9].astype(jnp.bfloat16), "slide").astype(jnp.float32),
        lax.psum(shares_grads[10].astype(jnp.bfloat16), "slide").astype(jnp.float32),
        lax.psum(shares_grads[11].astype(jnp.bfloat16), "slide").astype(jnp.float32),
        lax.psum(shares_grads[12].astype(jnp.bfloat16), "slide").astype(jnp.float32),
        lax.psum(shares_grads[13].astype(jnp.bfloat16), "slide").astype(jnp.float32),
        lax.psum(shares_grads[14].astype(jnp.bfloat16), "slide").astype(jnp.float32),
        lax.psum(shares_grads[15].astype(jnp.bfloat16), "slide").astype(jnp.float32),
    )
    return (decoded[None], divergence, table_grad) + tuple(summed)


def fits(mesh):
    return mesh.shape["slide"] == 4 and mesh.shape["blk"] == 8


def flipped(index, mask):
    for bit in (1, 2, 4):
        if mask & bit:
            index = index + bit - 2 * bit * ((index // bit) % 2)
    return index


def greet(slide, blk, peers):
    barrier = pltpu.get_barrier_semaphore()
    for far_slide, far_blk in peers:
        pl.semaphore_signal(
            barrier,
            inc=1,
            device_id={"slide": flipped(slide, far_slide), "blk": flipped(blk, far_blk)},
            device_id_type=MESH,
        )
    pl.semaphore_wait(barrier, len(peers))


BLK_PEERS = [(0, far) for far in range(1, 8)]
SLIDE_PEERS = [(far, 0) for far in range(1, 4)]


def panel_kernel(part_ref, out_ref, land, send_sem, recv_sem):
    slide, blk = lax.axis_index("slide"), lax.axis_index("blk")
    greet(slide, blk, BLK_PEERS + [(2, 0), (1, 0)])
    links = Links(slide, blk, send_sem, recv_sem)
    copies = [links.send(part_ref.at[flipped(blk, far)], land.at[far], 0, far) for far in range(1, 8)]
    total = part_ref[blk].astype(F32)
    for far in range(1, 8):
        copies[far - 1].wait_recv()
        total = total + land[far].astype(F32)
    out_ref[slide * 8 + blk] = total.astype(BF16)
    for _ in spread_everywhere(links, lambda far_slide, far_blk: out_ref.at[far_slide * 8 + far_blk]):
        pass
    links.finish()


def panel_rows(part):
    _, rows, width = part.shape
    return pl.pallas_call(
        panel_kernel,
        out_shape=jax.ShapeDtypeStruct((32, rows, width), BF16),
        in_specs=[pl.BlockSpec(memory_space=pltpu.VMEM)],
        out_specs=pl.BlockSpec(memory_space=pltpu.VMEM),
        scratch_shapes=[
            pltpu.VMEM((8, rows, width), BF16),
            pltpu.SemaphoreType.DMA((38,)),
            pltpu.SemaphoreType.DMA((38,)),
        ],
        compiler_params=pltpu.CompilerParams(
            collective_id=1, has_side_effects=True, vmem_limit_bytes=32 << 20
        ),
        name="panel_rows",
    )(part)


def exchange(slide, blk, peers, source_of, land, place, send_sem, recv_sem):
    copies = []
    for number, (far_slide, far_blk) in enumerate(peers):
        to_slide, to_blk = flipped(slide, far_slide), flipped(blk, far_blk)
        copies.append(
            pltpu.make_async_remote_copy(
                src_ref=source_of(to_slide, to_blk),
                dst_ref=land.at[place],
                send_sem=send_sem.at[number],
                recv_sem=recv_sem.at[number],
                device_id={"slide": to_slide, "blk": to_blk},
                device_id_type=MESH,
            )
        )
        copies[-1].start()
    return copies


def sum_all_kernel(in_ref, out_ref, land_one, land_two, own, send_one, recv_one, send_two, recv_two):
    slide, blk = lax.axis_index("slide"), lax.axis_index("blk")
    greet(slide, blk, SLIDE_PEERS + BLK_PEERS)
    copies = exchange(slide, blk, SLIDE_PEERS, lambda *_: in_ref, land_one, slide, send_one, recv_one)
    land_one[slide] = in_ref[...]
    for copy in copies:
        copy.wait()
    own[...] = (land_one[0] + land_one[1]) + (land_one[2] + land_one[3])
    copies = exchange(slide, blk, BLK_PEERS, lambda *_: own, land_two, blk, send_two, recv_two)
    land_two[blk] = own[...]
    for copy in copies:
        copy.wait()
    total = land_two[0]
    for place in range(1, 8):
        total = total + land_two[place]
    out_ref[...] = total


def sum_all(block):
    return pl.pallas_call(
        sum_all_kernel,
        out_shape=jax.ShapeDtypeStruct(block.shape, F32),
        in_specs=[pl.BlockSpec(memory_space=pltpu.VMEM)],
        out_specs=pl.BlockSpec(memory_space=pltpu.VMEM),
        scratch_shapes=[
            pltpu.VMEM((4,) + block.shape, F32),
            pltpu.VMEM((8,) + block.shape, F32),
            pltpu.VMEM(block.shape, F32),
            pltpu.SemaphoreType.DMA((3,)),
            pltpu.SemaphoreType.DMA((3,)),
            pltpu.SemaphoreType.DMA((7,)),
            pltpu.SemaphoreType.DMA((7,)),
        ],
        compiler_params=pltpu.CompilerParams(collective_id=3, has_side_effects=True),
        name="sum_all",
    )(block)


def dot_nt(left, right):
    return lax.dot_general(left, right, (((1,), (1,)), ((), ())), preferred_element_type=F32)


def dot_tn(left, right):
    return lax.dot_general(left, right, (((0,), (0,)), ((), ())), preferred_element_type=F32)


def head_scores(query, key, same_slide):
    scores = jnp.where(same_slide, dot_nt(query, key) * (HEAD_DIM**-0.5), -1e30)
    shifted = jnp.exp(scores - jnp.max(scores, axis=1, keepdims=True))
    return shifted / jnp.sum(shifted, axis=1, keepdims=True)


def attend_kernel(q_ref, k_ref, v_ref, row_ref, col_ref, out_ref):
    same_slide = row_ref[...] == col_ref[...]
    lanes = lax.broadcasted_iota(jnp.int32, q_ref.shape, 1)
    query, key, value = q_ref[...], k_ref[...], v_ref[...]
    out = None
    for head in range(q_ref.shape[1] // HEAD_DIM):
        mine = lanes // HEAD_DIM == head
        shares = head_scores(jnp.where(mine, query, 0), key, same_slide)
        part = jnp.dot(shares.astype(BF16), value, preferred_element_type=F32)
        out = part if out is None else jnp.where(mine, part, out)
    out_ref[...] = out.astype(BF16)


def attend(query, key, value, row_labels, col_labels, rows=256):
    count, width = query.shape
    whole = pl.BlockSpec((count, width), lambda i: (0, 0))
    part = pl.BlockSpec((rows, width), lambda i: (i, 0))
    return pl.pallas_call(
        attend_kernel,
        grid=(count // rows,),
        out_shape=jax.ShapeDtypeStruct((count, width), BF16),
        in_specs=[
            part,
            whole,
            whole,
            pl.BlockSpec((rows, 1), lambda i: (i, 0)),
            pl.BlockSpec((1, count), lambda i: (0, 0)),
        ],
        out_specs=part,
        compiler_params=pltpu.CompilerParams(vmem_limit_bytes=48 << 20),
        cost_estimate=pl.CostEstimate(
            flops=8 * count * count * width, bytes_accessed=8 * count * width, transcendentals=0
        ),
        name="attend",
    )(query, key, value, row_labels, col_labels)


class Links:
    def __init__(self, slide, blk, send_sem, recv_sem):
        self.slide, self.blk = slide, blk
        self.send_sem, self.recv_sem = send_sem, recv_sem
        self.copies = []

    def send(self, source, target, far_slide, far_blk):
        number = len(self.copies)
        copy = pltpu.make_async_remote_copy(
            src_ref=source,
            dst_ref=target,
            send_sem=self.send_sem.at[number],
            recv_sem=self.recv_sem.at[number],
            device_id={
                "slide": flipped(self.slide, far_slide),
                "blk": flipped(self.blk, far_blk),
            },
            device_id_type=MESH,
        )
        copy.start()
        self.copies.append(copy)
        return copy

    def finish(self):
        for copy in self.copies:
            copy.wait_send()


def spread_everywhere(links, slot):
    slide, blk = links.slide, links.blk
    copies = {}

    def push(rel_slide, rel_blk, to_slide, to_blk):
        block = slot(flipped(slide, rel_slide), flipped(blk, rel_blk))
        copies[(rel_slide ^ to_slide, rel_blk ^ to_blk)] = links.send(block, block, to_slide, to_blk)

    for far in (2, 4, 6):
        push(0, 0, 0, far)
    push(0, 0, 0, 1)
    push(0, 0, 2, 0)
    push(0, 0, 1, 0)
    yield
    for rel in (2, 4, 6):
        copies[0, rel].wait_recv()
        push(0, rel, 0, 1)
        push(0, rel, 2, 0)
        push(0, rel, 1, 0)
    yield
    for rel in (1, 3, 5, 7):
        copies[0, rel].wait_recv()
        push(0, rel, 2, 0)
        push(0, rel, 1, 0)
    yield
    for rel in (0, 2, 4, 6, 1, 3, 5, 7):
        copies[2, rel].wait_recv()
        push(2, rel, 1, 0)
    yield
    for far in (1, 3):
        for rel in (0, 2, 4, 6, 1, 3, 5, 7):
            copies[far, rel].wait_recv()
    yield


class Reduction:
    def __init__(self, links, left, right, rows, width, dense, buffers):
        self.links, self.left, self.right = links, left, right
        self.rows, self.width, self.dense = rows, width, dense
        self.away, self.came, self.kept, self.pieces = buffers
        self.along_x, self.along_z = links.blk % 2, links.blk // 2

    def tiles(self, which, store):
        def tile(i, carry):
            place = which * 2 + i if self.dense else i * 2 + which
            product = dot_tn(self.left(pl.multiple_of(place * 128, 128)), self.right())
            store(pl.ds(pl.multiple_of(i * 128, 128), 128), product)
            return carry

        lax.fori_loop(0, self.rows * 4 // 128, tile, 0)

    def send_x(self):
        def store(where, product):
            self.away[where, :] = product.astype(BF16)

        self.tiles(1 - self.along_x, store)
        self.copy_x = self.links.send(self.away, self.came, 0, 1)

    def send_z(self):
        self.copy_x.wait_recv()

        def store(where, product):
            self.kept[where, :] = (product + self.came[where, :].astype(F32)).astype(BF16)

        self.tiles(self.along_x, store)
        self.copies_z = []
        for far in (2, 1, 3):
            target = pl.multiple_of(flipped(self.along_z, far) * self.rows, self.rows)
            self.copies_z.append(
                self.links.send(self.kept.at[pl.ds(target, self.rows)], self.pieces.at[far - 1], 0, 2 * far)
            )

    def total(self):
        for copy in self.copies_z:
            copy.wait_recv()
        own = self.kept[pl.ds(pl.multiple_of(self.along_z * self.rows, self.rows), self.rows), :]
        return (
            (own.astype(F32) + self.pieces[0].astype(F32))
            + (self.pieces[1].astype(F32) + self.pieces[2].astype(F32))
        ).astype(BF16)


def spread_slide(links, slot, total):
    slide = links.slide
    own, far = slot(slide), slot(flipped(slide, 2))
    own[...] = total
    across = links.send(own, own, 2, 0)
    beside = links.send(own, own, 1, 0)
    yield
    across.wait_recv()
    last = links.send(far, far, 1, 0)
    yield
    beside.wait_recv()
    last.wait_recv()
    yield


def reductions_of(cells, width, inner, latents):
    return [
        ("decoder", latents // 8, width // 4, True),
        ("down0", inner // 32, width // 2, False),
        ("down1", inner // 32, width // 2, False),
        ("mean", width // 8, latents // 4, False),
        ("logvar", width // 8, latents // 4, False),
        ("hidden0", width // 8, inner // 8, False),
        ("hidden1", width // 8, inner // 8, False),
        ("output", width // 8, width // 4, False),
        ("panel", width // 8, width // 4, False),
        ("query", width // 8, width // 4, False),
        ("key", width // 8, width // 4, False),
        ("value", width // 8, width // 4, False),
    ]


def backward_kernel(
    q_ref, k_ref, v_ref, row_ref, col_ref, branch_ref, gmean_ref, glogvar_ref, ginner_ref, gout_ref,
    middle_ref, start_ref, gain_ref, small_ref,
    whole0, whole1, whole2, whole3, quarter0, quarter1, quarter2, quarter3, wq_hbm, wk_hbm, wv_hbm, wo_hbm,
    panel_out, query_out, key_out, value_out, output_out, hidden_out, down_out, mean_out, logvar_out, decoder_out, small_out,
    whole, quarter, wq, wk, wv, wo, branch_all, gmean_all, glogvar_all, ginner_all, gout_all, gqkv_all, genc_all,
    att_send, att_land, dqkv, dqkv_land, dk_sum, dv_sum, grad_qkv, encoded, small, small_land, small_own, small_slides,
    load_sem, send_sem, recv_sem, *unit_refs,
):
    slide, blk = lax.axis_index("slide"), lax.axis_index("blk")
    cells, width = middle_ref.shape
    inner, latents, per = ginner_ref.shape[1], gmean_ref.shape[1], width // 8
    loads = {}
    for number, (name, source, target) in enumerate(
        [("wo", wo_hbm, wo)]
        + [("q%d" % i, ref, quarter.at[pl.ds(i * cells, cells)]) for i, ref in enumerate((quarter0, quarter1, quarter2, quarter3))]
        + [("w%d" % i, ref, whole.at[pl.ds(i * cells, cells)]) for i, ref in enumerate((whole0, whole1, whole2, whole3))]
        + [("wq", wq_hbm, wq), ("wk", wk_hbm, wk), ("wv", wv_hbm, wv)]
    ):
        loads[name] = pltpu.make_async_copy(source, target, load_sem.at[number])
        loads[name].start()
    greet(slide, blk, SLIDE_PEERS + BLK_PEERS)
    links = Links(slide, blk, send_sem, recv_sem)

    def lanes(ref, which, size):
        return ref.at[:, pl.ds(pl.multiple_of(which * size, 128), size)]

    def swap(ref, size, target):
        copies = []
        for far in (2, 3, 1):
            copies.append(links.send(lanes(ref, flipped(slide, far), size), target.at[far], far, 0))
        target[0] = lanes(ref, slide, size)[...]
        return copies

    branch_far = links.send(branch_ref, branch_all.at[2], 2, 0)
    branch_near = links.send(branch_ref, branch_all.at[1], 1, 0)
    branch_all[0] = branch_ref[...]
    mean_swap = swap(gmean_ref, latents // 4, gmean_all)
    logvar_swap = swap(glogvar_ref, latents // 4, glogvar_all)
    inner_swap = swap(ginner_ref, inner // 4, ginner_all)
    out_swap = swap(gout_ref, width // 4, gout_all)

    loads["wo"].wait()

    def att_block(target, store):
        rows = wo[pl.ds(pl.multiple_of(target * per, per), per), :]
        store(dot_nt(gout_ref[...], rows).astype(BF16))

    att_copies = []
    for far in (6, 4, 2, 7, 5, 3, 1):
        target = flipped(blk, far)

        def keep(block, far=far):
            att_send[far] = block

        att_block(target, keep)
        att_copies.append(links.send(att_send.at[far], att_land.at[blk], 0, far))

    def keep_own(block):
        att_land[blk] = block

    att_block(blk, keep_own)

    width_at = {"express": 0, "one": width, "attended": 2 * width, "two": 3 * width, "base": 4 * width, "latent": 5 * width}

    def of_whole(name):
        def left(column):
            return whole[:, pl.ds(width_at[name] + column, 128)]

        return left

    def of_act(column):
        return quarter[:, pl.ds(column, 128)]

    def flat(ref, start=None, size=None):
        def right():
            block = ref[...] if start is None else ref[:, :, start : start + size]
            return block.reshape(4 * cells, block.shape[-1])

        return right

    def source_all():
        return quarter[:, inner // 4 :]

    half_w, half_i = width // 2, inner // 8
    operands = {
        "decoder": (of_whole("latent"), source_all),
        "down0": (of_act, flat(branch_all, 0, half_w)),
        "down1": (of_act, flat(branch_all, half_w, half_w)),
        "mean": (of_whole("base"), flat(gmean_all)),
        "logvar": (of_whole("base"), flat(glogvar_all)),
        "hidden0": (of_whole("two"), flat(ginner_all, 0, half_i)),
        "hidden1": (of_whole("two"), flat(ginner_all, half_i, half_i)),
        "output": (of_whole("attended"), flat(gout_all)),
        "panel": (of_whole("express"), flat(genc_all)),
        "query": (of_whole("one"), flat(gqkv_all.at[0])),
        "key": (of_whole("one"), flat(gqkv_all.at[1])),
        "value": (of_whole("one"), flat(gqkv_all.at[2])),
    }
    units = {}
    for number, (name, rows, columns, dense) in enumerate(reductions_of(cells, width, inner, latents)):
        left, right = operands[name]
        units[name] = Reduction(
            links, left, right, rows, columns, dense, unit_refs[4 * number : 4 * number + 4]
        )

    def columns_slot(ref, size, offset=0):
        return lambda place: ref.at[:, pl.ds(pl.multiple_of(place * size + offset, 128), size if not offset else size)]

    slots = {
        "decoder": lambda place: lanes(decoder_out, place, width // 4),
        "down0": lambda place: down_out.at[pl.ds(pl.multiple_of(place * (inner // 32), inner // 32), inner // 32), pl.ds(0, half_w)],
        "down1": lambda place: down_out.at[pl.ds(pl.multiple_of(place * (inner // 32), inner // 32), inner // 32), pl.ds(half_w, half_w)],
        "mean": lambda place: lanes(mean_out, place, latents // 4),
        "logvar": lambda place: lanes(logvar_out, place, latents // 4),
        "hidden0": lambda place: hidden_out.at[:, pl.ds(pl.multiple_of(place * (inner // 4), 128), half_i)],
        "hidden1": lambda place: hidden_out.at[:, pl.ds(pl.multiple_of(place * (inner // 4) + half_i, 128), half_i)],
        "output": lambda place: lanes(output_out, place, width // 4),
        "query": lambda place: lanes(query_out, place, width // 4),
        "key": lambda place: lanes(key_out, place, width // 4),
        "value": lambda place: lanes(value_out, place, width // 4),
    }
    spreads = {}

    def spread(name):
        spreads[name] = spread_slide(links, slots[name], units[name].total())
        next(spreads[name])

    for i in range(4):
        loads["q%d" % i].wait()
    for i in range(4):
        loads["w%d" % i].wait()
    units["decoder"].send_x()
    branch_far.wait_recv()
    branch_last = links.send(branch_all.at[2], branch_all.at[3], 1, 0)
    branch_near.wait_recv()
    branch_last.wait_recv()
    units["down0"].send_x()
    units["down1"].send_x()
    for copy in mean_swap + logvar_swap:
        copy.wait_recv()
    units["mean"].send_x()
    units["logvar"].send_x()

    for copy in att_copies:
        copy.wait_recv()
    dk_sum[...] = jnp.zeros_like(dk_sum)
    dv_sum[...] = jnp.zeros_like(dv_sum)
    scale = HEAD_DIM**-0.5
    rows = 2 * cells

    def rows_back(i, carry):
        where = pl.ds(pl.multiple_of(i * rows, rows), rows)
        same_slide = row_ref[where, :] == col_ref[...]
        query = q_ref[where, :]
        grad = att_land[pl.ds(2 * i, 2)].reshape(rows, per)
        key, value = k_ref[...], v_ref[...]
        lane = lax.broadcasted_iota(jnp.int32, query.shape, 1)
        grad_query = None
        for head in range(per // HEAD_DIM):
            mine = lane // HEAD_DIM == head
            own_query = jnp.where(mine, query, 0)
            own_grad = jnp.where(mine, grad, 0)
            shares = head_scores(own_query, key, same_slide)
            grad_shares = dot_nt(own_grad, value)
            inner_dot = jnp.sum(shares * grad_shares, axis=1, keepdims=True)
            grad_scores = (shares * (grad_shares - inner_dot)).astype(BF16)
            part = jnp.dot(grad_scores, key, preferred_element_type=F32)
            grad_query = part if grad_query is None else jnp.where(mine, part, grad_query)
            dk_sum[...] += dot_tn(grad_scores, own_query)
            dv_sum[...] += dot_tn(shares.astype(BF16), own_grad)
        dqkv[pl.ds(2 * i, 2), 0:cells, :] = (grad_query * scale).astype(BF16).reshape(2, cells, per)
        return carry

    lax.fori_loop(0, 8 * cells // rows, rows_back, 0)
    dqkv[:, cells : 2 * cells, :] = (dk_sum[...] * scale).astype(BF16).reshape(8, cells, per)
    dqkv[:, 2 * cells :, :] = dv_sum[...].astype(BF16).reshape(8, cells, per)
    back_copies = []
    for far in (6, 4, 2, 7, 5, 3, 1):
        back_copies.append(links.send(dqkv.at[flipped(blk, far)], dqkv_land.at[blk], 0, far))
    dqkv_land[blk] = dqkv[blk]

    for copy in inner_swap + out_swap:
        copy.wait_recv()
    units["hidden0"].send_x()
    units["hidden1"].send_x()
    units["output"].send_x()
    units["decoder"].send_z()
    units["down0"].send_z()

    for copy in back_copies:
        copy.wait_recv()
    for name in ("wq", "wk", "wv"):
        loads[name].wait()
    for part in range(3):
        for block in range(8):
            grad_qkv[part, :, block * per : (block + 1) * per] = dqkv_land[block, part * cells : (part + 1) * cells, :]
    qkv_swaps = [swap(grad_qkv.at[part], width // 4, gqkv_all.at[part]) for part in range(3)]

    def norm_input(i, carry):
        where = pl.ds(pl.multiple_of(i * 256, 256), 256)
        encoded_sum = (
            dot_nt(grad_qkv[0], wq[where, :]) + dot_nt(grad_qkv[1], wk[where, :]) + dot_nt(grad_qkv[2], wv[where, :])
        )
        encoded[:, where] = encoded_sum
        return carry

    lax.fori_loop(0, width // 256, norm_input, 0)
    hidden = start_ref[...]
    centre = hidden - jnp.mean(hidden, axis=1, keepdims=True)
    invert = lax.rsqrt(jnp.mean(centre * centre, axis=1, keepdims=True) + 1e-05)
    unit = centre * invert
    grad_normed = encoded[...]
    gain_grad = jnp.sum(grad_normed * unit, axis=0, keepdims=True)
    shift_grad = jnp.sum(grad_normed, axis=0, keepdims=True)
    grad_unit = grad_normed * gain_ref[...]
    grad_hidden = invert * (
        grad_unit
        - jnp.mean(grad_unit, axis=1, keepdims=True)
        - unit * jnp.mean(grad_unit * unit, axis=1, keepdims=True)
    )
    grad_qkv[3] = (middle_ref[...] + grad_hidden).astype(BF16)
    encoded_swap = swap(grad_qkv.at[3], width // 4, genc_all)

    small[...] = small_ref[...]
    for block in range(8):
        small[block, 0:1, :] = gain_grad[:, block * 128 : (block + 1) * 128]
        small[block, 1:2, :] = shift_grad[:, block * 128 : (block + 1) * 128]
    small_copies = [links.send(small.at[flipped(blk, far)], small_land.at[blk], 0, far) for far in range(1, 8)]
    small_land[blk] = small[blk]

    units["down1"].send_z()
    for copy in encoded_swap:
        copy.wait_recv()
    units["panel"].send_x()
    for part in range(3):
        for copy in qkv_swaps[part]:
            copy.wait_recv()
        units[("query", "key", "value")[part]].send_x()
    for copy in small_copies:
        copy.wait_recv()
    small_sum = small_land[0]
    for block in range(1, 8):
        small_sum = small_sum + small_land[block]
    small_own[...] = small_sum
    small_copies = [links.send(small_own, small_slides.at[slide], far, 0) for far in (2, 3, 1)]
    small_slides[slide] = small_sum
    units["mean"].send_z()
    units["logvar"].send_z()
    units["panel"].send_z()
    units["hidden0"].send_z()
    spread("decoder")
    spread("down0")
    spread("down1")

    panel_slot = lambda far_slide, far_blk: panel_out.at[
        pl.ds(pl.multiple_of(far_blk * (width // 8), 128), width // 8),
        pl.ds(pl.multiple_of(far_slide * (width // 4), 128), width // 4),
    ]
    own_slot = panel_slot(slide, blk)
    own_slot[...] = units["panel"].total()
    everywhere = spread_everywhere(links, panel_slot)
    next(everywhere)
    units["hidden1"].send_z()
    units["output"].send_z()
    next(everywhere)
    units["query"].send_z()
    units["key"].send_z()
    units["value"].send_z()
    next(everywhere)
    spread("mean")
    spread("logvar")
    spread("hidden0")
    spread("hidden1")
    next(everywhere)
    spread("output")
    spread("query")
    spread("key")
    spread("value")
    for name in spreads:
        next(spreads[name])
    for copy in small_copies:
        copy.wait_recv()
    small_out[...] = (small_slides[0] + small_slides[1]) + (small_slides[2] + small_slides[3])
    next(everywhere)
    for name in spreads:
        next(spreads[name])
    links.finish()


def backward(inputs, pieces, weights, cells, width, inner, latents, small_rows):
    per = width // 8
    shape = jax.ShapeDtypeStruct
    unit_scratch = []
    for _, rows, columns, _ in reductions_of(cells, width, inner, latents):
        unit_scratch += [pltpu.VMEM((4 * rows, columns), BF16)] * 3 + [pltpu.VMEM((3, rows, columns), BF16)]
    copies = 208
    vmem, left = pl.BlockSpec(memory_space=pltpu.VMEM), pl.BlockSpec(memory_space=pl.ANY)
    outs = (
        shape((width, width), BF16),
        shape((per, width), BF16),
        shape((per, width), BF16),
        shape((per, width), BF16),
        shape((per, width), BF16),
        shape((per, inner), BF16),
        shape((inner // 8, width), BF16),
        shape((per, latents), BF16),
        shape((per, latents), BF16),
        shape((latents // 8, width), BF16),
        shape((small_rows, 128), F32),
    )
    return pl.pallas_call(
        backward_kernel,
        out_shape=outs,
        in_specs=[vmem] * len(inputs) + [left] * (len(pieces) + len(weights)),
        out_specs=[vmem] * len(outs),
        scratch_shapes=[
            pltpu.VMEM((4 * cells, 5 * width + latents), BF16),
            pltpu.VMEM((4 * cells, inner // 4 + width // 4), BF16),
            pltpu.VMEM((width, width), BF16),
            pltpu.VMEM((width, width), BF16),
            pltpu.VMEM((width, width), BF16),
            pltpu.VMEM((width, width), BF16),
            pltpu.VMEM((4, cells, width), BF16),
            pltpu.VMEM((4, cells, latents // 4), BF16),
            pltpu.VMEM((4, cells, latents // 4), BF16),
            pltpu.VMEM((4, cells, inner // 4), BF16),
            pltpu.VMEM((4, cells, width // 4), BF16),
            pltpu.VMEM((3, 4, cells, width // 4), BF16),
            pltpu.VMEM((4, cells, width // 4), BF16),
            pltpu.VMEM((8, cells, per), BF16),
            pltpu.VMEM((8, cells, per), BF16),
            pltpu.VMEM((8, 3 * cells, per), BF16),
            pltpu.VMEM((8, 3 * cells, per), BF16),
            pltpu.VMEM((8 * cells, per), F32),
            pltpu.VMEM((8 * cells, per), F32),
            pltpu.VMEM((4, cells, width), BF16),
            pltpu.VMEM((cells, width), F32),
            pltpu.VMEM((8, small_rows, 128), F32),
            pltpu.VMEM((8, small_rows, 128), F32),
            pltpu.VMEM((small_rows, 128), F32),
            pltpu.VMEM((4, small_rows, 128), F32),
            pltpu.SemaphoreType.DMA((12,)),
            pltpu.SemaphoreType.DMA((copies,)),
            pltpu.SemaphoreType.DMA((copies,)),
        ]
        + unit_scratch,
        compiler_params=pltpu.CompilerParams(
            collective_id=5, has_side_effects=True, vmem_limit_bytes=60 << 20
        ),
        name="backward",
    )(*inputs, *pieces, *weights)


def table_kernel(first_ref, ids_ref, panel_ref, out_ref):
    rows = out_ref.shape[0]
    first = first_ref[0] + pl.program_id(0) * rows
    row_ids = first + lax.broadcasted_iota(jnp.int32, (rows, ids_ref.shape[1]), 0)
    spread = (row_ids == ids_ref[...]).astype(F32).astype(BF16)
    out_ref[...] = jnp.dot(spread, panel_ref[...], preferred_element_type=F32)


def table_rows_grad(first_row, gene_ids, panel, table_rows, rows=256):
    genes, width = panel.shape
    return pl.pallas_call(
        table_kernel,
        grid=(table_rows // rows,),
        out_shape=jax.ShapeDtypeStruct((table_rows, width), F32),
        in_specs=[
            pl.BlockSpec(memory_space=pltpu.SMEM),
            pl.BlockSpec((1, genes), lambda i: (0, 0)),
            pl.BlockSpec((genes, width), lambda i: (0, 0)),
        ],
        out_specs=pl.BlockSpec((rows, width), lambda i: (i, 0)),
        compiler_params=pltpu.CompilerParams(vmem_limit_bytes=40 << 20),
        name="table_rows_grad",
    )(first_row.reshape(1), gene_ids.reshape(1, genes), panel)


def over_slide(array, mask):
    return lax.ppermute(array, "slide", [(place, place ^ mask) for place in range(4)])


def over_blk(array, mask):
    return lax.ppermute(array, "blk", [(place, place ^ mask) for place in range(8)])


def gather_slide(array):
    far = over_slide(array, 2)
    return [array, over_slide(array, 1), far, over_slide(far, 1)]


def swap_slide(pick, slide):
    return [pick(slide)] + [over_slide(pick(jnp.bitwise_xor(slide, far)), far) for far in (1, 2, 3)]


def on_device_fast(
    counts,
    library,
    gene_ids,
    positions,
    slide_of_cell,
    latent_noise,
    decoded_grad,
    gene_table,
    first_gain,
    first_shift,
    query_weight,
    key_weight,
    value_weight,
    output_weight,
    second_gain,
    second_shift,
    hidden_weight,
    hidden_bias,
    down_weight,
    down_bias,
    mean_weight,
    logvar_weight,
    component_means,
    decoder_weight,
    divergence_weight,
    free_floor,
):
    cells = counts.shape[1]
    width = gene_table.shape[1]
    genes = gene_ids.shape[0]
    latents = mean_weight.shape[1]
    inner = hidden_weight.shape[1]
    slide, blk = lax.axis_index("slide"), lax.axis_index("blk")
    per = width // 8

    def columns(array, start, size):
        return lax.dynamic_slice_in_dim(array, start, size, 1)

    table_rows = gene_table.shape[0]
    first_row = blk * table_rows
    row_ids = first_row + jnp.arange(table_rows, dtype=jnp.int32)
    my_ids = lax.dynamic_slice_in_dim(gene_ids, slide * (genes // 4), genes // 4, 0)
    selector = (my_ids[:, None] == row_ids[None, :]).astype(BF16)
    part = matmul(selector, gene_table).astype(BF16).reshape(8, genes // 32, width)
    panel_weight = panel_rows(part).reshape(genes, width)

    express = normalized(counts[0], library[0]).astype(BF16)
    hidden_start = matmul(express, panel_weight) + position_code(positions[0], width)
    normed_one = layer_norm(hidden_start, first_gain, first_shift).astype(BF16)

    def to_blocks(array):
        return array.reshape(cells, 8, per).transpose(1, 0, 2)

    def from_blocks(array):
        return array.transpose(1, 0, 2).reshape(cells, 8 * per)

    labels = jnp.broadcast_to(
        jnp.pad(slide_of_cell[0].astype(BF16), (0, per - cells))[None, None, :], (8, 16, per)
    )
    qkv = jnp.concatenate(
        [to_blocks(matmul(normed_one, w).astype(BF16)) for w in (query_weight, key_weight, value_weight)]
        + [labels],
        axis=1,
    )
    qkv = lax.all_to_all(qkv, "blk", 0, 0)
    query, key, value = [
        qkv[:, i * cells : (i + 1) * cells].reshape(8 * cells, per) for i in range(3)
    ]
    labels_all = qkv[:, 3 * cells, :cells].reshape(8 * cells).astype(F32)
    row_labels, col_labels = labels_all[:, None], labels_all[None, :]
    attended = attend(query, key, value, row_labels, col_labels)
    attended = from_blocks(lax.all_to_all(attended.reshape(8, cells, per), "blk", 0, 0))

    hidden_middle = hidden_start + matmul(attended, output_weight)
    normed_two = layer_norm(hidden_middle, second_gain, second_shift).astype(BF16)
    inner_sum = matmul(normed_two, hidden_weight) + hidden_bias
    act_low = gelu_tanh(inner_sum).astype(BF16)
    hidden_final = hidden_middle + matmul(act_low, down_weight) + down_bias
    base_low = hidden_final.astype(BF16)
    mean_lat = matmul(base_low, mean_weight)
    log_var = matmul(base_low, logvar_weight)
    noise_local = latent_noise[0]

    def bottleneck(mean_part, logvar_part, centres):
        return (
            mean_part + jnp.exp(0.5 * logvar_part) * noise_local,
            divergence_cells(mean_part, logvar_part, centres),
        )

    (latent, kl_cell), pull_latent = jax.vjp(bottleneck, mean_lat, log_var, component_means)
    latent_low = latent.astype(BF16)
    decoded = matmul(latent_low, decoder_weight)
    everyone = cells * 32
    kl_rows = jnp.pad(jnp.sum(kl_cell, axis=0).reshape(-1, 128), ((0, 8 - latents // 128), (0, 0)))
    kl_mean = sum_all(kl_rows)[: latents // 128].reshape(latents) / everyone
    divergence = divergence_weight * jnp.mean(jnp.maximum(kl_mean, free_floor))
    binding = (kl_mean > free_floor).astype(F32)
    grad_source = decoded_grad[0]

    latent_turned = latent_low.reshape(cells, 4, 2, latents // 8).transpose(0, 2, 1, 3).reshape(cells, latents)
    whole_fwd = gather_slide(
        jnp.concatenate([express, normed_one, attended, normed_two, base_low, latent_turned], axis=1)
    )
    act_parts = act_low.reshape(cells, 8, 4, inner // 32)

    def pick_fwd(which):
        act = lax.dynamic_index_in_dim(act_parts, which, 2, keepdims=False).reshape(cells, inner // 4)
        return jnp.concatenate([act, columns(grad_source, which * (genes // 4), genes // 4)], axis=1)

    quarter_fwd = swap_slide(pick_fwd, slide)

    grad_latent = matmul(grad_source, decoder_weight.T)
    grad_kl = jnp.broadcast_to(divergence_weight * binding, kl_cell.shape)
    grad_mean, grad_logvar, centres_grad = pull_latent((grad_latent, grad_kl))
    grad_mean_low = grad_mean.astype(BF16)
    grad_logvar_low = grad_logvar.astype(BF16)
    grad_final = matmul(grad_mean_low, mean_weight.T) + matmul(grad_logvar_low, logvar_weight.T)
    grad_branch = grad_final.astype(BF16)
    down_bias_grad = jnp.sum(grad_branch.astype(F32), axis=0)
    grad_act = matmul(grad_branch, down_weight.T)
    gelu_pull = jax.vjp(gelu_tanh, inner_sum)[1]
    grad_inner = gelu_pull(grad_act)[0].astype(BF16)
    hidden_bias_grad = jnp.sum(grad_inner.astype(F32), axis=0)
    norm_two_pull = jax.vjp(layer_norm, hidden_middle, second_gain, second_shift)[1]
    grad_norm_two, second_gain_grad, second_shift_grad = norm_two_pull(matmul(grad_inner, hidden_weight.T))
    grad_middle = grad_final + grad_norm_two
    grad_out = grad_middle.astype(BF16)

    small = jnp.concatenate(
        [jnp.zeros((8, 2, 128), F32)]
        + [
            item.reshape(8, -1, 128)
            for item in (
                second_gain_grad,
                second_shift_grad,
                hidden_bias_grad,
                down_bias_grad,
                centres_grad.reshape(16, 8, -1).transpose(1, 0, 2),
            )
        ],
        axis=1,
    )
    count = small.shape[1]
    small = jnp.pad(small, ((0, 0), (0, -count % 8), (0, 0)))
    (
        panel_sum, query_grad, key_grad, value_grad, output_grad, hidden_grad, down_grad, mean_grad, logvar_grad,
        decoder_grad, small,
    ) = backward(
        (
            query, key, value, row_labels, col_labels, grad_branch, grad_mean_low, grad_logvar_low, grad_inner, grad_out,
            grad_middle, hidden_start, first_gain[None], small,
        ),
        tuple(whole_fwd) + tuple(quarter_fwd),
        (query_weight, key_weight, value_weight, output_weight),
        cells, width, inner, latents, small.shape[1],
    )
    table_grad = table_rows_grad(first_row, gene_ids, panel_sum, table_rows)
    bias_rows = inner // 8 // 128
    small_hidden = small[4 : 4 + bias_rows].reshape(-1)
    small_down = small[4 + bias_rows]
    small_centres = small[5 + bias_rows : count].reshape(16, -1)
    return (
        decoded[None],
        divergence,
        table_grad,
        small[0],
        small[1],
        query_grad.astype(F32),
        key_grad.astype(F32),
        value_grad.astype(F32),
        output_grad.astype(F32),
        small[2],
        small[3],
        hidden_grad.astype(F32),
        small_hidden,
        down_grad.astype(F32),
        small_down,
        mean_grad.astype(F32),
        logvar_grad.astype(F32),
        small_centres,
        decoder_grad.astype(F32),
    )


def solution(mesh):
    placed = (
        P("slide", "blk", None),
        P("slide", "blk"),
        P(),
        P("slide", None, "blk"),
        P("slide", "blk"),
        P("slide", "blk", None),
        P("slide", "blk", None),
        P("blk", None),
        P(),
        P(),
        P(),
        P(),
        P(),
        P(),
        P(),
        P(),
        P(),
        P(),
        P(),
        P(),
        P(),
        P(),
        P(),
        P(),
        P(),
        P(),
    )
    return jax.shard_map(
        on_device_fast if fits(mesh) else on_device_general,
        mesh=mesh,
        in_specs=placed,
        out_specs=(
            P("slide", "blk", None),
            P(),
            P("blk", None),
            P("blk"),
            P("blk"),
            P("blk", None),
            P("blk", None),
            P("blk", None),
            P("blk", None),
            P("blk"),
            P("blk"),
            P("blk", None),
            P("blk"),
            P("blk", None),
            P("blk"),
            P("blk", None),
            P("blk", None),
            P(None, "blk"),
            P("blk", None),
        ),
        check_vma=False,
    )
```

```python
import functools
import math

import jax
import jax.numpy as jnp
from jax import lax
from jax.experimental import pallas as pl
from jax.experimental.pallas import tpu as pltpu
from jax.sharding import PartitionSpec as P

HEAD_DIM = 64
MESH = pl.DeviceIdType.MESH
F32 = jnp.float32
BF16 = jnp.bfloat16


def normalized(counts, library):
    scaled = counts.astype(jnp.float32) * (10000.0 / library.astype(jnp.float32))[..., None]
    return jnp.log1p(scaled)


def position_code(coords, model_width):
    quarter = model_width // 4
    freqs = jnp.exp(-math.log(10000.0) * jnp.arange(quarter, dtype=jnp.float32) / quarter)
    along_x = coords[0].astype(jnp.float32)[:, None] * freqs[None, :]
    along_y = coords[1].astype(jnp.float32)[:, None] * freqs[None, :]
    return jnp.concatenate(
        [jnp.sin(along_x), jnp.cos(along_x), jnp.sin(along_y), jnp.cos(along_y)], axis=1
    )


def layer_norm(inputs, scaling, offsets):
    centre = inputs - jnp.mean(inputs, axis=-1, keepdims=True)
    spread = jnp.mean(centre * centre, axis=-1, keepdims=True)
    return centre * lax.rsqrt(spread + 1e-05) * scaling + offsets


def gelu_tanh(inputs):
    return (
        0.5
        * inputs
        * (1.0 + jnp.tanh(0.7978845608028654 * (inputs + 0.044715 * inputs * inputs * inputs)))
    )


def divergence_cells(mean_part, logvar_part, centres):
    latent_width = mean_part.shape[-1]
    crossed = jnp.dot(mean_part, centres.T, precision=lax.Precision.HIGHEST)
    centre_square = jnp.sum(centres * centres, axis=-1)
    logits = (crossed - 0.5 * centre_square[None, :]) / math.sqrt(latent_width)
    shifted = jnp.exp(logits - jnp.max(logits, axis=-1, keepdims=True))
    resp = shifted / jnp.sum(shifted, axis=-1, keepdims=True)
    mixed = jnp.dot(resp, centres, precision=lax.Precision.HIGHEST)
    mixed_square = jnp.dot(resp, centres * centres, precision=lax.Precision.HIGHEST)
    return 0.5 * (
        jnp.exp(logvar_part)
        - 1.0
        - logvar_part
        + mean_part * mean_part
        - 2.0 * mean_part * mixed
        + mixed_square
    )


def to_heads(array, head_count):
    return array.reshape(array.shape[0], head_count, -1).transpose(1, 0, 2)


def from_heads(array):
    return array.transpose(1, 0, 2).reshape(array.shape[1], -1)


def matmul(left, right):
    return jnp.dot(left, right, preferred_element_type=jnp.float32)


def on_device_general(
    counts,
    library,
    gene_ids,
    positions,
    slide_of_cell,
    latent_noise,
    decoded_grad,
    gene_table,
    first_gain,
    first_shift,
    query_weight,
    key_weight,
    value_weight,
    output_weight,
    second_gain,
    second_shift,
    hidden_weight,
    hidden_bias,
    down_weight,
    down_bias,
    mean_weight,
    logvar_weight,
    component_means,
    decoder_weight,
    divergence_weight,
    free_floor,
):
    cell_count = counts.shape[1]
    model_width = gene_table.shape[1]
    head_count = model_width // HEAD_DIM
    score_scale = HEAD_DIM ** (-0.5)
    express = normalized(counts[0], library[0]).astype(jnp.bfloat16)
    table_rows = gene_table.shape[0]
    first_row = lax.axis_index("blk") * table_rows
    selector = (
        gene_ids[:, None] == first_row + jnp.arange(table_rows, dtype=jnp.int32)[None, :]
    ).astype(jnp.bfloat16)
    panel_part = matmul(selector, gene_table)
    panel_weight = lax.psum(panel_part, "blk").astype(jnp.bfloat16)
    hidden_start = matmul(express, panel_weight) + position_code(positions[0], model_width)
    normed_one = layer_norm(hidden_start, first_gain, first_shift).astype(jnp.bfloat16)
    query_low = matmul(normed_one, query_weight).astype(jnp.bfloat16)
    key_low = matmul(normed_one, key_weight).astype(jnp.bfloat16)
    value_low = matmul(normed_one, value_weight).astype(jnp.bfloat16)
    slide_labels = slide_of_cell[0].astype(jnp.bfloat16)
    keys_all, values_all, labels_all = (
        lax.all_gather(key_low, "blk", axis=0, tiled=True),
        lax.all_gather(value_low, "blk", axis=0, tiled=True),
        lax.all_gather(slide_labels, "blk", axis=0, tiled=True),
    )
    same_slide = slide_labels[:, None] == labels_all[None, :]
    query_heads = to_heads(query_low, head_count)
    key_heads = to_heads(keys_all, head_count)
    value_heads = to_heads(values_all, head_count)

    def head_forward(head_items):
        query_head, key_head, value_head = head_items
        scores = (
            jnp.einsum("qd,kd->qk", query_head, key_head, preferred_element_type=jnp.float32)
            * score_scale
        )
        scores = jnp.where(same_slide, scores, -1e30)
        row_max = jnp.max(scores, axis=1, keepdims=True)
        shifted = jnp.exp(scores - row_max)
        row_sum = jnp.sum(shifted, axis=1, keepdims=True)
        shares = shifted / row_sum
        attended_head = jnp.einsum(
            "qk,kd->qd", shares.astype(jnp.bfloat16), value_head, preferred_element_type=jnp.float32
        )
        return (attended_head, row_max[:, 0], row_sum[:, 0])

    attended_heads, row_maxes, row_sums = lax.map(
        head_forward, (query_heads, key_heads, value_heads)
    )
    attended = from_heads(attended_heads).astype(jnp.bfloat16)
    hidden_middle = hidden_start + matmul(attended, output_weight)
    normed_two = layer_norm(hidden_middle, second_gain, second_shift).astype(jnp.bfloat16)
    inner_sum = matmul(normed_two, hidden_weight) + hidden_bias
    act_low = gelu_tanh(inner_sum).astype(jnp.bfloat16)
    hidden_final = hidden_middle + matmul(act_low, down_weight) + down_bias
    base_low = hidden_final.astype(jnp.bfloat16)
    mean_lat = matmul(base_low, mean_weight)
    log_var = matmul(base_low, logvar_weight)
    noise_local = latent_noise[0]

    def bottleneck(mean_part, logvar_part, centres):
        return (
            mean_part + jnp.exp(0.5 * logvar_part) * noise_local,
            divergence_cells(mean_part, logvar_part, centres),
        )

    (latent, kl_cell), pull_latent = jax.vjp(bottleneck, mean_lat, log_var, component_means)
    latent_low = latent.astype(jnp.bfloat16)
    decoded = matmul(latent_low, decoder_weight)
    everyone = cell_count * lax.axis_size("blk") * lax.axis_size("slide")
    kl_sum = lax.psum(jnp.sum(kl_cell, axis=0), ("slide", "blk"))
    kl_mean = kl_sum / everyone
    divergence = divergence_weight * jnp.mean(jnp.maximum(kl_mean, free_floor))
    binding = (kl_mean > free_floor).astype(jnp.float32)
    grad_source = decoded_grad[0]
    grad_latent = matmul(grad_source, decoder_weight.T)
    decoder_grad = matmul(latent_low.T, grad_source)
    grad_kl = jnp.broadcast_to(divergence_weight * binding, kl_cell.shape)
    grad_mean, grad_logvar, centres_grad = pull_latent((grad_latent, grad_kl))
    grad_mean_low = grad_mean.astype(jnp.bfloat16)
    grad_logvar_low = grad_logvar.astype(jnp.bfloat16)
    mean_grad = matmul(base_low.T, grad_mean_low)
    logvar_grad = matmul(base_low.T, grad_logvar_low)
    grad_final = matmul(grad_mean_low, mean_weight.T) + matmul(grad_logvar_low, logvar_weight.T)
    grad_branch = grad_final.astype(jnp.bfloat16)
    down_grad = matmul(act_low.T, grad_branch)
    down_bias_grad = jnp.sum(grad_branch.astype(jnp.float32), axis=0)
    grad_act = matmul(grad_branch, down_weight.T)
    gelu_pull = jax.vjp(gelu_tanh, inner_sum)[1]
    grad_inner = gelu_pull(grad_act)[0].astype(jnp.bfloat16)
    hidden_grad = matmul(normed_two.T, grad_inner)
    hidden_bias_grad = jnp.sum(grad_inner.astype(jnp.float32), axis=0)
    norm_two_pull = jax.vjp(layer_norm, hidden_middle, second_gain, second_shift)[1]
    grad_norm_two, second_gain_grad, second_shift_grad = norm_two_pull(
        matmul(grad_inner, hidden_weight.T)
    )
    grad_middle = grad_final + grad_norm_two
    grad_out = grad_middle.astype(jnp.bfloat16)
    output_grad = matmul(attended.T, grad_out)
    grad_attended = matmul(grad_out, output_weight.T).astype(jnp.bfloat16)
    keys_again, values_again = (
        lax.all_gather(key_low, "blk", axis=0, tiled=True),
        lax.all_gather(value_low, "blk", axis=0, tiled=True),
    )
    key_heads_back = to_heads(keys_again, head_count)
    value_heads_back = to_heads(values_again, head_count)
    grad_heads_local = to_heads(grad_attended, head_count)

    def head_queries(head_items):
        query_head, key_head, value_head, grad_head, row_max, row_sum = head_items
        scores = (
            jnp.einsum("qd,kd->qk", query_head, key_head, preferred_element_type=jnp.float32)
            * score_scale
        )
        scores = jnp.where(same_slide, scores, -1e30)
        shares = jnp.exp(scores - row_max[:, None]) / row_sum[:, None]
        grad_shares = jnp.einsum(
            "qd,kd->qk", grad_head, value_head, preferred_element_type=jnp.float32
        )
        inner_dot = jnp.sum(shares * grad_shares, axis=1, keepdims=True)
        grad_scores = (shares * (grad_shares - inner_dot)).astype(jnp.bfloat16)
        grad_query_head = (
            jnp.einsum("qk,kd->qd", grad_scores, key_head, preferred_element_type=jnp.float32)
            * score_scale
        )
        return (grad_query_head, inner_dot[:, 0])

    grad_query_heads, inner_dots = lax.map(
        head_queries,
        (query_heads, key_heads_back, value_heads_back, grad_heads_local, row_maxes, row_sums),
    )
    queries_group, grads_group = (
        lax.all_gather(query_low, "blk", axis=0, tiled=True),
        lax.all_gather(grad_attended, "blk", axis=0, tiled=True),
    )
    maxes_group, totals_group, dots_group = (
        lax.all_gather(row_maxes, "blk", axis=1, tiled=True),
        lax.all_gather(row_sums, "blk", axis=1, tiled=True),
        lax.all_gather(inner_dots, "blk", axis=1, tiled=True),
    )
    mask_back = labels_all[:, None] == slide_labels[None, :]

    def head_keys(head_items):
        query_head, key_head, value_head, grad_head, row_max, row_sum, inner_dot = head_items
        scores = (
            jnp.einsum("qd,kd->qk", query_head, key_head, preferred_element_type=jnp.float32)
            * score_scale
        )
        scores = jnp.where(mask_back, scores, -1e30)
        shares = jnp.exp(scores - row_max[:, None]) / row_sum[:, None]
        grad_shares = jnp.einsum(
            "qd,kd->qk", grad_head, value_head, preferred_element_type=jnp.float32
        )
        grad_scores = (shares * (grad_shares - inner_dot[:, None])).astype(jnp.bfloat16)
        grad_key_head = (
            jnp.einsum("qk,qd->kd", grad_scores, query_head, preferred_element_type=jnp.float32)
            * score_scale
        )
        grad_value_head = jnp.einsum(
            "qk,qd->kd", shares.astype(jnp.bfloat16), grad_head, preferred_element_type=jnp.float32
        )
        return (grad_key_head, grad_value_head)

    grad_key_heads, grad_value_heads = lax.map(
        head_keys,
        (
            to_heads(queries_group, head_count),
            to_heads(key_low, head_count),
            to_heads(value_low, head_count),
            to_heads(grads_group, head_count),
            maxes_group,
            totals_group,
            dots_group,
        ),
    )
    grad_query_low = from_heads(grad_query_heads).astype(jnp.bfloat16)
    grad_key = from_heads(grad_key_heads)
    grad_value = from_heads(grad_value_heads)
    grad_key_low = grad_key.astype(jnp.bfloat16)
    grad_value_low = grad_value.astype(jnp.bfloat16)
    query_grad = matmul(normed_one.T, grad_query_low)
    key_grad = matmul(normed_one.T, grad_key_low)
    value_grad = matmul(normed_one.T, grad_value_low)
    grad_norm_input = (
        matmul(grad_query_low, query_weight.T)
        + matmul(grad_key_low, key_weight.T)
        + matmul(grad_value_low, value_weight.T)
    )
    norm_one_pull = jax.vjp(layer_norm, hidden_start, first_gain, first_shift)[1]
    grad_norm_one, first_gain_grad, first_shift_grad = norm_one_pull(grad_norm_input)
    grad_start = grad_middle + grad_norm_one
    grad_encoded = grad_start.astype(jnp.bfloat16)
    panel_grad = matmul(express.T, grad_encoded)
    panel_total = lax.psum(panel_grad, ("slide", "blk"))
    table_grad = jnp.dot(
        selector.astype(jnp.float32).T, panel_total, precision=lax.Precision.HIGHEST
    )
    shares_grads = (
        lax.psum_scatter(first_gain_grad, "blk", scatter_dimension=0, tiled=True),
        lax.psum_scatter(first_shift_grad, "blk", scatter_dimension=0, tiled=True),
        lax.psum_scatter(query_grad, "blk", scatter_dimension=0, tiled=True),
        lax.psum_scatter(key_grad, "blk", scatter_dimension=0, tiled=True),
        lax.psum_scatter(value_grad, "blk", scatter_dimension=0, tiled=True),
        lax.psum_scatter(output_grad, "blk", scatter_dimension=0, tiled=True),
        lax.psum_scatter(second_gain_grad, "blk", scatter_dimension=0, tiled=True),
        lax.psum_scatter(second_shift_grad, "blk", scatter_dimension=0, tiled=True),
        lax.psum_scatter(hidden_grad, "blk", scatter_dimension=0, tiled=True),
        lax.psum_scatter(hidden_bias_grad, "blk", scatter_dimension=0, tiled=True),
        lax.psum_scatter(down_grad, "blk", scatter_dimension=0, tiled=True),
        lax.psum_scatter(down_bias_grad, "blk", scatter_dimension=0, tiled=True),
        lax.psum_scatter(mean_grad, "blk", scatter_dimension=0, tiled=True),
        lax.psum_scatter(logvar_grad, "blk", scatter_dimension=0, tiled=True),
        lax.psum_scatter(centres_grad, "blk", scatter_dimension=1, tiled=True),
        lax.psum_scatter(decoder_grad, "blk", scatter_dimension=0, tiled=True),
    )
    summed = (
        lax.psum(shares_grads[0].astype(jnp.bfloat16), "slide").astype(jnp.float32),
        lax.psum(shares_grads[1].astype(jnp.bfloat16), "slide").astype(jnp.float32),
        lax.psum(shares_grads[2].astype(jnp.bfloat16), "slide").astype(jnp.float32),
        lax.psum(shares_grads[3].astype(jnp.bfloat16), "slide").astype(jnp.float32),
        lax.psum(shares_grads[4].astype(jnp.bfloat16), "slide").astype(jnp.float32),
        lax.psum(shares_grads[5].astype(jnp.bfloat16), "slide").astype(jnp.float32),
        lax.psum(shares_grads[6].astype(jnp.bfloat16), "slide").astype(jnp.float32),
        lax.psum(shares_grads[7].astype(jnp.bfloat16), "slide").astype(jnp.float32),
        lax.psum(shares_grads[8].astype(jnp.bfloat16), "slide").astype(jnp.float32),
        lax.psum(shares_grads[9].astype(jnp.bfloat16), "slide").astype(jnp.float32),
        lax.psum(shares_grads[10].astype(jnp.bfloat16), "slide").astype(jnp.float32),
        lax.psum(shares_grads[11].astype(jnp.bfloat16), "slide").astype(jnp.float32),
        lax.psum(shares_grads[12].astype(jnp.bfloat16), "slide").astype(jnp.float32),
        lax.psum(shares_grads[13].astype(jnp.bfloat16), "slide").astype(jnp.float32),
        lax.psum(shares_grads[14].astype(jnp.bfloat16), "slide").astype(jnp.float32),
        lax.psum(shares_grads[15].astype(jnp.bfloat16), "slide").astype(jnp.float32),
    )
    return (decoded[None], divergence, table_grad) + tuple(summed)


def fits(mesh):
    return mesh.shape["slide"] == 4 and mesh.shape["blk"] == 8


def flipped(index, mask):
    for bit in (1, 2, 4):
        if mask & bit:
            index = index + bit - 2 * bit * ((index // bit) % 2)
    return index


def greet(slide, blk, peers):
    barrier = pltpu.get_barrier_semaphore()
    for far_slide, far_blk in peers:
        pl.semaphore_signal(
            barrier,
            inc=1,
            device_id={"slide": flipped(slide, far_slide), "blk": flipped(blk, far_blk)},
            device_id_type=MESH,
        )
    pl.semaphore_wait(barrier, len(peers))


BLK_PEERS = [(0, far) for far in range(1, 8)]
SLIDE_PEERS = [(far, 0) for far in range(1, 4)]


def dot_nt(left, right):
    return lax.dot_general(left, right, (((1,), (1,)), ((), ())), preferred_element_type=F32)


def dot_tn(left, right):
    return lax.dot_general(left, right, (((0,), (0,)), ((), ())), preferred_element_type=F32)


def head_scores(query, key, same_slide):
    scores = jnp.where(same_slide, dot_nt(query, key) * (HEAD_DIM**-0.5), -1e30)
    shifted = jnp.exp(scores - jnp.max(scores, axis=1, keepdims=True))
    return shifted / jnp.sum(shifted, axis=1, keepdims=True)


class Links:
    def __init__(self, slide, blk, send_sem, recv_sem):
        self.slide, self.blk = slide, blk
        self.send_sem, self.recv_sem = send_sem, recv_sem
        self.copies = []

    def send(self, source, target, far_slide, far_blk):
        number = len(self.copies)
        copy = pltpu.make_async_remote_copy(
            src_ref=source,
            dst_ref=target,
            send_sem=self.send_sem.at[number],
            recv_sem=self.recv_sem.at[number],
            device_id={
                "slide": flipped(self.slide, far_slide),
                "blk": flipped(self.blk, far_blk),
            },
            device_id_type=MESH,
        )
        copy.start()
        self.copies.append(copy)
        return copy

    def finish(self):
        for copy in self.copies:
            copy.wait_send()


def spread_everywhere(links, slot):
    slide, blk = links.slide, links.blk
    copies = {}

    def push(rel_slide, rel_blk, to_slide, to_blk):
        block = slot(flipped(slide, rel_slide), flipped(blk, rel_blk))
        copies[(rel_slide ^ to_slide, rel_blk ^ to_blk)] = links.send(block, block, to_slide, to_blk)

    for far in (2, 4, 6):
        push(0, 0, 0, far)
    push(0, 0, 0, 1)
    push(0, 0, 2, 0)
    push(0, 0, 1, 0)
    yield
    for rel in (2, 4, 6):
        copies[0, rel].wait_recv()
        push(0, rel, 0, 1)
        push(0, rel, 2, 0)
        push(0, rel, 1, 0)
    yield
    for rel in (1, 3, 5, 7):
        copies[0, rel].wait_recv()
        push(0, rel, 2, 0)
        push(0, rel, 1, 0)
    yield
    for rel in (0, 2, 4, 6, 1, 3, 5, 7):
        copies[2, rel].wait_recv()
        push(2, rel, 1, 0)
    yield
    for far in (1, 3):
        for rel in (0, 2, 4, 6, 1, 3, 5, 7):
            copies[far, rel].wait_recv()
    yield


class Reduction:
    def __init__(self, links, left, right, rows, width, dense, buffers):
        self.links, self.left, self.right = links, left, right
        self.rows, self.width, self.dense = rows, width, dense
        self.away, self.came, self.kept, self.pieces = buffers
        self.along_x, self.along_z = links.blk % 2, links.blk // 2

    def tiles(self, which, store):
        def tile(i, carry):
            place = which * 2 + i if self.dense else i * 2 + which
            product = dot_tn(self.left(pl.multiple_of(place * 128, 128)), self.right())
            store(pl.ds(pl.multiple_of(i * 128, 128), 128), product)
            return carry

        lax.fori_loop(0, self.rows * 4 // 128, tile, 0)

    def send_x(self):
        def store(where, product):
            self.away[where, :] = product.astype(BF16)

        self.tiles(1 - self.along_x, store)
        self.copy_x = self.links.send(self.away, self.came, 0, 1)

    def send_z(self):
        self.copy_x.wait_recv()

        def store(where, product):
            self.kept[where, :] = (product + self.came[where, :].astype(F32)).astype(BF16)

        self.tiles(self.along_x, store)
        self.copies_z = []
        for far in (2, 1, 3):
            target = pl.multiple_of(flipped(self.along_z, far) * self.rows, self.rows)
            self.copies_z.append(
                self.links.send(self.kept.at[pl.ds(target, self.rows)], self.pieces.at[far - 1], 0, 2 * far)
            )

    def total(self):
        for copy in self.copies_z:
            copy.wait_recv()
        own = self.kept[pl.ds(pl.multiple_of(self.along_z * self.rows, self.rows), self.rows), :]
        return (
            (own.astype(F32) + self.pieces[0].astype(F32))
            + (self.pieces[1].astype(F32) + self.pieces[2].astype(F32))
        ).astype(BF16)


def spread_slide(links, slot, total):
    slide = links.slide
    own, far = slot(slide), slot(flipped(slide, 2))
    own[...] = total
    across = links.send(own, own, 2, 0)
    beside = links.send(own, own, 1, 0)
    yield
    across.wait_recv()
    last = links.send(far, far, 1, 0)
    yield
    beside.wait_recv()
    last.wait_recv()
    yield


def reductions_of(cells, width, inner, latents):
    return [
        ("decoder", latents // 8, width // 4, True),
        ("down0", inner // 32, width // 2, False),
        ("down1", inner // 32, width // 2, False),
        ("mean", width // 8, latents // 4, False),
        ("logvar", width // 8, latents // 4, False),
        ("hidden0", width // 8, inner // 8, False),
        ("hidden1", width // 8, inner // 8, False),
        ("output", width // 8, width // 4, False),
        ("panel", width // 8, width // 4, False),
        ("query", width // 8, width // 4, False),
        ("key", width // 8, width // 4, False),
        ("value", width // 8, width // 4, False),
    ]


def across(links, ref, columns, cells):
    def rows(place):
        return ref.at[pl.ds(place * cells, cells), columns]

    far = links.send(rows(0), rows(2), 2, 0)
    near = links.send(rows(0), rows(1), 1, 0)
    yield
    far.wait_recv()
    last = links.send(rows(2), rows(3), 1, 0)
    yield
    near.wait_recv()
    last.wait_recv()
    yield


def norm_parts(hidden):
    centre = hidden - jnp.mean(hidden, axis=1, keepdims=True)
    invert = lax.rsqrt(jnp.mean(centre * centre, axis=1, keepdims=True) + 1e-05)
    return centre * invert, invert


def norm_back(hidden, gain, grad):
    unit, invert = norm_parts(hidden)
    gain_grad = jnp.sum(grad * unit, axis=0, keepdims=True)
    shift_grad = jnp.sum(grad, axis=0, keepdims=True)
    grad_unit = grad * gain
    grad_hidden = invert * (
        grad_unit
        - jnp.mean(grad_unit, axis=1, keepdims=True)
        - unit * jnp.mean(grad_unit * unit, axis=1, keepdims=True)
    )
    return grad_hidden, gain_grad, shift_grad


def exact_dot(left, right, dims):
    return lax.dot_general(
        left, right, (dims, ((), ())), precision=lax.Precision.HIGHEST, preferred_element_type=F32
    )


def mixture(mean_part, centres):
    crossed = exact_dot(mean_part, centres, ((1,), (1,)))
    ones = jnp.ones((8, centres.shape[1]), F32)
    centre_square = exact_dot(ones, centres * centres, ((1,), (1,)))[0:1]
    logits = (crossed - 0.5 * centre_square) / math.sqrt(centres.shape[1])
    shifted = jnp.exp(logits - jnp.max(logits, axis=1, keepdims=True))
    resp = shifted / jnp.sum(shifted, axis=1, keepdims=True)
    return resp, exact_dot(resp, centres, ((1,), (0,)))


def slide_masks(land, row_labels, col_labels, cells):
    for block in range(8):
        line = land[block, 3 * cells : 3 * cells + 1, :].astype(F32)
        col_labels[:, block * cells : (block + 1) * cells] = line
        row_labels[block * cells : (block + 1) * cells, :] = jnp.broadcast_to(line, (cells, cells)).T


def forward_kernel(
    part_ref, counts_ref, library_ref, positions_ref, freqs_ref, labels_ref, noise_ref, source_ref, gain_one, shift_one,
    gain_two, shift_two, hidden_bias, down_bias, centres_ref,
    wq_hbm, wk_hbm, wv_hbm, wo_hbm, wh_hbm, wd_hbm, wm_hbm, wl_hbm, wdec_hbm,
    land_out, start_out, middle_out, inner_out, mean_out, logvar_out, glatent_out, base_out, latent_out, kl_out, decoded_out,
    whole_out, quarter_out,
    wq, wk, wv, wo, wh, wd, wm, wl, wdec, panel_land, panel, qkv_send, att_send, att_land, row_labels, col_labels,
    act_parts, final, kl_own, kl_slides, kl_sum, kl_blks, load_sem, send_sem, recv_sem,
):
    slide, blk = lax.axis_index("slide"), lax.axis_index("blk")
    cells, width = counts_ref.shape
    inner, latents, per = inner_out.shape[1], mean_out.shape[1], width // 8
    loads = []
    for number, (source, target) in enumerate(
        [(wq_hbm, wq), (wk_hbm, wk), (wv_hbm, wv), (wo_hbm, wo), (wh_hbm, wh), (wd_hbm, wd), (wm_hbm, wm), (wl_hbm, wl), (wdec_hbm, wdec)]
    ):
        loads.append(pltpu.make_async_copy(source, target, load_sem.at[number]))
        loads[-1].start()
    greet(slide, blk, SLIDE_PEERS + BLK_PEERS)
    links = Links(slide, blk, send_sem, recv_sem)

    part_copies = [links.send(part_ref.at[flipped(blk, far)], panel_land.at[far], 0, far) for far in (6, 4, 2, 7, 5, 3, 1)]
    express = jnp.log(1.0 + counts_ref[...].astype(F32) * (10000.0 / library_ref[...].astype(F32))).astype(BF16)
    whole_out[0:cells, 0:width] = express
    quarter = width // 4
    for block in range(4):
        angle = positions_ref[:, block // 2 : block // 2 + 1].astype(F32) * freqs_ref[...]
        start_out[:, block * quarter : (block + 1) * quarter] = jnp.cos(angle) if block % 2 else jnp.sin(angle)
    total = part_ref[blk].astype(F32)
    for place, far in enumerate((6, 4, 2, 7, 5, 3, 1)):
        part_copies[place].wait_recv()
        total = total + panel_land[far].astype(F32)
    panel[slide * 8 + blk] = total.astype(BF16)
    spread = spread_everywhere(links, lambda far_slide, far_blk: panel.at[far_slide * 8 + far_blk])
    for _ in spread:
        pass
    send_express = across(links, whole_out, pl.ds(0, width), cells)
    next(send_express)

    def source_part(which):
        return source_ref.at[:, pl.ds(pl.multiple_of(which * quarter, 128), quarter)]

    def source_slot(place):
        return quarter_out.at[pl.ds(place * cells, cells), pl.ds(inner // 4, quarter)]

    source_copies = [links.send(source_part(flipped(slide, far)), source_slot(far), far, 0) for far in (2, 3, 1)]
    source_slot(0)[...] = source_part(slide)[...]

    hidden_start = start_out[...] + jnp.dot(express, panel[...].reshape(width, width), preferred_element_type=F32)
    start_out[...] = hidden_start
    normed = (norm_parts(hidden_start)[0] * gain_one[...] + shift_one[...]).astype(BF16)
    whole_out[0:cells, width : 2 * width] = normed
    qkv_send[:, 3 * cells :, :] = jnp.broadcast_to(labels_ref[...].astype(BF16)[None], (8, 16, per))
    for number in range(3):
        loads[number].wait()

    along_x, along_z = blk % 2, blk // 2
    qkv_copies = []
    for far in (3, 2, 1, 0):
        pair = flipped(along_z, far)
        columns = pl.ds(pl.multiple_of(pair * 2 * per, 128), 2 * per)
        for number, weight in enumerate((wq, wk, wv)):
            product = jnp.dot(normed, weight[:, columns], preferred_element_type=F32).astype(BF16)
            for side in range(2):
                qkv_send[pair * 2 + side, number * cells : (number + 1) * cells, :] = product[:, side * per : (side + 1) * per]
        for side in (1, 0):
            if far or side:
                target = flipped(pair * 2 + along_x, side)
                qkv_copies.append(links.send(qkv_send.at[target], land_out.at[blk], 0, 2 * far + side))
    land_out[blk] = qkv_send[blk]
    next(send_express)
    send_normed = across(links, whole_out, pl.ds(width, width), cells)
    next(send_normed)
    for copy in qkv_copies:
        copy.wait_recv()

    slide_masks(land_out, row_labels, col_labels, cells)
    key = land_out[:, cells : 2 * cells, :].reshape(8 * cells, per)
    value = land_out[:, 2 * cells : 3 * cells, :].reshape(8 * cells, per)
    att_copies = []
    for far in (3, 2, 1, 0):
        pair = flipped(along_z, far)
        query = land_out[pl.ds(pair * 2, 2), 0:cells, :].reshape(2 * cells, per)
        same_slide = row_labels[pl.ds(pl.multiple_of(pair * 2 * cells, 128), 2 * cells), 0:1] == col_labels[...]
        lane = lax.broadcasted_iota(jnp.int32, query.shape, 1)
        out = None
        for head in range(per // HEAD_DIM):
            mine = lane // HEAD_DIM == head
            shares = head_scores(jnp.where(mine, query, 0), key, same_slide)
            part = jnp.dot(shares.astype(BF16), value, preferred_element_type=F32)
            out = part if out is None else jnp.where(mine, part, out)
        att_send[pl.ds(pair * 2, 2)] = out.astype(BF16).reshape(2, cells, per)
        for side in (1, 0):
            if far or side:
                target = flipped(pair * 2 + along_x, side)
                att_copies.append(links.send(att_send.at[target], att_land.at[blk], 0, 2 * far + side))
    att_land[blk] = att_send[blk]
    next(send_normed)
    for copy in att_copies:
        copy.wait_recv()
    for block in range(8):
        whole_out[0:cells, 2 * width + block * per : 2 * width + (block + 1) * per] = att_land[block]
    send_attended = across(links, whole_out, pl.ds(2 * width, width), cells)
    next(send_attended)

    loads[3].wait()
    hidden_middle = start_out[...] + jnp.dot(
        whole_out[0:cells, 2 * width : 3 * width], wo[...], preferred_element_type=F32
    )
    middle_out[...] = hidden_middle
    normed_two = (norm_parts(hidden_middle)[0] * gain_two[...] + shift_two[...]).astype(BF16)
    whole_out[0:cells, 3 * width :] = normed_two
    send_two = across(links, whole_out, pl.ds(3 * width, width), cells)
    next(send_two)
    loads[4].wait()
    loads[5].wait()
    final[...] = hidden_middle + down_bias[...]
    chunk = inner // 8

    def feed(j, carry):
        where = pl.ds(pl.multiple_of(j * chunk, 128), chunk)
        inner_sum = jnp.dot(whole_out[0:cells, 3 * width :], wh[:, where], preferred_element_type=F32) + hidden_bias[:, where]
        inner_out[:, where] = inner_sum
        act = gelu_tanh(inner_sum).astype(BF16)
        for block in range(4):
            act_parts[block, :, pl.ds(pl.multiple_of(j * (chunk // 4), 128), chunk // 4)] = act[:, block * (chunk // 4) : (block + 1) * (chunk // 4)]
        final[...] += jnp.dot(act, wd[where, :], preferred_element_type=F32)
        return carry

    lax.fori_loop(0, 8, feed, 0)
    act_copies = [
        links.send(act_parts.at[flipped(slide, far)], quarter_out.at[pl.ds(far * cells, cells), pl.ds(0, inner // 4)], far, 0)
        for far in (2, 3, 1)
    ]
    quarter_out[0:cells, 0 : inner // 4] = act_parts[slide]
    base = final[...].astype(BF16)
    base_out[...] = base
    for number in (6, 7, 8):
        loads[number].wait()
    mean_lat = jnp.dot(base, wm[...], preferred_element_type=F32)
    log_var = jnp.dot(base, wl[...], preferred_element_type=F32)
    mean_out[...] = mean_lat
    logvar_out[...] = log_var
    centres = centres_ref[...]
    resp, mixed = mixture(mean_lat, centres)
    mixed_square = exact_dot(resp, centres * centres, ((1,), (0,)))
    kl_cell = 0.5 * (
        jnp.exp(log_var) - 1.0 - log_var + mean_lat * mean_lat - 2.0 * mean_lat * mixed + mixed_square
    )
    kl_line = jnp.sum(kl_cell, axis=0, keepdims=True)
    kl_own[...] = jnp.zeros_like(kl_own)
    for block in range(latents // 128):
        kl_own[block : block + 1, :] = kl_line[:, block * 128 : (block + 1) * 128]
    kl_copies = [links.send(kl_own, kl_slides.at[slide], far, 0) for far in (2, 3, 1)]
    kl_slides[slide] = kl_own[...]
    latent = (mean_lat + jnp.exp(0.5 * log_var) * noise_ref[...]).astype(BF16)
    latent_out[...] = latent
    decoded_out[...] = jnp.dot(latent, wdec[...], preferred_element_type=F32)
    for copy in kl_copies:
        copy.wait_recv()
    kl_sum[...] = (kl_slides[0] + kl_slides[1]) + (kl_slides[2] + kl_slides[3])
    kl_copies = [links.send(kl_sum, kl_blks.at[blk], 0, far) for far in (6, 4, 2, 7, 5, 3, 1)]
    kl_blks[blk] = kl_sum[...]
    glatent_out[...] = dot_nt(source_ref[...], wdec[...])
    next(send_attended)
    next(send_two)
    for copy in kl_copies:
        copy.wait_recv()
    kl_total = kl_blks[0]
    for block in range(1, 8):
        kl_total = kl_total + kl_blks[block]
    kl_out[...] = kl_total
    for copy in source_copies + act_copies:
        copy.wait_recv()
    for sent in (send_express, send_normed, send_attended, send_two):
        next(sent)
    links.finish()


def forward(inputs, weights, cells, width, inner, latents):
    per = width // 8
    shape = jax.ShapeDtypeStruct
    vmem, left = pl.BlockSpec(memory_space=pltpu.VMEM), pl.BlockSpec(memory_space=pl.ANY)
    outs = (
        shape((8, 3 * cells + 16, per), BF16),
        shape((cells, width), F32),
        shape((cells, width), F32),
        shape((cells, inner), F32),
        shape((cells, latents), F32),
        shape((cells, latents), F32),
        shape((cells, latents), F32),
        shape((cells, width), BF16),
        shape((cells, latents), BF16),
        shape((8, 128), F32),
        shape((cells, width), F32),
        shape((4 * cells, 4 * width), BF16),
        shape((4 * cells, inner // 4 + width // 4), BF16),
    )
    copies = 96
    return pl.pallas_call(
        forward_kernel,
        out_shape=outs,
        in_specs=[vmem] * len(inputs) + [left] * len(weights),
        out_specs=[vmem] * len(outs),
        scratch_shapes=[pltpu.VMEM(weight.shape, BF16) for weight in weights]
        + [
            pltpu.VMEM((8, width // 32, width), BF16),
            pltpu.VMEM((32, width // 32, width), BF16),
            pltpu.VMEM((8, 3 * cells + 16, per), BF16),
            pltpu.VMEM((8, cells, per), BF16),
            pltpu.VMEM((8, cells, per), BF16),
            pltpu.VMEM((8 * cells, cells), F32),
            pltpu.VMEM((1, 8 * cells), F32),
            pltpu.VMEM((4, cells, inner // 4), BF16),
            pltpu.VMEM((cells, width), F32),
            pltpu.VMEM((8, 128), F32),
            pltpu.VMEM((4, 8, 128), F32),
            pltpu.VMEM((8, 128), F32),
            pltpu.VMEM((8, 8, 128), F32),
            pltpu.SemaphoreType.DMA((len(weights),)),
            pltpu.SemaphoreType.DMA((copies,)),
            pltpu.SemaphoreType.DMA((copies,)),
        ],
        compiler_params=pltpu.CompilerParams(
            collective_id=1, has_side_effects=True, vmem_limit_bytes=62 << 20
        ),
        name="forward",
    )(*inputs, *weights)


def backward_kernel(
    land_ref, start_ref, middle_ref, inner_ref, mean_ref, logvar_ref, glatent_ref, base_ref, latent_ref, kl_ref, noise_ref,
    centres_ref, weight_ref, floor_ref, gain_one, gain_two,
    whole_hbm, quarter_hbm, wq_hbm, wk_hbm, wv_hbm, wo_hbm, wh_hbm, wd_hbm, wm_hbm, wl_hbm,
    panel_out, query_out, key_out, value_out, output_out, hidden_out, down_out, mean_out, logvar_out, decoder_out, small_out,
    whole, base_all, latent_all, quarter, wide_slots, wo, wm, wl, branch_all, gmean, glogvar, gmean_all, glogvar_all, ginner,
    ginner_all, gout, gout_all, gmiddle, gqkv_all, genc_all, row_ref, col_ref,
    att_send, att_land, dqkv, dqkv_land, dk_sum, dv_sum, grad_qkv, encoded, small, small_land, small_own, small_slides,
    load_sem, send_sem, recv_sem, *unit_refs,
):
    slide, blk = lax.axis_index("slide"), lax.axis_index("blk")
    cells, width = middle_ref.shape
    inner, latents, per = inner_ref.shape[1], mean_ref.shape[1], width // 8
    loads = {}

    def load(name, source, target):
        loads[name] = pltpu.make_async_copy(source, target, load_sem.at[len(loads)])
        loads[name].start()

    def load_feed(far, slot):
        which = pl.ds(pl.multiple_of(flipped(slide, far) * (inner // 4), 128), inner // 4)
        load("wd%d" % far, wd_hbm.at[which, :], wide_slots.at[2 * slot])
        load("wh%d" % far, wh_hbm.at[:, which], wide_slots.at[2 * slot + 1])

    load("wm", wm_hbm, wm)
    load("wl", wl_hbm, wl)
    load_feed(2, 0)
    load_feed(3, 1)
    load("wo", wo_hbm, wo)
    load("quarter", quarter_hbm, quarter)
    load("whole", whole_hbm, whole)
    greet(slide, blk, SLIDE_PEERS + BLK_PEERS)
    links = Links(slide, blk, send_sem, recv_sem)

    def lanes(ref, which, size):
        return ref.at[:, pl.ds(pl.multiple_of(which * size, 128), size)]

    def swap(ref, size, target):
        copies = []
        for far in (2, 3, 1):
            copies.append(links.send(lanes(ref, flipped(slide, far), size), target.at[far], far, 0))
        target[0] = lanes(ref, slide, size)[...]
        return copies

    small[...] = jnp.zeros_like(small)

    kl_mean = jnp.concatenate([kl_ref[block : block + 1, :] for block in range(latents // 128)], axis=1) / (32 * cells)
    grad_kl = weight_ref[0, 0] * (kl_mean > floor_ref[...]).astype(F32)
    mean_lat, log_var, centres = mean_ref[...], logvar_ref[...], centres_ref[...]
    grad_latent = glatent_ref[...]
    resp, mixed = mixture(mean_lat, centres)
    weighted = mean_lat * grad_kl
    half_square = exact_dot(jnp.broadcast_to(0.5 * grad_kl, (8, latents)), centres * centres, ((1,), (1,)))[0:1]
    grad_resp = half_square - exact_dot(weighted, centres, ((1,), (1,)))
    grad_logits = resp * (grad_resp - jnp.sum(resp * grad_resp, axis=1, keepdims=True)) / math.sqrt(latents)
    grad_mean = grad_latent + grad_kl * (mean_lat - mixed) + exact_dot(grad_logits, centres, ((1,), (0,)))
    grad_logvar = grad_latent * (0.5 * jnp.exp(0.5 * log_var) * noise_ref[...]) + 0.5 * grad_kl * (jnp.exp(log_var) - 1.0)
    gmean[...] = grad_mean.astype(BF16)
    glogvar[...] = grad_logvar.astype(BF16)
    loads["wm"].wait()
    loads["wl"].wait()
    grad_final = dot_nt(gmean[...], wm[...]) + dot_nt(glogvar[...], wl[...])
    gmiddle[...] = grad_final
    branch_all[0] = grad_final.astype(BF16)
    branch_far = links.send(branch_all.at[0], branch_all.at[2], 2, 0)
    branch_near = links.send(branch_all.at[0], branch_all.at[1], 1, 0)
    mean_swap = swap(gmean, latents // 4, gmean_all)
    logvar_swap = swap(glogvar, latents // 4, glogvar_all)
    base_all[0:cells, :] = base_ref[...]
    send_base = across(links, base_all, pl.ds(0, width), cells)
    next(send_base)
    rows = latents // 8
    for along_x in range(2):
        for along_z in range(4):
            place = (along_z * 2 + along_x) * rows
            latent_all[0:cells, (along_x * 4 + along_z) * rows : (along_x * 4 + along_z + 1) * rows] = latent_ref[:, place : place + rows]
    send_latent = across(links, latent_all, pl.ds(0, latents), cells)
    next(send_latent)
    ones = jnp.ones((cells, 128), F32)
    logit_sum = exact_dot(grad_logits, ones, ((0,), (0,)))[:, 0:1]
    resp_sum = exact_dot(resp, ones, ((0,), (0,)))[:, 0:1]
    centres_grad = (
        exact_dot(grad_logits, mean_lat, ((0,), (0,)))
        - logit_sum * centres
        - exact_dot(resp, weighted, ((0,), (0,)))
        + resp_sum * grad_kl * centres
    )
    count = centres.shape[0]
    for block in range(8):
        small[block, 16 : 16 + count, 0 : latents // 8] = centres_grad[:, block * (latents // 8) : (block + 1) * (latents // 8)]
    bias_line = jnp.sum(branch_all[0].astype(F32), axis=0, keepdims=True)
    for block in range(8):
        small[block, 8:9, :] = bias_line[:, block * 128 : (block + 1) * 128]

    encoded[...] = jnp.zeros_like(encoded)
    chunk = inner // 8
    inner_swap = []
    for turn, far in enumerate((2, 3, 1, 0)):
        slot = turn % 2
        loads["wd%d" % far].wait()
        loads["wh%d" % far].wait()
        which = flipped(slide, far)

        def feed(j, carry, slot=slot, which=which):
            near = pl.ds(pl.multiple_of(j * chunk, 128), chunk)
            where = pl.ds(pl.multiple_of(which * (inner // 4) + j * chunk, 128), chunk)
            values = inner_ref[:, where]
            squared = values * values
            bent = jnp.tanh(0.7978845608028654 * (values + 0.044715 * squared * values))
            slope = 0.5 * (1.0 + bent) + 0.5 * values * (1.0 - bent * bent) * (
                0.7978845608028654 * (1.0 + 3 * 0.044715 * squared)
            )
            grad = (dot_nt(branch_all[0], wide_slots[2 * slot, near, :]) * slope).astype(BF16)
            ginner[:, where] = grad
            line = jnp.sum(grad.astype(F32), axis=0, keepdims=True)
            for block in range(chunk // 128):
                small[which * 2 + j, 4 + block : 5 + block, :] = line[:, block * 128 : (block + 1) * 128]
            encoded[...] += dot_nt(grad, wide_slots[2 * slot + 1, :, near])
            return carry

        lax.fori_loop(0, 2, feed, 0)
        if far:
            inner_swap.append(links.send(lanes(ginner, which, inner // 4), ginner_all.at[far], far, 0))
        else:
            ginner_all[0] = lanes(ginner, slide, inner // 4)[...]
        if turn < 2:
            load_feed((1, 0)[turn], slot)
        if turn == 1:
            branch_far.wait_recv()
            branch_last = links.send(branch_all.at[2], branch_all.at[3], 1, 0)
    for number, (name, source) in enumerate((("wq", wq_hbm), ("wk", wk_hbm), ("wv", wv_hbm))):
        load(name, source, wide_slots.at[number])
    wq, wk, wv = wide_slots.at[0], wide_slots.at[1], wide_slots.at[2]

    grad_hidden, gain_grad, shift_grad = norm_back(middle_ref[...], gain_two[...], encoded[...])
    for block in range(8):
        small[block, 2:3, :] = gain_grad[:, block * 128 : (block + 1) * 128]
        small[block, 3:4, :] = shift_grad[:, block * 128 : (block + 1) * 128]
    gmiddle[...] += grad_hidden
    gout[...] = gmiddle[...].astype(BF16)

    loads["wo"].wait()

    def att_block(target, store):
        rows = wo[pl.ds(pl.multiple_of(target * per, per), per), :]
        store(dot_nt(gout[...], rows).astype(BF16))

    att_copies = []
    for far in (6, 4, 2, 7, 5, 3, 1):
        target = flipped(blk, far)

        def keep(block, far=far):
            att_send[far] = block

        att_block(target, keep)
        att_copies.append(links.send(att_send.at[far], att_land.at[blk], 0, far))

    def keep_own(block):
        att_land[blk] = block

    att_block(blk, keep_own)
    out_swap = swap(gout, width // 4, gout_all)

    width_at = {"express": 0, "one": width, "attended": 2 * width, "two": 3 * width}

    def of_whole(name):
        def left(column):
            return whole[:, pl.ds(width_at[name] + column, 128)]

        return left

    def of_base(column):
        return base_all[:, pl.ds(column, 128)]

    def of_latent(column):
        return latent_all[:, pl.ds(column, 128)]

    def of_act(column):
        return quarter[:, pl.ds(column, 128)]

    def flat(ref, start=None, size=None):
        def right():
            block = ref[...] if start is None else ref[:, :, start : start + size]
            return block.reshape(4 * cells, block.shape[-1])

        return right

    def source_all():
        return quarter[:, inner // 4 :]

    half_w, half_i = width // 2, inner // 8
    operands = {
        "decoder": (of_latent, source_all),
        "down0": (of_act, flat(branch_all, 0, half_w)),
        "down1": (of_act, flat(branch_all, half_w, half_w)),
        "mean": (of_base, flat(gmean_all)),
        "logvar": (of_base, flat(glogvar_all)),
        "hidden0": (of_whole("two"), flat(ginner_all, 0, half_i)),
        "hidden1": (of_whole("two"), flat(ginner_all, half_i, half_i)),
        "output": (of_whole("attended"), flat(gout_all)),
        "panel": (of_whole("express"), flat(genc_all)),
        "query": (of_whole("one"), flat(gqkv_all.at[0])),
        "key": (of_whole("one"), flat(gqkv_all.at[1])),
        "value": (of_whole("one"), flat(gqkv_all.at[2])),
    }
    units = {}
    for number, (name, rows, columns, dense) in enumerate(reductions_of(cells, width, inner, latents)):
        left, right = operands[name]
        units[name] = Reduction(
            links, left, right, rows, columns, dense, unit_refs[4 * number : 4 * number + 4]
        )

    slots = {
        "decoder": lambda place: lanes(decoder_out, place, width // 4),
        "down0": lambda place: down_out.at[pl.ds(pl.multiple_of(place * (inner // 32), inner // 32), inner // 32), pl.ds(0, half_w)],
        "down1": lambda place: down_out.at[pl.ds(pl.multiple_of(place * (inner // 32), inner // 32), inner // 32), pl.ds(half_w, half_w)],
        "mean": lambda place: lanes(mean_out, place, latents // 4),
        "logvar": lambda place: lanes(logvar_out, place, latents // 4),
        "hidden0": lambda place: hidden_out.at[:, pl.ds(pl.multiple_of(place * (inner // 4), 128), half_i)],
        "hidden1": lambda place: hidden_out.at[:, pl.ds(pl.multiple_of(place * (inner // 4) + half_i, 128), half_i)],
        "output": lambda place: lanes(output_out, place, width // 4),
        "query": lambda place: lanes(query_out, place, width // 4),
        "key": lambda place: lanes(key_out, place, width // 4),
        "value": lambda place: lanes(value_out, place, width // 4),
    }
    spreads = {}

    def spread(name):
        spreads[name] = spread_slide(links, slots[name], units[name].total())
        next(spreads[name])

    loads["quarter"].wait()
    loads["whole"].wait()
    branch_near.wait_recv()
    branch_last.wait_recv()
    units["down0"].send_x()
    units["down1"].send_x()
    next(send_base)
    next(send_latent)
    for copy in mean_swap + logvar_swap:
        copy.wait_recv()
    next(send_latent)
    units["decoder"].send_x()
    next(send_base)
    units["mean"].send_x()
    units["logvar"].send_x()

    for copy in att_copies:
        copy.wait_recv()
    slide_masks(land_ref, row_ref, col_ref, cells)
    dk_sum[...] = jnp.zeros_like(dk_sum)
    dv_sum[...] = jnp.zeros_like(dv_sum)
    scale = HEAD_DIM**-0.5
    rows = 2 * cells

    def rows_back(i, carry):
        where = pl.ds(pl.multiple_of(i * rows, rows), rows)
        same_slide = row_ref[where, 0:1] == col_ref[...]
        query = land_ref[pl.ds(2 * i, 2), 0:cells, :].reshape(rows, per)
        grad = att_land[pl.ds(2 * i, 2)].reshape(rows, per)
        key = land_ref[:, cells : 2 * cells, :].reshape(8 * cells, per)
        value = land_ref[:, 2 * cells : 3 * cells, :].reshape(8 * cells, per)
        lane = lax.broadcasted_iota(jnp.int32, query.shape, 1)
        grad_query = None
        for head in range(per // HEAD_DIM):
            mine = lane // HEAD_DIM == head
            own_query = jnp.where(mine, query, 0)
            own_grad = jnp.where(mine, grad, 0)
            shares = head_scores(own_query, key, same_slide)
            grad_shares = dot_nt(own_grad, value)
            inner_dot = jnp.sum(shares * grad_shares, axis=1, keepdims=True)
            grad_scores = (shares * (grad_shares - inner_dot)).astype(BF16)
            part = jnp.dot(grad_scores, key, preferred_element_type=F32)
            grad_query = part if grad_query is None else jnp.where(mine, part, grad_query)
            dk_sum[...] += dot_tn(grad_scores, own_query)
            dv_sum[...] += dot_tn(shares.astype(BF16), own_grad)
        dqkv[pl.ds(2 * i, 2), 0:cells, :] = (grad_query * scale).astype(BF16).reshape(2, cells, per)
        return carry

    lax.fori_loop(0, 8 * cells // rows, rows_back, 0)
    dqkv[:, cells : 2 * cells, :] = (dk_sum[...] * scale).astype(BF16).reshape(8, cells, per)
    dqkv[:, 2 * cells :, :] = dv_sum[...].astype(BF16).reshape(8, cells, per)
    back_copies = []
    for far in (6, 4, 2, 7, 5, 3, 1):
        back_copies.append(links.send(dqkv.at[flipped(blk, far)], dqkv_land.at[blk], 0, far))
    dqkv_land[blk] = dqkv[blk]

    for copy in inner_swap + out_swap:
        copy.wait_recv()
    units["hidden0"].send_x()
    units["hidden1"].send_x()
    units["output"].send_x()
    units["decoder"].send_z()
    units["down0"].send_z()

    for copy in back_copies:
        copy.wait_recv()
    for name in ("wq", "wk", "wv"):
        loads[name].wait()
    for part in range(3):
        for block in range(8):
            grad_qkv[part, :, block * per : (block + 1) * per] = dqkv_land[block, part * cells : (part + 1) * cells, :]
    qkv_swaps = [swap(grad_qkv.at[part], width // 4, gqkv_all.at[part]) for part in range(3)]

    def norm_input(i, carry):
        where = pl.ds(pl.multiple_of(i * 256, 256), 256)
        encoded_sum = (
            dot_nt(grad_qkv[0], wq[where, :]) + dot_nt(grad_qkv[1], wk[where, :]) + dot_nt(grad_qkv[2], wv[where, :])
        )
        encoded[:, where] = encoded_sum
        return carry

    lax.fori_loop(0, width // 256, norm_input, 0)
    grad_hidden, gain_grad, shift_grad = norm_back(start_ref[...], gain_one[...], encoded[...])
    grad_qkv[3] = (gmiddle[...] + grad_hidden).astype(BF16)
    encoded_swap = swap(grad_qkv.at[3], width // 4, genc_all)

    for block in range(8):
        small[block, 0:1, :] = gain_grad[:, block * 128 : (block + 1) * 128]
        small[block, 1:2, :] = shift_grad[:, block * 128 : (block + 1) * 128]
    small_copies = [links.send(small.at[flipped(blk, far)], small_land.at[blk], 0, far) for far in range(1, 8)]
    small_land[blk] = small[blk]

    units["down1"].send_z()
    for copy in encoded_swap:
        copy.wait_recv()
    units["panel"].send_x()
    for part in range(3):
        for copy in qkv_swaps[part]:
            copy.wait_recv()
        units[("query", "key", "value")[part]].send_x()
    for copy in small_copies:
        copy.wait_recv()
    small_sum = small_land[0]
    for block in range(1, 8):
        small_sum = small_sum + small_land[block]
    small_own[...] = small_sum
    small_copies = [links.send(small_own, small_slides.at[slide], far, 0) for far in (2, 3, 1)]
    small_slides[slide] = small_sum
    units["mean"].send_z()
    units["logvar"].send_z()
    units["panel"].send_z()
    units["hidden0"].send_z()
    spread("decoder")
    spread("down0")
    spread("down1")

    panel_slot = lambda far_slide, far_blk: panel_out.at[
        pl.ds(pl.multiple_of(far_blk * (width // 8), 128), width // 8),
        pl.ds(pl.multiple_of(far_slide * (width // 4), 128), width // 4),
    ]
    own_slot = panel_slot(slide, blk)
    own_slot[...] = units["panel"].total()
    everywhere = spread_everywhere(links, panel_slot)
    next(everywhere)
    units["hidden1"].send_z()
    units["output"].send_z()
    next(everywhere)
    units["query"].send_z()
    units["key"].send_z()
    units["value"].send_z()
    next(everywhere)
    spread("mean")
    spread("logvar")
    spread("hidden0")
    spread("hidden1")
    next(everywhere)
    spread("output")
    spread("query")
    spread("key")
    spread("value")
    for name in spreads:
        next(spreads[name])
    for copy in small_copies:
        copy.wait_recv()
    small_out[...] = (small_slides[0] + small_slides[1]) + (small_slides[2] + small_slides[3])
    next(everywhere)
    for name in spreads:
        next(spreads[name])
    links.finish()


def backward(inputs, weights, cells, width, inner, latents):
    per = width // 8
    small_rows = 32
    shape = jax.ShapeDtypeStruct
    unit_scratch = []
    for _, rows, columns, _ in reductions_of(cells, width, inner, latents):
        unit_scratch += [pltpu.VMEM((4 * rows, columns), BF16)] * 3 + [pltpu.VMEM((3, rows, columns), BF16)]
    copies = 208
    vmem, left = pl.BlockSpec(memory_space=pltpu.VMEM), pl.BlockSpec(memory_space=pl.ANY)
    outs = (
        shape((width, width), BF16),
        shape((per, width), BF16),
        shape((per, width), BF16),
        shape((per, width), BF16),
        shape((per, width), BF16),
        shape((per, inner), BF16),
        shape((inner // 8, width), BF16),
        shape((per, latents), BF16),
        shape((per, latents), BF16),
        shape((latents // 8, width), BF16),
        shape((small_rows, 128), F32),
    )
    scratch = [
        ((4 * cells, 4 * width), BF16),
        ((4 * cells, width), BF16),
        ((4 * cells, latents), BF16),
        ((4 * cells, inner // 4 + width // 4), BF16),
        ((4, width, width), BF16),
        ((width, width), BF16),
        ((width, latents), BF16),
        ((width, latents), BF16),
        ((4, cells, width), BF16),
        ((cells, latents), BF16),
        ((cells, latents), BF16),
        ((4, cells, latents // 4), BF16),
        ((4, cells, latents // 4), BF16),
        ((cells, inner), BF16),
        ((4, cells, inner // 4), BF16),
        ((cells, width), BF16),
        ((4, cells, width // 4), BF16),
        ((cells, width), F32),
        ((3, 4, cells, width // 4), BF16),
        ((4, cells, width // 4), BF16),
        ((8 * cells, cells), F32),
        ((1, 8 * cells), F32),
        ((8, cells, per), BF16),
        ((8, cells, per), BF16),
        ((8, 3 * cells, per), BF16),
        ((8, 3 * cells, per), BF16),
        ((8 * cells, per), F32),
        ((8 * cells, per), F32),
        ((4, cells, width), BF16),
        ((cells, width), F32),
        ((8, small_rows, 128), F32),
        ((8, small_rows, 128), F32),
        ((small_rows, 128), F32),
        ((4, small_rows, 128), F32),
    ]
    return pl.pallas_call(
        backward_kernel,
        out_shape=outs,
        in_specs=[vmem] * len(inputs) + [left] * len(weights),
        out_specs=[vmem] * len(outs),
        scratch_shapes=[pltpu.VMEM(*item) for item in scratch]
        + [
            pltpu.SemaphoreType.DMA((16,)),
            pltpu.SemaphoreType.DMA((copies,)),
            pltpu.SemaphoreType.DMA((copies,)),
        ]
        + unit_scratch,
        compiler_params=pltpu.CompilerParams(
            collective_id=2, has_side_effects=True, vmem_limit_bytes=62 << 20
        ),
        name="backward",
    )(*inputs, *weights)


def table_kernel(first_ref, ids_ref, panel_ref, out_ref):
    rows = out_ref.shape[0]
    first = first_ref[0] + pl.program_id(0) * rows
    row_ids = first + lax.broadcasted_iota(jnp.int32, (rows, ids_ref.shape[1]), 0)
    spread = (row_ids == ids_ref[...]).astype(F32).astype(BF16)
    out_ref[...] = jnp.dot(spread, panel_ref[...], preferred_element_type=F32)


def table_rows_grad(first_row, gene_ids, panel, table_rows, rows=256):
    genes, width = panel.shape
    return pl.pallas_call(
        table_kernel,
        grid=(table_rows // rows,),
        out_shape=jax.ShapeDtypeStruct((table_rows, width), F32),
        in_specs=[
            pl.BlockSpec(memory_space=pltpu.SMEM),
            pl.BlockSpec((1, genes), lambda i: (0, 0)),
            pl.BlockSpec((genes, width), lambda i: (0, 0)),
        ],
        out_specs=pl.BlockSpec((rows, width), lambda i: (i, 0)),
        compiler_params=pltpu.CompilerParams(vmem_limit_bytes=40 << 20),
        name="table_rows_grad",
    )(first_row.reshape(1), gene_ids.reshape(1, genes), panel)


def on_device_fast(
    counts,
    library,
    gene_ids,
    positions,
    slide_of_cell,
    latent_noise,
    decoded_grad,
    gene_table,
    first_gain,
    first_shift,
    query_weight,
    key_weight,
    value_weight,
    output_weight,
    second_gain,
    second_shift,
    hidden_weight,
    hidden_bias,
    down_weight,
    down_bias,
    mean_weight,
    logvar_weight,
    component_means,
    decoder_weight,
    divergence_weight,
    free_floor,
):
    cells = counts.shape[1]
    width = gene_table.shape[1]
    genes = gene_ids.shape[0]
    latents = mean_weight.shape[1]
    inner = hidden_weight.shape[1]
    slide, blk = lax.axis_index("slide"), lax.axis_index("blk")
    table_rows = gene_table.shape[0]
    first_row = blk * table_rows
    row_ids = first_row + jnp.arange(table_rows, dtype=jnp.int32)
    my_ids = lax.dynamic_slice_in_dim(gene_ids, slide * (genes // 4), genes // 4, 0)
    selector = (my_ids[:, None] == row_ids[None, :]).astype(BF16)
    part = matmul(selector, gene_table).astype(BF16).reshape(8, genes // 32, width)
    quarter = width // 4
    freqs = jnp.exp(-math.log(10000.0) * jnp.arange(quarter, dtype=F32) / quarter)
    labels = jnp.broadcast_to(slide_of_cell[0].astype(F32)[None], (16, cells))
    (
        land, hidden_start, hidden_middle, inner_sum, mean_lat, log_var, grad_latent, base, latent, kl_total, decoded,
        whole, quarters,
    ) = forward(
        (
            part, counts[0], library[0][:, None], positions[0].T, freqs[None], labels, latent_noise[0], decoded_grad[0],
            first_gain[None], first_shift[None], second_gain[None], second_shift[None], hidden_bias[None],
            down_bias[None], component_means,
        ),
        (
            query_weight, key_weight, value_weight, output_weight, hidden_weight, down_weight, mean_weight,
            logvar_weight, decoder_weight,
        ),
        cells, width, inner, latents,
    )
    kl_mean = kl_total[: latents // 128].reshape(latents) / (32 * cells)
    divergence = divergence_weight * jnp.mean(jnp.maximum(kl_mean, free_floor))
    (
        panel_sum, query_grad, key_grad, value_grad, output_grad, hidden_grad, down_grad, mean_grad, logvar_grad,
        decoder_grad, small,
    ) = backward(
        (
            land, hidden_start, hidden_middle, inner_sum, mean_lat, log_var, grad_latent, base, latent, kl_total,
            latent_noise[0], component_means, divergence_weight[None], free_floor[None], first_gain[None],
            second_gain[None],
        ),
        (
            whole, quarters, query_weight, key_weight, value_weight, output_weight, hidden_weight, down_weight,
            mean_weight, logvar_weight,
        ),
        cells, width, inner, latents,
    )
    table_grad = table_rows_grad(first_row, gene_ids, panel_sum, table_rows)
    bias_rows = inner // 8 // 128
    small_hidden = small[4 : 4 + bias_rows].reshape(-1)
    small_down = small[8]
    small_centres = small[16 : 16 + component_means.shape[0], : latents // 8]
    return (
        decoded[None],
        divergence,
        table_grad,
        small[0],
        small[1],
        query_grad.astype(F32),
        key_grad.astype(F32),
        value_grad.astype(F32),
        output_grad.astype(F32),
        small[2],
        small[3],
        hidden_grad.astype(F32),
        small_hidden,
        down_grad.astype(F32),
        small_down,
        mean_grad.astype(F32),
        logvar_grad.astype(F32),
        small_centres,
        decoder_grad.astype(F32),
    )


def solution(mesh):
    placed = (
        P("slide", "blk", None),
        P("slide", "blk"),
        P(),
        P("slide", None, "blk"),
        P("slide", "blk"),
        P("slide", "blk", None),
        P("slide", "blk", None),
        P("blk", None),
        P(),
        P(),
        P(),
        P(),
        P(),
        P(),
        P(),
        P(),
        P(),
        P(),
        P(),
        P(),
        P(),
        P(),
        P(),
        P(),
        P(),
        P(),
    )
    return jax.shard_map(
        on_device_fast if fits(mesh) else on_device_general,
        mesh=mesh,
        in_specs=placed,
        out_specs=(
            P("slide", "blk", None),
            P(),
            P("blk", None),
            P("blk"),
            P("blk"),
            P("blk", None),
            P("blk", None),
            P("blk", None),
            P("blk", None),
            P("blk"),
            P("blk"),
            P("blk", None),
            P("blk"),
            P("blk", None),
            P("blk"),
            P("blk", None),
            P("blk", None),
            P(None, "blk"),
            P("blk", None),
        ),
        check_vma=False,
    )
```

```python
import functools
import math

import jax
import jax.numpy as jnp
import numpy as np
from jax import lax
from jax.experimental import pallas as pl
from jax.experimental.pallas import tpu as pltpu
from jax.sharding import PartitionSpec as P

HEAD_DIM = 64
MESH = pl.DeviceIdType.MESH
F32 = jnp.float32
BF16 = jnp.bfloat16


def normalized(counts, library):
    scaled = counts.astype(jnp.float32) * (10000.0 / library.astype(jnp.float32))[..., None]
    return jnp.log1p(scaled)


def position_code(coords, model_width):
    quarter = model_width // 4
    freqs = jnp.exp(-math.log(10000.0) * jnp.arange(quarter, dtype=jnp.float32) / quarter)
    along_x = coords[0].astype(jnp.float32)[:, None] * freqs[None, :]
    along_y = coords[1].astype(jnp.float32)[:, None] * freqs[None, :]
    return jnp.concatenate(
        [jnp.sin(along_x), jnp.cos(along_x), jnp.sin(along_y), jnp.cos(along_y)], axis=1
    )


def layer_norm(inputs, scaling, offsets):
    centre = inputs - jnp.mean(inputs, axis=-1, keepdims=True)
    spread = jnp.mean(centre * centre, axis=-1, keepdims=True)
    return centre * lax.rsqrt(spread + 1e-05) * scaling + offsets


def gelu_tanh(inputs):
    return (
        0.5
        * inputs
        * (1.0 + jnp.tanh(0.7978845608028654 * (inputs + 0.044715 * inputs * inputs * inputs)))
    )


def divergence_cells(mean_part, logvar_part, centres):
    latent_width = mean_part.shape[-1]
    crossed = jnp.dot(mean_part, centres.T, precision=lax.Precision.HIGHEST)
    centre_square = jnp.sum(centres * centres, axis=-1)
    logits = (crossed - 0.5 * centre_square[None, :]) / math.sqrt(latent_width)
    shifted = jnp.exp(logits - jnp.max(logits, axis=-1, keepdims=True))
    resp = shifted / jnp.sum(shifted, axis=-1, keepdims=True)
    mixed = jnp.dot(resp, centres, precision=lax.Precision.HIGHEST)
    mixed_square = jnp.dot(resp, centres * centres, precision=lax.Precision.HIGHEST)
    return 0.5 * (
        jnp.exp(logvar_part)
        - 1.0
        - logvar_part
        + mean_part * mean_part
        - 2.0 * mean_part * mixed
        + mixed_square
    )


def to_heads(array, head_count):
    return array.reshape(array.shape[0], head_count, -1).transpose(1, 0, 2)


def from_heads(array):
    return array.transpose(1, 0, 2).reshape(array.shape[1], -1)


def matmul(left, right):
    return jnp.dot(left, right, preferred_element_type=jnp.float32)


def on_device_general(
    counts,
    library,
    gene_ids,
    positions,
    slide_of_cell,
    latent_noise,
    decoded_grad,
    gene_table,
    first_gain,
    first_shift,
    query_weight,
    key_weight,
    value_weight,
    output_weight,
    second_gain,
    second_shift,
    hidden_weight,
    hidden_bias,
    down_weight,
    down_bias,
    mean_weight,
    logvar_weight,
    component_means,
    decoder_weight,
    divergence_weight,
    free_floor,
):
    cell_count = counts.shape[1]
    model_width = gene_table.shape[1]
    head_count = model_width // HEAD_DIM
    score_scale = HEAD_DIM ** (-0.5)
    express = normalized(counts[0], library[0]).astype(jnp.bfloat16)
    table_rows = gene_table.shape[0]
    first_row = lax.axis_index("blk") * table_rows
    selector = (
        gene_ids[:, None] == first_row + jnp.arange(table_rows, dtype=jnp.int32)[None, :]
    ).astype(jnp.bfloat16)
    panel_part = matmul(selector, gene_table)
    panel_weight = lax.psum(panel_part, "blk").astype(jnp.bfloat16)
    hidden_start = matmul(express, panel_weight) + position_code(positions[0], model_width)
    normed_one = layer_norm(hidden_start, first_gain, first_shift).astype(jnp.bfloat16)
    query_low = matmul(normed_one, query_weight).astype(jnp.bfloat16)
    key_low = matmul(normed_one, key_weight).astype(jnp.bfloat16)
    value_low = matmul(normed_one, value_weight).astype(jnp.bfloat16)
    slide_labels = slide_of_cell[0].astype(jnp.bfloat16)
    keys_all, values_all, labels_all = (
        lax.all_gather(key_low, "blk", axis=0, tiled=True),
        lax.all_gather(value_low, "blk", axis=0, tiled=True),
        lax.all_gather(slide_labels, "blk", axis=0, tiled=True),
    )
    same_slide = slide_labels[:, None] == labels_all[None, :]
    query_heads = to_heads(query_low, head_count)
    key_heads = to_heads(keys_all, head_count)
    value_heads = to_heads(values_all, head_count)

    def head_forward(head_items):
        query_head, key_head, value_head = head_items
        scores = (
            jnp.einsum("qd,kd->qk", query_head, key_head, preferred_element_type=jnp.float32)
            * score_scale
        )
        scores = jnp.where(same_slide, scores, -1e30)
        row_max = jnp.max(scores, axis=1, keepdims=True)
        shifted = jnp.exp(scores - row_max)
        row_sum = jnp.sum(shifted, axis=1, keepdims=True)
        shares = shifted / row_sum
        attended_head = jnp.einsum(
            "qk,kd->qd", shares.astype(jnp.bfloat16), value_head, preferred_element_type=jnp.float32
        )
        return (attended_head, row_max[:, 0], row_sum[:, 0])

    attended_heads, row_maxes, row_sums = lax.map(
        head_forward, (query_heads, key_heads, value_heads)
    )
    attended = from_heads(attended_heads).astype(jnp.bfloat16)
    hidden_middle = hidden_start + matmul(attended, output_weight)
    normed_two = layer_norm(hidden_middle, second_gain, second_shift).astype(jnp.bfloat16)
    inner_sum = matmul(normed_two, hidden_weight) + hidden_bias
    act_low = gelu_tanh(inner_sum).astype(jnp.bfloat16)
    hidden_final = hidden_middle + matmul(act_low, down_weight) + down_bias
    base_low = hidden_final.astype(jnp.bfloat16)
    mean_lat = matmul(base_low, mean_weight)
    log_var = matmul(base_low, logvar_weight)
    noise_local = latent_noise[0]

    def bottleneck(mean_part, logvar_part, centres):
        return (
            mean_part + jnp.exp(0.5 * logvar_part) * noise_local,
            divergence_cells(mean_part, logvar_part, centres),
        )

    (latent, kl_cell), pull_latent = jax.vjp(bottleneck, mean_lat, log_var, component_means)
    latent_low = latent.astype(jnp.bfloat16)
    decoded = matmul(latent_low, decoder_weight)
    everyone = cell_count * lax.axis_size("blk") * lax.axis_size("slide")
    kl_sum = lax.psum(jnp.sum(kl_cell, axis=0), ("slide", "blk"))
    kl_mean = kl_sum / everyone
    divergence = divergence_weight * jnp.mean(jnp.maximum(kl_mean, free_floor))
    binding = (kl_mean > free_floor).astype(jnp.float32)
    grad_source = decoded_grad[0]
    grad_latent = matmul(grad_source, decoder_weight.T)
    decoder_grad = matmul(latent_low.T, grad_source)
    grad_kl = jnp.broadcast_to(divergence_weight * binding, kl_cell.shape)
    grad_mean, grad_logvar, centres_grad = pull_latent((grad_latent, grad_kl))
    grad_mean_low = grad_mean.astype(jnp.bfloat16)
    grad_logvar_low = grad_logvar.astype(jnp.bfloat16)
    mean_grad = matmul(base_low.T, grad_mean_low)
    logvar_grad = matmul(base_low.T, grad_logvar_low)
    grad_final = matmul(grad_mean_low, mean_weight.T) + matmul(grad_logvar_low, logvar_weight.T)
    grad_branch = grad_final.astype(jnp.bfloat16)
    down_grad = matmul(act_low.T, grad_branch)
    down_bias_grad = jnp.sum(grad_branch.astype(jnp.float32), axis=0)
    grad_act = matmul(grad_branch, down_weight.T)
    gelu_pull = jax.vjp(gelu_tanh, inner_sum)[1]
    grad_inner = gelu_pull(grad_act)[0].astype(jnp.bfloat16)
    hidden_grad = matmul(normed_two.T, grad_inner)
    hidden_bias_grad = jnp.sum(grad_inner.astype(jnp.float32), axis=0)
    norm_two_pull = jax.vjp(layer_norm, hidden_middle, second_gain, second_shift)[1]
    grad_norm_two, second_gain_grad, second_shift_grad = norm_two_pull(
        matmul(grad_inner, hidden_weight.T)
    )
    grad_middle = grad_final + grad_norm_two
    grad_out = grad_middle.astype(jnp.bfloat16)
    output_grad = matmul(attended.T, grad_out)
    grad_attended = matmul(grad_out, output_weight.T).astype(jnp.bfloat16)
    keys_again, values_again = (
        lax.all_gather(key_low, "blk", axis=0, tiled=True),
        lax.all_gather(value_low, "blk", axis=0, tiled=True),
    )
    key_heads_back = to_heads(keys_again, head_count)
    value_heads_back = to_heads(values_again, head_count)
    grad_heads_local = to_heads(grad_attended, head_count)

    def head_queries(head_items):
        query_head, key_head, value_head, grad_head, row_max, row_sum = head_items
        scores = (
            jnp.einsum("qd,kd->qk", query_head, key_head, preferred_element_type=jnp.float32)
            * score_scale
        )
        scores = jnp.where(same_slide, scores, -1e30)
        shares = jnp.exp(scores - row_max[:, None]) / row_sum[:, None]
        grad_shares = jnp.einsum(
            "qd,kd->qk", grad_head, value_head, preferred_element_type=jnp.float32
        )
        inner_dot = jnp.sum(shares * grad_shares, axis=1, keepdims=True)
        grad_scores = (shares * (grad_shares - inner_dot)).astype(jnp.bfloat16)
        grad_query_head = (
            jnp.einsum("qk,kd->qd", grad_scores, key_head, preferred_element_type=jnp.float32)
            * score_scale
        )
        return (grad_query_head, inner_dot[:, 0])

    grad_query_heads, inner_dots = lax.map(
        head_queries,
        (query_heads, key_heads_back, value_heads_back, grad_heads_local, row_maxes, row_sums),
    )
    queries_group, grads_group = (
        lax.all_gather(query_low, "blk", axis=0, tiled=True),
        lax.all_gather(grad_attended, "blk", axis=0, tiled=True),
    )
    maxes_group, totals_group, dots_group = (
        lax.all_gather(row_maxes, "blk", axis=1, tiled=True),
        lax.all_gather(row_sums, "blk", axis=1, tiled=True),
        lax.all_gather(inner_dots, "blk", axis=1, tiled=True),
    )
    mask_back = labels_all[:, None] == slide_labels[None, :]

    def head_keys(head_items):
        query_head, key_head, value_head, grad_head, row_max, row_sum, inner_dot = head_items
        scores = (
            jnp.einsum("qd,kd->qk", query_head, key_head, preferred_element_type=jnp.float32)
            * score_scale
        )
        scores = jnp.where(mask_back, scores, -1e30)
        shares = jnp.exp(scores - row_max[:, None]) / row_sum[:, None]
        grad_shares = jnp.einsum(
            "qd,kd->qk", grad_head, value_head, preferred_element_type=jnp.float32
        )
        grad_scores = (shares * (grad_shares - inner_dot[:, None])).astype(jnp.bfloat16)
        grad_key_head = (
            jnp.einsum("qk,qd->kd", grad_scores, query_head, preferred_element_type=jnp.float32)
            * score_scale
        )
        grad_value_head = jnp.einsum(
            "qk,qd->kd", shares.astype(jnp.bfloat16), grad_head, preferred_element_type=jnp.float32
        )
        return (grad_key_head, grad_value_head)

    grad_key_heads, grad_value_heads = lax.map(
        head_keys,
        (
            to_heads(queries_group, head_count),
            to_heads(key_low, head_count),
            to_heads(value_low, head_count),
            to_heads(grads_group, head_count),
            maxes_group,
            totals_group,
            dots_group,
        ),
    )
    grad_query_low = from_heads(grad_query_heads).astype(jnp.bfloat16)
    grad_key = from_heads(grad_key_heads)
    grad_value = from_heads(grad_value_heads)
    grad_key_low = grad_key.astype(jnp.bfloat16)
    grad_value_low = grad_value.astype(jnp.bfloat16)
    query_grad = matmul(normed_one.T, grad_query_low)
    key_grad = matmul(normed_one.T, grad_key_low)
    value_grad = matmul(normed_one.T, grad_value_low)
    grad_norm_input = (
        matmul(grad_query_low, query_weight.T)
        + matmul(grad_key_low, key_weight.T)
        + matmul(grad_value_low, value_weight.T)
    )
    norm_one_pull = jax.vjp(layer_norm, hidden_start, first_gain, first_shift)[1]
    grad_norm_one, first_gain_grad, first_shift_grad = norm_one_pull(grad_norm_input)
    grad_start = grad_middle + grad_norm_one
    grad_encoded = grad_start.astype(jnp.bfloat16)
    panel_grad = matmul(express.T, grad_encoded)
    panel_total = lax.psum(panel_grad, ("slide", "blk"))
    table_grad = jnp.dot(
        selector.astype(jnp.float32).T, panel_total, precision=lax.Precision.HIGHEST
    )
    shares_grads = (
        lax.psum_scatter(first_gain_grad, "blk", scatter_dimension=0, tiled=True),
        lax.psum_scatter(first_shift_grad, "blk", scatter_dimension=0, tiled=True),
        lax.psum_scatter(query_grad, "blk", scatter_dimension=0, tiled=True),
        lax.psum_scatter(key_grad, "blk", scatter_dimension=0, tiled=True),
        lax.psum_scatter(value_grad, "blk", scatter_dimension=0, tiled=True),
        lax.psum_scatter(output_grad, "blk", scatter_dimension=0, tiled=True),
        lax.psum_scatter(second_gain_grad, "blk", scatter_dimension=0, tiled=True),
        lax.psum_scatter(second_shift_grad, "blk", scatter_dimension=0, tiled=True),
        lax.psum_scatter(hidden_grad, "blk", scatter_dimension=0, tiled=True),
        lax.psum_scatter(hidden_bias_grad, "blk", scatter_dimension=0, tiled=True),
        lax.psum_scatter(down_grad, "blk", scatter_dimension=0, tiled=True),
        lax.psum_scatter(down_bias_grad, "blk", scatter_dimension=0, tiled=True),
        lax.psum_scatter(mean_grad, "blk", scatter_dimension=0, tiled=True),
        lax.psum_scatter(logvar_grad, "blk", scatter_dimension=0, tiled=True),
        lax.psum_scatter(centres_grad, "blk", scatter_dimension=1, tiled=True),
        lax.psum_scatter(decoder_grad, "blk", scatter_dimension=0, tiled=True),
    )
    summed = (
        lax.psum(shares_grads[0].astype(jnp.bfloat16), "slide").astype(jnp.float32),
        lax.psum(shares_grads[1].astype(jnp.bfloat16), "slide").astype(jnp.float32),
        lax.psum(shares_grads[2].astype(jnp.bfloat16), "slide").astype(jnp.float32),
        lax.psum(shares_grads[3].astype(jnp.bfloat16), "slide").astype(jnp.float32),
        lax.psum(shares_grads[4].astype(jnp.bfloat16), "slide").astype(jnp.float32),
        lax.psum(shares_grads[5].astype(jnp.bfloat16), "slide").astype(jnp.float32),
        lax.psum(shares_grads[6].astype(jnp.bfloat16), "slide").astype(jnp.float32),
        lax.psum(shares_grads[7].astype(jnp.bfloat16), "slide").astype(jnp.float32),
        lax.psum(shares_grads[8].astype(jnp.bfloat16), "slide").astype(jnp.float32),
        lax.psum(shares_grads[9].astype(jnp.bfloat16), "slide").astype(jnp.float32),
        lax.psum(shares_grads[10].astype(jnp.bfloat16), "slide").astype(jnp.float32),
        lax.psum(shares_grads[11].astype(jnp.bfloat16), "slide").astype(jnp.float32),
        lax.psum(shares_grads[12].astype(jnp.bfloat16), "slide").astype(jnp.float32),
        lax.psum(shares_grads[13].astype(jnp.bfloat16), "slide").astype(jnp.float32),
        lax.psum(shares_grads[14].astype(jnp.bfloat16), "slide").astype(jnp.float32),
        lax.psum(shares_grads[15].astype(jnp.bfloat16), "slide").astype(jnp.float32),
    )
    return (decoded[None], divergence, table_grad) + tuple(summed)


def fits(mesh):
    return mesh.shape["slide"] == 4 and mesh.shape["blk"] == 8


def flipped(index, mask):
    for bit in (1, 2, 4):
        if mask & bit:
            index = index + bit - 2 * bit * ((index // bit) % 2)
    return index


def greet(slide, blk, peers):
    barrier = pltpu.get_barrier_semaphore()
    for far_slide, far_blk in peers:
        pl.semaphore_signal(
            barrier,
            inc=1,
            device_id={"slide": flipped(slide, far_slide), "blk": flipped(blk, far_blk)},
            device_id_type=MESH,
        )
    pl.semaphore_wait(barrier, len(peers))


BLK_PEERS = [(0, far) for far in range(1, 8)]
SLIDE_PEERS = [(far, 0) for far in range(1, 4)]


def dot_nt(left, right):
    return lax.dot_general(left, right, (((1,), (1,)), ((), ())), preferred_element_type=F32)


def dot_tn(left, right):
    return lax.dot_general(left, right, (((0,), (0,)), ((), ())), preferred_element_type=F32)


def head_scores(query, key, same_slide):
    scores = jnp.where(same_slide, dot_nt(query, key) * (HEAD_DIM**-0.5), -1e30)
    shifted = jnp.exp(scores - jnp.max(scores, axis=1, keepdims=True))
    return shifted / jnp.sum(shifted, axis=1, keepdims=True)


Z_FIRST = ("hidden1",)


class Links:
    def __init__(self, slide, blk, send_sem, recv_sem):
        self.slide, self.blk = slide, blk
        self.send_sem, self.recv_sem = send_sem, recv_sem
        self.copies = []

    def send(self, source, target, far_slide, far_blk):
        number = len(self.copies)
        copy = pltpu.make_async_remote_copy(
            src_ref=source,
            dst_ref=target,
            send_sem=self.send_sem.at[number],
            recv_sem=self.recv_sem.at[number],
            device_id={
                "slide": flipped(self.slide, far_slide),
                "blk": flipped(self.blk, far_blk),
            },
            device_id_type=MESH,
        )
        copy.start()
        self.copies.append(copy)
        return copy

    def finish(self):
        for copy in self.copies:
            copy.wait_send()


def spread_everywhere(links, slot):
    slide, blk = links.slide, links.blk
    copies = {}

    def push(rel_slide, rel_blk, to_slide, to_blk):
        block = slot(flipped(slide, rel_slide), flipped(blk, rel_blk))
        copies[(rel_slide ^ to_slide, rel_blk ^ to_blk)] = links.send(block, block, to_slide, to_blk)

    for far in (2, 4, 6):
        push(0, 0, 0, far)
    push(0, 0, 0, 1)
    push(0, 0, 2, 0)
    push(0, 0, 1, 0)
    yield
    for rel in (2, 4, 6):
        copies[0, rel].wait_recv()
        push(0, rel, 0, 1)
        push(0, rel, 2, 0)
        push(0, rel, 1, 0)
    yield
    for rel in (1, 3, 5, 7):
        copies[0, rel].wait_recv()
        push(0, rel, 2, 0)
        push(0, rel, 1, 0)
    yield
    for rel in (0, 2, 4, 6, 1, 3, 5, 7):
        copies[2, rel].wait_recv()
        push(2, rel, 1, 0)
    yield
    for far in (1, 3):
        for rel in (0, 2, 4, 6, 1, 3, 5, 7):
            copies[far, rel].wait_recv()
    yield


class Reduction:
    def __init__(self, links, left, right, rows, width, dense, buffers):
        self.links, self.left, self.right = links, left, right
        self.rows, self.width, self.dense = rows, width, dense
        self.away, self.came, self.kept, self.pieces = buffers
        self.along_x, self.along_z = links.blk % 2, links.blk // 2

    def tiles(self, which, store):
        def tile(i, carry):
            place = which * 2 + i if self.dense else i * 2 + which
            product = dot_tn(self.left(pl.multiple_of(place * 128, 128)), self.right())
            store(pl.ds(pl.multiple_of(i * 128, 128), 128), product)
            return carry

        lax.fori_loop(0, self.rows * 4 // 128, tile, 0)

    def send_x(self):
        def store(where, product):
            self.away[where, :] = product.astype(BF16)

        self.tiles(1 - self.along_x, store)
        self.copy_x = self.links.send(self.away, self.came, 0, 1)

    def piece(self, far):
        return pl.ds(pl.multiple_of(flipped(self.along_z, far) * self.rows, self.rows), self.rows)

    def send_z(self):
        self.copy_x.wait_recv()

        def store(where, product):
            self.kept[where, :] = (product + self.came[where, :].astype(F32)).astype(BF16)

        self.tiles(self.along_x, store)
        self.copies_z = [
            self.links.send(self.kept.at[self.piece(far)], self.pieces.at[far // 2], 0, 2) for far in (3, 1)
        ]

    def send_far(self):
        for copy in self.copies_z:
            copy.wait_recv()
        where = self.piece(2)
        self.kept[where, :] = (self.kept[where, :].astype(F32) + self.pieces[1].astype(F32)).astype(BF16)
        self.copy_far = self.links.send(self.kept.at[where], self.pieces.at[2], 0, 4)

    def total(self):
        self.copy_far.wait_recv()
        own = self.kept[self.piece(0), :]
        return ((own.astype(F32) + self.pieces[0].astype(F32)) + self.pieces[2].astype(F32)).astype(BF16)


class ReductionAlongZ(Reduction):
    def tiles(self, start, store):
        step = 2 - 4 * ((start // 2) % 2)

        def tile(i, carry):
            place = (start + (i // 2) * step) * 2 + i % 2
            product = dot_tn(self.left(pl.multiple_of(place * 128, 128)), self.right())
            store(pl.ds(pl.multiple_of(i * 128, 128), 128), product)
            return carry

        lax.fori_loop(0, 4, tile, 0)

    def send_x(self):
        def store(where, product):
            self.away[where, :] = product.astype(BF16)

        self.tiles(flipped(self.along_z, 1), store)
        self.copy_x = self.links.send(self.away, self.came, 0, 2)

    def send_z(self):
        self.copy_x.wait_recv()

        def store(where, product):
            self.kept[where, :] = (product + self.came[where, :].astype(F32)).astype(BF16)

        self.tiles(self.along_z, store)
        self.copies_z = [
            self.links.send(self.kept.at[pl.ds((2 + side) * self.rows, self.rows)], self.pieces.at[side], 0, 4)
            for side in range(2)
        ]

    def block(self, side):
        return pl.ds(pl.multiple_of(side * self.rows, self.rows), self.rows)

    def send_far(self):
        for copy in self.copies_z:
            copy.wait_recv()
        other = 1 - self.along_x
        where = self.block(other)
        self.kept[where, :] = (self.kept[where, :].astype(F32) + self.pieces[other].astype(F32)).astype(BF16)
        self.copy_far = self.links.send(self.kept.at[where], self.pieces.at[2], 0, 1)

    def total(self):
        self.copy_far.wait_recv()
        own = self.kept[self.block(self.along_x), :].astype(F32) + self.pieces[self.along_x].astype(F32)
        return (own + self.pieces[2].astype(F32)).astype(BF16)


def spread_slide(links, slot, total):
    slide = links.slide
    own, far = slot(slide), slot(flipped(slide, 2))
    own[...] = total
    across = links.send(own, own, 2, 0)
    beside = links.send(own, own, 1, 0)
    yield
    across.wait_recv()
    last = links.send(far, far, 1, 0)
    yield
    beside.wait_recv()
    last.wait_recv()
    yield


def reductions_of(cells, width, inner, latents):
    return [
        ("decoder", latents // 8, width // 4, True),
        ("down0", inner // 32, width // 2, False),
        ("down1", inner // 32, width // 2, False),
        ("mean", width // 8, latents // 4, False),
        ("logvar", width // 8, latents // 4, False),
        ("hidden0", width // 8, inner // 8, False),
        ("hidden1", width // 8, inner // 8, False),
        ("output", width // 8, width // 4, False),
        ("panel", width // 8, width // 4, False),
        ("query", width // 8, width // 4, False),
        ("key", width // 8, width // 4, False),
        ("value", width // 8, width // 4, False),
    ]


def across(links, ref, columns, cells):
    def rows(place):
        return ref.at[pl.ds(place * cells, cells), columns]

    far = links.send(rows(0), rows(2), 2, 0)
    near = links.send(rows(0), rows(1), 1, 0)
    yield
    far.wait_recv()
    last = links.send(rows(2), rows(3), 1, 0)
    yield
    near.wait_recv()
    last.wait_recv()
    yield


def norm_parts(hidden):
    centre = hidden - jnp.mean(hidden, axis=1, keepdims=True)
    invert = lax.rsqrt(jnp.mean(centre * centre, axis=1, keepdims=True) + 1e-05)
    return centre * invert, invert


def norm_back(hidden, gain, grad):
    unit, invert = norm_parts(hidden)
    gain_grad = jnp.sum(grad * unit, axis=0, keepdims=True)
    shift_grad = jnp.sum(grad, axis=0, keepdims=True)
    grad_unit = grad * gain
    grad_hidden = invert * (
        grad_unit
        - jnp.mean(grad_unit, axis=1, keepdims=True)
        - unit * jnp.mean(grad_unit * unit, axis=1, keepdims=True)
    )
    return grad_hidden, gain_grad, shift_grad


def exact_dot(left, right, dims):
    return lax.dot_general(
        left, right, (dims, ((), ())), precision=lax.Precision.HIGHEST, preferred_element_type=F32
    )


def mixture(mean_part, centres):
    crossed = exact_dot(mean_part, centres, ((1,), (1,)))
    ones = jnp.ones((8, centres.shape[1]), F32)
    centre_square = exact_dot(ones, centres * centres, ((1,), (1,)))[0:1]
    logits = (crossed - 0.5 * centre_square) / math.sqrt(centres.shape[1])
    shifted = jnp.exp(logits - jnp.max(logits, axis=1, keepdims=True))
    resp = shifted / jnp.sum(shifted, axis=1, keepdims=True)
    return resp, exact_dot(resp, centres, ((1,), (0,)))


def slide_masks(land, row_labels, col_labels, cells):
    for block in range(8):
        line = land[block, 3 * cells : 3 * cells + 1, :].astype(F32)
        col_labels[:, block * cells : (block + 1) * cells] = line
        row_labels[block * cells : (block + 1) * cells, :] = jnp.broadcast_to(line, (cells, cells)).T


def forward_kernel(
    ids_ref, counts_ref, library_ref, positions_ref, freqs_ref, labels_ref, noise_ref, source_ref, gain_one, shift_one,
    gain_two, shift_two, hidden_bias, down_bias, centres_ref,
    table_hbm, wq_hbm, wk_hbm, wv_hbm, wo_hbm, wh_hbm, wd_hbm, wm_hbm, wl_hbm, wdec_hbm,
    land_out, start_out, middle_out, inner_out, mean_out, logvar_out, glatent_out, base_out, latent_out, kl_out, decoded_out,
    whole_out, quarter_out,
    table, wq, wk, wv, wo, wh, wd, wm, wl, wdec, part, panel_land, panel, qkv_send, att_send, att_land, row_labels, col_labels,
    act_parts, final, kl_own, kl_slides, kl_sum, kl_blks, load_sem, send_sem, recv_sem,
):
    slide, blk = lax.axis_index("slide"), lax.axis_index("blk")
    cells, width = counts_ref.shape
    inner, latents, per = inner_out.shape[1], mean_out.shape[1], width // 8
    loads = []
    for number, (source, target) in enumerate(
        [(table_hbm, table), (wq_hbm, wq), (wk_hbm, wk), (wv_hbm, wv), (wo_hbm, wo), (wh_hbm, wh), (wd_hbm, wd), (wm_hbm, wm), (wl_hbm, wl), (wdec_hbm, wdec)]
    ):
        loads.append(pltpu.make_async_copy(source, target, load_sem.at[number]))
        loads[-1].start()
    greet(slide, blk, SLIDE_PEERS + BLK_PEERS)
    links = Links(slide, blk, send_sem, recv_sem)

    def column(line):
        return jnp.broadcast_to(line, (line.shape[1], line.shape[1])).T[:, 0:1]

    genes = ids_ref.shape[1]
    table_rows, block_rows = table.shape[0], genes // 64
    first = (blk * table_rows).astype(F32)
    loads[0].wait()
    for side in range(2):
        ids = ids_ref[:, pl.ds(pl.multiple_of(slide * (genes // 4) + side * 128, 128), 128)].astype(F32)
        places = lax.broadcasted_iota(jnp.int32, (128, table_rows), 1).astype(F32) + first
        selector = (places == column(ids)).astype(F32).astype(BF16)
        rows = jnp.dot(selector, table[...], preferred_element_type=F32).astype(BF16)
        part[side] = rows.reshape(8, block_rows, width)
    part_copies = [
        [links.send(part.at[side, flipped(blk, far)], panel_land.at[side, far], 0, far) for far in (6, 4, 2, 7, 5, 3, 1)]
        for side in range(2)
    ]
    scale = column(10000.0 / library_ref[...].astype(F32))
    express = jnp.log(1.0 + counts_ref[...].astype(F32) * scale).astype(BF16)
    whole_out[0:cells, 0:width] = express
    quarter = width // 4
    for axis in range(2):
        angle = column(positions_ref[axis : axis + 1, :].astype(F32)) * freqs_ref[...]
        start_out[:, 2 * axis * quarter : (2 * axis + 1) * quarter] = jnp.sin(angle)
        start_out[:, (2 * axis + 1) * quarter : (2 * axis + 2) * quarter] = jnp.cos(angle)
    spreads = []
    for side in range(2):
        total = part[side, blk].astype(F32)
        for place, far in enumerate((6, 4, 2, 7, 5, 3, 1)):
            part_copies[side][place].wait_recv()
            total = total + panel_land[side, far].astype(F32)
        panel[slide, side, blk] = total.astype(BF16)
        spreads.append(spread_everywhere(links, lambda far_slide, far_blk, side=side: panel.at[far_slide, side, far_blk]))
        next(spreads[side])
        if side:
            next(spreads[1])
            next(spreads[0])
        else:
            next(spreads[0])
    next(spreads[1])
    next(spreads[0])
    next(spreads[1])
    next(spreads[0])
    next(spreads[1])
    send_express = across(links, whole_out, pl.ds(0, width), cells)
    next(send_express)

    def source_part(which):
        return source_ref.at[:, pl.ds(pl.multiple_of(which * quarter, 128), quarter)]

    def source_slot(place):
        return quarter_out.at[pl.ds(place * cells, cells), pl.ds(inner // 4, quarter)]

    source_copies = [links.send(source_part(flipped(slide, far)), source_slot(far), far, 0) for far in (2, 3, 1)]
    source_slot(0)[...] = source_part(slide)[...]

    hidden_start = start_out[...] + jnp.dot(express, panel[...].reshape(width, width), preferred_element_type=F32)
    start_out[...] = hidden_start
    normed = (norm_parts(hidden_start)[0] * gain_one[...] + shift_one[...]).astype(BF16)
    whole_out[0:cells, width : 2 * width] = normed
    qkv_send[:, 3 * cells :, :] = jnp.broadcast_to(labels_ref[...].astype(F32).astype(BF16).reshape(1, 1, cells), (8, 16, per))
    for number in (1, 2, 3):
        loads[number].wait()

    along_x, along_z = blk % 2, blk // 2
    qkv_copies = []
    for far in (3, 2, 1, 0):
        pair = flipped(along_z, far)
        columns = pl.ds(pl.multiple_of(pair * 2 * per, 128), 2 * per)
        for number, weight in enumerate((wq, wk, wv)):
            product = jnp.dot(normed, weight[:, columns], preferred_element_type=F32).astype(BF16)
            for side in range(2):
                qkv_send[pair * 2 + side, number * cells : (number + 1) * cells, :] = product[:, side * per : (side + 1) * per]
        for side in (1, 0):
            if far or side:
                target = flipped(pair * 2 + along_x, side)
                qkv_copies.append(links.send(qkv_send.at[target], land_out.at[blk], 0, 2 * far + side))
    land_out[blk] = qkv_send[blk]
    next(send_express)
    send_normed = across(links, whole_out, pl.ds(width, width), cells)
    next(send_normed)
    for copy in qkv_copies:
        copy.wait_recv()

    slide_masks(land_out, row_labels, col_labels, cells)
    key = land_out[:, cells : 2 * cells, :].reshape(8 * cells, per)
    value = land_out[:, 2 * cells : 3 * cells, :].reshape(8 * cells, per)
    att_copies = []
    for far in (3, 2, 1, 0):
        pair = flipped(along_z, far)
        query = land_out[pl.ds(pair * 2, 2), 0:cells, :].reshape(2 * cells, per)
        same_slide = row_labels[pl.ds(pl.multiple_of(pair * 2 * cells, 128), 2 * cells), 0:1] == col_labels[...]
        lane = lax.broadcasted_iota(jnp.int32, query.shape, 1)
        out = None
        for head in range(per // HEAD_DIM):
            mine = lane // HEAD_DIM == head
            shares = head_scores(jnp.where(mine, query, 0), key, same_slide)
            part = jnp.dot(shares.astype(BF16), value, preferred_element_type=F32)
            out = part if out is None else jnp.where(mine, part, out)
        att_send[pl.ds(pair * 2, 2)] = out.astype(BF16).reshape(2, cells, per)
        for side in (1, 0):
            if far or side:
                target = flipped(pair * 2 + along_x, side)
                att_copies.append(links.send(att_send.at[target], att_land.at[blk], 0, 2 * far + side))
    att_land[blk] = att_send[blk]
    next(send_normed)
    for copy in att_copies:
        copy.wait_recv()
    for block in range(8):
        whole_out[0:cells, 2 * width + block * per : 2 * width + (block + 1) * per] = att_land[block]
    send_attended = across(links, whole_out, pl.ds(2 * width, width), cells)
    next(send_attended)

    loads[4].wait()
    hidden_middle = start_out[...] + jnp.dot(
        whole_out[0:cells, 2 * width : 3 * width], wo[...], preferred_element_type=F32
    )
    middle_out[...] = hidden_middle
    normed_two = (norm_parts(hidden_middle)[0] * gain_two[...] + shift_two[...]).astype(BF16)
    whole_out[0:cells, 3 * width :] = normed_two
    send_two = across(links, whole_out, pl.ds(3 * width, width), cells)
    next(send_two)
    loads[5].wait()
    loads[6].wait()
    final[...] = hidden_middle + down_bias[...]
    chunk = inner // 8

    def feed(j, carry):
        where = pl.ds(pl.multiple_of(j * chunk, 128), chunk)
        inner_sum = jnp.dot(whole_out[0:cells, 3 * width :], wh[:, where], preferred_element_type=F32) + hidden_bias[:, where]
        inner_out[:, where] = inner_sum
        act = gelu_tanh(inner_sum).astype(BF16)
        for block in range(4):
            act_parts[block, :, pl.ds(pl.multiple_of(j * (chunk // 4), 128), chunk // 4)] = act[:, block * (chunk // 4) : (block + 1) * (chunk // 4)]
        final[...] += jnp.dot(act, wd[where, :], preferred_element_type=F32)
        return carry

    lax.fori_loop(0, 8, feed, 0)
    act_copies = [
        links.send(act_parts.at[flipped(slide, far)], quarter_out.at[pl.ds(far * cells, cells), pl.ds(0, inner // 4)], far, 0)
        for far in (2, 3, 1)
    ]
    quarter_out[0:cells, 0 : inner // 4] = act_parts[slide]
    base = final[...].astype(BF16)
    base_out[...] = base
    for number in (7, 8, 9):
        loads[number].wait()
    mean_lat = jnp.dot(base, wm[...], preferred_element_type=F32)
    log_var = jnp.dot(base, wl[...], preferred_element_type=F32)
    mean_out[...] = mean_lat
    logvar_out[...] = log_var
    centres = centres_ref[...]
    resp, mixed = mixture(mean_lat, centres)
    mixed_square = exact_dot(resp, centres * centres, ((1,), (0,)))
    kl_cell = 0.5 * (
        jnp.exp(log_var) - 1.0 - log_var + mean_lat * mean_lat - 2.0 * mean_lat * mixed + mixed_square
    )
    kl_line = jnp.sum(kl_cell, axis=0, keepdims=True)
    kl_own[...] = jnp.zeros_like(kl_own)
    for block in range(latents // 128):
        kl_own[block : block + 1, :] = kl_line[:, block * 128 : (block + 1) * 128]
    kl_copies = [links.send(kl_own, kl_slides.at[slide], far, 0) for far in (2, 3, 1)]
    kl_slides[slide] = kl_own[...]
    latent = (mean_lat + jnp.exp(0.5 * log_var) * noise_ref[...]).astype(BF16)
    latent_out[...] = latent
    decoded_out[...] = jnp.dot(latent, wdec[...], preferred_element_type=F32)
    for copy in kl_copies:
        copy.wait_recv()
    kl_sum[...] = (kl_slides[0] + kl_slides[1]) + (kl_slides[2] + kl_slides[3])
    kl_copies = [links.send(kl_sum, kl_blks.at[blk], 0, far) for far in (6, 4, 2, 7, 5, 3, 1)]
    kl_blks[blk] = kl_sum[...]
    glatent_out[...] = dot_nt(source_ref[...], wdec[...])
    next(send_attended)
    next(send_two)
    for copy in kl_copies:
        copy.wait_recv()
    kl_total = kl_blks[0]
    for block in range(1, 8):
        kl_total = kl_total + kl_blks[block]
    kl_out[...] = kl_total
    for copy in source_copies + act_copies:
        copy.wait_recv()
    for sent in (send_express, send_normed, send_attended, send_two):
        next(sent)
    links.finish()


def forward(inputs, weights, cells, width, inner, latents):
    per = width // 8
    shape = jax.ShapeDtypeStruct
    vmem, left = pl.BlockSpec(memory_space=pltpu.VMEM), pl.BlockSpec(memory_space=pl.ANY)
    outs = (
        shape((8, 3 * cells + 16, per), BF16),
        shape((cells, width), F32),
        shape((cells, width), F32),
        shape((cells, inner), F32),
        shape((cells, latents), F32),
        shape((cells, latents), F32),
        shape((cells, latents), F32),
        shape((cells, width), BF16),
        shape((cells, latents), BF16),
        shape((8, 128), F32),
        shape((cells, width), F32),
        shape((4 * cells, 4 * width), BF16),
        shape((4 * cells, inner // 4 + width // 4), BF16),
    )
    copies = 144
    return pl.pallas_call(
        forward_kernel,
        out_shape=outs,
        in_specs=[vmem] * len(inputs) + [left] * len(weights),
        out_specs=[vmem] * len(outs),
        scratch_shapes=[pltpu.VMEM(weight.shape, BF16) for weight in weights]
        + [
            pltpu.VMEM((2, 8, width // 64, width), BF16),
            pltpu.VMEM((2, 8, width // 64, width), BF16),
            pltpu.VMEM((4, 2, 8, width // 64, width), BF16),
            pltpu.VMEM((8, 3 * cells + 16, per), BF16),
            pltpu.VMEM((8, cells, per), BF16),
            pltpu.VMEM((8, cells, per), BF16),
            pltpu.VMEM((8 * cells, cells), F32),
            pltpu.VMEM((1, 8 * cells), F32),
            pltpu.VMEM((4, cells, inner // 4), BF16),
            pltpu.VMEM((cells, width), F32),
            pltpu.VMEM((8, 128), F32),
            pltpu.VMEM((4, 8, 128), F32),
            pltpu.VMEM((8, 128), F32),
            pltpu.VMEM((8, 8, 128), F32),
            pltpu.SemaphoreType.DMA((len(weights),)),
            pltpu.SemaphoreType.DMA((copies,)),
            pltpu.SemaphoreType.DMA((copies,)),
        ],
        compiler_params=pltpu.CompilerParams(
            collective_id=1, has_side_effects=True, vmem_limit_bytes=62 << 20
        ),
        name="forward",
    )(*inputs, *weights)


ORDER = (
    ("bottleneck",), ("feed", 0), ("feed", 1), ("branch",), ("feed", 2), ("feed", 3), ("norm2",), ("att",),
    ("x", "down0"), ("gout",), ("masks",), ("lats",), ("base",), ("latent",), ("rows", 0), ("rows", 1),
    ("rows", 2), ("rows", 3), ("back",), ("x", "down1"), ("z", "down0"), ("relay", "latent"), ("relay", "base"),
    ("x", "hidden0"), ("f", "down0"), ("z", "down1"), ("in",), ("qkv",), ("norm1",), ("small",),
    ("relay", "latent"), ("relay", "base"), ("x", "hidden1"), ("x", "panel"), ("x", "query"), ("x", "key"),
    ("x", "value"), ("x", "mean"), ("x", "logvar"), ("x", "decoder"), ("x", "output"), ("f", "down1"), ("sums",),
    ("z", "hidden0"), ("s", "down0"), ("z", "panel"), ("s", "down1"), ("f", "hidden0"), ("f", "panel"),
    ("z", "hidden1"), ("z", "query"), ("z", "key"), ("z", "value"), ("panel",), ("z", "mean"), ("z", "logvar"),
    ("z", "decoder"), ("relay", "panel"), ("z", "output"), ("s", "hidden0"), ("f", "hidden1"), ("f", "query"),
    ("f", "key"), ("f", "value"), ("relay", "panel"), ("f", "mean"), ("f", "logvar"), ("f", "decoder"),
    ("f", "output"), ("relay", "panel"), ("s", "hidden1"), ("s", "query"), ("s", "key"), ("s", "value"),
    ("s", "mean"), ("s", "logvar"), ("s", "decoder"), ("s", "output"), ("s2", "decoder"), ("s2", "down0"),
    ("s2", "down1"), ("s2", "mean"), ("s2", "logvar"), ("s2", "hidden0"), ("s2", "output"), ("s2", "hidden1"),
    ("s2", "query"), ("s2", "key"), ("s2", "value"), ("done",), ("relay", "panel"), ("s2", "decoder"),
    ("s2", "down0"), ("s2", "down1"), ("s2", "mean"), ("s2", "logvar"), ("s2", "hidden0"), ("s2", "output"),
    ("s2", "hidden1"), ("s2", "query"), ("s2", "key"), ("s2", "value"),
)


def backward_kernel(
    land_ref, start_ref, middle_ref, inner_ref, mean_ref, logvar_ref, glatent_ref, base_ref, latent_ref, kl_ref, noise_ref,
    centres_ref, weight_ref, floor_ref, gain_one, gain_two,
    whole_hbm, quarter_hbm, wq_hbm, wk_hbm, wv_hbm, wo_hbm, wh_hbm, wd_hbm, wm_hbm, wl_hbm,
    panel_out, query_out, key_out, value_out, output_out, hidden_out, down_out, mean_out, logvar_out, decoder_out, small_out,
    whole, base_all, latent_all, quarter, wide_slots, wo, wm, wl, branch_all, gmean, glogvar, gmean_all, glogvar_all, ginner,
    ginner_all, gout, gout_all, gmiddle, gqkv_all, genc_all, row_ref, col_ref,
    att_send, att_land, dqkv, dqkv_land, dk_sum, dv_sum, grad_qkv, encoded, small, small_land, small_own, small_slides,
    load_sem, send_sem, recv_sem, *unit_refs,
):
    slide, blk = lax.axis_index("slide"), lax.axis_index("blk")
    cells, width = middle_ref.shape
    inner, latents, per = inner_ref.shape[1], mean_ref.shape[1], width // 8
    loads = {}

    def load(name, source, target):
        loads[name] = pltpu.make_async_copy(source, target, load_sem.at[len(loads)])
        loads[name].start()

    def load_feed(far, slot):
        which = pl.ds(pl.multiple_of(flipped(slide, far) * (inner // 4), 128), inner // 4)
        load("wd%d" % far, wd_hbm.at[which, :], wide_slots.at[2 * slot])
        load("wh%d" % far, wh_hbm.at[:, which], wide_slots.at[2 * slot + 1])

    load("wm", wm_hbm, wm)
    load("wl", wl_hbm, wl)
    load_feed(2, 0)
    load_feed(3, 1)
    load("wo", wo_hbm, wo)
    load("quarter", quarter_hbm, quarter)
    load("whole", whole_hbm, whole)
    greet(slide, blk, SLIDE_PEERS + BLK_PEERS)
    links = Links(slide, blk, send_sem, recv_sem)

    def lanes(ref, which, size):
        return ref.at[:, pl.ds(pl.multiple_of(which * size, 128), size)]

    def swap(ref, size, target):
        copies = []
        for far in (2, 3, 1):
            copies.append(links.send(lanes(ref, flipped(slide, far), size), target.at[far], far, 0))
        target[0] = lanes(ref, slide, size)[...]
        return copies

    flows = {}
    waited = set()

    def arrived(*names):
        for name in names:
            if name not in waited:
                waited.add(name)
                for copy in flows[name]:
                    copy.wait_recv()

    loaded = set()

    def have(*names):
        for name in names:
            if name not in loaded:
                loaded.add(name)
                loads[name].wait()

    def start_latent():
        rows = latents // 8
        for along_x in range(2):
            for along_z in range(4):
                place = (along_z * 2 + along_x) * rows
                latent_all[0:cells, (along_x * 4 + along_z) * rows : (along_x * 4 + along_z + 1) * rows] = latent_ref[:, place : place + rows]
        flows["latent"] = across(links, latent_all, pl.ds(0, latents), cells)
        next(flows["latent"])

    def start_base():
        base_all[0:cells, :] = base_ref[...]
        flows["base"] = across(links, base_all, pl.ds(0, width), cells)
        next(flows["base"])

    def relay(name):
        next(flows[name])

    small[...] = jnp.zeros_like(small)

    def bottleneck():
        kl_mean = jnp.concatenate([kl_ref[block : block + 1, :] for block in range(latents // 128)], axis=1) / (32 * cells)
        grad_kl = weight_ref[0, 0] * (kl_mean > floor_ref[...]).astype(F32)
        mean_lat, log_var, centres = mean_ref[...], logvar_ref[...], centres_ref[...]
        grad_latent = glatent_ref[...]
        resp, mixed = mixture(mean_lat, centres)
        weighted = mean_lat * grad_kl
        half_square = exact_dot(jnp.broadcast_to(0.5 * grad_kl, (8, latents)), centres * centres, ((1,), (1,)))[0:1]
        grad_resp = half_square - exact_dot(weighted, centres, ((1,), (1,)))
        grad_logits = resp * (grad_resp - jnp.sum(resp * grad_resp, axis=1, keepdims=True)) / math.sqrt(latents)
        grad_mean = grad_latent + grad_kl * (mean_lat - mixed) + exact_dot(grad_logits, centres, ((1,), (0,)))
        grad_logvar = grad_latent * (0.5 * jnp.exp(0.5 * log_var) * noise_ref[...]) + 0.5 * grad_kl * (jnp.exp(log_var) - 1.0)
        gmean[...] = grad_mean.astype(BF16)
        glogvar[...] = grad_logvar.astype(BF16)
        have("wm", "wl")
        grad_final = dot_nt(gmean[...], wm[...]) + dot_nt(glogvar[...], wl[...])
        gmiddle[...] = grad_final
        branch_all[0] = grad_final.astype(BF16)
        flows["far"] = [links.send(branch_all.at[0], branch_all.at[2], 2, 0)]
        flows["near"] = [links.send(branch_all.at[0], branch_all.at[1], 1, 0)]
        ones = jnp.ones((cells, 128), F32)
        logit_sum = exact_dot(grad_logits, ones, ((0,), (0,)))[:, 0:1]
        resp_sum = exact_dot(resp, ones, ((0,), (0,)))[:, 0:1]
        centres_grad = (
            exact_dot(grad_logits, mean_lat, ((0,), (0,)))
            - logit_sum * centres
            - exact_dot(resp, weighted, ((0,), (0,)))
            + resp_sum * grad_kl * centres
        )
        count = centres.shape[0]
        for block in range(8):
            small[block, 16 : 16 + count, 0 : latents // 8] = centres_grad[:, block * (latents // 8) : (block + 1) * (latents // 8)]
        bias_line = jnp.sum(branch_all[0].astype(F32), axis=0, keepdims=True)
        for block in range(8):
            small[block, 8:9, :] = bias_line[:, block * 128 : (block + 1) * 128]


    def swap_latents():
        flows["gmean"] = swap(gmean, latents // 4, gmean_all)
        flows["glogvar"] = swap(glogvar, latents // 4, glogvar_all)

    def branch_on():
        arrived("far")
        flows["near"].append(links.send(branch_all.at[2], branch_all.at[3], 1, 0))

    width_at = {"express": 0, "one": width, "attended": 2 * width, "two": 3 * width}

    def of_whole(name):
        def left(column):
            return whole[:, pl.ds(width_at[name] + column, 128)]

        return left

    def of_base(column):
        return base_all[:, pl.ds(column, 128)]

    def of_latent(column):
        return latent_all[:, pl.ds(column, 128)]

    def of_act(column):
        return quarter[:, pl.ds(column, 128)]

    def flat(ref, start=None, size=None):
        def right():
            block = ref[...] if start is None else ref[:, :, start : start + size]
            return block.reshape(4 * cells, block.shape[-1])

        return right

    def source_all():
        return quarter[:, inner // 4 :]

    half_w, half_i = width // 2, inner // 8
    operands = {
        "decoder": (of_latent, source_all),
        "down0": (of_act, flat(branch_all, 0, half_w)),
        "down1": (of_act, flat(branch_all, half_w, half_w)),
        "mean": (of_base, flat(gmean_all)),
        "logvar": (of_base, flat(glogvar_all)),
        "hidden0": (of_whole("two"), flat(ginner_all, 0, half_i)),
        "hidden1": (of_whole("two"), flat(ginner_all, half_i, half_i)),
        "output": (of_whole("attended"), flat(gout_all)),
        "panel": (of_whole("express"), flat(genc_all)),
        "query": (of_whole("one"), flat(gqkv_all.at[0])),
        "key": (of_whole("one"), flat(gqkv_all.at[1])),
        "value": (of_whole("one"), flat(gqkv_all.at[2])),
    }
    units = {}
    for number, (name, rows, columns, dense) in enumerate(reductions_of(cells, width, inner, latents)):
        left, right = operands[name]
        units[name] = (ReductionAlongZ if name in Z_FIRST else Reduction)(
            links, left, right, rows, columns, dense, unit_refs[4 * number : 4 * number + 4]
        )

    slots = {
        "decoder": lambda place: lanes(decoder_out, place, width // 4),
        "down0": lambda place: down_out.at[pl.ds(pl.multiple_of(place * (inner // 32), inner // 32), inner // 32), pl.ds(0, half_w)],
        "down1": lambda place: down_out.at[pl.ds(pl.multiple_of(place * (inner // 32), inner // 32), inner // 32), pl.ds(half_w, half_w)],
        "mean": lambda place: lanes(mean_out, place, latents // 4),
        "logvar": lambda place: lanes(logvar_out, place, latents // 4),
        "hidden0": lambda place: hidden_out.at[:, pl.ds(pl.multiple_of(place * (inner // 4), 128), half_i)],
        "hidden1": lambda place: hidden_out.at[:, pl.ds(pl.multiple_of(place * (inner // 4) + half_i, 128), half_i)],
        "output": lambda place: lanes(output_out, place, width // 4),
        "query": lambda place: lanes(query_out, place, width // 4),
        "key": lambda place: lanes(key_out, place, width // 4),
        "value": lambda place: lanes(value_out, place, width // 4),
    }
    spreads = {}

    def spread(name):
        spreads[name] = spread_slide(links, slots[name], units[name].total())
        next(spreads[name])

    chunk = inner // 8
    encoded[...] = jnp.zeros_like(encoded)

    def feed_back(turn):
        far = (2, 3, 1, 0)[turn]
        slot = turn % 2
        have("wd%d" % far, "wh%d" % far)
        which = flipped(slide, far)

        def feed(j, carry, slot=slot, which=which):
            near = pl.ds(pl.multiple_of(j * chunk, 128), chunk)
            where = pl.ds(pl.multiple_of(which * (inner // 4) + j * chunk, 128), chunk)
            values = inner_ref[:, where]
            squared = values * values
            bent = jnp.tanh(0.7978845608028654 * (values + 0.044715 * squared * values))
            slope = 0.5 * (1.0 + bent) + 0.5 * values * (1.0 - bent * bent) * (
                0.7978845608028654 * (1.0 + 3 * 0.044715 * squared)
            )
            grad = (dot_nt(branch_all[0], wide_slots[2 * slot, near, :]) * slope).astype(BF16)
            ginner[:, where] = grad
            line = jnp.sum(grad.astype(F32), axis=0, keepdims=True)
            for block in range(chunk // 128):
                small[which * 2 + j, 4 + block : 5 + block, :] = line[:, block * 128 : (block + 1) * 128]
            encoded[...] += dot_nt(grad, wide_slots[2 * slot + 1, :, near])
            return carry

        lax.fori_loop(0, 2, feed, 0)
        if far:
            flows["inner"] = flows.get("inner", []) + [
                links.send(lanes(ginner, which, inner // 4), ginner_all.at[far], far, 0)
            ]
        else:
            ginner_all[0] = lanes(ginner, slide, inner // 4)[...]
        if turn < 2:
            load_feed((1, 0)[turn], slot)
        if turn == 3:
            for number, (name, source) in enumerate((("wq", wq_hbm), ("wk", wk_hbm), ("wv", wv_hbm))):
                load(name, source, wide_slots.at[number])

    wq, wk, wv = wide_slots.at[0], wide_slots.at[1], wide_slots.at[2]

    def norm_two():
        grad_hidden, gain_grad, shift_grad = norm_back(middle_ref[...], gain_two[...], encoded[...])
        for block in range(8):
            small[block, 2:3, :] = gain_grad[:, block * 128 : (block + 1) * 128]
            small[block, 3:4, :] = shift_grad[:, block * 128 : (block + 1) * 128]
        gmiddle[...] += grad_hidden
        gout[...] = gmiddle[...].astype(BF16)

    def att_out():
        have("wo")

        def att_block(target, store):
            rows = wo[pl.ds(pl.multiple_of(target * per, per), per), :]
            store(dot_nt(gout[...], rows).astype(BF16))

        att_copies = flows["att"] = []
        for far in (6, 4, 2, 7, 5, 3, 1):
            target = flipped(blk, far)

            def keep(block, far=far):
                att_send[far] = block

            att_block(target, keep)
            att_copies.append(links.send(att_send.at[far], att_land.at[blk], 0, far))

        def keep_own(block):
            att_land[blk] = block

        att_block(blk, keep_own)

    def swap_out():
        flows["gout"] = swap(gout, width // 4, gout_all)

    def masks():
        slide_masks(land_ref, row_ref, col_ref, cells)
        dk_sum[...] = jnp.zeros_like(dk_sum)
        dv_sum[...] = jnp.zeros_like(dv_sum)

    scale = HEAD_DIM**-0.5
    rows = 2 * cells

    def rows_back(i):
        arrived("att")
        where = pl.ds(pl.multiple_of(i * rows, rows), rows)
        same_slide = row_ref[where, 0:1] == col_ref[...]
        query = land_ref[pl.ds(2 * i, 2), 0:cells, :].reshape(rows, per)
        grad = att_land[pl.ds(2 * i, 2)].reshape(rows, per)
        key = land_ref[:, cells : 2 * cells, :].reshape(8 * cells, per)
        value = land_ref[:, 2 * cells : 3 * cells, :].reshape(8 * cells, per)
        lane = lax.broadcasted_iota(jnp.int32, query.shape, 1)
        grad_query = None
        for head in range(per // HEAD_DIM):
            mine = lane // HEAD_DIM == head
            own_query = jnp.where(mine, query, 0)
            own_grad = jnp.where(mine, grad, 0)
            shares = head_scores(own_query, key, same_slide)
            grad_shares = dot_nt(own_grad, value)
            inner_dot = jnp.sum(shares * grad_shares, axis=1, keepdims=True)
            grad_scores = (shares * (grad_shares - inner_dot)).astype(BF16)
            part = jnp.dot(grad_scores, key, preferred_element_type=F32)
            grad_query = part if grad_query is None else jnp.where(mine, part, grad_query)
            dk_sum[...] += dot_tn(grad_scores, own_query)
            dv_sum[...] += dot_tn(shares.astype(BF16), own_grad)
        dqkv[pl.ds(2 * i, 2), 0:cells, :] = (grad_query * scale).astype(BF16).reshape(2, cells, per)

    def back_out():
        dqkv[:, cells : 2 * cells, :] = (dk_sum[...] * scale).astype(BF16).reshape(8, cells, per)
        dqkv[:, 2 * cells :, :] = dv_sum[...].astype(BF16).reshape(8, cells, per)
        back_copies = flows["back"] = []
        for far in (6, 4, 2, 7, 5, 3, 1):
            back_copies.append(links.send(dqkv.at[flipped(blk, far)], dqkv_land.at[blk], 0, far))
        dqkv_land[blk] = dqkv[blk]

    def back_in():
        arrived("back")
        have("wq", "wk", "wv")
        for part in range(3):
            for block in range(8):
                grad_qkv[part, :, block * per : (block + 1) * per] = dqkv_land[block, part * cells : (part + 1) * cells, :]


    def swap_qkv():
        for part in range(3):
            flows["qkv%d" % part] = swap(grad_qkv.at[part], width // 4, gqkv_all.at[part])

    def norm_input(i, carry):
        where = pl.ds(pl.multiple_of(i * 256, 256), 256)
        encoded_sum = (
            dot_nt(grad_qkv[0], wq[where, :]) + dot_nt(grad_qkv[1], wk[where, :]) + dot_nt(grad_qkv[2], wv[where, :])
        )
        encoded[:, where] = encoded_sum
        return carry

    def norm_one():
        lax.fori_loop(0, width // 256, norm_input, 0)
        grad_hidden, gain_grad, shift_grad = norm_back(start_ref[...], gain_one[...], encoded[...])
        grad_qkv[3] = (gmiddle[...] + grad_hidden).astype(BF16)
        flows["genc"] = swap(grad_qkv.at[3], width // 4, genc_all)
        for block in range(8):
            small[block, 0:1, :] = gain_grad[:, block * 128 : (block + 1) * 128]
            small[block, 1:2, :] = shift_grad[:, block * 128 : (block + 1) * 128]

    def small_out_blk():
        flows["small"] = [links.send(small.at[flipped(blk, far)], small_land.at[blk], 0, far) for far in range(1, 8)]
        small_land[blk] = small[blk]

    def small_out_slide():
        arrived("small")
        small_sum = small_land[0]
        for block in range(1, 8):
            small_sum = small_sum + small_land[block]
        small_own[...] = small_sum
        flows["sums"] = [links.send(small_own, small_slides.at[slide], far, 0) for far in (2, 3, 1)]
        small_slides[slide] = small_sum

    def small_done():
        arrived("sums")
        small_out[...] = (small_slides[0] + small_slides[1]) + (small_slides[2] + small_slides[3])

    panel_slot = lambda far_slide, far_blk: panel_out.at[
        pl.ds(pl.multiple_of(far_blk * (width // 8), 128), width // 8),
        pl.ds(pl.multiple_of(far_slide * (width // 4), 128), width // 4),
    ]
    needs = {
        "decoder": (), "down0": ("near",), "down1": ("near",), "mean": ("gmean",), "logvar": ("glogvar",),
        "hidden0": ("inner",), "hidden1": ("inner",), "output": ("gout",), "panel": ("genc",), "query": ("qkv0",),
        "key": ("qkv1",), "value": ("qkv2",),
    }

    def along(name):
        arrived(*needs[name])
        have("quarter" if name in ("decoder", "down0", "down1") else "whole")
        units[name].send_x()

    def panel_out_start():
        own_slot = panel_slot(slide, blk)
        own_slot[...] = units["panel"].total()
        flows["panel"] = spread_everywhere(links, panel_slot)
        next(flows["panel"])

    def spread_on(name):
        next(spreads[name])

    steps = {
        "latent": start_latent, "base": start_base, "relay": relay, "bottleneck": bottleneck, "lats": swap_latents,
        "branch": branch_on, "feed": feed_back, "norm2": norm_two, "att": att_out, "gout": swap_out, "masks": masks,
        "rows": rows_back, "back": back_out, "in": back_in, "qkv": swap_qkv, "norm1": norm_one, "small": small_out_blk,
        "sums": small_out_slide, "done": small_done, "x": along, "z": lambda name: units[name].send_z(),
        "f": lambda name: units[name].send_far(), "s": spread, "s2": spread_on, "panel": panel_out_start,
    }
    for step in ORDER:
        steps[step[0]](*step[1:])
    links.finish()


def backward(inputs, weights, cells, width, inner, latents):
    per = width // 8
    small_rows = 32
    shape = jax.ShapeDtypeStruct
    unit_scratch = []
    for _, rows, columns, _ in reductions_of(cells, width, inner, latents):
        unit_scratch += [pltpu.VMEM((4 * rows, columns), BF16)] * 3 + [pltpu.VMEM((3, rows, columns), BF16)]
    copies = 208
    vmem, left = pl.BlockSpec(memory_space=pltpu.VMEM), pl.BlockSpec(memory_space=pl.ANY)
    outs = (
        shape((width, width), BF16),
        shape((per, width), BF16),
        shape((per, width), BF16),
        shape((per, width), BF16),
        shape((per, width), BF16),
        shape((per, inner), BF16),
        shape((inner // 8, width), BF16),
        shape((per, latents), BF16),
        shape((per, latents), BF16),
        shape((latents // 8, width), BF16),
        shape((small_rows, 128), F32),
    )
    scratch = [
        ((4 * cells, 4 * width), BF16),
        ((4 * cells, width), BF16),
        ((4 * cells, latents), BF16),
        ((4 * cells, inner // 4 + width // 4), BF16),
        ((4, width, width), BF16),
        ((width, width), BF16),
        ((width, latents), BF16),
        ((width, latents), BF16),
        ((4, cells, width), BF16),
        ((cells, latents), BF16),
        ((cells, latents), BF16),
        ((4, cells, latents // 4), BF16),
        ((4, cells, latents // 4), BF16),
        ((cells, inner), BF16),
        ((4, cells, inner // 4), BF16),
        ((cells, width), BF16),
        ((4, cells, width // 4), BF16),
        ((cells, width), F32),
        ((3, 4, cells, width // 4), BF16),
        ((4, cells, width // 4), BF16),
        ((8 * cells, cells), F32),
        ((1, 8 * cells), F32),
        ((8, cells, per), BF16),
        ((8, cells, per), BF16),
        ((8, 3 * cells, per), BF16),
        ((8, 3 * cells, per), BF16),
        ((8 * cells, per), F32),
        ((8 * cells, per), F32),
        ((4, cells, width), BF16),
        ((cells, width), F32),
        ((8, small_rows, 128), F32),
        ((8, small_rows, 128), F32),
        ((small_rows, 128), F32),
        ((4, small_rows, 128), F32),
    ]
    return pl.pallas_call(
        backward_kernel,
        out_shape=outs,
        in_specs=[vmem] * len(inputs) + [left] * len(weights),
        out_specs=[vmem] * len(outs),
        scratch_shapes=[pltpu.VMEM(*item) for item in scratch]
        + [
            pltpu.SemaphoreType.DMA((16,)),
            pltpu.SemaphoreType.DMA((copies,)),
            pltpu.SemaphoreType.DMA((copies,)),
        ]
        + unit_scratch,
        compiler_params=pltpu.CompilerParams(
            collective_id=2, has_side_effects=True, vmem_limit_bytes=62 << 20
        ),
        name="backward",
    )(*inputs, *weights)


def finish_kernel(ids_ref, panel_ref, small_ref, kl_ref, weight_ref, floor_ref, *refs):
    count = (len(refs) - 9) // 2
    table_out, grads, outs, tiny = refs[count], refs[:count], refs[count + 1 : 2 * count + 1], refs[2 * count + 1 :]
    rows = table_out.shape[0]
    first = (lax.axis_index("blk") * pl.num_programs(0) + pl.program_id(0)) * rows
    row_ids = first + lax.broadcasted_iota(jnp.int32, (rows, ids_ref.shape[1]), 0)
    spread = (row_ids == ids_ref[...]).astype(F32).astype(BF16)
    table_out[...] = jnp.dot(spread, panel_ref[...], preferred_element_type=F32)
    for grad, out in zip(grads, outs):
        out[...] = grad[...].astype(F32)

    @pl.when(pl.program_id(0) == 0)
    def _():
        start = 0
        for out in tiny[:6]:
            out[...] = small_ref[start : start + out.shape[0], :]
            start += out.shape[0]
        centres = tiny[6]
        centres[...] = small_ref[16 : 16 + centres.shape[0], 0 : centres.shape[1]]
        total = jnp.zeros((1, 128), F32)
        for block in range(floor_ref.shape[1] // 128):
            lanes = slice(block * 128, (block + 1) * 128)
            total = total + jnp.maximum(kl_ref[block : block + 1, :] / weight_ref[0, 1], floor_ref[:, lanes])
        tiny[7][...] = weight_ref[0, 0] * (jnp.sum(total, axis=1, keepdims=True) / floor_ref.shape[1])


def finish(gene_ids, panel, grads, small, kl_total, weight, floor, table_rows, centres_shape, bias_rows, rows=256):
    genes, width = panel.shape
    steps = table_rows // rows
    shape = jax.ShapeDtypeStruct
    tiny = [(1, 128)] * 4 + [(bias_rows, 128), (1, 128), centres_shape, (1, 1)]

    def cut(grad):
        if grad.shape[0] // steps % 16 == 0:
            return pl.BlockSpec((grad.shape[0] // steps, grad.shape[1]), lambda i: (i, 0))
        return pl.BlockSpec((grad.shape[0], grad.shape[1] // steps), lambda i: (0, i))

    def whole(size):
        return pl.BlockSpec(size, lambda i: (0, 0))

    return pl.pallas_call(
        finish_kernel,
        grid=(steps,),
        out_shape=[shape((table_rows, width), F32)] + [shape(grad.shape, F32) for grad in grads] + [shape(size, F32) for size in tiny],
        in_specs=[
            whole((1, genes)), whole(panel.shape), whole(small.shape), whole(kl_total.shape),
            pl.BlockSpec(memory_space=pltpu.SMEM), whole(floor.shape),
        ]
        + [cut(grad) for grad in grads],
        out_specs=[pl.BlockSpec((rows, width), lambda i: (i, 0))] + [cut(grad) for grad in grads] + [whole(size) for size in tiny],
        compiler_params=pltpu.CompilerParams(vmem_limit_bytes=62 << 20),
        name="finish",
    )(gene_ids, panel, small, kl_total, weight, floor, *grads)


def on_device_fast(
    counts,
    library,
    gene_ids,
    positions,
    slide_of_cell,
    latent_noise,
    decoded_grad,
    gene_table,
    first_gain,
    first_shift,
    query_weight,
    key_weight,
    value_weight,
    output_weight,
    second_gain,
    second_shift,
    hidden_weight,
    hidden_bias,
    down_weight,
    down_bias,
    mean_weight,
    logvar_weight,
    component_means,
    decoder_weight,
    divergence_weight,
    free_floor,
):
    cells = counts.shape[1]
    width = gene_table.shape[1]
    latents = mean_weight.shape[1]
    inner = hidden_weight.shape[1]
    table_rows = gene_table.shape[0]
    quarter = width // 4
    freqs = np.exp(-math.log(10000.0) * np.arange(quarter, dtype=np.float32) / quarter).astype(np.float32)
    (
        land, hidden_start, hidden_middle, inner_sum, mean_lat, log_var, grad_latent, base, latent, kl_total, decoded,
        whole, quarters,
    ) = forward(
        (
            gene_ids[None], counts[0], library, positions[0], freqs[None], slide_of_cell, latent_noise[0], decoded_grad[0],
            first_gain[None], first_shift[None], second_gain[None], second_shift[None], hidden_bias[None],
            down_bias[None], component_means,
        ),
        (
            gene_table, query_weight, key_weight, value_weight, output_weight, hidden_weight, down_weight, mean_weight,
            logvar_weight, decoder_weight,
        ),
        cells, width, inner, latents,
    )
    (
        panel_sum, query_grad, key_grad, value_grad, output_grad, hidden_grad, down_grad, mean_grad, logvar_grad,
        decoder_grad, small,
    ) = backward(
        (
            land, hidden_start, hidden_middle, inner_sum, mean_lat, log_var, grad_latent, base, latent, kl_total,
            latent_noise[0], component_means, divergence_weight[None], free_floor[None], first_gain[None],
            second_gain[None],
        ),
        (
            whole, quarters, query_weight, key_weight, value_weight, output_weight, hidden_weight, down_weight,
            mean_weight, logvar_weight,
        ),
        cells, width, inner, latents,
    )
    (
        table_grad, query_grad, key_grad, value_grad, output_grad, hidden_grad, down_grad, mean_grad, logvar_grad,
        decoder_grad, gain_one, shift_one, gain_two, shift_two, hidden_small, down_small, centres_grad, divergence,
    ) = finish(
        gene_ids[None], panel_sum,
        (
            query_grad, key_grad, value_grad, output_grad, hidden_grad, down_grad, mean_grad, logvar_grad,
            decoder_grad,
        ),
        small, kl_total, jnp.stack([divergence_weight[0], jnp.float32(32 * cells)])[None], free_floor[None], table_rows,
        (component_means.shape[0], latents // 8), inner // 8 // 128,
    )
    return (
        decoded[None],
        divergence.reshape(1),
        table_grad,
        gain_one.reshape(-1),
        shift_one.reshape(-1),
        query_grad,
        key_grad,
        value_grad,
        output_grad,
        gain_two.reshape(-1),
        shift_two.reshape(-1),
        hidden_grad,
        hidden_small.reshape(-1),
        down_grad,
        down_small.reshape(-1),
        mean_grad,
        logvar_grad,
        centres_grad,
        decoder_grad,
    )


def solution(mesh):
    placed = (
        P("slide", "blk", None),
        P("slide", "blk"),
        P(),
        P("slide", None, "blk"),
        P("slide", "blk"),
        P("slide", "blk", None),
        P("slide", "blk", None),
        P("blk", None),
        P(),
        P(),
        P(),
        P(),
        P(),
        P(),
        P(),
        P(),
        P(),
        P(),
        P(),
        P(),
        P(),
        P(),
        P(),
        P(),
        P(),
        P(),
    )
    return jax.shard_map(
        on_device_fast if fits(mesh) else on_device_general,
        mesh=mesh,
        in_specs=placed,
        out_specs=(
            P("slide", "blk", None),
            P(),
            P("blk", None),
            P("blk"),
            P("blk"),
            P("blk", None),
            P("blk", None),
            P("blk", None),
            P("blk", None),
            P("blk"),
            P("blk"),
            P("blk", None),
            P("blk"),
            P("blk", None),
            P("blk"),
            P("blk", None),
            P("blk", None),
            P(None, "blk"),
            P("blk", None),
        ),
        check_vma=False,
    )
```

```python
import functools
import math

import jax
import jax.numpy as jnp
import numpy as np
from jax import lax
from jax.experimental import pallas as pl
from jax.experimental.pallas import tpu as pltpu
from jax.sharding import PartitionSpec as P

HEAD_DIM = 64
MESH = pl.DeviceIdType.MESH
F32 = jnp.float32
BF16 = jnp.bfloat16


def normalized(counts, library):
    scaled = counts.astype(jnp.float32) * (10000.0 / library.astype(jnp.float32))[..., None]
    return jnp.log1p(scaled)


def position_code(coords, model_width):
    quarter = model_width // 4
    freqs = jnp.exp(-math.log(10000.0) * jnp.arange(quarter, dtype=jnp.float32) / quarter)
    along_x = coords[0].astype(jnp.float32)[:, None] * freqs[None, :]
    along_y = coords[1].astype(jnp.float32)[:, None] * freqs[None, :]
    return jnp.concatenate(
        [jnp.sin(along_x), jnp.cos(along_x), jnp.sin(along_y), jnp.cos(along_y)], axis=1
    )


def layer_norm(inputs, scaling, offsets):
    centre = inputs - jnp.mean(inputs, axis=-1, keepdims=True)
    spread = jnp.mean(centre * centre, axis=-1, keepdims=True)
    return centre * lax.rsqrt(spread + 1e-05) * scaling + offsets


def gelu_tanh(inputs):
    return (
        0.5
        * inputs
        * (1.0 + jnp.tanh(0.7978845608028654 * (inputs + 0.044715 * inputs * inputs * inputs)))
    )


def divergence_cells(mean_part, logvar_part, centres):
    latent_width = mean_part.shape[-1]
    crossed = jnp.dot(mean_part, centres.T, precision=lax.Precision.HIGHEST)
    centre_square = jnp.sum(centres * centres, axis=-1)
    logits = (crossed - 0.5 * centre_square[None, :]) / math.sqrt(latent_width)
    shifted = jnp.exp(logits - jnp.max(logits, axis=-1, keepdims=True))
    resp = shifted / jnp.sum(shifted, axis=-1, keepdims=True)
    mixed = jnp.dot(resp, centres, precision=lax.Precision.HIGHEST)
    mixed_square = jnp.dot(resp, centres * centres, precision=lax.Precision.HIGHEST)
    return 0.5 * (
        jnp.exp(logvar_part)
        - 1.0
        - logvar_part
        + mean_part * mean_part
        - 2.0 * mean_part * mixed
        + mixed_square
    )


def to_heads(array, head_count):
    return array.reshape(array.shape[0], head_count, -1).transpose(1, 0, 2)


def from_heads(array):
    return array.transpose(1, 0, 2).reshape(array.shape[1], -1)


def matmul(left, right):
    return jnp.dot(left, right, preferred_element_type=jnp.float32)


def on_device_general(
    counts,
    library,
    gene_ids,
    positions,
    slide_of_cell,
    latent_noise,
    decoded_grad,
    gene_table,
    first_gain,
    first_shift,
    query_weight,
    key_weight,
    value_weight,
    output_weight,
    second_gain,
    second_shift,
    hidden_weight,
    hidden_bias,
    down_weight,
    down_bias,
    mean_weight,
    logvar_weight,
    component_means,
    decoder_weight,
    divergence_weight,
    free_floor,
):
    cell_count = counts.shape[1]
    model_width = gene_table.shape[1]
    head_count = model_width // HEAD_DIM
    score_scale = HEAD_DIM ** (-0.5)
    express = normalized(counts[0], library[0]).astype(jnp.bfloat16)
    table_rows = gene_table.shape[0]
    first_row = lax.axis_index("blk") * table_rows
    selector = (
        gene_ids[:, None] == first_row + jnp.arange(table_rows, dtype=jnp.int32)[None, :]
    ).astype(jnp.bfloat16)
    panel_part = matmul(selector, gene_table)
    panel_weight = lax.psum(panel_part, "blk").astype(jnp.bfloat16)
    hidden_start = matmul(express, panel_weight) + position_code(positions[0], model_width)
    normed_one = layer_norm(hidden_start, first_gain, first_shift).astype(jnp.bfloat16)
    query_low = matmul(normed_one, query_weight).astype(jnp.bfloat16)
    key_low = matmul(normed_one, key_weight).astype(jnp.bfloat16)
    value_low = matmul(normed_one, value_weight).astype(jnp.bfloat16)
    slide_labels = slide_of_cell[0].astype(jnp.bfloat16)
    keys_all, values_all, labels_all = (
        lax.all_gather(key_low, "blk", axis=0, tiled=True),
        lax.all_gather(value_low, "blk", axis=0, tiled=True),
        lax.all_gather(slide_labels, "blk", axis=0, tiled=True),
    )
    same_slide = slide_labels[:, None] == labels_all[None, :]
    query_heads = to_heads(query_low, head_count)
    key_heads = to_heads(keys_all, head_count)
    value_heads = to_heads(values_all, head_count)

    def head_forward(head_items):
        query_head, key_head, value_head = head_items
        scores = (
            jnp.einsum("qd,kd->qk", query_head, key_head, preferred_element_type=jnp.float32)
            * score_scale
        )
        scores = jnp.where(same_slide, scores, -1e30)
        row_max = jnp.max(scores, axis=1, keepdims=True)
        shifted = jnp.exp(scores - row_max)
        row_sum = jnp.sum(shifted, axis=1, keepdims=True)
        shares = shifted / row_sum
        attended_head = jnp.einsum(
            "qk,kd->qd", shares.astype(jnp.bfloat16), value_head, preferred_element_type=jnp.float32
        )
        return (attended_head, row_max[:, 0], row_sum[:, 0])

    attended_heads, row_maxes, row_sums = lax.map(
        head_forward, (query_heads, key_heads, value_heads)
    )
    attended = from_heads(attended_heads).astype(jnp.bfloat16)
    hidden_middle = hidden_start + matmul(attended, output_weight)
    normed_two = layer_norm(hidden_middle, second_gain, second_shift).astype(jnp.bfloat16)
    inner_sum = matmul(normed_two, hidden_weight) + hidden_bias
    act_low = gelu_tanh(inner_sum).astype(jnp.bfloat16)
    hidden_final = hidden_middle + matmul(act_low, down_weight) + down_bias
    base_low = hidden_final.astype(jnp.bfloat16)
    mean_lat = matmul(base_low, mean_weight)
    log_var = matmul(base_low, logvar_weight)
    noise_local = latent_noise[0]

    def bottleneck(mean_part, logvar_part, centres):
        return (
            mean_part + jnp.exp(0.5 * logvar_part) * noise_local,
            divergence_cells(mean_part, logvar_part, centres),
        )

    (latent, kl_cell), pull_latent = jax.vjp(bottleneck, mean_lat, log_var, component_means)
    latent_low = latent.astype(jnp.bfloat16)
    decoded = matmul(latent_low, decoder_weight)
    everyone = cell_count * lax.axis_size("blk") * lax.axis_size("slide")
    kl_sum = lax.psum(jnp.sum(kl_cell, axis=0), ("slide", "blk"))
    kl_mean = kl_sum / everyone
    divergence = divergence_weight * jnp.mean(jnp.maximum(kl_mean, free_floor))
    binding = (kl_mean > free_floor).astype(jnp.float32)
    grad_source = decoded_grad[0]
    grad_latent = matmul(grad_source, decoder_weight.T)
    decoder_grad = matmul(latent_low.T, grad_source)
    grad_kl = jnp.broadcast_to(divergence_weight * binding, kl_cell.shape)
    grad_mean, grad_logvar, centres_grad = pull_latent((grad_latent, grad_kl))
    grad_mean_low = grad_mean.astype(jnp.bfloat16)
    grad_logvar_low = grad_logvar.astype(jnp.bfloat16)
    mean_grad = matmul(base_low.T, grad_mean_low)
    logvar_grad = matmul(base_low.T, grad_logvar_low)
    grad_final = matmul(grad_mean_low, mean_weight.T) + matmul(grad_logvar_low, logvar_weight.T)
    grad_branch = grad_final.astype(jnp.bfloat16)
    down_grad = matmul(act_low.T, grad_branch)
    down_bias_grad = jnp.sum(grad_branch.astype(jnp.float32), axis=0)
    grad_act = matmul(grad_branch, down_weight.T)
    gelu_pull = jax.vjp(gelu_tanh, inner_sum)[1]
    grad_inner = gelu_pull(grad_act)[0].astype(jnp.bfloat16)
    hidden_grad = matmul(normed_two.T, grad_inner)
    hidden_bias_grad = jnp.sum(grad_inner.astype(jnp.float32), axis=0)
    norm_two_pull = jax.vjp(layer_norm, hidden_middle, second_gain, second_shift)[1]
    grad_norm_two, second_gain_grad, second_shift_grad = norm_two_pull(
        matmul(grad_inner, hidden_weight.T)
    )
    grad_middle = grad_final + grad_norm_two
    grad_out = grad_middle.astype(jnp.bfloat16)
    output_grad = matmul(attended.T, grad_out)
    grad_attended = matmul(grad_out, output_weight.T).astype(jnp.bfloat16)
    keys_again, values_again = (
        lax.all_gather(key_low, "blk", axis=0, tiled=True),
        lax.all_gather(value_low, "blk", axis=0, tiled=True),
    )
    key_heads_back = to_heads(keys_again, head_count)
    value_heads_back = to_heads(values_again, head_count)
    grad_heads_local = to_heads(grad_attended, head_count)

    def head_queries(head_items):
        query_head, key_head, value_head, grad_head, row_max, row_sum = head_items
        scores = (
            jnp.einsum("qd,kd->qk", query_head, key_head, preferred_element_type=jnp.float32)
            * score_scale
        )
        scores = jnp.where(same_slide, scores, -1e30)
        shares = jnp.exp(scores - row_max[:, None]) / row_sum[:, None]
        grad_shares = jnp.einsum(
            "qd,kd->qk", grad_head, value_head, preferred_element_type=jnp.float32
        )
        inner_dot = jnp.sum(shares * grad_shares, axis=1, keepdims=True)
        grad_scores = (shares * (grad_shares - inner_dot)).astype(jnp.bfloat16)
        grad_query_head = (
            jnp.einsum("qk,kd->qd", grad_scores, key_head, preferred_element_type=jnp.float32)
            * score_scale
        )
        return (grad_query_head, inner_dot[:, 0])

    grad_query_heads, inner_dots = lax.map(
        head_queries,
        (query_heads, key_heads_back, value_heads_back, grad_heads_local, row_maxes, row_sums),
    )
    queries_group, grads_group = (
        lax.all_gather(query_low, "blk", axis=0, tiled=True),
        lax.all_gather(grad_attended, "blk", axis=0, tiled=True),
    )
    maxes_group, totals_group, dots_group = (
        lax.all_gather(row_maxes, "blk", axis=1, tiled=True),
        lax.all_gather(row_sums, "blk", axis=1, tiled=True),
        lax.all_gather(inner_dots, "blk", axis=1, tiled=True),
    )
    mask_back = labels_all[:, None] == slide_labels[None, :]

    def head_keys(head_items):
        query_head, key_head, value_head, grad_head, row_max, row_sum, inner_dot = head_items
        scores = (
            jnp.einsum("qd,kd->qk", query_head, key_head, preferred_element_type=jnp.float32)
            * score_scale
        )
        scores = jnp.where(mask_back, scores, -1e30)
        shares = jnp.exp(scores - row_max[:, None]) / row_sum[:, None]
        grad_shares = jnp.einsum(
            "qd,kd->qk", grad_head, value_head, preferred_element_type=jnp.float32
        )
        grad_scores = (shares * (grad_shares - inner_dot[:, None])).astype(jnp.bfloat16)
        grad_key_head = (
            jnp.einsum("qk,qd->kd", grad_scores, query_head, preferred_element_type=jnp.float32)
            * score_scale
        )
        grad_value_head = jnp.einsum(
            "qk,qd->kd", shares.astype(jnp.bfloat16), grad_head, preferred_element_type=jnp.float32
        )
        return (grad_key_head, grad_value_head)

    grad_key_heads, grad_value_heads = lax.map(
        head_keys,
        (
            to_heads(queries_group, head_count),
            to_heads(key_low, head_count),
            to_heads(value_low, head_count),
            to_heads(grads_group, head_count),
            maxes_group,
            totals_group,
            dots_group,
        ),
    )
    grad_query_low = from_heads(grad_query_heads).astype(jnp.bfloat16)
    grad_key = from_heads(grad_key_heads)
    grad_value = from_heads(grad_value_heads)
    grad_key_low = grad_key.astype(jnp.bfloat16)
    grad_value_low = grad_value.astype(jnp.bfloat16)
    query_grad = matmul(normed_one.T, grad_query_low)
    key_grad = matmul(normed_one.T, grad_key_low)
    value_grad = matmul(normed_one.T, grad_value_low)
    grad_norm_input = (
        matmul(grad_query_low, query_weight.T)
        + matmul(grad_key_low, key_weight.T)
        + matmul(grad_value_low, value_weight.T)
    )
    norm_one_pull = jax.vjp(layer_norm, hidden_start, first_gain, first_shift)[1]
    grad_norm_one, first_gain_grad, first_shift_grad = norm_one_pull(grad_norm_input)
    grad_start = grad_middle + grad_norm_one
    grad_encoded = grad_start.astype(jnp.bfloat16)
    panel_grad = matmul(express.T, grad_encoded)
    panel_total = lax.psum(panel_grad, ("slide", "blk"))
    table_grad = jnp.dot(
        selector.astype(jnp.float32).T, panel_total, precision=lax.Precision.HIGHEST
    )
    shares_grads = (
        lax.psum_scatter(first_gain_grad, "blk", scatter_dimension=0, tiled=True),
        lax.psum_scatter(first_shift_grad, "blk", scatter_dimension=0, tiled=True),
        lax.psum_scatter(query_grad, "blk", scatter_dimension=0, tiled=True),
        lax.psum_scatter(key_grad, "blk", scatter_dimension=0, tiled=True),
        lax.psum_scatter(value_grad, "blk", scatter_dimension=0, tiled=True),
        lax.psum_scatter(output_grad, "blk", scatter_dimension=0, tiled=True),
        lax.psum_scatter(second_gain_grad, "blk", scatter_dimension=0, tiled=True),
        lax.psum_scatter(second_shift_grad, "blk", scatter_dimension=0, tiled=True),
        lax.psum_scatter(hidden_grad, "blk", scatter_dimension=0, tiled=True),
        lax.psum_scatter(hidden_bias_grad, "blk", scatter_dimension=0, tiled=True),
        lax.psum_scatter(down_grad, "blk", scatter_dimension=0, tiled=True),
        lax.psum_scatter(down_bias_grad, "blk", scatter_dimension=0, tiled=True),
        lax.psum_scatter(mean_grad, "blk", scatter_dimension=0, tiled=True),
        lax.psum_scatter(logvar_grad, "blk", scatter_dimension=0, tiled=True),
        lax.psum_scatter(centres_grad, "blk", scatter_dimension=1, tiled=True),
        lax.psum_scatter(decoder_grad, "blk", scatter_dimension=0, tiled=True),
    )
    summed = (
        lax.psum(shares_grads[0].astype(jnp.bfloat16), "slide").astype(jnp.float32),
        lax.psum(shares_grads[1].astype(jnp.bfloat16), "slide").astype(jnp.float32),
        lax.psum(shares_grads[2].astype(jnp.bfloat16), "slide").astype(jnp.float32),
        lax.psum(shares_grads[3].astype(jnp.bfloat16), "slide").astype(jnp.float32),
        lax.psum(shares_grads[4].astype(jnp.bfloat16), "slide").astype(jnp.float32),
        lax.psum(shares_grads[5].astype(jnp.bfloat16), "slide").astype(jnp.float32),
        lax.psum(shares_grads[6].astype(jnp.bfloat16), "slide").astype(jnp.float32),
        lax.psum(shares_grads[7].astype(jnp.bfloat16), "slide").astype(jnp.float32),
        lax.psum(shares_grads[8].astype(jnp.bfloat16), "slide").astype(jnp.float32),
        lax.psum(shares_grads[9].astype(jnp.bfloat16), "slide").astype(jnp.float32),
        lax.psum(shares_grads[10].astype(jnp.bfloat16), "slide").astype(jnp.float32),
        lax.psum(shares_grads[11].astype(jnp.bfloat16), "slide").astype(jnp.float32),
        lax.psum(shares_grads[12].astype(jnp.bfloat16), "slide").astype(jnp.float32),
        lax.psum(shares_grads[13].astype(jnp.bfloat16), "slide").astype(jnp.float32),
        lax.psum(shares_grads[14].astype(jnp.bfloat16), "slide").astype(jnp.float32),
        lax.psum(shares_grads[15].astype(jnp.bfloat16), "slide").astype(jnp.float32),
    )
    return (decoded[None], divergence, table_grad) + tuple(summed)


def fits(mesh):
    return mesh.shape["slide"] == 4 and mesh.shape["blk"] == 8


def flipped(index, mask):
    for bit in (1, 2, 4):
        if mask & bit:
            index = index + bit - 2 * bit * ((index // bit) % 2)
    return index


def greet(slide, blk, peers):
    barrier = pltpu.get_barrier_semaphore()
    for far_slide, far_blk in peers:
        pl.semaphore_signal(
            barrier,
            inc=1,
            device_id={"slide": flipped(slide, far_slide), "blk": flipped(blk, far_blk)},
            device_id_type=MESH,
        )
    pl.semaphore_wait(barrier, len(peers))


BLK_PEERS = [(0, far) for far in range(1, 8)]
SLIDE_PEERS = [(far, 0) for far in range(1, 4)]


def dot_nt(left, right):
    return lax.dot_general(left, right, (((1,), (1,)), ((), ())), preferred_element_type=F32)


def dot_tn(left, right):
    return lax.dot_general(left, right, (((0,), (0,)), ((), ())), preferred_element_type=F32)


def head_scores(query, key, same_slide):
    scores = jnp.where(same_slide, dot_nt(query, key) * (HEAD_DIM**-0.5), -1e30)
    shifted = jnp.exp(scores - jnp.max(scores, axis=1, keepdims=True))
    return shifted / jnp.sum(shifted, axis=1, keepdims=True)


(
    ACT_, ATTENDED_, ATT_, BACK_, BASE_, BOTTLENECK_, BRANCH_, B_, DECODER_, DONE_, DOWN0_, DOWN1_, EXPRESS_,
    FAR_, FEED_, F_, GENC_, GLOGVAR_, GMEAN_, GOUT_, HIDDEN0_, HIDDEN1_, INNER_, IN_, KEY_, LATENT_, LATS_,
    LOGVAR_, MASKS_, MEAN_, NEAR_, NORM1_, NORM2_, NORMED_, ONE_, OUTPUT_, PANEL_, QKV_, QUERY_, RELAY_,
    ROWS_, S2_, SMALL_, SOURCE_, SUMS_, S_, T0_, T1_, TWO_, VALUE_, WDEC_, WD_, WH_, WK_, WL_, WM_, WO_, WQ_,
    WV_, X_, Z_,
) = range(61)

Z_FIRST = (HIDDEN1_,)


class Links:
    def __init__(self, slide, blk, send_sem, recv_sem):
        self.slide, self.blk = slide, blk
        self.send_sem, self.recv_sem = send_sem, recv_sem
        self.copies, self.count = [], 0

    def send(self, source, target, far_slide, far_blk):
        number = self.count
        self.count += 1
        copy = pltpu.make_async_remote_copy(
            src_ref=source,
            dst_ref=target,
            send_sem=self.send_sem.at[number],
            recv_sem=self.recv_sem.at[number],
            device_id={
                "slide": flipped(self.slide, far_slide),
                "blk": flipped(self.blk, far_blk),
            },
            device_id_type=MESH,
        )
        copy.start()
        self.copies.append(copy)
        return copy

    def drain(self, copy):
        copy.wait_send()
        self.copies = [other for other in self.copies if other is not copy]

    def finish(self):
        for copy in self.copies:
            copy.wait_send()


def spread_everywhere(links, slot):
    slide, blk = links.slide, links.blk
    copies = {}

    def push(rel_slide, rel_blk, to_slide, to_blk):
        block = slot(flipped(slide, rel_slide), flipped(blk, rel_blk))
        copies[(rel_slide ^ to_slide, rel_blk ^ to_blk)] = links.send(block, block, to_slide, to_blk)

    for far in (2, 4, 6):
        push(0, 0, 0, far)
    push(0, 0, 0, 1)
    push(0, 0, 2, 0)
    push(0, 0, 1, 0)
    yield
    for rel in (2, 4, 6):
        copies[0, rel].wait_recv()
        push(0, rel, 0, 1)
        push(0, rel, 2, 0)
        push(0, rel, 1, 0)
    yield
    for rel in (1, 3, 5, 7):
        copies[0, rel].wait_recv()
        push(0, rel, 2, 0)
        push(0, rel, 1, 0)
    yield
    for rel in (0, 2, 4, 6, 1, 3, 5, 7):
        copies[2, rel].wait_recv()
        push(2, rel, 1, 0)
    yield
    for far in (1, 3):
        for rel in (0, 2, 4, 6, 1, 3, 5, 7):
            copies[far, rel].wait_recv()
    yield


class Reduction:
    def __init__(self, links, left, right, rows, width, dense, buffers):
        self.links, self.left, self.right = links, left, right
        self.rows, self.width, self.dense = rows, width, dense
        self.away, self.came, self.pieces = buffers
        self.kept = self.away
        self.along_x, self.along_z = links.blk % 2, links.blk // 2

    def tiles(self, which, store):
        def tile(i, carry):
            place = which * 2 + i if self.dense else i * 2 + which
            product = dot_tn(self.left(pl.multiple_of(place * 128, 128)), self.right())
            store(pl.ds(pl.multiple_of(i * 128, 128), 128), product)
            return carry

        lax.fori_loop(0, self.rows * 4 // 128, tile, 0)

    def send_x(self):
        def store(where, product):
            self.away[where, :] = product.astype(BF16)

        self.tiles(1 - self.along_x, store)
        self.copy_x = self.links.send(self.away, self.came, 0, 1)

    def piece(self, far):
        return pl.ds(pl.multiple_of(flipped(self.along_z, far) * self.rows, self.rows), self.rows)

    def send_z(self):
        self.links.drain(self.copy_x)
        self.copy_x.wait_recv()

        def store(where, product):
            self.kept[where, :] = (product + self.came[where, :].astype(F32)).astype(BF16)

        self.tiles(self.along_x, store)
        self.copies_z = [
            self.links.send(self.kept.at[self.piece(far)], self.pieces.at[far // 2], 0, 2) for far in (3, 1)
        ]

    def send_far(self):
        for copy in self.copies_z:
            copy.wait_recv()
        where = self.piece(2)
        self.kept[where, :] = (self.kept[where, :].astype(F32) + self.pieces[1].astype(F32)).astype(BF16)
        self.copy_far = self.links.send(self.kept.at[where], self.pieces.at[2], 0, 4)

    def total(self):
        self.copy_far.wait_recv()
        own = self.kept[self.piece(0), :]
        return ((own.astype(F32) + self.pieces[0].astype(F32)) + self.pieces[2].astype(F32)).astype(BF16)


class ReductionAlongZ(Reduction):
    def tiles(self, start, store):
        step = 2 - 4 * ((start // 2) % 2)

        def tile(i, carry):
            place = (start + (i // 2) * step) * 2 + i % 2
            product = dot_tn(self.left(pl.multiple_of(place * 128, 128)), self.right())
            store(pl.ds(pl.multiple_of(i * 128, 128), 128), product)
            return carry

        lax.fori_loop(0, 4, tile, 0)

    def send_x(self):
        def store(where, product):
            self.away[where, :] = product.astype(BF16)

        self.tiles(flipped(self.along_z, 1), store)
        self.copy_x = self.links.send(self.away, self.came, 0, 2)

    def send_z(self):
        self.links.drain(self.copy_x)
        self.copy_x.wait_recv()

        def store(where, product):
            self.kept[where, :] = (product + self.came[where, :].astype(F32)).astype(BF16)

        self.tiles(self.along_z, store)
        self.copies_z = [
            self.links.send(self.kept.at[pl.ds((2 + side) * self.rows, self.rows)], self.pieces.at[side], 0, 4)
            for side in range(2)
        ]

    def block(self, side):
        return pl.ds(pl.multiple_of(side * self.rows, self.rows), self.rows)

    def send_far(self):
        for copy in self.copies_z:
            copy.wait_recv()
        other = 1 - self.along_x
        where = self.block(other)
        self.kept[where, :] = (self.kept[where, :].astype(F32) + self.pieces[other].astype(F32)).astype(BF16)
        self.copy_far = self.links.send(self.kept.at[where], self.pieces.at[2], 0, 1)

    def total(self):
        self.copy_far.wait_recv()
        own = self.kept[self.block(self.along_x), :].astype(F32) + self.pieces[self.along_x].astype(F32)
        return (own + self.pieces[2].astype(F32)).astype(BF16)


def spread_slide(links, slot, total):
    slide = links.slide
    own, far = slot(slide), slot(flipped(slide, 2))
    own[...] = total
    across = links.send(own, own, 2, 0)
    beside = links.send(own, own, 1, 0)
    yield
    across.wait_recv()
    last = links.send(far, far, 1, 0)
    yield
    beside.wait_recv()
    last.wait_recv()
    yield


def reductions_of(cells, width, inner, latents):
    return [
        (DECODER_, latents // 8, width // 4, True),
        (DOWN0_, inner // 32, width // 2, False),
        (DOWN1_, inner // 32, width // 2, False),
        (MEAN_, width // 8, latents // 4, False),
        (LOGVAR_, width // 8, latents // 4, False),
        (HIDDEN0_, width // 8, inner // 8, False),
        (HIDDEN1_, width // 8, inner // 8, False),
        (OUTPUT_, width // 8, width // 4, False),
        (PANEL_, width // 8, width // 4, False),
        (QUERY_, width // 8, width // 4, False),
        (KEY_, width // 8, width // 4, False),
        (VALUE_, width // 8, width // 4, False),
    ]


def across(links, ref, columns, cells):
    def rows(place):
        return ref.at[pl.ds(place * cells, cells), columns]

    far = links.send(rows(0), rows(2), 2, 0)
    near = links.send(rows(0), rows(1), 1, 0)
    yield
    far.wait_recv()
    last = links.send(rows(2), rows(3), 1, 0)
    yield
    near.wait_recv()
    last.wait_recv()
    yield


def norm_parts(hidden):
    centre = hidden - jnp.mean(hidden, axis=1, keepdims=True)
    invert = lax.rsqrt(jnp.mean(centre * centre, axis=1, keepdims=True) + 1e-05)
    return centre * invert, invert


def norm_back(hidden, gain, grad):
    unit, invert = norm_parts(hidden)
    gain_grad = jnp.sum(grad * unit, axis=0, keepdims=True)
    shift_grad = jnp.sum(grad, axis=0, keepdims=True)
    grad_unit = grad * gain
    grad_hidden = invert * (
        grad_unit
        - jnp.mean(grad_unit, axis=1, keepdims=True)
        - unit * jnp.mean(grad_unit * unit, axis=1, keepdims=True)
    )
    return grad_hidden, gain_grad, shift_grad


def exact_dot(left, right, dims):
    return lax.dot_general(
        left, right, (dims, ((), ())), precision=lax.Precision.HIGHEST, preferred_element_type=F32
    )


def mixture(mean_part, centres):
    crossed = exact_dot(mean_part, centres, ((1,), (1,)))
    ones = jnp.ones((8, centres.shape[1]), F32)
    centre_square = exact_dot(ones, centres * centres, ((1,), (1,)))[0:1]
    logits = (crossed - 0.5 * centre_square) / math.sqrt(centres.shape[1])
    shifted = jnp.exp(logits - jnp.max(logits, axis=1, keepdims=True))
    resp = shifted / jnp.sum(shifted, axis=1, keepdims=True)
    return resp, exact_dot(resp, centres, ((1,), (0,)))


def slide_masks(land, row_labels, col_labels, cells):
    for block in range(8):
        line = land[block, 3 * cells : 3 * cells + 1, :].astype(F32)
        col_labels[:, block * cells : (block + 1) * cells] = line
        row_labels[block * cells : (block + 1) * cells, :] = jnp.broadcast_to(line, (cells, cells)).T


ORDER = (
    (BOTTLENECK_,), (FEED_, 0), (FEED_, 1), (BRANCH_,), (FEED_, 2), (FEED_, 3), (NORM2_,), (ATT_,),
    (X_, DOWN0_), (GOUT_,), (MASKS_,), (X_, DOWN1_), (LATS_,), (BASE_,), (ROWS_, 0), (ROWS_, 1),
    (ROWS_, 2), (ROWS_, 3), (BACK_,), (Z_, DOWN0_), (RELAY_, LATENT_), (RELAY_, BASE_), (X_, HIDDEN0_),
    (F_, DOWN0_), (Z_, DOWN1_), (IN_,), (NORM1_,), (QKV_,), (SMALL_,), (RELAY_, LATENT_),
    (RELAY_, BASE_), (X_, HIDDEN1_), (X_, PANEL_), (X_, QUERY_), (X_, KEY_), (X_, VALUE_),
    (X_, MEAN_), (X_, LOGVAR_), (X_, DECODER_), (X_, OUTPUT_), (F_, DOWN1_), (SUMS_,),
    (Z_, HIDDEN0_), (S_, DOWN0_), (Z_, PANEL_), (S_, DOWN1_), (F_, HIDDEN0_), (F_, PANEL_),
    (Z_, HIDDEN1_), (Z_, QUERY_), (Z_, KEY_), (Z_, VALUE_), (PANEL_,), (Z_, MEAN_), (Z_, LOGVAR_),
    (Z_, DECODER_), (RELAY_, PANEL_), (Z_, OUTPUT_), (S_, HIDDEN0_), (F_, HIDDEN1_), (F_, QUERY_),
    (F_, KEY_), (F_, VALUE_), (RELAY_, PANEL_), (F_, MEAN_), (F_, LOGVAR_), (F_, DECODER_),
    (F_, OUTPUT_), (RELAY_, PANEL_), (S_, HIDDEN1_), (S_, QUERY_), (S_, KEY_), (S_, VALUE_),
    (S_, MEAN_), (S_, LOGVAR_), (S_, DECODER_), (S_, OUTPUT_), (S2_, DECODER_), (S2_, DOWN0_),
    (S2_, DOWN1_), (S2_, MEAN_), (S2_, LOGVAR_), (S2_, HIDDEN0_), (S2_, OUTPUT_), (S2_, HIDDEN1_),
    (S2_, QUERY_), (S2_, KEY_), (S2_, VALUE_), (DONE_,), (RELAY_, PANEL_), (S2_, DECODER_),
    (S2_, DOWN0_), (S2_, DOWN1_), (S2_, MEAN_), (S2_, LOGVAR_), (S2_, HIDDEN0_), (S2_, OUTPUT_),
    (S2_, HIDDEN1_), (S2_, QUERY_), (S2_, KEY_), (S2_, VALUE_),
)


def layer_kernel(
    ids_ref, counts_ref, library_ref, positions_ref, freqs_ref, labels_ref, noise_ref, source_ref, gain_one, shift_one,
    gain_two, shift_two, hidden_bias, down_bias, centres_ref, weight_ref, floor_ref,
    table_hbm, wq_hbm, wk_hbm, wv_hbm, wo_hbm, wh_hbm, wd_hbm, wm_hbm, wl_hbm, wdec_hbm,
    decoded_out, kl_out, panel_out, query_out, key_out, value_out, output_out, hidden_out, down_out, mean_out, logvar_out,
    decoder_out, small_out,
    slots, wo, wm, wl, wdec, part, panel_land, qkv_send, land, att_send_fwd, att_land_fwd, row_labels, col_labels,
    act_parts, final, kl_own, kl_slides, kl_sum, kl_blks, start, middle, inner_sums, mean_part, logvar_part, glatent, whole,
    quarters, base_all, latent_all, branch_all, gmean, glogvar, gmean_all, glogvar_all, ginner, ginner_all, gout, gout_all,
    gmiddle, gqkv_all, genc_all, att_send, att_land, dqkv, dqkv_land, dk_sum, dv_sum, grad_qkv, encoded, small, small_land,
    small_own, small_slides, load_sem, send_sem, recv_sem, *unit_refs,
):
    slide, blk = lax.axis_index("slide"), lax.axis_index("blk")
    cells, width = counts_ref.shape
    inner, latents, per = inner_sums.shape[1], mean_part.shape[1], width // 8
    loads = {}
    loaded = set()

    def load(name, source, target):
        loads[name] = pltpu.make_async_copy(source, target, load_sem.at[len(loads)])
        loads[name].start()

    def have(*names):
        for name in names:
            if name not in loaded:
                loaded.add(name)
                loads[name].wait()

    def load_quarter(name, which, wide, tall):
        columns = pl.ds(which * width if isinstance(which, int) else pl.multiple_of(which * width, 128), width)
        load((WH_, *name), wh_hbm.at[:, columns], slots.at[wide])
        load((WD_, *name), wd_hbm.at[columns, :], slots.at[tall])

    load(T0_, table_hbm.at[pl.ds(0, width)], slots.at[0])
    load(T1_, table_hbm.at[pl.ds(width, width)], slots.at[1])
    load(WQ_, wq_hbm, slots.at[2])
    load(WK_, wk_hbm, slots.at[3])
    load(WO_, wo_hbm, wo)
    load(WM_, wm_hbm, wm)
    load(WL_, wl_hbm, wl)
    load(WDEC_, wdec_hbm, wdec)
    greet(slide, blk, SLIDE_PEERS + BLK_PEERS)
    links = Links(slide, blk, send_sem, recv_sem)

    def column(line):
        return jnp.broadcast_to(line, (line.shape[1], line.shape[1])).T[:, 0:1]

    genes = ids_ref.shape[1]
    table_rows, block_rows = 2 * width, genes // 64
    first = (blk * table_rows).astype(F32)
    have(T0_, T1_)
    for side in range(2):
        ids = ids_ref[:, pl.ds(pl.multiple_of(slide * (genes // 4) + side * 128, 128), 128)].astype(F32)
        places = lax.broadcasted_iota(jnp.int32, (128, table_rows), 1).astype(F32) + first
        selector = (places == column(ids)).astype(F32).astype(BF16)
        rows = jnp.dot(selector[:, 0:width], slots[0], preferred_element_type=F32) + jnp.dot(
            selector[:, width:], slots[1], preferred_element_type=F32
        )
        part[side] = rows.astype(BF16).reshape(8, block_rows, width)
    load(WV_, wv_hbm, slots.at[0])
    part_copies = [
        [links.send(part.at[side, flipped(blk, far)], panel_land.at[side, far], 0, far) for far in (6, 4, 2, 7, 5, 3, 1)]
        for side in range(2)
    ]
    scale = column(10000.0 / library_ref[...].astype(F32))
    express = jnp.log(1.0 + counts_ref[...].astype(F32) * scale).astype(BF16)
    whole[0:cells, 0:width] = express
    quarter = width // 4
    for axis in range(2):
        angle = column(positions_ref[axis : axis + 1, :].astype(F32)) * freqs_ref[...]
        start[:, 2 * axis * quarter : (2 * axis + 1) * quarter] = jnp.sin(angle)
        start[:, (2 * axis + 1) * quarter : (2 * axis + 2) * quarter] = jnp.cos(angle)

    def panel_rows(far_slide, far_blk, side):
        first_gene = (far_slide * 2 + side) * 8 * block_rows + far_blk * block_rows
        return panel_out.at[pl.ds(pl.multiple_of(first_gene, 16), block_rows)]

    row_spreads = []
    for side in range(2):
        total = part[side, blk].astype(F32)
        for place, far in enumerate((6, 4, 2, 7, 5, 3, 1)):
            part_copies[side][place].wait_recv()
            total = total + panel_land[side, far].astype(F32)
        own_rows = panel_rows(slide, blk, side)
        own_rows[...] = total.astype(BF16)
        row_spreads.append(spread_everywhere(links, lambda far_slide, far_blk, side=side: panel_rows(far_slide, far_blk, side)))
        next(row_spreads[side])
        if side:
            next(row_spreads[1])
            next(row_spreads[0])
        else:
            next(row_spreads[0])
    next(row_spreads[1])
    next(row_spreads[0])
    next(row_spreads[1])
    next(row_spreads[0])
    next(row_spreads[1])
    panel_copies = list(links.copies)
    send_express = across(links, whole, pl.ds(0, width), cells)
    next(send_express)

    def source_part(which):
        return source_ref.at[:, pl.ds(pl.multiple_of(which * quarter, 128), quarter)]

    def source_slot(place):
        return quarters.at[pl.ds(place * cells, cells), pl.ds(inner // 4, quarter)]

    source_copies = [links.send(source_part(flipped(slide, far)), source_slot(far), far, 0) for far in (2, 3, 1)]
    source_slot(0)[...] = source_part(slide)[...]

    hidden_start = start[...] + jnp.dot(express, panel_out[...], preferred_element_type=F32)
    start[...] = hidden_start
    normed = (norm_parts(hidden_start)[0] * gain_one[...] + shift_one[...]).astype(BF16)
    whole[0:cells, width : 2 * width] = normed
    qkv_send[:, 3 * cells :, :] = jnp.broadcast_to(labels_ref[...].astype(F32).astype(BF16).reshape(1, 1, cells), (8, 16, per))
    have(WQ_, WK_, WV_)
    load((WH_, 0), wh_hbm.at[:, pl.ds(0, width)], slots.at[1])

    along_x, along_z = blk % 2, blk // 2
    qkv_copies = []
    for far in (3, 2, 1, 0):
        pair = flipped(along_z, far)
        columns = pl.ds(pl.multiple_of(pair * 2 * per, 128), 2 * per)
        for number, weight in enumerate((slots.at[2], slots.at[3], slots.at[0])):
            product = jnp.dot(normed, weight[:, columns], preferred_element_type=F32).astype(BF16)
            for side in range(2):
                qkv_send[pair * 2 + side, number * cells : (number + 1) * cells, :] = product[:, side * per : (side + 1) * per]
        for side in (1, 0):
            if far or side:
                target = flipped(pair * 2 + along_x, side)
                qkv_copies.append(links.send(qkv_send.at[target], land.at[blk], 0, 2 * far + side))
    land[blk] = qkv_send[blk]
    load((WD_, 0), wd_hbm.at[pl.ds(0, width), :], slots.at[2])
    load_quarter((1,), 1, 3, 0)
    next(send_express)
    send_normed = across(links, whole, pl.ds(width, width), cells)
    next(send_normed)
    for copy in panel_copies:
        links.drain(copy)
    for copy in qkv_copies:
        copy.wait_recv()

    slide_masks(land, row_labels, col_labels, cells)
    key = land[:, cells : 2 * cells, :].reshape(8 * cells, per)
    value = land[:, 2 * cells : 3 * cells, :].reshape(8 * cells, per)
    att_copies = []
    for far in (3, 2, 1, 0):
        pair = flipped(along_z, far)
        query = land[pl.ds(pair * 2, 2), 0:cells, :].reshape(2 * cells, per)
        same_slide = row_labels[pl.ds(pl.multiple_of(pair * 2 * cells, 128), 2 * cells), 0:1] == col_labels[...]
        lane = lax.broadcasted_iota(jnp.int32, query.shape, 1)
        out = None
        for head in range(per // HEAD_DIM):
            mine = lane // HEAD_DIM == head
            shares = head_scores(jnp.where(mine, query, 0), key, same_slide)
            part = jnp.dot(shares.astype(BF16), value, preferred_element_type=F32)
            out = part if out is None else jnp.where(mine, part, out)
        att_send_fwd[pl.ds(pair * 2, 2)] = out.astype(BF16).reshape(2, cells, per)
        for side in (1, 0):
            if far or side:
                target = flipped(pair * 2 + along_x, side)
                att_copies.append(links.send(att_send_fwd.at[target], att_land_fwd.at[blk], 0, 2 * far + side))
    att_land_fwd[blk] = att_send_fwd[blk]
    next(send_normed)
    for copy in att_copies:
        copy.wait_recv()
    for block in range(8):
        whole[0:cells, 2 * width + block * per : 2 * width + (block + 1) * per] = att_land_fwd[block]
    send_attended = across(links, whole, pl.ds(2 * width, width), cells)
    next(send_attended)

    have(WO_)
    hidden_middle = start[...] + jnp.dot(
        whole[0:cells, 2 * width : 3 * width], wo[...], preferred_element_type=F32
    )
    middle[...] = hidden_middle
    normed_two = (norm_parts(hidden_middle)[0] * gain_two[...] + shift_two[...]).astype(BF16)
    whole[0:cells, 3 * width :] = normed_two
    send_two = across(links, whole, pl.ds(3 * width, width), cells)
    next(send_two)
    final[...] = hidden_middle + down_bias[...]
    chunk = inner // 8

    for which in range(4):
        wide, tall = ((1, 2), (3, 0))[which % 2]
        have((WH_, which), (WD_, which))

        def feed_on(j, carry, which=which, wide=wide, tall=tall):
            near = pl.ds(pl.multiple_of(j * chunk, 128), chunk)
            where = pl.ds(pl.multiple_of(which * width + j * chunk, 128), chunk)
            inner_sum = jnp.dot(whole[0:cells, 3 * width :], slots[wide, :, near], preferred_element_type=F32) + hidden_bias[:, where]
            inner_sums[:, where] = inner_sum
            act = gelu_tanh(inner_sum).astype(BF16)
            place = pl.ds(pl.multiple_of((which * 2 + j) * (chunk // 4), 128), chunk // 4)
            for block in range(4):
                act_parts[block, :, place] = act[:, block * (chunk // 4) : (block + 1) * (chunk // 4)]
            final[...] += jnp.dot(act, slots[tall, near, :], preferred_element_type=F32)
            return carry

        lax.fori_loop(0, 2, feed_on, 0)
        if which < 2:
            load_quarter((which + 2,), which + 2, wide, tall)
        else:
            load_quarter((B_, which), flipped(slide, which), wide, tall)
    act_copies = [
        links.send(act_parts.at[flipped(slide, far)], quarters.at[pl.ds(far * cells, cells), pl.ds(0, inner // 4)], far, 0)
        for far in (2, 3, 1)
    ]
    quarters[0:cells, 0 : inner // 4] = act_parts[slide]
    base = final[...].astype(BF16)
    base_all[0:cells, :] = base
    have(WM_, WL_, WDEC_)
    mean_lat = jnp.dot(base, wm[...], preferred_element_type=F32)
    log_var = jnp.dot(base, wl[...], preferred_element_type=F32)
    mean_part[...] = mean_lat
    logvar_part[...] = log_var
    centres = centres_ref[...]
    resp, mixed = mixture(mean_lat, centres)
    mixed_square = exact_dot(resp, centres * centres, ((1,), (0,)))
    kl_cell = 0.5 * (
        jnp.exp(log_var) - 1.0 - log_var + mean_lat * mean_lat - 2.0 * mean_lat * mixed + mixed_square
    )
    kl_line = jnp.sum(kl_cell, axis=0, keepdims=True)
    kl_own[...] = jnp.zeros_like(kl_own)
    for block in range(latents // 128):
        kl_own[block : block + 1, :] = kl_line[:, block * 128 : (block + 1) * 128]
    kl_copies = [links.send(kl_own, kl_slides.at[slide], far, 0) for far in (2, 3, 1)]
    kl_slides[slide] = kl_own[...]
    latent = (mean_lat + jnp.exp(0.5 * log_var) * noise_ref[...]).astype(BF16)
    rows = latents // 8
    for side in range(2):
        for step in range(4):
            place = (step * 2 + side) * rows
            latent_all[0:cells, (side * 4 + step) * rows : (side * 4 + step + 1) * rows] = latent[:, place : place + rows]
    flows = {LATENT_: across(links, latent_all, pl.ds(0, latents), cells)}
    next(flows[LATENT_])
    decoded_out[...] = jnp.dot(latent, wdec[...], preferred_element_type=F32)
    for copy in kl_copies:
        copy.wait_recv()
    kl_sum[...] = (kl_slides[0] + kl_slides[1]) + (kl_slides[2] + kl_slides[3])
    kl_copies = [links.send(kl_sum, kl_blks.at[blk], 0, far) for far in (6, 4, 2, 7, 5, 3, 1)]
    kl_blks[blk] = kl_sum[...]
    glatent[...] = dot_nt(source_ref[...], wdec[...])
    next(send_attended)
    next(send_two)
    for copy in kl_copies:
        copy.wait_recv()
    kl_total = kl_blks[0]
    for block in range(1, 8):
        kl_total = kl_total + kl_blks[block]
    kl_out[...] = kl_total
    flows[ACT_], flows[SOURCE_] = act_copies, source_copies
    flows[EXPRESS_], flows[NORMED_], flows[ATTENDED_], flows[TWO_] = send_express, send_normed, send_attended, send_two

    def lanes(ref, which, size):
        return ref.at[:, pl.ds(pl.multiple_of(which * size, 128), size)]

    def swap(ref, size, target):
        copies = []
        for far in (2, 3, 1):
            copies.append(links.send(lanes(ref, flipped(slide, far), size), target.at[far], far, 0))
        target[0] = lanes(ref, slide, size)[...]
        return copies

    waited = set()

    def arrived(*names):
        for name in names:
            if name not in waited:
                waited.add(name)
                for copy in flows[name]:
                    copy.wait_recv()

    def start_base():
        flows[BASE_] = across(links, base_all, pl.ds(0, width), cells)
        next(flows[BASE_])

    def relay(name):
        next(flows[name])

    small[...] = jnp.zeros_like(small)

    def bottleneck():
        kl_mean = jnp.concatenate([kl_out[block : block + 1, :] for block in range(latents // 128)], axis=1) / (32 * cells)
        grad_kl = weight_ref[0, 0] * (kl_mean > floor_ref[...]).astype(F32)
        mean_lat, log_var, centres = mean_part[...], logvar_part[...], centres_ref[...]
        grad_latent = glatent[...]
        resp, mixed = mixture(mean_lat, centres)
        weighted = mean_lat * grad_kl
        half_square = exact_dot(jnp.broadcast_to(0.5 * grad_kl, (8, latents)), centres * centres, ((1,), (1,)))[0:1]
        grad_resp = half_square - exact_dot(weighted, centres, ((1,), (1,)))
        grad_logits = resp * (grad_resp - jnp.sum(resp * grad_resp, axis=1, keepdims=True)) / math.sqrt(latents)
        grad_mean = grad_latent + grad_kl * (mean_lat - mixed) + exact_dot(grad_logits, centres, ((1,), (0,)))
        grad_logvar = grad_latent * (0.5 * jnp.exp(0.5 * log_var) * noise_ref[...]) + 0.5 * grad_kl * (jnp.exp(log_var) - 1.0)
        gmean[...] = grad_mean.astype(BF16)
        glogvar[...] = grad_logvar.astype(BF16)
        have(WM_, WL_)
        grad_final = dot_nt(gmean[...], wm[...]) + dot_nt(glogvar[...], wl[...])
        gmiddle[...] = grad_final
        branch_all[0] = grad_final.astype(BF16)
        flows[FAR_] = [links.send(branch_all.at[0], branch_all.at[2], 2, 0)]
        flows[NEAR_] = [links.send(branch_all.at[0], branch_all.at[1], 1, 0)]
        ones = jnp.ones((cells, 128), F32)
        logit_sum = exact_dot(grad_logits, ones, ((0,), (0,)))[:, 0:1]
        resp_sum = exact_dot(resp, ones, ((0,), (0,)))[:, 0:1]
        centres_grad = (
            exact_dot(grad_logits, mean_lat, ((0,), (0,)))
            - logit_sum * centres
            - exact_dot(resp, weighted, ((0,), (0,)))
            + resp_sum * grad_kl * centres
        )
        count = centres.shape[0]
        for block in range(8):
            small[block, 16 : 16 + count, 0 : latents // 8] = centres_grad[:, block * (latents // 8) : (block + 1) * (latents // 8)]
        bias_line = jnp.sum(branch_all[0].astype(F32), axis=0, keepdims=True)
        for block in range(8):
            small[block, 8:9, :] = bias_line[:, block * 128 : (block + 1) * 128]


    def swap_latents():
        flows[GMEAN_] = swap(gmean, latents // 4, gmean_all)
        flows[GLOGVAR_] = swap(glogvar, latents // 4, glogvar_all)

    def branch_on():
        arrived(FAR_)
        flows[NEAR_].append(links.send(branch_all.at[2], branch_all.at[3], 1, 0))

    width_at = {EXPRESS_: 0, ONE_: width, ATTENDED_: 2 * width, TWO_: 3 * width}

    def of_whole(name):
        def left(column):
            return whole[:, pl.ds(width_at[name] + column, 128)]

        return left

    def of_base(column):
        return base_all[:, pl.ds(column, 128)]

    def of_latent(column):
        return latent_all[:, pl.ds(column, 128)]

    def of_act(column):
        return quarters[:, pl.ds(column, 128)]

    def flat(ref, start=None, size=None):
        def right():
            block = ref[...] if start is None else ref[:, :, start : start + size]
            return block.reshape(4 * cells, block.shape[-1])

        return right

    def source_all():
        return quarters[:, inner // 4 :]

    half_w, half_i = width // 2, inner // 8
    operands = {
        DECODER_: (of_latent, source_all),
        DOWN0_: (of_act, flat(branch_all, 0, half_w)),
        DOWN1_: (of_act, flat(branch_all, half_w, half_w)),
        MEAN_: (of_base, flat(gmean_all)),
        LOGVAR_: (of_base, flat(glogvar_all)),
        HIDDEN0_: (of_whole(TWO_), flat(ginner_all, 0, half_i)),
        HIDDEN1_: (of_whole(TWO_), flat(ginner_all, half_i, half_i)),
        OUTPUT_: (of_whole(ATTENDED_), flat(gout_all)),
        PANEL_: (of_whole(EXPRESS_), flat(genc_all)),
        QUERY_: (of_whole(ONE_), flat(gqkv_all.at[0])),
        KEY_: (of_whole(ONE_), flat(gqkv_all.at[1])),
        VALUE_: (of_whole(ONE_), flat(gqkv_all.at[2])),
    }
    units = {}
    for number, (name, rows, columns, dense) in enumerate(reductions_of(cells, width, inner, latents)):
        left, right = operands[name]
        units[name] = (ReductionAlongZ if name in Z_FIRST else Reduction)(
            links, left, right, rows, columns, dense, unit_refs[3 * number : 3 * number + 3]
        )

    result_slots = {
        DECODER_: lambda place: lanes(decoder_out, place, width // 4),
        DOWN0_: lambda place: down_out.at[pl.ds(pl.multiple_of(place * (inner // 32), inner // 32), inner // 32), pl.ds(0, half_w)],
        DOWN1_: lambda place: down_out.at[pl.ds(pl.multiple_of(place * (inner // 32), inner // 32), inner // 32), pl.ds(half_w, half_w)],
        MEAN_: lambda place: lanes(mean_out, place, latents // 4),
        LOGVAR_: lambda place: lanes(logvar_out, place, latents // 4),
        HIDDEN0_: lambda place: hidden_out.at[:, pl.ds(pl.multiple_of(place * (inner // 4), 128), half_i)],
        HIDDEN1_: lambda place: hidden_out.at[:, pl.ds(pl.multiple_of(place * (inner // 4) + half_i, 128), half_i)],
        OUTPUT_: lambda place: lanes(output_out, place, width // 4),
        QUERY_: lambda place: lanes(query_out, place, width // 4),
        KEY_: lambda place: lanes(key_out, place, width // 4),
        VALUE_: lambda place: lanes(value_out, place, width // 4),
    }
    spreads = {}

    def spread(name):
        spreads[name] = spread_slide(links, result_slots[name], units[name].total())
        next(spreads[name])

    chunk = inner // 8
    encoded[...] = jnp.zeros_like(encoded)

    def feed_back(turn):
        far = (2, 3, 1, 0)[turn]
        wide, tall = ((1, 2), (3, 0))[turn % 2]
        have((WD_, B_, far), (WH_, B_, far))
        which = flipped(slide, far)

        def feed(j, carry, wide=wide, tall=tall, which=which):
            near = pl.ds(pl.multiple_of(j * chunk, 128), chunk)
            where = pl.ds(pl.multiple_of(which * (inner // 4) + j * chunk, 128), chunk)
            values = inner_sums[:, where]
            squared = values * values
            bent = jnp.tanh(0.7978845608028654 * (values + 0.044715 * squared * values))
            slope = 0.5 * (1.0 + bent) + 0.5 * values * (1.0 - bent * bent) * (
                0.7978845608028654 * (1.0 + 3 * 0.044715 * squared)
            )
            grad = (dot_nt(branch_all[0], slots[tall, near, :]) * slope).astype(BF16)
            ginner[:, where] = grad
            line = jnp.sum(grad.astype(F32), axis=0, keepdims=True)
            for block in range(chunk // 128):
                small[which * 2 + j, 4 + block : 5 + block, :] = line[:, block * 128 : (block + 1) * 128]
            encoded[...] += dot_nt(grad, slots[wide, :, near])
            return carry

        lax.fori_loop(0, 2, feed, 0)
        if far:
            flows[INNER_] = flows.get(INNER_, []) + [
                links.send(lanes(ginner, which, inner // 4), ginner_all.at[far], far, 0)
            ]
        else:
            ginner_all[0] = lanes(ginner, slide, inner // 4)[...]
        if turn < 2:
            load_quarter((B_, (1, 0)[turn]), flipped(slide, (1, 0)[turn]), wide, tall)
        if turn == 3:
            for number, (name, source) in enumerate(((WQ_, wq_hbm), (WK_, wk_hbm), (WV_, wv_hbm))):
                load((B_, name), source, slots.at[number])

    wq, wk, wv = slots.at[0], slots.at[1], slots.at[2]

    def norm_two():
        grad_hidden, gain_grad, shift_grad = norm_back(middle[...], gain_two[...], encoded[...])
        for block in range(8):
            small[block, 2:3, :] = gain_grad[:, block * 128 : (block + 1) * 128]
            small[block, 3:4, :] = shift_grad[:, block * 128 : (block + 1) * 128]
        gmiddle[...] += grad_hidden
        gout[...] = gmiddle[...].astype(BF16)

    def att_out():
        have(WO_)

        def att_block(target, store):
            rows = wo[pl.ds(pl.multiple_of(target * per, per), per), :]
            store(dot_nt(gout[...], rows).astype(BF16))

        att_copies = flows[ATT_] = []
        for far in (6, 4, 2, 7, 5, 3, 1):
            target = flipped(blk, far)

            def keep(block, far=far):
                att_send[far] = block

            att_block(target, keep)
            att_copies.append(links.send(att_send.at[far], att_land.at[blk], 0, far))

        def keep_own(block):
            att_land[blk] = block

        att_block(blk, keep_own)

    def swap_out():
        flows[GOUT_] = swap(gout, width // 4, gout_all)

    def masks():
        dk_sum[...] = jnp.zeros_like(dk_sum)
        dv_sum[...] = jnp.zeros_like(dv_sum)

    scale = HEAD_DIM**-0.5
    rows = 2 * cells

    def rows_back(i):
        arrived(ATT_)
        where = pl.ds(pl.multiple_of(i * rows, rows), rows)
        same_slide = row_labels[where, 0:1] == col_labels[...]
        query = land[pl.ds(2 * i, 2), 0:cells, :].reshape(rows, per)
        grad = att_land[pl.ds(2 * i, 2)].reshape(rows, per)
        key = land[:, cells : 2 * cells, :].reshape(8 * cells, per)
        value = land[:, 2 * cells : 3 * cells, :].reshape(8 * cells, per)
        lane = lax.broadcasted_iota(jnp.int32, query.shape, 1)
        grad_query = None
        for head in range(per // HEAD_DIM):
            mine = lane // HEAD_DIM == head
            own_query = jnp.where(mine, query, 0)
            own_grad = jnp.where(mine, grad, 0)
            shares = head_scores(own_query, key, same_slide)
            grad_shares = dot_nt(own_grad, value)
            inner_dot = jnp.sum(shares * grad_shares, axis=1, keepdims=True)
            grad_scores = (shares * (grad_shares - inner_dot)).astype(BF16)
            part = jnp.dot(grad_scores, key, preferred_element_type=F32)
            grad_query = part if grad_query is None else jnp.where(mine, part, grad_query)
            dk_sum[...] += dot_tn(grad_scores, own_query)
            dv_sum[...] += dot_tn(shares.astype(BF16), own_grad)
        dqkv[pl.ds(2 * i, 2), 0:cells, :] = (grad_query * scale).astype(BF16).reshape(2, cells, per)

    def back_out():
        dqkv[:, cells : 2 * cells, :] = (dk_sum[...] * scale).astype(BF16).reshape(8, cells, per)
        dqkv[:, 2 * cells :, :] = dv_sum[...].astype(BF16).reshape(8, cells, per)
        back_copies = flows[BACK_] = []
        for far in (6, 4, 2, 7, 5, 3, 1):
            back_copies.append(links.send(dqkv.at[flipped(blk, far)], dqkv_land.at[blk], 0, far))
        dqkv_land[blk] = dqkv[blk]

    def back_in():
        arrived(BACK_)
        have((B_, WQ_), (B_, WK_), (B_, WV_))
        for part in range(3):
            for block in range(8):
                grad_qkv[part, :, block * per : (block + 1) * per] = dqkv_land[block, part * cells : (part + 1) * cells, :]


    def swap_qkv():
        for part in range(3):
            flows[(QKV_, part)] = swap(grad_qkv.at[part], width // 4, gqkv_all.at[part])

    def norm_input(i, carry):
        where = pl.ds(pl.multiple_of(i * 256, 256), 256)
        encoded_sum = (
            dot_nt(grad_qkv[0], wq[where, :]) + dot_nt(grad_qkv[1], wk[where, :]) + dot_nt(grad_qkv[2], wv[where, :])
        )
        encoded[:, where] = encoded_sum
        return carry

    def norm_one():
        lax.fori_loop(0, width // 256, norm_input, 0)
        grad_hidden, gain_grad, shift_grad = norm_back(start[...], gain_one[...], encoded[...])
        grad_qkv[3] = (gmiddle[...] + grad_hidden).astype(BF16)
        flows[GENC_] = swap(grad_qkv.at[3], width // 4, genc_all)
        for block in range(8):
            small[block, 0:1, :] = gain_grad[:, block * 128 : (block + 1) * 128]
            small[block, 1:2, :] = shift_grad[:, block * 128 : (block + 1) * 128]

    def small_out_blk():
        flows[SMALL_] = [links.send(small.at[flipped(blk, far)], small_land.at[blk], 0, far) for far in range(1, 8)]
        small_land[blk] = small[blk]

    def small_out_slide():
        arrived(SMALL_)
        small_sum = small_land[0]
        for block in range(1, 8):
            small_sum = small_sum + small_land[block]
        small_own[...] = small_sum
        flows[SUMS_] = [links.send(small_own, small_slides.at[slide], far, 0) for far in (2, 3, 1)]
        small_slides[slide] = small_sum

    def small_done():
        arrived(SUMS_)
        small_out[...] = (small_slides[0] + small_slides[1]) + (small_slides[2] + small_slides[3])

    panel_slot = lambda far_slide, far_blk: panel_out.at[
        pl.ds(pl.multiple_of(far_blk * (width // 8), 128), width // 8),
        pl.ds(pl.multiple_of(far_slide * (width // 4), 128), width // 4),
    ]
    needs = {
        DECODER_: (SOURCE_,), DOWN0_: (ACT_, NEAR_), DOWN1_: (ACT_, NEAR_), MEAN_: (GMEAN_,), LOGVAR_: (GLOGVAR_,),
        HIDDEN0_: (INNER_,), HIDDEN1_: (INNER_,), OUTPUT_: (GOUT_,), PANEL_: (GENC_,), QUERY_: ((QKV_, 0),),
        KEY_: ((QKV_, 1),), VALUE_: ((QKV_, 2),),
    }

    def along(name):
        arrived(*needs[name])
        held = {HIDDEN0_: TWO_, HIDDEN1_: TWO_, OUTPUT_: ATTENDED_, PANEL_: EXPRESS_}
        held = held.get(name, NORMED_ if name in (QUERY_, KEY_, VALUE_) else None)
        if held and held not in waited:
            waited.add(held)
            next(flows[held])
        units[name].send_x()

    def panel_out_start():
        own_slot = panel_slot(slide, blk)
        own_slot[...] = units[PANEL_].total()
        flows[PANEL_] = spread_everywhere(links, panel_slot)
        next(flows[PANEL_])

    def spread_on(name):
        next(spreads[name])

    steps = {
        BASE_: start_base, RELAY_: relay, BOTTLENECK_: bottleneck, LATS_: swap_latents,
        BRANCH_: branch_on, FEED_: feed_back, NORM2_: norm_two, ATT_: att_out, GOUT_: swap_out, MASKS_: masks,
        ROWS_: rows_back, BACK_: back_out, IN_: back_in, QKV_: swap_qkv, NORM1_: norm_one, SMALL_: small_out_blk,
        SUMS_: small_out_slide, DONE_: small_done, X_: along, Z_: lambda name: units[name].send_z(),
        F_: lambda name: units[name].send_far(), S_: spread, S2_: spread_on, PANEL_: panel_out_start,
    }
    for step in ORDER:
        steps[step[0]](*step[1:])
    links.finish()


def layer(inputs, weights, cells, width, inner, latents):
    per = width // 8
    small_rows = 32
    shape = jax.ShapeDtypeStruct
    unit_scratch = []
    for _, rows, columns, _ in reductions_of(cells, width, inner, latents):
        unit_scratch += [pltpu.VMEM((4 * rows, columns), BF16)] * 2 + [pltpu.VMEM((3, rows, columns), BF16)]
    copies = 352
    vmem, left = pl.BlockSpec(memory_space=pltpu.VMEM), pl.BlockSpec(memory_space=pl.ANY)
    outs = (
        shape((cells, width), F32),
        shape((8, 128), F32),
        shape((width, width), BF16),
        shape((per, width), BF16),
        shape((per, width), BF16),
        shape((per, width), BF16),
        shape((per, width), BF16),
        shape((per, inner), BF16),
        shape((inner // 8, width), BF16),
        shape((per, latents), BF16),
        shape((per, latents), BF16),
        shape((latents // 8, width), BF16),
        shape((small_rows, 128), F32),
    )
    scratch = [
        ((4, width, width), BF16),
        ((width, width), BF16),
        ((width, latents), BF16),
        ((width, latents), BF16),
        ((latents, width), BF16),
        ((2, 8, width // 64, width), BF16),
        ((2, 8, width // 64, width), BF16),
        ((8, 3 * cells + 16, per), BF16),
        ((8, 3 * cells + 16, per), BF16),
        ((8, cells, per), BF16),
        ((8, cells, per), BF16),
        ((8 * cells, cells), F32),
        ((1, 8 * cells), F32),
        ((4, cells, inner // 4), BF16),
        ((cells, width), F32),
        ((8, 128), F32),
        ((4, 8, 128), F32),
        ((8, 128), F32),
        ((8, 8, 128), F32),
        ((cells, width), F32),
        ((cells, width), F32),
        ((cells, inner), F32),
        ((cells, latents), F32),
        ((cells, latents), F32),
        ((cells, latents), F32),
        ((4 * cells, 4 * width), BF16),
        ((4 * cells, inner // 4 + width // 4), BF16),
        ((4 * cells, width), BF16),
        ((4 * cells, latents), BF16),
        ((4, cells, width), BF16),
        ((cells, latents), BF16),
        ((cells, latents), BF16),
        ((4, cells, latents // 4), BF16),
        ((4, cells, latents // 4), BF16),
        ((cells, inner), BF16),
        ((4, cells, inner // 4), BF16),
        ((cells, width), BF16),
        ((4, cells, width // 4), BF16),
        ((cells, width), F32),
        ((3, 4, cells, width // 4), BF16),
        ((4, cells, width // 4), BF16),
        ((8, cells, per), BF16),
        ((8, cells, per), BF16),
        ((8, 3 * cells, per), BF16),
        ((8, 3 * cells, per), BF16),
        ((8 * cells, per), F32),
        ((8 * cells, per), F32),
        ((4, cells, width), BF16),
        ((cells, width), F32),
        ((8, small_rows, 128), F32),
        ((8, small_rows, 128), F32),
        ((small_rows, 128), F32),
        ((4, small_rows, 128), F32),
    ]
    return pl.pallas_call(
        layer_kernel,
        out_shape=outs,
        in_specs=[vmem] * len(inputs) + [left] * len(weights),
        out_specs=[vmem] * len(outs),
        scratch_shapes=[pltpu.VMEM(*item) for item in scratch]
        + [
            pltpu.SemaphoreType.DMA((28,)),
            pltpu.SemaphoreType.DMA((copies,)),
            pltpu.SemaphoreType.DMA((copies,)),
        ]
        + unit_scratch,
        compiler_params=pltpu.CompilerParams(
            collective_id=1, has_side_effects=True, vmem_limit_bytes=63 << 20
        ),
        name="layer",
    )(*inputs, *weights)


def finish_kernel(ids_ref, panel_ref, small_ref, kl_ref, weight_ref, floor_ref, *refs):
    count = (len(refs) - 9) // 2
    table_out, grads, outs, tiny = refs[count], refs[:count], refs[count + 1 : 2 * count + 1], refs[2 * count + 1 :]
    rows = table_out.shape[0]
    first = (lax.axis_index("blk") * pl.num_programs(0) + pl.program_id(0)) * rows
    row_ids = first + lax.broadcasted_iota(jnp.int32, (rows, ids_ref.shape[1]), 0)
    spread = (row_ids == ids_ref[...]).astype(F32).astype(BF16)
    table_out[...] = jnp.dot(spread, panel_ref[...], preferred_element_type=F32)
    for grad, out in zip(grads, outs):
        out[...] = grad[...].astype(F32)

    @pl.when(pl.program_id(0) == 0)
    def _():
        start = 0
        for out in tiny[:6]:
            out[...] = small_ref[start : start + out.shape[0], :]
            start += out.shape[0]
        centres = tiny[6]
        centres[...] = small_ref[16 : 16 + centres.shape[0], 0 : centres.shape[1]]
        total = jnp.zeros((1, 128), F32)
        for block in range(floor_ref.shape[1] // 128):
            lanes = slice(block * 128, (block + 1) * 128)
            total = total + jnp.maximum(kl_ref[block : block + 1, :] / weight_ref[0, 1], floor_ref[:, lanes])
        tiny[7][...] = weight_ref[0, 0] * (jnp.sum(total, axis=1, keepdims=True) / floor_ref.shape[1])


def finish(gene_ids, panel, grads, small, kl_total, weight, floor, table_rows, centres_shape, bias_rows, rows=256):
    genes, width = panel.shape
    steps = table_rows // rows
    shape = jax.ShapeDtypeStruct
    tiny = [(1, 128)] * 4 + [(bias_rows, 128), (1, 128), centres_shape, (1, 1)]

    def cut(grad):
        if grad.shape[0] // steps % 16 == 0:
            return pl.BlockSpec((grad.shape[0] // steps, grad.shape[1]), lambda i: (i, 0))
        return pl.BlockSpec((grad.shape[0], grad.shape[1] // steps), lambda i: (0, i))

    def whole(size):
        return pl.BlockSpec(size, lambda i: (0, 0))

    return pl.pallas_call(
        finish_kernel,
        grid=(steps,),
        out_shape=[shape((table_rows, width), F32)] + [shape(grad.shape, F32) for grad in grads] + [shape(size, F32) for size in tiny],
        in_specs=[
            whole((1, genes)), whole(panel.shape), whole(small.shape), whole(kl_total.shape),
            pl.BlockSpec(memory_space=pltpu.SMEM), whole(floor.shape),
        ]
        + [cut(grad) for grad in grads],
        out_specs=[pl.BlockSpec((rows, width), lambda i: (i, 0))] + [cut(grad) for grad in grads] + [whole(size) for size in tiny],
        compiler_params=pltpu.CompilerParams(vmem_limit_bytes=62 << 20),
        name="finish",
    )(gene_ids, panel, small, kl_total, weight, floor, *grads)


def on_device_fast(
    counts,
    library,
    gene_ids,
    positions,
    slide_of_cell,
    latent_noise,
    decoded_grad,
    gene_table,
    first_gain,
    first_shift,
    query_weight,
    key_weight,
    value_weight,
    output_weight,
    second_gain,
    second_shift,
    hidden_weight,
    hidden_bias,
    down_weight,
    down_bias,
    mean_weight,
    logvar_weight,
    component_means,
    decoder_weight,
    divergence_weight,
    free_floor,
):
    cells = counts.shape[1]
    width = gene_table.shape[1]
    latents = mean_weight.shape[1]
    inner = hidden_weight.shape[1]
    table_rows = gene_table.shape[0]
    quarter = width // 4
    freqs = np.exp(-math.log(10000.0) * np.arange(quarter, dtype=np.float32) / quarter).astype(np.float32)
    (
        decoded, kl_total, panel_sum, query_grad, key_grad, value_grad, output_grad, hidden_grad, down_grad, mean_grad,
        logvar_grad, decoder_grad, small,
    ) = layer(
        (
            gene_ids[None], counts[0], library, positions[0], freqs[None], slide_of_cell, latent_noise[0], decoded_grad[0],
            first_gain[None], first_shift[None], second_gain[None], second_shift[None], hidden_bias[None],
            down_bias[None], component_means, divergence_weight[None], free_floor[None],
        ),
        (
            gene_table, query_weight, key_weight, value_weight, output_weight, hidden_weight, down_weight, mean_weight,
            logvar_weight, decoder_weight,
        ),
        cells, width, inner, latents,
    )
    (
        table_grad, query_grad, key_grad, value_grad, output_grad, hidden_grad, down_grad, mean_grad, logvar_grad,
        decoder_grad, gain_one, shift_one, gain_two, shift_two, hidden_small, down_small, centres_grad, divergence,
    ) = finish(
        gene_ids[None], panel_sum,
        (
            query_grad, key_grad, value_grad, output_grad, hidden_grad, down_grad, mean_grad, logvar_grad,
            decoder_grad,
        ),
        small, kl_total, jnp.stack([divergence_weight[0], jnp.float32(32 * cells)])[None], free_floor[None], table_rows,
        (component_means.shape[0], latents // 8), inner // 8 // 128,
    )
    return (
        decoded[None],
        divergence.reshape(1),
        table_grad,
        gain_one.reshape(-1),
        shift_one.reshape(-1),
        query_grad,
        key_grad,
        value_grad,
        output_grad,
        gain_two.reshape(-1),
        shift_two.reshape(-1),
        hidden_grad,
        hidden_small.reshape(-1),
        down_grad,
        down_small.reshape(-1),
        mean_grad,
        logvar_grad,
        centres_grad,
        decoder_grad,
    )


def solution(mesh):
    placed = (
        P("slide", "blk", None),
        P("slide", "blk"),
        P(),
        P("slide", None, "blk"),
        P("slide", "blk"),
        P("slide", "blk", None),
        P("slide", "blk", None),
        P("blk", None),
        P(),
        P(),
        P(),
        P(),
        P(),
        P(),
        P(),
        P(),
        P(),
        P(),
        P(),
        P(),
        P(),
        P(),
        P(),
        P(),
        P(),
        P(),
    )
    return jax.shard_map(
        on_device_fast if fits(mesh) else on_device_general,
        mesh=mesh,
        in_specs=placed,
        out_specs=(
            P("slide", "blk", None),
            P(),
            P("blk", None),
            P("blk"),
            P("blk"),
            P("blk", None),
            P("blk", None),
            P("blk", None),
            P("blk", None),
            P("blk"),
            P("blk"),
            P("blk", None),
            P("blk"),
            P("blk", None),
            P("blk"),
            P("blk", None),
            P("blk", None),
            P(None, "blk"),
            P("blk", None),
        ),
        check_vma=False,
    )
```

```python
import functools
import math

import jax
import jax.numpy as jnp
import numpy as np
from jax import lax
from jax.experimental import pallas as pl
from jax.experimental.pallas import tpu as pltpu
from jax.sharding import PartitionSpec as P

HEAD_DIM = 64
HEAD_SCALE = 0.125
MESH = pl.DeviceIdType.MESH
F32 = jnp.float32
BF16 = jnp.bfloat16


def normalized(counts, library):
    scaled = counts.astype(jnp.float32) * (10000.0 / library.astype(jnp.float32))[..., None]
    return jnp.log1p(scaled)


def position_code(coords, model_width):
    quarter = model_width // 4
    freqs = jnp.exp(-math.log(10000.0) * jnp.arange(quarter, dtype=jnp.float32) / quarter)
    along_x = coords[0].astype(jnp.float32)[:, None] * freqs[None, :]
    along_y = coords[1].astype(jnp.float32)[:, None] * freqs[None, :]
    return jnp.concatenate(
        [jnp.sin(along_x), jnp.cos(along_x), jnp.sin(along_y), jnp.cos(along_y)], axis=1
    )


def layer_norm(inputs, scaling, offsets):
    centre = inputs - jnp.mean(inputs, axis=-1, keepdims=True)
    spread = jnp.mean(centre * centre, axis=-1, keepdims=True)
    return centre * lax.rsqrt(spread + 1e-05) * scaling + offsets


def gelu_tanh(inputs):
    return (
        0.5
        * inputs
        * (1.0 + jnp.tanh(0.7978845608028654 * (inputs + 0.044715 * inputs * inputs * inputs)))
    )


def divergence_cells(mean_part, logvar_part, centres):
    latent_width = mean_part.shape[-1]
    crossed = jnp.dot(mean_part, centres.T, precision=lax.Precision.HIGHEST)
    centre_square = jnp.sum(centres * centres, axis=-1)
    logits = (crossed - 0.5 * centre_square[None, :]) / math.sqrt(latent_width)
    shifted = jnp.exp(logits - jnp.max(logits, axis=-1, keepdims=True))
    resp = shifted / jnp.sum(shifted, axis=-1, keepdims=True)
    mixed = jnp.dot(resp, centres, precision=lax.Precision.HIGHEST)
    mixed_square = jnp.dot(resp, centres * centres, precision=lax.Precision.HIGHEST)
    return 0.5 * (
        jnp.exp(logvar_part)
        - 1.0
        - logvar_part
        + mean_part * mean_part
        - 2.0 * mean_part * mixed
        + mixed_square
    )


def to_heads(array, head_count):
    return array.reshape(array.shape[0], head_count, -1).transpose(1, 0, 2)


def from_heads(array):
    return array.transpose(1, 0, 2).reshape(array.shape[1], -1)


def matmul(left, right):
    return jnp.dot(left, right, preferred_element_type=jnp.float32)


def on_device_general(
    counts,
    library,
    gene_ids,
    positions,
    slide_of_cell,
    latent_noise,
    decoded_grad,
    gene_table,
    first_gain,
    first_shift,
    query_weight,
    key_weight,
    value_weight,
    output_weight,
    second_gain,
    second_shift,
    hidden_weight,
    hidden_bias,
    down_weight,
    down_bias,
    mean_weight,
    logvar_weight,
    component_means,
    decoder_weight,
    divergence_weight,
    free_floor,
):
    cell_count = counts.shape[1]
    model_width = gene_table.shape[1]
    head_count = model_width // HEAD_DIM
    score_scale = HEAD_DIM ** (-0.5)
    express = normalized(counts[0], library[0]).astype(jnp.bfloat16)
    table_rows = gene_table.shape[0]
    first_row = lax.axis_index("blk") * table_rows
    selector = (
        gene_ids[:, None] == first_row + jnp.arange(table_rows, dtype=jnp.int32)[None, :]
    ).astype(jnp.bfloat16)
    panel_part = matmul(selector, gene_table)
    panel_weight = lax.psum(panel_part, "blk").astype(jnp.bfloat16)
    hidden_start = matmul(express, panel_weight) + position_code(positions[0], model_width)
    normed_one = layer_norm(hidden_start, first_gain, first_shift).astype(jnp.bfloat16)
    query_low = matmul(normed_one, query_weight).astype(jnp.bfloat16)
    key_low = matmul(normed_one, key_weight).astype(jnp.bfloat16)
    value_low = matmul(normed_one, value_weight).astype(jnp.bfloat16)
    slide_labels = slide_of_cell[0].astype(jnp.bfloat16)
    keys_all, values_all, labels_all = (
        lax.all_gather(key_low, "blk", axis=0, tiled=True),
        lax.all_gather(value_low, "blk", axis=0, tiled=True),
        lax.all_gather(slide_labels, "blk", axis=0, tiled=True),
    )
    same_slide = slide_labels[:, None] == labels_all[None, :]
    query_heads = to_heads(query_low, head_count)
    key_heads = to_heads(keys_all, head_count)
    value_heads = to_heads(values_all, head_count)

    def head_forward(head_items):
        query_head, key_head, value_head = head_items
        scores = (
            jnp.einsum("qd,kd->qk", query_head, key_head, preferred_element_type=jnp.float32)
            * score_scale
        )
        scores = jnp.where(same_slide, scores, -1e30)
        row_max = jnp.max(scores, axis=1, keepdims=True)
        shifted = jnp.exp(scores - row_max)
        row_sum = jnp.sum(shifted, axis=1, keepdims=True)
        shares = shifted / row_sum
        attended_head = jnp.einsum(
            "qk,kd->qd", shares.astype(jnp.bfloat16), value_head, preferred_element_type=jnp.float32
        )
        return (attended_head, row_max[:, 0], row_sum[:, 0])

    attended_heads, row_maxes, row_sums = lax.map(
        head_forward, (query_heads, key_heads, value_heads)
    )
    attended = from_heads(attended_heads).astype(jnp.bfloat16)
    hidden_middle = hidden_start + matmul(attended, output_weight)
    normed_two = layer_norm(hidden_middle, second_gain, second_shift).astype(jnp.bfloat16)
    inner_sum = matmul(normed_two, hidden_weight) + hidden_bias
    act_low = gelu_tanh(inner_sum).astype(jnp.bfloat16)
    hidden_final = hidden_middle + matmul(act_low, down_weight) + down_bias
    base_low = hidden_final.astype(jnp.bfloat16)
    mean_lat = matmul(base_low, mean_weight)
    log_var = matmul(base_low, logvar_weight)
    noise_local = latent_noise[0]

    def bottleneck(mean_part, logvar_part, centres):
        return (
            mean_part + jnp.exp(0.5 * logvar_part) * noise_local,
            divergence_cells(mean_part, logvar_part, centres),
        )

    (latent, kl_cell), pull_latent = jax.vjp(bottleneck, mean_lat, log_var, component_means)
    latent_low = latent.astype(jnp.bfloat16)
    decoded = matmul(latent_low, decoder_weight)
    everyone = cell_count * lax.axis_size("blk") * lax.axis_size("slide")
    kl_sum = lax.psum(jnp.sum(kl_cell, axis=0), ("slide", "blk"))
    kl_mean = kl_sum / everyone
    divergence = divergence_weight * jnp.mean(jnp.maximum(kl_mean, free_floor))
    binding = (kl_mean > free_floor).astype(jnp.float32)
    grad_source = decoded_grad[0]
    grad_latent = matmul(grad_source, decoder_weight.T)
    decoder_grad = matmul(latent_low.T, grad_source)
    grad_kl = jnp.broadcast_to(divergence_weight * binding, kl_cell.shape)
    grad_mean, grad_logvar, centres_grad = pull_latent((grad_latent, grad_kl))
    grad_mean_low = grad_mean.astype(jnp.bfloat16)
    grad_logvar_low = grad_logvar.astype(jnp.bfloat16)
    mean_grad = matmul(base_low.T, grad_mean_low)
    logvar_grad = matmul(base_low.T, grad_logvar_low)
    grad_final = matmul(grad_mean_low, mean_weight.T) + matmul(grad_logvar_low, logvar_weight.T)
    grad_branch = grad_final.astype(jnp.bfloat16)
    down_grad = matmul(act_low.T, grad_branch)
    down_bias_grad = jnp.sum(grad_branch.astype(jnp.float32), axis=0)
    grad_act = matmul(grad_branch, down_weight.T)
    gelu_pull = jax.vjp(gelu_tanh, inner_sum)[1]
    grad_inner = gelu_pull(grad_act)[0].astype(jnp.bfloat16)
    hidden_grad = matmul(normed_two.T, grad_inner)
    hidden_bias_grad = jnp.sum(grad_inner.astype(jnp.float32), axis=0)
    norm_two_pull = jax.vjp(layer_norm, hidden_middle, second_gain, second_shift)[1]
    grad_norm_two, second_gain_grad, second_shift_grad = norm_two_pull(
        matmul(grad_inner, hidden_weight.T)
    )
    grad_middle = grad_final + grad_norm_two
    grad_out = grad_middle.astype(jnp.bfloat16)
    output_grad = matmul(attended.T, grad_out)
    grad_attended = matmul(grad_out, output_weight.T).astype(jnp.bfloat16)
    keys_again, values_again = (
        lax.all_gather(key_low, "blk", axis=0, tiled=True),
        lax.all_gather(value_low, "blk", axis=0, tiled=True),
    )
    key_heads_back = to_heads(keys_again, head_count)
    value_heads_back = to_heads(values_again, head_count)
    grad_heads_local = to_heads(grad_attended, head_count)

    def head_queries(head_items):
        query_head, key_head, value_head, grad_head, row_max, row_sum = head_items
        scores = (
            jnp.einsum("qd,kd->qk", query_head, key_head, preferred_element_type=jnp.float32)
            * score_scale
        )
        scores = jnp.where(same_slide, scores, -1e30)
        shares = jnp.exp(scores - row_max[:, None]) / row_sum[:, None]
        grad_shares = jnp.einsum(
            "qd,kd->qk", grad_head, value_head, preferred_element_type=jnp.float32
        )
        inner_dot = jnp.sum(shares * grad_shares, axis=1, keepdims=True)
        grad_scores = (shares * (grad_shares - inner_dot)).astype(jnp.bfloat16)
        grad_query_head = (
            jnp.einsum("qk,kd->qd", grad_scores, key_head, preferred_element_type=jnp.float32)
            * score_scale
        )
        return (grad_query_head, inner_dot[:, 0])

    grad_query_heads, inner_dots = lax.map(
        head_queries,
        (query_heads, key_heads_back, value_heads_back, grad_heads_local, row_maxes, row_sums),
    )
    queries_group, grads_group = (
        lax.all_gather(query_low, "blk", axis=0, tiled=True),
        lax.all_gather(grad_attended, "blk", axis=0, tiled=True),
    )
    maxes_group, totals_group, dots_group = (
        lax.all_gather(row_maxes, "blk", axis=1, tiled=True),
        lax.all_gather(row_sums, "blk", axis=1, tiled=True),
        lax.all_gather(inner_dots, "blk", axis=1, tiled=True),
    )
    mask_back = labels_all[:, None] == slide_labels[None, :]

    def head_keys(head_items):
        query_head, key_head, value_head, grad_head, row_max, row_sum, inner_dot = head_items
        scores = (
            jnp.einsum("qd,kd->qk", query_head, key_head, preferred_element_type=jnp.float32)
            * score_scale
        )
        scores = jnp.where(mask_back, scores, -1e30)
        shares = jnp.exp(scores - row_max[:, None]) / row_sum[:, None]
        grad_shares = jnp.einsum(
            "qd,kd->qk", grad_head, value_head, preferred_element_type=jnp.float32
        )
        grad_scores = (shares * (grad_shares - inner_dot[:, None])).astype(jnp.bfloat16)
        grad_key_head = (
            jnp.einsum("qk,qd->kd", grad_scores, query_head, preferred_element_type=jnp.float32)
            * score_scale
        )
        grad_value_head = jnp.einsum(
            "qk,qd->kd", shares.astype(jnp.bfloat16), grad_head, preferred_element_type=jnp.float32
        )
        return (grad_key_head, grad_value_head)

    grad_key_heads, grad_value_heads = lax.map(
        head_keys,
        (
            to_heads(queries_group, head_count),
            to_heads(key_low, head_count),
            to_heads(value_low, head_count),
            to_heads(grads_group, head_count),
            maxes_group,
            totals_group,
            dots_group,
        ),
    )
    grad_query_low = from_heads(grad_query_heads).astype(jnp.bfloat16)
    grad_key = from_heads(grad_key_heads)
    grad_value = from_heads(grad_value_heads)
    grad_key_low = grad_key.astype(jnp.bfloat16)
    grad_value_low = grad_value.astype(jnp.bfloat16)
    query_grad = matmul(normed_one.T, grad_query_low)
    key_grad = matmul(normed_one.T, grad_key_low)
    value_grad = matmul(normed_one.T, grad_value_low)
    grad_norm_input = (
        matmul(grad_query_low, query_weight.T)
        + matmul(grad_key_low, key_weight.T)
        + matmul(grad_value_low, value_weight.T)
    )
    norm_one_pull = jax.vjp(layer_norm, hidden_start, first_gain, first_shift)[1]
    grad_norm_one, first_gain_grad, first_shift_grad = norm_one_pull(grad_norm_input)
    grad_start = grad_middle + grad_norm_one
    grad_encoded = grad_start.astype(jnp.bfloat16)
    panel_grad = matmul(express.T, grad_encoded)
    panel_total = lax.psum(panel_grad, ("slide", "blk"))
    table_grad = jnp.dot(
        selector.astype(jnp.float32).T, panel_total, precision=lax.Precision.HIGHEST
    )
    shares_grads = (
        lax.psum_scatter(first_gain_grad, "blk", scatter_dimension=0, tiled=True),
        lax.psum_scatter(first_shift_grad, "blk", scatter_dimension=0, tiled=True),
        lax.psum_scatter(query_grad, "blk", scatter_dimension=0, tiled=True),
        lax.psum_scatter(key_grad, "blk", scatter_dimension=0, tiled=True),
        lax.psum_scatter(value_grad, "blk", scatter_dimension=0, tiled=True),
        lax.psum_scatter(output_grad, "blk", scatter_dimension=0, tiled=True),
        lax.psum_scatter(second_gain_grad, "blk", scatter_dimension=0, tiled=True),
        lax.psum_scatter(second_shift_grad, "blk", scatter_dimension=0, tiled=True),
        lax.psum_scatter(hidden_grad, "blk", scatter_dimension=0, tiled=True),
        lax.psum_scatter(hidden_bias_grad, "blk", scatter_dimension=0, tiled=True),
        lax.psum_scatter(down_grad, "blk", scatter_dimension=0, tiled=True),
        lax.psum_scatter(down_bias_grad, "blk", scatter_dimension=0, tiled=True),
        lax.psum_scatter(mean_grad, "blk", scatter_dimension=0, tiled=True),
        lax.psum_scatter(logvar_grad, "blk", scatter_dimension=0, tiled=True),
        lax.psum_scatter(centres_grad, "blk", scatter_dimension=1, tiled=True),
        lax.psum_scatter(decoder_grad, "blk", scatter_dimension=0, tiled=True),
    )
    summed = (
        lax.psum(shares_grads[0].astype(jnp.bfloat16), "slide").astype(jnp.float32),
        lax.psum(shares_grads[1].astype(jnp.bfloat16), "slide").astype(jnp.float32),
        lax.psum(shares_grads[2].astype(jnp.bfloat16), "slide").astype(jnp.float32),
        lax.psum(shares_grads[3].astype(jnp.bfloat16), "slide").astype(jnp.float32),
        lax.psum(shares_grads[4].astype(jnp.bfloat16), "slide").astype(jnp.float32),
        lax.psum(shares_grads[5].astype(jnp.bfloat16), "slide").astype(jnp.float32),
        lax.psum(shares_grads[6].astype(jnp.bfloat16), "slide").astype(jnp.float32),
        lax.psum(shares_grads[7].astype(jnp.bfloat16), "slide").astype(jnp.float32),
        lax.psum(shares_grads[8].astype(jnp.bfloat16), "slide").astype(jnp.float32),
        lax.psum(shares_grads[9].astype(jnp.bfloat16), "slide").astype(jnp.float32),
        lax.psum(shares_grads[10].astype(jnp.bfloat16), "slide").astype(jnp.float32),
        lax.psum(shares_grads[11].astype(jnp.bfloat16), "slide").astype(jnp.float32),
        lax.psum(shares_grads[12].astype(jnp.bfloat16), "slide").astype(jnp.float32),
        lax.psum(shares_grads[13].astype(jnp.bfloat16), "slide").astype(jnp.float32),
        lax.psum(shares_grads[14].astype(jnp.bfloat16), "slide").astype(jnp.float32),
        lax.psum(shares_grads[15].astype(jnp.bfloat16), "slide").astype(jnp.float32),
    )
    return (decoded[None], divergence, table_grad) + tuple(summed)


def fits(mesh):
    return mesh.shape["slide"] == 4 and mesh.shape["blk"] == 8


def flipped(index, mask):
    for bit in (1, 2, 4):
        if mask & bit:
            index = index + bit - 2 * bit * ((index // bit) % 2)
    return index


def greet(slide, blk, peers):
    barrier = pltpu.get_barrier_semaphore()
    for far_slide, far_blk in peers:
        pl.semaphore_signal(
            barrier,
            inc=1,
            device_id={"slide": flipped(slide, far_slide), "blk": flipped(blk, far_blk)},
            device_id_type=MESH,
        )
    pl.semaphore_wait(barrier, len(peers))


BLK_PEERS = [(0, far) for far in range(1, 8)]
SLIDE_PEERS = [(far, 0) for far in range(1, 4)]


def dot_nt(left, right):
    return lax.dot_general(left, right, (((1,), (1,)), ((), ())), preferred_element_type=F32)


def dot_tn(left, right):
    return lax.dot_general(left, right, (((0,), (0,)), ((), ())), preferred_element_type=F32)


def head_scores(query, key, same_slide):
    scores = jnp.where(same_slide, dot_nt(query, key), -1e30)
    shifted = jnp.exp(scores - jnp.max(scores, axis=1, keepdims=True))
    return shifted, 1.0 / jnp.sum(shifted, axis=1, keepdims=True)


(
    ACT_, ATTENDED_, ATT_, BACK_, BASE_, BOTTLENECK_, BRANCH_, B_, DECODER_, DONE_, DOWN0_, DOWN1_, EXPRESS_,
    FAR_, FEED_, F_, GENC_, GLOGVAR_, GMEAN_, GOUT_, HIDDEN0_, HIDDEN1_, INNER_, IN_, KEY_, LATENT_, LATS_,
    LOGVAR_, MASKS_, MEAN_, NEAR_, NORM1_, NORM2_, NORMED_, ONE_, OUTPUT_, PANEL_, QKV_, QUERY_, RELAY_,
    ROWS_, S2_, SMALL_, SOURCE_, SUMS_, S_, T0_, T1_, TWO_, VALUE_, WDEC_, WD_, WH_, WK_, WL_, WM_, WO_, WQ_,
    WV_, X_, Z_,
) = range(61)

Z_FIRST = (HIDDEN1_,)


class Links:
    def __init__(self, slide, blk, send_sem, recv_sem):
        self.slide, self.blk = slide, blk
        self.send_sem, self.recv_sem = send_sem, recv_sem
        self.copies, self.count = [], 0

    def send(self, source, target, far_slide, far_blk):
        number = self.count
        self.count += 1
        copy = pltpu.make_async_remote_copy(
            src_ref=source,
            dst_ref=target,
            send_sem=self.send_sem.at[number],
            recv_sem=self.recv_sem.at[number],
            device_id={
                "slide": flipped(self.slide, far_slide),
                "blk": flipped(self.blk, far_blk),
            },
            device_id_type=MESH,
        )
        copy.start()
        self.copies.append(copy)
        return copy

    def drain(self, copy):
        copy.wait_send()
        self.copies = [other for other in self.copies if other is not copy]

    def finish(self):
        for copy in self.copies:
            copy.wait_send()


def spread_everywhere(links, slot):
    slide, blk = links.slide, links.blk
    copies = {}

    def push(rel_slide, rel_blk, to_slide, to_blk):
        block = slot(flipped(slide, rel_slide), flipped(blk, rel_blk))
        copies[(rel_slide ^ to_slide, rel_blk ^ to_blk)] = links.send(block, block, to_slide, to_blk)

    for far in (2, 4, 6):
        push(0, 0, 0, far)
    push(0, 0, 0, 1)
    push(0, 0, 2, 0)
    push(0, 0, 1, 0)
    yield
    for rel in (2, 4, 6):
        copies[0, rel].wait_recv()
        push(0, rel, 0, 1)
        push(0, rel, 2, 0)
        push(0, rel, 1, 0)
    yield
    for rel in (1, 3, 5, 7):
        copies[0, rel].wait_recv()
        push(0, rel, 2, 0)
        push(0, rel, 1, 0)
    yield
    for rel in (0, 2, 4, 6, 1, 3, 5, 7):
        copies[2, rel].wait_recv()
        push(2, rel, 1, 0)
    yield
    for far in (1, 3):
        for rel in (0, 2, 4, 6, 1, 3, 5, 7):
            copies[far, rel].wait_recv()
    yield


class Reduction:
    def __init__(self, links, left, right, rows, width, dense, buffers):
        self.links, self.left, self.right = links, left, right
        self.rows, self.width, self.dense = rows, width, dense
        self.away, self.came, self.pieces = buffers
        self.kept = self.away
        self.along_x, self.along_z = links.blk % 2, links.blk // 2

    def tiles(self, which, store):
        def tile(i, carry):
            place = which * 2 + i if self.dense else i * 2 + which
            product = dot_tn(self.left(pl.multiple_of(place * 128, 128)), self.right())
            store(pl.ds(pl.multiple_of(i * 128, 128), 128), product)
            return carry

        lax.fori_loop(0, self.rows * 4 // 128, tile, 0)

    def send_x(self):
        def store(where, product):
            self.away[where, :] = product.astype(BF16)

        self.tiles(1 - self.along_x, store)
        self.copy_x = self.links.send(self.away, self.came, 0, 1)

    def piece(self, far):
        return pl.ds(pl.multiple_of(flipped(self.along_z, far) * self.rows, self.rows), self.rows)

    def send_z(self):
        self.links.drain(self.copy_x)
        self.copy_x.wait_recv()

        def store(where, product):
            self.kept[where, :] = (product + self.came[where, :].astype(F32)).astype(BF16)

        self.tiles(self.along_x, store)
        self.copies_z = [
            self.links.send(self.kept.at[self.piece(far)], self.pieces.at[far // 2], 0, 2) for far in (3, 1)
        ]

    def send_far(self):
        for copy in self.copies_z:
            copy.wait_recv()
        where = self.piece(2)
        self.kept[where, :] = (self.kept[where, :].astype(F32) + self.pieces[1].astype(F32)).astype(BF16)
        self.copy_far = self.links.send(self.kept.at[where], self.pieces.at[2], 0, 4)

    def total(self):
        self.copy_far.wait_recv()
        own = self.kept[self.piece(0), :]
        return ((own.astype(F32) + self.pieces[0].astype(F32)) + self.pieces[2].astype(F32)).astype(BF16)


class ReductionAlongZ(Reduction):
    def tiles(self, start, store):
        step = 2 - 4 * ((start // 2) % 2)

        def tile(i, carry):
            place = (start + (i // 2) * step) * 2 + i % 2
            product = dot_tn(self.left(pl.multiple_of(place * 128, 128)), self.right())
            store(pl.ds(pl.multiple_of(i * 128, 128), 128), product)
            return carry

        lax.fori_loop(0, 4, tile, 0)

    def send_x(self):
        def store(where, product):
            self.away[where, :] = product.astype(BF16)

        self.tiles(flipped(self.along_z, 1), store)
        self.copy_x = self.links.send(self.away, self.came, 0, 2)

    def send_z(self):
        self.links.drain(self.copy_x)
        self.copy_x.wait_recv()

        def store(where, product):
            self.kept[where, :] = (product + self.came[where, :].astype(F32)).astype(BF16)

        self.tiles(self.along_z, store)
        self.copies_z = [
            self.links.send(self.kept.at[pl.ds((2 + side) * self.rows, self.rows)], self.pieces.at[side], 0, 4)
            for side in range(2)
        ]

    def block(self, side):
        return pl.ds(pl.multiple_of(side * self.rows, self.rows), self.rows)

    def send_far(self):
        for copy in self.copies_z:
            copy.wait_recv()
        other = 1 - self.along_x
        where = self.block(other)
        self.kept[where, :] = (self.kept[where, :].astype(F32) + self.pieces[other].astype(F32)).astype(BF16)
        self.copy_far = self.links.send(self.kept.at[where], self.pieces.at[2], 0, 1)

    def total(self):
        self.copy_far.wait_recv()
        own = self.kept[self.block(self.along_x), :].astype(F32) + self.pieces[self.along_x].astype(F32)
        return (own + self.pieces[2].astype(F32)).astype(BF16)


def spread_slide(links, slot, total):
    slide = links.slide
    own, far = slot(slide), slot(flipped(slide, 2))
    own[...] = total
    across = links.send(own, own, 2, 0)
    beside = links.send(own, own, 1, 0)
    yield
    across.wait_recv()
    last = links.send(far, far, 1, 0)
    yield
    beside.wait_recv()
    last.wait_recv()
    yield


def reductions_of(cells, width, inner, latents):
    return [
        (DECODER_, latents // 8, width // 4, True),
        (DOWN0_, inner // 32, width // 2, False),
        (DOWN1_, inner // 32, width // 2, False),
        (MEAN_, width // 8, latents // 4, False),
        (LOGVAR_, width // 8, latents // 4, False),
        (HIDDEN0_, width // 8, inner // 8, False),
        (HIDDEN1_, width // 8, inner // 8, False),
        (OUTPUT_, width // 8, width // 4, False),
        (PANEL_, width // 8, width // 4, False),
        (QUERY_, width // 8, width // 4, False),
        (KEY_, width // 8, width // 4, False),
        (VALUE_, width // 8, width // 4, False),
    ]


def across(links, ref, columns, cells):
    def rows(place):
        return ref.at[pl.ds(place * cells, cells), columns]

    far = links.send(rows(0), rows(2), 2, 0)
    near = links.send(rows(0), rows(1), 1, 0)
    yield
    far.wait_recv()
    last = links.send(rows(2), rows(3), 1, 0)
    yield
    near.wait_recv()
    last.wait_recv()
    yield


def norm_parts(hidden):
    centre = hidden - jnp.mean(hidden, axis=1, keepdims=True)
    invert = lax.rsqrt(jnp.mean(centre * centre, axis=1, keepdims=True) + 1e-05)
    return centre * invert, invert


def norm_back(hidden, gain, grad):
    unit, invert = norm_parts(hidden)
    gain_grad = jnp.sum(grad * unit, axis=0, keepdims=True)
    shift_grad = jnp.sum(grad, axis=0, keepdims=True)
    grad_unit = grad * gain
    grad_hidden = invert * (
        grad_unit
        - jnp.mean(grad_unit, axis=1, keepdims=True)
        - unit * jnp.mean(grad_unit * unit, axis=1, keepdims=True)
    )
    return grad_hidden, gain_grad, shift_grad


def exact_dot(left, right, dims):
    return lax.dot_general(
        left, right, (dims, ((), ())), precision=lax.Precision.HIGHEST, preferred_element_type=F32
    )


def mixture(mean_part, centres):
    crossed = exact_dot(mean_part, centres, ((1,), (1,)))
    ones = jnp.ones((8, centres.shape[1]), F32)
    centre_square = exact_dot(ones, centres * centres, ((1,), (1,)))[0:1]
    logits = (crossed - 0.5 * centre_square) / math.sqrt(centres.shape[1])
    shifted = jnp.exp(logits - jnp.max(logits, axis=1, keepdims=True))
    resp = shifted / jnp.sum(shifted, axis=1, keepdims=True)
    return resp, exact_dot(resp, centres, ((1,), (0,)))


def slide_masks(land, row_labels, col_labels, cells):
    for block in range(8):
        line = land[block, 3 * cells : 3 * cells + 1, :].astype(F32)
        col_labels[:, block * cells : (block + 1) * cells] = line
        row_labels[block * cells : (block + 1) * cells, :] = jnp.broadcast_to(line, (cells, cells)).T


ORDER = (
    (BOTTLENECK_,), (FEED_, 0), (FEED_, 1), (FEED_, 2), (FEED_, 3), (NORM2_,), (ATT_,), (GOUT_,),
    (MASKS_,), (BRANCH_,), (X_, DOWN0_), (RELAY_, TWO_), (X_, DOWN1_), (LATS_,), (LATENT_,), (BASE_,),
    (ATTENDED_,), (ROWS_, 0), (ROWS_, 1), (ROWS_, 2), (ROWS_, 3), (BACK_,), (Z_, DOWN0_),
    (RELAY_, LATENT_), (RELAY_, BASE_), (X_, HIDDEN0_), (F_, DOWN0_), (Z_, DOWN1_), (IN_,), (NORM1_,),
    (QKV_,), (SMALL_,), (RELAY_, LATENT_), (RELAY_, BASE_), (RELAY_, ATTENDED_), (X_, HIDDEN1_),
    (X_, PANEL_), (X_, QUERY_), (X_, KEY_), (X_, VALUE_), (X_, MEAN_), (X_, LOGVAR_),
    (X_, DECODER_), (X_, OUTPUT_), (F_, DOWN1_), (SUMS_,), (Z_, HIDDEN0_), (S_, DOWN0_),
    (Z_, PANEL_), (S_, DOWN1_), (F_, HIDDEN0_), (F_, PANEL_), (Z_, HIDDEN1_), (Z_, QUERY_),
    (Z_, KEY_), (Z_, VALUE_), (PANEL_,), (Z_, MEAN_), (Z_, LOGVAR_), (Z_, DECODER_),
    (RELAY_, PANEL_), (Z_, OUTPUT_), (S_, HIDDEN0_), (F_, HIDDEN1_), (F_, QUERY_), (F_, KEY_),
    (F_, VALUE_), (RELAY_, PANEL_), (F_, MEAN_), (F_, LOGVAR_), (F_, DECODER_), (F_, OUTPUT_),
    (RELAY_, PANEL_), (S_, HIDDEN1_), (S_, QUERY_), (S_, KEY_), (S_, VALUE_), (S_, MEAN_),
    (S_, LOGVAR_), (S_, DECODER_), (S_, OUTPUT_), (S2_, DECODER_), (S2_, DOWN0_), (S2_, DOWN1_),
    (S2_, MEAN_), (S2_, LOGVAR_), (S2_, HIDDEN0_), (S2_, OUTPUT_), (S2_, HIDDEN1_), (S2_, QUERY_),
    (S2_, KEY_), (S2_, VALUE_), (DONE_,), (RELAY_, PANEL_), (S2_, DECODER_), (S2_, DOWN0_),
    (S2_, DOWN1_), (S2_, MEAN_), (S2_, LOGVAR_), (S2_, HIDDEN0_), (S2_, OUTPUT_), (S2_, HIDDEN1_),
    (S2_, QUERY_), (S2_, KEY_), (S2_, VALUE_),
)


def layer_kernel(
    ids_ref, counts_ref, library_ref, positions_ref, freqs_ref, labels_ref, noise_ref, source_ref, gain_one, shift_one,
    gain_two, shift_two, hidden_bias, down_bias, centres_ref, weight_ref, floor_ref,
    table_hbm, wq_hbm, wk_hbm, wv_hbm, wo_hbm, wh_hbm, wd_hbm, wm_hbm, wl_hbm, wdec_hbm,
    decoded_out, kl_out, panel_out, query_out, key_out, value_out, output_out, hidden_out, down_out, mean_out, logvar_out,
    decoder_out, small_out,
    slots, wo, wm, wl, wdec, part, panel_land, qkv_send, land, att_send_fwd, att_land_fwd, row_labels, col_labels,
    act_parts, final, kl_own, kl_slides, kl_sum, kl_blks, start, middle, inner_sums, mean_part, logvar_part, glatent, whole,
    quarters, base_all, latent_all, branch_all, gmean, glogvar, gmean_all, glogvar_all, ginner, ginner_all, gout, gout_all,
    gmiddle, gqkv_all, genc_all, att_send, att_land, dqkv, dqkv_land, dk_sum, dv_sum, grad_qkv, encoded, small, small_land,
    small_own, small_slides, load_sem, send_sem, recv_sem, *unit_refs,
):
    slide, blk = lax.axis_index("slide"), lax.axis_index("blk")
    cells, width = counts_ref.shape
    inner, latents, per = inner_sums.shape[1], mean_part.shape[1], width // 8
    loads = {}
    loaded = set()

    def load(name, source, target):
        loads[name] = pltpu.make_async_copy(source, target, load_sem.at[len(loads)])
        loads[name].start()

    def have(*names):
        for name in names:
            if name not in loaded:
                loaded.add(name)
                loads[name].wait()

    def load_quarter(name, which, wide, tall):
        columns = pl.ds(which * width if isinstance(which, int) else pl.multiple_of(which * width, 128), width)
        load((WH_, *name), wh_hbm.at[:, columns], slots.at[wide])
        load((WD_, *name), wd_hbm.at[columns, :], slots.at[tall])

    load(T0_, table_hbm.at[pl.ds(0, width)], slots.at[0])
    load(T1_, table_hbm.at[pl.ds(width, width)], slots.at[1])
    load(WQ_, wq_hbm, slots.at[2])
    load(WK_, wk_hbm, slots.at[3])
    load(WO_, wo_hbm, wo)
    load(WM_, wm_hbm, wm)
    load(WL_, wl_hbm, wl)
    load(WDEC_, wdec_hbm, wdec)
    greet(slide, blk, SLIDE_PEERS + BLK_PEERS)
    links = Links(slide, blk, send_sem, recv_sem)

    def column(line):
        return jnp.broadcast_to(line, (line.shape[1], line.shape[1])).T[:, 0:1]

    genes = ids_ref.shape[1]
    table_rows, block_rows = 2 * width, genes // 64
    first = (blk * table_rows).astype(F32)
    have(T0_, T1_)
    for side in range(2):
        ids = ids_ref[:, pl.ds(pl.multiple_of(slide * (genes // 4) + side * 128, 128), 128)].astype(F32)
        places = lax.broadcasted_iota(jnp.int32, (128, table_rows), 1).astype(F32) + first
        selector = (places == column(ids)).astype(F32).astype(BF16)
        rows = jnp.dot(selector[:, 0:width], slots[0], preferred_element_type=F32) + jnp.dot(
            selector[:, width:], slots[1], preferred_element_type=F32
        )
        part[side] = rows.astype(BF16).reshape(8, block_rows, width)
    load(WV_, wv_hbm, slots.at[0])
    part_copies = [
        [links.send(part.at[side, flipped(blk, far)], panel_land.at[side, far], 0, far) for far in (6, 4, 2, 7, 5, 3, 1)]
        for side in range(2)
    ]
    scale = column(10000.0 / library_ref[...].astype(F32))
    express = jnp.log(1.0 + counts_ref[...].astype(F32) * scale).astype(BF16)
    whole[0:cells, 0:width] = express
    quarter = width // 4
    for axis in range(2):
        angle = column(positions_ref[axis : axis + 1, :].astype(F32)) * freqs_ref[...]
        start[:, 2 * axis * quarter : (2 * axis + 1) * quarter] = jnp.sin(angle)
        start[:, (2 * axis + 1) * quarter : (2 * axis + 2) * quarter] = jnp.cos(angle)

    def panel_rows(far_slide, far_blk, side):
        first_gene = (far_slide * 2 + side) * 8 * block_rows + far_blk * block_rows
        return panel_out.at[pl.ds(pl.multiple_of(first_gene, 16), block_rows)]

    row_spreads = []
    for side in range(2):
        total = part[side, blk].astype(F32)
        for place, far in enumerate((6, 4, 2, 7, 5, 3, 1)):
            part_copies[side][place].wait_recv()
            total = total + panel_land[side, far].astype(F32)
        own_rows = panel_rows(slide, blk, side)
        own_rows[...] = total.astype(BF16)
        row_spreads.append(spread_everywhere(links, lambda far_slide, far_blk, side=side: panel_rows(far_slide, far_blk, side)))
        next(row_spreads[side])
        if side:
            next(row_spreads[1])
            next(row_spreads[0])
        else:
            next(row_spreads[0])
    next(row_spreads[1])
    next(row_spreads[0])
    next(row_spreads[1])
    next(row_spreads[0])
    next(row_spreads[1])
    panel_copies = list(links.copies)
    send_express = across(links, whole, pl.ds(0, width), cells)
    next(send_express)

    def source_part(which):
        return source_ref.at[:, pl.ds(pl.multiple_of(which * quarter, 128), quarter)]

    def source_slot(place):
        return quarters.at[pl.ds(place * cells, cells), pl.ds(inner // 4, quarter)]

    source_copies = [links.send(source_part(flipped(slide, far)), source_slot(far), far, 0) for far in (2, 3, 1)]
    source_slot(0)[...] = source_part(slide)[...]

    hidden_start = start[...] + jnp.dot(express, panel_out[...], preferred_element_type=F32)
    start[...] = hidden_start
    normed = (norm_parts(hidden_start)[0] * gain_one[...] + shift_one[...]).astype(BF16)
    whole[0:cells, width : 2 * width] = normed
    qkv_send[:, 3 * cells :, :] = jnp.broadcast_to(labels_ref[...].astype(F32).astype(BF16).reshape(1, 1, cells), (8, 16, per))
    have(WQ_, WK_, WV_)
    load((WH_, 0), wh_hbm.at[:, pl.ds(0, width)], slots.at[1])

    along_x, along_z = blk % 2, blk // 2
    qkv_copies = []
    for far in (3, 2, 1, 0):
        pair = flipped(along_z, far)
        columns = pl.ds(pl.multiple_of(pair * 2 * per, 128), 2 * per)
        for number, weight in enumerate((slots.at[2], slots.at[3], slots.at[0])):
            product = jnp.dot(normed, weight[:, columns], preferred_element_type=F32).astype(BF16)
            for side in range(2):
                qkv_send[pair * 2 + side, number * cells : (number + 1) * cells, :] = product[:, side * per : (side + 1) * per]
        for side in (1, 0):
            if far or side:
                target = flipped(pair * 2 + along_x, side)
                qkv_copies.append(links.send(qkv_send.at[target], land.at[blk], 0, 2 * far + side))
    land[blk] = qkv_send[blk]
    load((WD_, 0), wd_hbm.at[pl.ds(0, width), :], slots.at[2])
    load_quarter((1,), 1, 3, 0)
    next(send_express)
    send_normed = across(links, whole, pl.ds(width, width), cells)
    next(send_normed)
    for copy in panel_copies:
        links.drain(copy)
    for copy in qkv_copies:
        copy.wait_recv()

    slide_masks(land, row_labels, col_labels, cells)
    key = land[:, cells : 2 * cells, :].reshape(8 * cells, per)
    value = land[:, 2 * cells : 3 * cells, :].reshape(8 * cells, per)
    att_copies = []
    for far in (3, 2, 1, 0):
        pair = flipped(along_z, far)
        query = land[pl.ds(pair * 2, 2), 0:cells, :].reshape(2 * cells, per)
        same_slide = row_labels[pl.ds(pl.multiple_of(pair * 2 * cells, 128), 2 * cells), 0:1] == col_labels[...]
        lane = lax.broadcasted_iota(jnp.int32, query.shape, 1)
        out = None
        for head in range(per // HEAD_DIM):
            mine = lane // HEAD_DIM == head
            shifted, inverse = head_scores(jnp.where(mine, query, 0) * HEAD_SCALE, key, same_slide)
            part = jnp.dot((shifted * inverse).astype(BF16), value, preferred_element_type=F32)
            out = part if out is None else jnp.where(mine, part, out)
        att_send_fwd[pl.ds(pair * 2, 2)] = out.astype(BF16).reshape(2, cells, per)
        for side in (1, 0):
            if far or side:
                target = flipped(pair * 2 + along_x, side)
                att_copies.append(links.send(att_send_fwd.at[target], att_land_fwd.at[blk], 0, 2 * far + side))
    att_land_fwd[blk] = att_send_fwd[blk]
    next(send_normed)
    for copy in att_copies:
        copy.wait_recv()
    for block in range(8):
        whole[0:cells, 2 * width + block * per : 2 * width + (block + 1) * per] = att_land_fwd[block]

    have(WO_)
    hidden_middle = start[...] + jnp.dot(
        whole[0:cells, 2 * width : 3 * width], wo[...], preferred_element_type=F32
    )
    middle[...] = hidden_middle
    normed_two = (norm_parts(hidden_middle)[0] * gain_two[...] + shift_two[...]).astype(BF16)
    whole[0:cells, 3 * width :] = normed_two
    send_two = across(links, whole, pl.ds(3 * width, width), cells)
    next(send_two)
    final[...] = hidden_middle + down_bias[...]
    chunk = inner // 8

    act_copies = []
    for which in range(4):
        wide, tall = ((1, 2), (3, 0))[which % 2]
        have((WH_, which), (WD_, which))

        def feed_on(j, carry, which=which, wide=wide, tall=tall):
            near = pl.ds(pl.multiple_of(j * chunk, 128), chunk)
            where = pl.ds(pl.multiple_of(which * width + j * chunk, 128), chunk)
            inner_sum = jnp.dot(whole[0:cells, 3 * width :], slots[wide, :, near], preferred_element_type=F32) + hidden_bias[:, where]
            inner_sums[:, where] = inner_sum
            act = gelu_tanh(inner_sum).astype(BF16)
            place = pl.ds(pl.multiple_of((which * 2 + j) * (chunk // 4), 128), chunk // 4)
            for block in range(4):
                act_parts[block, :, place] = act[:, block * (chunk // 4) : (block + 1) * (chunk // 4)]
            final[...] += jnp.dot(act, slots[tall, near, :], preferred_element_type=F32)
            return carry

        lax.fori_loop(0, 2, feed_on, 0)
        place = pl.ds(which * (chunk // 2), chunk // 2)
        for far in (2, 3, 1):
            act_copies.append(
                links.send(
                    act_parts.at[flipped(slide, far), :, place], quarters.at[pl.ds(far * cells, cells), place], far, 0
                )
            )
        if which < 2:
            load_quarter((which + 2,), which + 2, wide, tall)
        else:
            load_quarter((B_, which), flipped(slide, which), wide, tall)
    quarters[0:cells, 0 : inner // 4] = act_parts[slide]
    base = final[...].astype(BF16)
    base_all[0:cells, :] = base
    have(WM_, WL_, WDEC_)
    mean_lat = jnp.dot(base, wm[...], preferred_element_type=F32)
    log_var = jnp.dot(base, wl[...], preferred_element_type=F32)
    mean_part[...] = mean_lat
    logvar_part[...] = log_var
    centres = centres_ref[...]
    resp, mixed = mixture(mean_lat, centres)
    mixed_square = exact_dot(resp, centres * centres, ((1,), (0,)))
    kl_cell = 0.5 * (
        jnp.exp(log_var) - 1.0 - log_var + mean_lat * mean_lat - 2.0 * mean_lat * mixed + mixed_square
    )
    kl_line = jnp.sum(kl_cell, axis=0, keepdims=True)
    kl_own[...] = jnp.zeros_like(kl_own)
    for block in range(latents // 128):
        kl_own[block : block + 1, :] = kl_line[:, block * 128 : (block + 1) * 128]
    kl_copies = [links.send(kl_own, kl_slides.at[slide], far, 0) for far in (2, 3, 1)]
    kl_slides[slide] = kl_own[...]
    latent = (mean_lat + jnp.exp(0.5 * log_var) * noise_ref[...]).astype(BF16)
    rows = latents // 8
    for side in range(2):
        for step in range(4):
            place = (step * 2 + side) * rows
            latent_all[0:cells, (side * 4 + step) * rows : (side * 4 + step + 1) * rows] = latent[:, place : place + rows]
    flows = {}
    decoded_out[...] = jnp.dot(latent, wdec[...], preferred_element_type=F32)
    for copy in kl_copies:
        copy.wait_recv()
    kl_sum[...] = (kl_slides[0] + kl_slides[1]) + (kl_slides[2] + kl_slides[3])
    kl_copies = [links.send(kl_sum, kl_blks.at[blk], 0, far) for far in (6, 4, 2, 7, 5, 3, 1)]
    kl_blks[blk] = kl_sum[...]
    glatent[...] = dot_nt(source_ref[...], wdec[...])
    for copy in kl_copies:
        copy.wait_recv()
    kl_total = kl_blks[0]
    for block in range(1, 8):
        kl_total = kl_total + kl_blks[block]
    kl_out[...] = kl_total
    flows[ACT_], flows[SOURCE_] = act_copies, source_copies
    flows[EXPRESS_], flows[NORMED_], flows[TWO_] = send_express, send_normed, send_two

    def lanes(ref, which, size):
        return ref.at[:, pl.ds(pl.multiple_of(which * size, 128), size)]

    def swap(ref, size, target):
        copies = []
        for far in (2, 3, 1):
            copies.append(links.send(lanes(ref, flipped(slide, far), size), target.at[far], far, 0))
        target[0] = lanes(ref, slide, size)[...]
        return copies

    waited = set()

    def arrived(*names):
        for name in names:
            if name not in waited:
                waited.add(name)
                for copy in flows[name]:
                    copy.wait_recv()

    def start_latent():
        flows[LATENT_] = across(links, latent_all, pl.ds(0, latents), cells)
        next(flows[LATENT_])

    def start_attended():
        flows[ATTENDED_] = across(links, whole, pl.ds(2 * width, width), cells)
        next(flows[ATTENDED_])

    def start_base():
        flows[BASE_] = across(links, base_all, pl.ds(0, width), cells)
        next(flows[BASE_])

    def relay(name):
        next(flows[name])

    small[...] = jnp.zeros_like(small)

    def bottleneck():
        kl_mean = jnp.concatenate([kl_out[block : block + 1, :] for block in range(latents // 128)], axis=1) / (32 * cells)
        grad_kl = weight_ref[0, 0] * (kl_mean > floor_ref[...]).astype(F32)
        mean_lat, log_var, centres = mean_part[...], logvar_part[...], centres_ref[...]
        grad_latent = glatent[...]
        resp, mixed = mixture(mean_lat, centres)
        weighted = mean_lat * grad_kl
        half_square = exact_dot(jnp.broadcast_to(0.5 * grad_kl, (8, latents)), centres * centres, ((1,), (1,)))[0:1]
        grad_resp = half_square - exact_dot(weighted, centres, ((1,), (1,)))
        grad_logits = resp * (grad_resp - jnp.sum(resp * grad_resp, axis=1, keepdims=True)) / math.sqrt(latents)
        grad_mean = grad_latent + grad_kl * (mean_lat - mixed) + exact_dot(grad_logits, centres, ((1,), (0,)))
        grad_logvar = grad_latent * (0.5 * jnp.exp(0.5 * log_var) * noise_ref[...]) + 0.5 * grad_kl * (jnp.exp(log_var) - 1.0)
        gmean[...] = grad_mean.astype(BF16)
        glogvar[...] = grad_logvar.astype(BF16)
        have(WM_, WL_)
        grad_final = dot_nt(gmean[...], wm[...]) + dot_nt(glogvar[...], wl[...])
        gmiddle[...] = grad_final
        branch_all[0] = grad_final.astype(BF16)
        flows[FAR_] = [links.send(branch_all.at[0], branch_all.at[2], 2, 0)]
        flows[NEAR_] = [links.send(branch_all.at[0], branch_all.at[1], 1, 0)]
        ones = jnp.ones((cells, 128), F32)
        logit_sum = exact_dot(grad_logits, ones, ((0,), (0,)))[:, 0:1]
        resp_sum = exact_dot(resp, ones, ((0,), (0,)))[:, 0:1]
        centres_grad = (
            exact_dot(grad_logits, mean_lat, ((0,), (0,)))
            - logit_sum * centres
            - exact_dot(resp, weighted, ((0,), (0,)))
            + resp_sum * grad_kl * centres
        )
        count = centres.shape[0]
        for block in range(8):
            small[block, 16 : 16 + count, 0 : latents // 8] = centres_grad[:, block * (latents // 8) : (block + 1) * (latents // 8)]
        bias_line = jnp.sum(branch_all[0].astype(F32), axis=0, keepdims=True)
        for block in range(8):
            small[block, 8:9, :] = bias_line[:, block * 128 : (block + 1) * 128]


    def swap_latents():
        flows[GMEAN_] = swap(gmean, latents // 4, gmean_all)
        flows[GLOGVAR_] = swap(glogvar, latents // 4, glogvar_all)

    def branch_on():
        arrived(FAR_)
        flows[NEAR_].append(links.send(branch_all.at[2], branch_all.at[3], 1, 0))

    width_at = {EXPRESS_: 0, ONE_: width, ATTENDED_: 2 * width, TWO_: 3 * width}

    def of_whole(name):
        def left(column):
            return whole[:, pl.ds(width_at[name] + column, 128)]

        return left

    def of_base(column):
        return base_all[:, pl.ds(column, 128)]

    def of_latent(column):
        return latent_all[:, pl.ds(column, 128)]

    def of_act(column):
        return quarters[:, pl.ds(column, 128)]

    def flat(ref, start=None, size=None):
        def right():
            block = ref[...] if start is None else ref[:, :, start : start + size]
            return block.reshape(4 * cells, block.shape[-1])

        return right

    def source_all():
        return quarters[:, inner // 4 :]

    half_w, half_i = width // 2, inner // 8
    operands = {
        DECODER_: (of_latent, source_all),
        DOWN0_: (of_act, flat(branch_all, 0, half_w)),
        DOWN1_: (of_act, flat(branch_all, half_w, half_w)),
        MEAN_: (of_base, flat(gmean_all)),
        LOGVAR_: (of_base, flat(glogvar_all)),
        HIDDEN0_: (of_whole(TWO_), flat(ginner_all, 0, half_i)),
        HIDDEN1_: (of_whole(TWO_), flat(ginner_all, half_i, half_i)),
        OUTPUT_: (of_whole(ATTENDED_), flat(gout_all)),
        PANEL_: (of_whole(EXPRESS_), flat(genc_all)),
        QUERY_: (of_whole(ONE_), flat(gqkv_all.at[0])),
        KEY_: (of_whole(ONE_), flat(gqkv_all.at[1])),
        VALUE_: (of_whole(ONE_), flat(gqkv_all.at[2])),
    }
    units = {}
    for number, (name, rows, columns, dense) in enumerate(reductions_of(cells, width, inner, latents)):
        left, right = operands[name]
        units[name] = (ReductionAlongZ if name in Z_FIRST else Reduction)(
            links, left, right, rows, columns, dense, unit_refs[3 * number : 3 * number + 3]
        )

    result_slots = {
        DECODER_: lambda place: lanes(decoder_out, place, width // 4),
        DOWN0_: lambda place: down_out.at[pl.ds(pl.multiple_of(place * (inner // 32), inner // 32), inner // 32), pl.ds(0, half_w)],
        DOWN1_: lambda place: down_out.at[pl.ds(pl.multiple_of(place * (inner // 32), inner // 32), inner // 32), pl.ds(half_w, half_w)],
        MEAN_: lambda place: lanes(mean_out, place, latents // 4),
        LOGVAR_: lambda place: lanes(logvar_out, place, latents // 4),
        HIDDEN0_: lambda place: hidden_out.at[:, pl.ds(pl.multiple_of(place * (inner // 4), 128), half_i)],
        HIDDEN1_: lambda place: hidden_out.at[:, pl.ds(pl.multiple_of(place * (inner // 4) + half_i, 128), half_i)],
        OUTPUT_: lambda place: lanes(output_out, place, width // 4),
        QUERY_: lambda place: lanes(query_out, place, width // 4),
        KEY_: lambda place: lanes(key_out, place, width // 4),
        VALUE_: lambda place: lanes(value_out, place, width // 4),
    }
    spreads = {}

    def spread(name):
        spreads[name] = spread_slide(links, result_slots[name], units[name].total())
        next(spreads[name])

    chunk = inner // 8
    encoded[...] = jnp.zeros_like(encoded)

    def feed_back(turn):
        far = (2, 3, 1, 0)[turn]
        wide, tall = ((1, 2), (3, 0))[turn % 2]
        have((WD_, B_, far), (WH_, B_, far))
        which = flipped(slide, far)

        def feed(j, carry, wide=wide, tall=tall, which=which):
            near = pl.ds(pl.multiple_of(j * chunk, 128), chunk)
            where = pl.ds(pl.multiple_of(which * (inner // 4) + j * chunk, 128), chunk)
            values = inner_sums[:, where]
            squared = values * values
            bent = jnp.tanh(0.7978845608028654 * (values + 0.044715 * squared * values))
            slope = 0.5 * (1.0 + bent) + 0.5 * values * (1.0 - bent * bent) * (
                0.7978845608028654 * (1.0 + 3 * 0.044715 * squared)
            )
            grad = (dot_nt(branch_all[0], slots[tall, near, :]) * slope).astype(BF16)
            ginner[:, where] = grad
            line = jnp.sum(grad.astype(F32), axis=0, keepdims=True)
            for block in range(chunk // 128):
                small[which * 2 + j, 4 + block : 5 + block, :] = line[:, block * 128 : (block + 1) * 128]
            encoded[...] += dot_nt(grad, slots[wide, :, near])
            return carry

        lax.fori_loop(0, 2, feed, 0)
        if far:
            flows[INNER_] = flows.get(INNER_, []) + [
                links.send(lanes(ginner, which, inner // 4), ginner_all.at[far], far, 0)
            ]
        else:
            ginner_all[0] = lanes(ginner, slide, inner // 4)[...]
        if turn < 2:
            load_quarter((B_, (1, 0)[turn]), flipped(slide, (1, 0)[turn]), wide, tall)
        if turn == 3:
            for number, (name, source) in enumerate(((WQ_, wq_hbm), (WK_, wk_hbm), (WV_, wv_hbm))):
                load((B_, name), source, slots.at[number])

    wq, wk, wv = slots.at[0], slots.at[1], slots.at[2]

    def norm_two():
        grad_hidden, gain_grad, shift_grad = norm_back(middle[...], gain_two[...], encoded[...])
        for block in range(8):
            small[block, 2:3, :] = gain_grad[:, block * 128 : (block + 1) * 128]
            small[block, 3:4, :] = shift_grad[:, block * 128 : (block + 1) * 128]
        gmiddle[...] += grad_hidden
        gout[...] = gmiddle[...].astype(BF16)

    def att_out():
        have(WO_)

        def att_block(target, store):
            rows = wo[pl.ds(pl.multiple_of(target * per, per), per), :]
            store(dot_nt(gout[...], rows).astype(BF16))

        att_copies = flows[ATT_] = []
        for far in (6, 4, 2, 7, 5, 3, 1):
            target = flipped(blk, far)

            def keep(block, far=far):
                att_send[far] = block

            att_block(target, keep)
            att_copies.append(links.send(att_send.at[far], att_land.at[blk], 0, far))

        def keep_own(block):
            att_land[blk] = block

        att_block(blk, keep_own)

    def swap_out():
        flows[GOUT_] = swap(gout, width // 4, gout_all)

    def masks():
        dk_sum[...] = jnp.zeros_like(dk_sum)
        dv_sum[...] = jnp.zeros_like(dv_sum)

    scale = HEAD_DIM**-0.5
    rows = 2 * cells

    def rows_back(i):
        arrived(ATT_)
        where = pl.ds(pl.multiple_of(i * rows, rows), rows)
        same_slide = row_labels[where, 0:1] == col_labels[...]
        query = land[pl.ds(2 * i, 2), 0:cells, :].reshape(rows, per)
        grad = att_land[pl.ds(2 * i, 2)].reshape(rows, per)
        key = land[:, cells : 2 * cells, :].reshape(8 * cells, per)
        value = land[:, 2 * cells : 3 * cells, :].reshape(8 * cells, per)
        lane = lax.broadcasted_iota(jnp.int32, query.shape, 1)
        grad_query = None
        for head in range(per // HEAD_DIM):
            mine = lane // HEAD_DIM == head
            own_query = jnp.where(mine, query, 0) * HEAD_SCALE
            own_grad = jnp.where(mine, grad, 0)
            shifted, inverse = head_scores(own_query, key, same_slide)
            shares = shifted * inverse
            grad_shares = dot_nt(own_grad, value)
            inner_dot = jnp.sum(shares * grad_shares, axis=1, keepdims=True)
            grad_scores = (shares * (grad_shares - inner_dot)).astype(BF16)
            part = jnp.dot(grad_scores, key, preferred_element_type=F32)
            grad_query = part if grad_query is None else jnp.where(mine, part, grad_query)
            dk_sum[...] += dot_tn(grad_scores, own_query)
            dv_sum[...] += dot_tn(shares.astype(BF16), own_grad)
        dqkv[pl.ds(2 * i, 2), 0:cells, :] = (grad_query * scale).astype(BF16).reshape(2, cells, per)

    def back_out():
        dqkv[:, cells : 2 * cells, :] = dk_sum[...].astype(BF16).reshape(8, cells, per)
        dqkv[:, 2 * cells :, :] = dv_sum[...].astype(BF16).reshape(8, cells, per)
        back_copies = flows[BACK_] = []
        for far in (6, 4, 2, 7, 5, 3, 1):
            back_copies.append(links.send(dqkv.at[flipped(blk, far)], dqkv_land.at[blk], 0, far))
        dqkv_land[blk] = dqkv[blk]

    def back_in():
        arrived(BACK_)
        have((B_, WQ_), (B_, WK_), (B_, WV_))
        for part in range(3):
            for block in range(8):
                grad_qkv[part, :, block * per : (block + 1) * per] = dqkv_land[block, part * cells : (part + 1) * cells, :]


    def swap_qkv():
        for part in range(3):
            flows[(QKV_, part)] = swap(grad_qkv.at[part], width // 4, gqkv_all.at[part])

    def norm_input(i, carry):
        where = pl.ds(pl.multiple_of(i * 256, 256), 256)
        encoded_sum = (
            dot_nt(grad_qkv[0], wq[where, :]) + dot_nt(grad_qkv[1], wk[where, :]) + dot_nt(grad_qkv[2], wv[where, :])
        )
        encoded[:, where] = encoded_sum
        return carry

    def norm_one():
        lax.fori_loop(0, width // 256, norm_input, 0)
        grad_hidden, gain_grad, shift_grad = norm_back(start[...], gain_one[...], encoded[...])
        grad_qkv[3] = (gmiddle[...] + grad_hidden).astype(BF16)
        flows[GENC_] = swap(grad_qkv.at[3], width // 4, genc_all)
        for block in range(8):
            small[block, 0:1, :] = gain_grad[:, block * 128 : (block + 1) * 128]
            small[block, 1:2, :] = shift_grad[:, block * 128 : (block + 1) * 128]

    def small_out_blk():
        flows[SMALL_] = [links.send(small.at[flipped(blk, far)], small_land.at[blk], 0, far) for far in range(1, 8)]
        small_land[blk] = small[blk]

    def small_out_slide():
        arrived(SMALL_)
        small_sum = small_land[0]
        for block in range(1, 8):
            small_sum = small_sum + small_land[block]
        small_own[...] = small_sum
        flows[SUMS_] = [links.send(small_own, small_slides.at[slide], far, 0) for far in (2, 3, 1)]
        small_slides[slide] = small_sum

    def small_done():
        arrived(SUMS_)
        small_out[...] = (small_slides[0] + small_slides[1]) + (small_slides[2] + small_slides[3])

    panel_slot = lambda far_slide, far_blk: panel_out.at[
        pl.ds(pl.multiple_of(far_blk * (width // 8), 128), width // 8),
        pl.ds(pl.multiple_of(far_slide * (width // 4), 128), width // 4),
    ]
    needs = {
        DECODER_: (SOURCE_,), DOWN0_: (ACT_, NEAR_), DOWN1_: (ACT_, NEAR_), MEAN_: (GMEAN_,), LOGVAR_: (GLOGVAR_,),
        HIDDEN0_: (INNER_,), HIDDEN1_: (INNER_,), OUTPUT_: (GOUT_,), PANEL_: (GENC_,), QUERY_: ((QKV_, 0),),
        KEY_: ((QKV_, 1),), VALUE_: ((QKV_, 2),),
    }

    def along(name):
        arrived(*needs[name])
        held = {HIDDEN0_: TWO_, HIDDEN1_: TWO_, OUTPUT_: ATTENDED_, PANEL_: EXPRESS_}
        held = held.get(name, NORMED_ if name in (QUERY_, KEY_, VALUE_) else None)
        if held and held not in waited:
            waited.add(held)
            next(flows[held])
        units[name].send_x()

    def panel_out_start():
        own_slot = panel_slot(slide, blk)
        own_slot[...] = units[PANEL_].total()
        flows[PANEL_] = spread_everywhere(links, panel_slot)
        next(flows[PANEL_])

    def spread_on(name):
        next(spreads[name])

    steps = {
        LATENT_: start_latent, ATTENDED_: start_attended, BASE_: start_base, RELAY_: relay, BOTTLENECK_: bottleneck, LATS_: swap_latents,
        BRANCH_: branch_on, FEED_: feed_back, NORM2_: norm_two, ATT_: att_out, GOUT_: swap_out, MASKS_: masks,
        ROWS_: rows_back, BACK_: back_out, IN_: back_in, QKV_: swap_qkv, NORM1_: norm_one, SMALL_: small_out_blk,
        SUMS_: small_out_slide, DONE_: small_done, X_: along, Z_: lambda name: units[name].send_z(),
        F_: lambda name: units[name].send_far(), S_: spread, S2_: spread_on, PANEL_: panel_out_start,
    }
    for step in ORDER:
        steps[step[0]](*step[1:])
    links.finish()


def layer(inputs, weights, cells, width, inner, latents):
    per = width // 8
    small_rows = 32
    shape = jax.ShapeDtypeStruct
    unit_scratch = []
    for _, rows, columns, _ in reductions_of(cells, width, inner, latents):
        unit_scratch += [pltpu.VMEM((4 * rows, columns), BF16)] * 2 + [pltpu.VMEM((3, rows, columns), BF16)]
    copies = 352
    vmem, left = pl.BlockSpec(memory_space=pltpu.VMEM), pl.BlockSpec(memory_space=pl.ANY)
    outs = (
        shape((cells, width), F32),
        shape((8, 128), F32),
        shape((width, width), BF16),
        shape((per, width), BF16),
        shape((per, width), BF16),
        shape((per, width), BF16),
        shape((per, width), BF16),
        shape((per, inner), BF16),
        shape((inner // 8, width), BF16),
        shape((per, latents), BF16),
        shape((per, latents), BF16),
        shape((latents // 8, width), BF16),
        shape((small_rows, 128), F32),
    )
    scratch = [
        ((4, width, width), BF16),
        ((width, width), BF16),
        ((width, latents), BF16),
        ((width, latents), BF16),
        ((latents, width), BF16),
        ((2, 8, width // 64, width), BF16),
        ((2, 8, width // 64, width), BF16),
        ((8, 3 * cells + 16, per), BF16),
        ((8, 3 * cells + 16, per), BF16),
        ((8, cells, per), BF16),
        ((8, cells, per), BF16),
        ((8 * cells, cells), F32),
        ((1, 8 * cells), F32),
        ((4, cells, inner // 4), BF16),
        ((cells, width), F32),
        ((8, 128), F32),
        ((4, 8, 128), F32),
        ((8, 128), F32),
        ((8, 8, 128), F32),
        ((cells, width), F32),
        ((cells, width), F32),
        ((cells, inner), F32),
        ((cells, latents), F32),
        ((cells, latents), F32),
        ((cells, latents), F32),
        ((4 * cells, 4 * width), BF16),
        ((4 * cells, inner // 4 + width // 4), BF16),
        ((4 * cells, width), BF16),
        ((4 * cells, latents), BF16),
        ((4, cells, width), BF16),
        ((cells, latents), BF16),
        ((cells, latents), BF16),
        ((4, cells, latents // 4), BF16),
        ((4, cells, latents // 4), BF16),
        ((cells, inner), BF16),
        ((4, cells, inner // 4), BF16),
        ((cells, width), BF16),
        ((4, cells, width // 4), BF16),
        ((cells, width), F32),
        ((3, 4, cells, width // 4), BF16),
        ((4, cells, width // 4), BF16),
        ((8, cells, per), BF16),
        ((8, cells, per), BF16),
        ((8, 3 * cells, per), BF16),
        ((8, 3 * cells, per), BF16),
        ((8 * cells, per), F32),
        ((8 * cells, per), F32),
        ((4, cells, width), BF16),
        ((cells, width), F32),
        ((8, small_rows, 128), F32),
        ((8, small_rows, 128), F32),
        ((small_rows, 128), F32),
        ((4, small_rows, 128), F32),
    ]
    return pl.pallas_call(
        layer_kernel,
        out_shape=outs,
        in_specs=[vmem] * len(inputs) + [left] * len(weights),
        out_specs=[vmem] * len(outs),
        scratch_shapes=[pltpu.VMEM(*item) for item in scratch]
        + [
            pltpu.SemaphoreType.DMA((28,)),
            pltpu.SemaphoreType.DMA((copies,)),
            pltpu.SemaphoreType.DMA((copies,)),
        ]
        + unit_scratch,
        compiler_params=pltpu.CompilerParams(
            collective_id=1, has_side_effects=True, vmem_limit_bytes=63 << 20
        ),
        name="layer",
    )(*inputs, *weights)


def finish_kernel(ids_ref, panel_ref, small_ref, kl_ref, weight_ref, floor_ref, *refs):
    count = (len(refs) - 9) // 2
    table_out, grads, outs, tiny = refs[count], refs[:count], refs[count + 1 : 2 * count + 1], refs[2 * count + 1 :]
    rows = table_out.shape[0]
    first = (lax.axis_index("blk") * pl.num_programs(0) + pl.program_id(0)) * rows
    row_ids = first + lax.broadcasted_iota(jnp.int32, (rows, ids_ref.shape[1]), 0)
    spread = (row_ids == ids_ref[...]).astype(F32).astype(BF16)
    table_out[...] = jnp.dot(spread, panel_ref[...], preferred_element_type=F32)
    for grad, out in zip(grads, outs):
        out[...] = grad[...].astype(F32)

    @pl.when(pl.program_id(0) == 0)
    def _():
        start = 0
        for out in tiny[:6]:
            out[...] = small_ref[start : start + out.shape[0], :]
            start += out.shape[0]
        centres = tiny[6]
        centres[...] = small_ref[16 : 16 + centres.shape[0], 0 : centres.shape[1]]
        total = jnp.zeros((1, 128), F32)
        for block in range(floor_ref.shape[1] // 128):
            lanes = slice(block * 128, (block + 1) * 128)
            total = total + jnp.maximum(kl_ref[block : block + 1, :] / weight_ref[0, 1], floor_ref[:, lanes])
        tiny[7][...] = weight_ref[0, 0] * (jnp.sum(total, axis=1, keepdims=True) / floor_ref.shape[1])


def finish(gene_ids, panel, grads, small, kl_total, weight, floor, table_rows, centres_shape, bias_rows, rows=512):
    genes, width = panel.shape
    steps = table_rows // rows
    shape = jax.ShapeDtypeStruct
    tiny = [(1, 128)] * 4 + [(bias_rows, 128), (1, 128), centres_shape, (1, 1)]

    def cut(grad):
        if grad.shape[0] // steps % 16 == 0:
            return pl.BlockSpec((grad.shape[0] // steps, grad.shape[1]), lambda i: (i, 0))
        return pl.BlockSpec((grad.shape[0], grad.shape[1] // steps), lambda i: (0, i))

    def whole(size):
        return pl.BlockSpec(size, lambda i: (0, 0))

    return pl.pallas_call(
        finish_kernel,
        grid=(steps,),
        out_shape=[shape((table_rows, width), F32)] + [shape(grad.shape, F32) for grad in grads] + [shape(size, F32) for size in tiny],
        in_specs=[
            whole((1, genes)), whole(panel.shape), whole(small.shape), whole(kl_total.shape),
            pl.BlockSpec(memory_space=pltpu.SMEM), whole(floor.shape),
        ]
        + [cut(grad) for grad in grads],
        out_specs=[pl.BlockSpec((rows, width), lambda i: (i, 0))] + [cut(grad) for grad in grads] + [whole(size) for size in tiny],
        compiler_params=pltpu.CompilerParams(vmem_limit_bytes=62 << 20),
        name="finish",
    )(gene_ids, panel, small, kl_total, weight, floor, *grads)


def on_device_fast(
    counts,
    library,
    gene_ids,
    positions,
    slide_of_cell,
    latent_noise,
    decoded_grad,
    gene_table,
    first_gain,
    first_shift,
    query_weight,
    key_weight,
    value_weight,
    output_weight,
    second_gain,
    second_shift,
    hidden_weight,
    hidden_bias,
    down_weight,
    down_bias,
    mean_weight,
    logvar_weight,
    component_means,
    decoder_weight,
    divergence_weight,
    free_floor,
):
    cells = counts.shape[1]
    width = gene_table.shape[1]
    latents = mean_weight.shape[1]
    inner = hidden_weight.shape[1]
    table_rows = gene_table.shape[0]
    quarter = width // 4
    freqs = np.exp(-math.log(10000.0) * np.arange(quarter, dtype=np.float32) / quarter).astype(np.float32)
    (
        decoded, kl_total, panel_sum, query_grad, key_grad, value_grad, output_grad, hidden_grad, down_grad, mean_grad,
        logvar_grad, decoder_grad, small,
    ) = layer(
        (
            gene_ids[None], counts[0], library, positions[0], freqs[None], slide_of_cell, latent_noise[0], decoded_grad[0],
            first_gain[None], first_shift[None], second_gain[None], second_shift[None], hidden_bias[None],
            down_bias[None], component_means, divergence_weight[None], free_floor[None],
        ),
        (
            gene_table, query_weight, key_weight, value_weight, output_weight, hidden_weight, down_weight, mean_weight,
            logvar_weight, decoder_weight,
        ),
        cells, width, inner, latents,
    )
    (
        table_grad, query_grad, key_grad, value_grad, output_grad, hidden_grad, down_grad, mean_grad, logvar_grad,
        decoder_grad, gain_one, shift_one, gain_two, shift_two, hidden_small, down_small, centres_grad, divergence,
    ) = finish(
        gene_ids[None], panel_sum,
        (
            query_grad, key_grad, value_grad, output_grad, hidden_grad, down_grad, mean_grad, logvar_grad,
            decoder_grad,
        ),
        small, kl_total, jnp.stack([divergence_weight[0], jnp.float32(32 * cells)])[None], free_floor[None], table_rows,
        (component_means.shape[0], latents // 8), inner // 8 // 128,
    )
    return (
        decoded[None],
        divergence.reshape(1),
        table_grad,
        gain_one.reshape(-1),
        shift_one.reshape(-1),
        query_grad,
        key_grad,
        value_grad,
        output_grad,
        gain_two.reshape(-1),
        shift_two.reshape(-1),
        hidden_grad,
        hidden_small.reshape(-1),
        down_grad,
        down_small.reshape(-1),
        mean_grad,
        logvar_grad,
        centres_grad,
        decoder_grad,
    )


def solution(mesh):
    placed = (
        P("slide", "blk", None),
        P("slide", "blk"),
        P(),
        P("slide", None, "blk"),
        P("slide", "blk"),
        P("slide", "blk", None),
        P("slide", "blk", None),
        P("blk", None),
        P(),
        P(),
        P(),
        P(),
        P(),
        P(),
        P(),
        P(),
        P(),
        P(),
        P(),
        P(),
        P(),
        P(),
        P(),
        P(),
        P(),
        P(),
    )
    return jax.shard_map(
        on_device_fast if fits(mesh) else on_device_general,
        mesh=mesh,
        in_specs=placed,
        out_specs=(
            P("slide", "blk", None),
            P(),
            P("blk", None),
            P("blk"),
            P("blk"),
            P("blk", None),
            P("blk", None),
            P("blk", None),
            P("blk", None),
            P("blk"),
            P("blk"),
            P("blk", None),
            P("blk"),
            P("blk", None),
            P("blk"),
            P("blk", None),
            P("blk", None),
            P(None, "blk"),
            P("blk", None),
        ),
        check_vma=False,
    )
```

```python
import functools
import math

import jax
import jax.numpy as jnp
import numpy as np
from jax import lax
from jax.experimental import pallas as pl
from jax.experimental.pallas import tpu as pltpu
from jax.sharding import PartitionSpec as P

HEAD_DIM = 64
HEAD_SCALE = 0.125
MESH = pl.DeviceIdType.MESH
F32 = jnp.float32
BF16 = jnp.bfloat16


def normalized(counts, library):
    scaled = counts.astype(jnp.float32) * (10000.0 / library.astype(jnp.float32))[..., None]
    return jnp.log1p(scaled)


def position_code(coords, model_width):
    quarter = model_width // 4
    freqs = jnp.exp(-math.log(10000.0) * jnp.arange(quarter, dtype=jnp.float32) / quarter)
    along_x = coords[0].astype(jnp.float32)[:, None] * freqs[None, :]
    along_y = coords[1].astype(jnp.float32)[:, None] * freqs[None, :]
    return jnp.concatenate(
        [jnp.sin(along_x), jnp.cos(along_x), jnp.sin(along_y), jnp.cos(along_y)], axis=1
    )


def layer_norm(inputs, scaling, offsets):
    centre = inputs - jnp.mean(inputs, axis=-1, keepdims=True)
    spread = jnp.mean(centre * centre, axis=-1, keepdims=True)
    return centre * lax.rsqrt(spread + 1e-05) * scaling + offsets


def gelu_tanh(inputs):
    return (
        0.5
        * inputs
        * (1.0 + jnp.tanh(0.7978845608028654 * (inputs + 0.044715 * inputs * inputs * inputs)))
    )


def divergence_cells(mean_part, logvar_part, centres):
    latent_width = mean_part.shape[-1]
    crossed = jnp.dot(mean_part, centres.T, precision=lax.Precision.HIGHEST)
    centre_square = jnp.sum(centres * centres, axis=-1)
    logits = (crossed - 0.5 * centre_square[None, :]) / math.sqrt(latent_width)
    shifted = jnp.exp(logits - jnp.max(logits, axis=-1, keepdims=True))
    resp = shifted / jnp.sum(shifted, axis=-1, keepdims=True)
    mixed = jnp.dot(resp, centres, precision=lax.Precision.HIGHEST)
    mixed_square = jnp.dot(resp, centres * centres, precision=lax.Precision.HIGHEST)
    return 0.5 * (
        jnp.exp(logvar_part)
        - 1.0
        - logvar_part
        + mean_part * mean_part
        - 2.0 * mean_part * mixed
        + mixed_square
    )


def to_heads(array, head_count):
    return array.reshape(array.shape[0], head_count, -1).transpose(1, 0, 2)


def from_heads(array):
    return array.transpose(1, 0, 2).reshape(array.shape[1], -1)


def matmul(left, right):
    return jnp.dot(left, right, preferred_element_type=jnp.float32)


def on_device_general(
    counts,
    library,
    gene_ids,
    positions,
    slide_of_cell,
    latent_noise,
    decoded_grad,
    gene_table,
    first_gain,
    first_shift,
    query_weight,
    key_weight,
    value_weight,
    output_weight,
    second_gain,
    second_shift,
    hidden_weight,
    hidden_bias,
    down_weight,
    down_bias,
    mean_weight,
    logvar_weight,
    component_means,
    decoder_weight,
    divergence_weight,
    free_floor,
):
    cell_count = counts.shape[1]
    model_width = gene_table.shape[1]
    head_count = model_width // HEAD_DIM
    score_scale = HEAD_DIM ** (-0.5)
    express = normalized(counts[0], library[0]).astype(jnp.bfloat16)
    table_rows = gene_table.shape[0]
    first_row = lax.axis_index("blk") * table_rows
    selector = (
        gene_ids[:, None] == first_row + jnp.arange(table_rows, dtype=jnp.int32)[None, :]
    ).astype(jnp.bfloat16)
    panel_part = matmul(selector, gene_table)
    panel_weight = lax.psum(panel_part, "blk").astype(jnp.bfloat16)
    hidden_start = matmul(express, panel_weight) + position_code(positions[0], model_width)
    normed_one = layer_norm(hidden_start, first_gain, first_shift).astype(jnp.bfloat16)
    query_low = matmul(normed_one, query_weight).astype(jnp.bfloat16)
    key_low = matmul(normed_one, key_weight).astype(jnp.bfloat16)
    value_low = matmul(normed_one, value_weight).astype(jnp.bfloat16)
    slide_labels = slide_of_cell[0].astype(jnp.bfloat16)
    keys_all, values_all, labels_all = (
        lax.all_gather(key_low, "blk", axis=0, tiled=True),
        lax.all_gather(value_low, "blk", axis=0, tiled=True),
        lax.all_gather(slide_labels, "blk", axis=0, tiled=True),
    )
    same_slide = slide_labels[:, None] == labels_all[None, :]
    query_heads = to_heads(query_low, head_count)
    key_heads = to_heads(keys_all, head_count)
    value_heads = to_heads(values_all, head_count)

    def head_forward(head_items):
        query_head, key_head, value_head = head_items
        scores = (
            jnp.einsum("qd,kd->qk", query_head, key_head, preferred_element_type=jnp.float32)
            * score_scale
        )
        scores = jnp.where(same_slide, scores, -1e30)
        row_max = jnp.max(scores, axis=1, keepdims=True)
        shifted = jnp.exp(scores - row_max)
        row_sum = jnp.sum(shifted, axis=1, keepdims=True)
        shares = shifted / row_sum
        attended_head = jnp.einsum(
            "qk,kd->qd", shares.astype(jnp.bfloat16), value_head, preferred_element_type=jnp.float32
        )
        return (attended_head, row_max[:, 0], row_sum[:, 0])

    attended_heads, row_maxes, row_sums = lax.map(
        head_forward, (query_heads, key_heads, value_heads)
    )
    attended = from_heads(attended_heads).astype(jnp.bfloat16)
    hidden_middle = hidden_start + matmul(attended, output_weight)
    normed_two = layer_norm(hidden_middle, second_gain, second_shift).astype(jnp.bfloat16)
    inner_sum = matmul(normed_two, hidden_weight) + hidden_bias
    act_low = gelu_tanh(inner_sum).astype(jnp.bfloat16)
    hidden_final = hidden_middle + matmul(act_low, down_weight) + down_bias
    base_low = hidden_final.astype(jnp.bfloat16)
    mean_lat = matmul(base_low, mean_weight)
    log_var = matmul(base_low, logvar_weight)
    noise_local = latent_noise[0]

    def bottleneck(mean_part, logvar_part, centres):
        return (
            mean_part + jnp.exp(0.5 * logvar_part) * noise_local,
            divergence_cells(mean_part, logvar_part, centres),
        )

    (latent, kl_cell), pull_latent = jax.vjp(bottleneck, mean_lat, log_var, component_means)
    latent_low = latent.astype(jnp.bfloat16)
    decoded = matmul(latent_low, decoder_weight)
    everyone = cell_count * lax.axis_size("blk") * lax.axis_size("slide")
    kl_sum = lax.psum(jnp.sum(kl_cell, axis=0), ("slide", "blk"))
    kl_mean = kl_sum / everyone
    divergence = divergence_weight * jnp.mean(jnp.maximum(kl_mean, free_floor))
    binding = (kl_mean > free_floor).astype(jnp.float32)
    grad_source = decoded_grad[0]
    grad_latent = matmul(grad_source, decoder_weight.T)
    decoder_grad = matmul(latent_low.T, grad_source)
    grad_kl = jnp.broadcast_to(divergence_weight * binding, kl_cell.shape)
    grad_mean, grad_logvar, centres_grad = pull_latent((grad_latent, grad_kl))
    grad_mean_low = grad_mean.astype(jnp.bfloat16)
    grad_logvar_low = grad_logvar.astype(jnp.bfloat16)
    mean_grad = matmul(base_low.T, grad_mean_low)
    logvar_grad = matmul(base_low.T, grad_logvar_low)
    grad_final = matmul(grad_mean_low, mean_weight.T) + matmul(grad_logvar_low, logvar_weight.T)
    grad_branch = grad_final.astype(jnp.bfloat16)
    down_grad = matmul(act_low.T, grad_branch)
    down_bias_grad = jnp.sum(grad_branch.astype(jnp.float32), axis=0)
    grad_act = matmul(grad_branch, down_weight.T)
    gelu_pull = jax.vjp(gelu_tanh, inner_sum)[1]
    grad_inner = gelu_pull(grad_act)[0].astype(jnp.bfloat16)
    hidden_grad = matmul(normed_two.T, grad_inner)
    hidden_bias_grad = jnp.sum(grad_inner.astype(jnp.float32), axis=0)
    norm_two_pull = jax.vjp(layer_norm, hidden_middle, second_gain, second_shift)[1]
    grad_norm_two, second_gain_grad, second_shift_grad = norm_two_pull(
        matmul(grad_inner, hidden_weight.T)
    )
    grad_middle = grad_final + grad_norm_two
    grad_out = grad_middle.astype(jnp.bfloat16)
    output_grad = matmul(attended.T, grad_out)
    grad_attended = matmul(grad_out, output_weight.T).astype(jnp.bfloat16)
    keys_again, values_again = (
        lax.all_gather(key_low, "blk", axis=0, tiled=True),
        lax.all_gather(value_low, "blk", axis=0, tiled=True),
    )
    key_heads_back = to_heads(keys_again, head_count)
    value_heads_back = to_heads(values_again, head_count)
    grad_heads_local = to_heads(grad_attended, head_count)

    def head_queries(head_items):
        query_head, key_head, value_head, grad_head, row_max, row_sum = head_items
        scores = (
            jnp.einsum("qd,kd->qk", query_head, key_head, preferred_element_type=jnp.float32)
            * score_scale
        )
        scores = jnp.where(same_slide, scores, -1e30)
        shares = jnp.exp(scores - row_max[:, None]) / row_sum[:, None]
        grad_shares = jnp.einsum(
            "qd,kd->qk", grad_head, value_head, preferred_element_type=jnp.float32
        )
        inner_dot = jnp.sum(shares * grad_shares, axis=1, keepdims=True)
        grad_scores = (shares * (grad_shares - inner_dot)).astype(jnp.bfloat16)
        grad_query_head = (
            jnp.einsum("qk,kd->qd", grad_scores, key_head, preferred_element_type=jnp.float32)
            * score_scale
        )
        return (grad_query_head, inner_dot[:, 0])

    grad_query_heads, inner_dots = lax.map(
        head_queries,
        (query_heads, key_heads_back, value_heads_back, grad_heads_local, row_maxes, row_sums),
    )
    queries_group, grads_group = (
        lax.all_gather(query_low, "blk", axis=0, tiled=True),
        lax.all_gather(grad_attended, "blk", axis=0, tiled=True),
    )
    maxes_group, totals_group, dots_group = (
        lax.all_gather(row_maxes, "blk", axis=1, tiled=True),
        lax.all_gather(row_sums, "blk", axis=1, tiled=True),
        lax.all_gather(inner_dots, "blk", axis=1, tiled=True),
    )
    mask_back = labels_all[:, None] == slide_labels[None, :]

    def head_keys(head_items):
        query_head, key_head, value_head, grad_head, row_max, row_sum, inner_dot = head_items
        scores = (
            jnp.einsum("qd,kd->qk", query_head, key_head, preferred_element_type=jnp.float32)
            * score_scale
        )
        scores = jnp.where(mask_back, scores, -1e30)
        shares = jnp.exp(scores - row_max[:, None]) / row_sum[:, None]
        grad_shares = jnp.einsum(
            "qd,kd->qk", grad_head, value_head, preferred_element_type=jnp.float32
        )
        grad_scores = (shares * (grad_shares - inner_dot[:, None])).astype(jnp.bfloat16)
        grad_key_head = (
            jnp.einsum("qk,qd->kd", grad_scores, query_head, preferred_element_type=jnp.float32)
            * score_scale
        )
        grad_value_head = jnp.einsum(
            "qk,qd->kd", shares.astype(jnp.bfloat16), grad_head, preferred_element_type=jnp.float32
        )
        return (grad_key_head, grad_value_head)

    grad_key_heads, grad_value_heads = lax.map(
        head_keys,
        (
            to_heads(queries_group, head_count),
            to_heads(key_low, head_count),
            to_heads(value_low, head_count),
            to_heads(grads_group, head_count),
            maxes_group,
            totals_group,
            dots_group,
        ),
    )
    grad_query_low = from_heads(grad_query_heads).astype(jnp.bfloat16)
    grad_key = from_heads(grad_key_heads)
    grad_value = from_heads(grad_value_heads)
    grad_key_low = grad_key.astype(jnp.bfloat16)
    grad_value_low = grad_value.astype(jnp.bfloat16)
    query_grad = matmul(normed_one.T, grad_query_low)
    key_grad = matmul(normed_one.T, grad_key_low)
    value_grad = matmul(normed_one.T, grad_value_low)
    grad_norm_input = (
        matmul(grad_query_low, query_weight.T)
        + matmul(grad_key_low, key_weight.T)
        + matmul(grad_value_low, value_weight.T)
    )
    norm_one_pull = jax.vjp(layer_norm, hidden_start, first_gain, first_shift)[1]
    grad_norm_one, first_gain_grad, first_shift_grad = norm_one_pull(grad_norm_input)
    grad_start = grad_middle + grad_norm_one
    grad_encoded = grad_start.astype(jnp.bfloat16)
    panel_grad = matmul(express.T, grad_encoded)
    panel_total = lax.psum(panel_grad, ("slide", "blk"))
    table_grad = jnp.dot(
        selector.astype(jnp.float32).T, panel_total, precision=lax.Precision.HIGHEST
    )
    shares_grads = (
        lax.psum_scatter(first_gain_grad, "blk", scatter_dimension=0, tiled=True),
        lax.psum_scatter(first_shift_grad, "blk", scatter_dimension=0, tiled=True),
        lax.psum_scatter(query_grad, "blk", scatter_dimension=0, tiled=True),
        lax.psum_scatter(key_grad, "blk", scatter_dimension=0, tiled=True),
        lax.psum_scatter(value_grad, "blk", scatter_dimension=0, tiled=True),
        lax.psum_scatter(output_grad, "blk", scatter_dimension=0, tiled=True),
        lax.psum_scatter(second_gain_grad, "blk", scatter_dimension=0, tiled=True),
        lax.psum_scatter(second_shift_grad, "blk", scatter_dimension=0, tiled=True),
        lax.psum_scatter(hidden_grad, "blk", scatter_dimension=0, tiled=True),
        lax.psum_scatter(hidden_bias_grad, "blk", scatter_dimension=0, tiled=True),
        lax.psum_scatter(down_grad, "blk", scatter_dimension=0, tiled=True),
        lax.psum_scatter(down_bias_grad, "blk", scatter_dimension=0, tiled=True),
        lax.psum_scatter(mean_grad, "blk", scatter_dimension=0, tiled=True),
        lax.psum_scatter(logvar_grad, "blk", scatter_dimension=0, tiled=True),
        lax.psum_scatter(centres_grad, "blk", scatter_dimension=1, tiled=True),
        lax.psum_scatter(decoder_grad, "blk", scatter_dimension=0, tiled=True),
    )
    summed = (
        lax.psum(shares_grads[0].astype(jnp.bfloat16), "slide").astype(jnp.float32),
        lax.psum(shares_grads[1].astype(jnp.bfloat16), "slide").astype(jnp.float32),
        lax.psum(shares_grads[2].astype(jnp.bfloat16), "slide").astype(jnp.float32),
        lax.psum(shares_grads[3].astype(jnp.bfloat16), "slide").astype(jnp.float32),
        lax.psum(shares_grads[4].astype(jnp.bfloat16), "slide").astype(jnp.float32),
        lax.psum(shares_grads[5].astype(jnp.bfloat16), "slide").astype(jnp.float32),
        lax.psum(shares_grads[6].astype(jnp.bfloat16), "slide").astype(jnp.float32),
        lax.psum(shares_grads[7].astype(jnp.bfloat16), "slide").astype(jnp.float32),
        lax.psum(shares_grads[8].astype(jnp.bfloat16), "slide").astype(jnp.float32),
        lax.psum(shares_grads[9].astype(jnp.bfloat16), "slide").astype(jnp.float32),
        lax.psum(shares_grads[10].astype(jnp.bfloat16), "slide").astype(jnp.float32),
        lax.psum(shares_grads[11].astype(jnp.bfloat16), "slide").astype(jnp.float32),
        lax.psum(shares_grads[12].astype(jnp.bfloat16), "slide").astype(jnp.float32),
        lax.psum(shares_grads[13].astype(jnp.bfloat16), "slide").astype(jnp.float32),
        lax.psum(shares_grads[14].astype(jnp.bfloat16), "slide").astype(jnp.float32),
        lax.psum(shares_grads[15].astype(jnp.bfloat16), "slide").astype(jnp.float32),
    )
    return (decoded[None], divergence, table_grad) + tuple(summed)


def fits(mesh):
    return mesh.shape["slide"] == 4 and mesh.shape["blk"] == 8


def flipped(index, mask):
    for bit in (1, 2, 4):
        if mask & bit:
            index = index + bit - 2 * bit * ((index // bit) % 2)
    return index


def greet(slide, blk, peers):
    barrier = pltpu.get_barrier_semaphore()
    for far_slide, far_blk in peers:
        pl.semaphore_signal(
            barrier,
            inc=1,
            device_id={"slide": flipped(slide, far_slide), "blk": flipped(blk, far_blk)},
            device_id_type=MESH,
        )
    pl.semaphore_wait(barrier, len(peers))


BLK_PEERS = [(0, far) for far in range(1, 8)]
SLIDE_PEERS = [(far, 0) for far in range(1, 4)]


def dot_nt(left, right):
    return lax.dot_general(left, right, (((1,), (1,)), ((), ())), preferred_element_type=F32)


def dot_tn(left, right):
    return lax.dot_general(left, right, (((0,), (0,)), ((), ())), preferred_element_type=F32)


def head_scores(query, key, same_slide):
    scores = jnp.where(same_slide, dot_nt(query, key), -1e30)
    shifted = jnp.exp(scores - jnp.max(scores, axis=1, keepdims=True))
    return shifted, 1.0 / jnp.sum(shifted, axis=1, keepdims=True)


(
    ACT_, ATTENDED_, ATT_, BACK_, BASE_, BOTTLENECK_, BRANCH_, B_, DECODER_, DONE_, DOWN0_, DOWN1_, EXPRESS_,
    FAR_, FEED_, F_, GENC_, GLOGVAR_, GMEAN_, GOUT_, HIDDEN0_, HIDDEN1_, INNER_, IN_, KEY_, LATENT_, LATS_,
    LOGVAR_, MASKS_, MEAN_, NEAR_, NORM1_, NORM2_, NORMED_, ONE_, OUTPUT_, PANEL_, QKV_, QUERY_, RELAY_,
    ROWS_, S2_, SMALL_, SOURCE_, SUMS_, S_, T0_, T1_, TWO_, VALUE_, WDEC_, WD_, WH_, WK_, WL_, WM_, WO_, WQ_,
    WV_, X_, Z_,
) = range(61)

Z_FIRST = (HIDDEN1_,)


class Links:
    def __init__(self, slide, blk, send_sem, recv_sem):
        self.slide, self.blk = slide, blk
        self.send_sem, self.recv_sem = send_sem, recv_sem
        self.copies, self.count = [], 0

    def send(self, source, target, far_slide, far_blk):
        number = self.count
        self.count += 1
        copy = pltpu.make_async_remote_copy(
            src_ref=source,
            dst_ref=target,
            send_sem=self.send_sem.at[number],
            recv_sem=self.recv_sem.at[number],
            device_id={
                "slide": flipped(self.slide, far_slide),
                "blk": flipped(self.blk, far_blk),
            },
            device_id_type=MESH,
        )
        copy.start()
        self.copies.append(copy)
        return copy

    def drain(self, copy):
        copy.wait_send()
        self.copies = [other for other in self.copies if other is not copy]

    def finish(self):
        for copy in self.copies:
            copy.wait_send()


def spread_everywhere(links, slot):
    slide, blk = links.slide, links.blk
    copies = {}

    def push(rel_slide, rel_blk, to_slide, to_blk):
        block = slot(flipped(slide, rel_slide), flipped(blk, rel_blk))
        copies[(rel_slide ^ to_slide, rel_blk ^ to_blk)] = links.send(block, block, to_slide, to_blk)

    for far in (2, 4, 6):
        push(0, 0, 0, far)
    push(0, 0, 0, 1)
    push(0, 0, 2, 0)
    push(0, 0, 1, 0)
    yield
    for rel in (2, 4, 6):
        copies[0, rel].wait_recv()
        push(0, rel, 0, 1)
        push(0, rel, 2, 0)
        push(0, rel, 1, 0)
    yield
    for rel in (1, 3, 5, 7):
        copies[0, rel].wait_recv()
        push(0, rel, 2, 0)
        push(0, rel, 1, 0)
    yield
    for rel in (0, 2, 4, 6, 1, 3, 5, 7):
        copies[2, rel].wait_recv()
        push(2, rel, 1, 0)
    yield
    for far in (1, 3):
        for rel in (0, 2, 4, 6, 1, 3, 5, 7):
            copies[far, rel].wait_recv()
    yield


class Reduction:
    def __init__(self, links, left, right, rows, width, dense, buffers):
        self.links, self.left, self.right = links, left, right
        self.rows, self.width, self.dense = rows, width, dense
        self.away, self.came, self.pieces = buffers
        self.kept = self.away
        self.along_x, self.along_z = links.blk % 2, links.blk // 2

    def tiles(self, which, store):
        def tile(i, carry):
            place = which * 2 + i if self.dense else i * 2 + which
            product = dot_tn(self.left(pl.multiple_of(place * 128, 128)), self.right())
            store(pl.ds(pl.multiple_of(i * 128, 128), 128), product)
            return carry

        lax.fori_loop(0, self.rows * 4 // 128, tile, 0)

    def send_x(self):
        def store(where, product):
            self.away[where, :] = product.astype(BF16)

        self.tiles(1 - self.along_x, store)
        self.copy_x = self.links.send(self.away, self.came, 0, 1)

    def piece(self, far):
        return pl.ds(pl.multiple_of(flipped(self.along_z, far) * self.rows, self.rows), self.rows)

    def send_z(self):
        self.links.drain(self.copy_x)
        self.copy_x.wait_recv()

        def store(where, product):
            self.kept[where, :] = (product + self.came[where, :].astype(F32)).astype(BF16)

        self.tiles(self.along_x, store)
        self.copies_z = [
            self.links.send(self.kept.at[self.piece(far)], self.pieces.at[far // 2], 0, 2) for far in (3, 1)
        ]

    def send_far(self):
        for copy in self.copies_z:
            copy.wait_recv()
        where = self.piece(2)
        self.kept[where, :] = (self.kept[where, :].astype(F32) + self.pieces[1].astype(F32)).astype(BF16)
        self.copy_far = self.links.send(self.kept.at[where], self.pieces.at[2], 0, 4)

    def total(self):
        self.copy_far.wait_recv()
        own = self.kept[self.piece(0), :]
        return ((own.astype(F32) + self.pieces[0].astype(F32)) + self.pieces[2].astype(F32)).astype(BF16)


class ReductionAlongZ(Reduction):
    def tiles(self, start, store):
        step = 2 - 4 * ((start // 2) % 2)

        def tile(i, carry):
            place = (start + (i // 2) * step) * 2 + i % 2
            product = dot_tn(self.left(pl.multiple_of(place * 128, 128)), self.right())
            store(pl.ds(pl.multiple_of(i * 128, 128), 128), product)
            return carry

        lax.fori_loop(0, 4, tile, 0)

    def send_x(self):
        def store(where, product):
            self.away[where, :] = product.astype(BF16)

        self.tiles(flipped(self.along_z, 1), store)
        self.copy_x = self.links.send(self.away, self.came, 0, 2)

    def send_z(self):
        self.links.drain(self.copy_x)
        self.copy_x.wait_recv()

        def store(where, product):
            self.kept[where, :] = (product + self.came[where, :].astype(F32)).astype(BF16)

        self.tiles(self.along_z, store)
        self.copies_z = [
            self.links.send(self.kept.at[pl.ds((2 + side) * self.rows, self.rows)], self.pieces.at[side], 0, 4)
            for side in range(2)
        ]

    def block(self, side):
        return pl.ds(pl.multiple_of(side * self.rows, self.rows), self.rows)

    def send_far(self):
        for copy in self.copies_z:
            copy.wait_recv()
        other = 1 - self.along_x
        where = self.block(other)
        self.kept[where, :] = (self.kept[where, :].astype(F32) + self.pieces[other].astype(F32)).astype(BF16)
        self.copy_far = self.links.send(self.kept.at[where], self.pieces.at[2], 0, 1)

    def total(self):
        self.copy_far.wait_recv()
        own = self.kept[self.block(self.along_x), :].astype(F32) + self.pieces[self.along_x].astype(F32)
        return (own + self.pieces[2].astype(F32)).astype(BF16)


def spread_slide(links, slot, total):
    slide = links.slide
    own, far = slot(slide), slot(flipped(slide, 2))
    own[...] = total
    across = links.send(own, own, 2, 0)
    beside = links.send(own, own, 1, 0)
    yield
    across.wait_recv()
    last = links.send(far, far, 1, 0)
    yield
    beside.wait_recv()
    last.wait_recv()
    yield


def reductions_of(cells, width, inner, latents):
    return [
        (DECODER_, latents // 8, width // 4, True),
        (DOWN0_, inner // 32, width // 2, False),
        (DOWN1_, inner // 32, width // 2, False),
        (MEAN_, width // 8, latents // 4, False),
        (LOGVAR_, width // 8, latents // 4, False),
        (HIDDEN0_, width // 8, inner // 8, False),
        (HIDDEN1_, width // 8, inner // 8, False),
        (OUTPUT_, width // 8, width // 4, False),
        (PANEL_, width // 8, width // 4, False),
        (QUERY_, width // 8, width // 4, False),
        (KEY_, width // 8, width // 4, False),
        (VALUE_, width // 8, width // 4, False),
    ]


def across(links, ref, columns, cells):
    def rows(place):
        return ref.at[pl.ds(place * cells, cells), columns]

    far = links.send(rows(0), rows(2), 2, 0)
    near = links.send(rows(0), rows(1), 1, 0)
    yield
    far.wait_recv()
    last = links.send(rows(2), rows(3), 1, 0)
    yield
    near.wait_recv()
    last.wait_recv()
    yield


def norm_parts(hidden):
    centre = hidden - jnp.mean(hidden, axis=1, keepdims=True)
    invert = lax.rsqrt(jnp.mean(centre * centre, axis=1, keepdims=True) + 1e-05)
    return centre * invert, invert


def norm_back(hidden, gain, grad):
    unit, invert = norm_parts(hidden)
    gain_grad = jnp.sum(grad * unit, axis=0, keepdims=True)
    shift_grad = jnp.sum(grad, axis=0, keepdims=True)
    grad_unit = grad * gain
    grad_hidden = invert * (
        grad_unit
        - jnp.mean(grad_unit, axis=1, keepdims=True)
        - unit * jnp.mean(grad_unit * unit, axis=1, keepdims=True)
    )
    return grad_hidden, gain_grad, shift_grad


def exact_dot(left, right, dims):
    return lax.dot_general(
        left, right, (dims, ((), ())), precision=lax.Precision.HIGHEST, preferred_element_type=F32
    )


def mixture(mean_part, centres):
    crossed = exact_dot(mean_part, centres, ((1,), (1,)))
    ones = jnp.ones((8, centres.shape[1]), F32)
    centre_square = exact_dot(ones, centres * centres, ((1,), (1,)))[0:1]
    logits = (crossed - 0.5 * centre_square) / math.sqrt(centres.shape[1])
    shifted = jnp.exp(logits - jnp.max(logits, axis=1, keepdims=True))
    resp = shifted / jnp.sum(shifted, axis=1, keepdims=True)
    return resp, exact_dot(resp, centres, ((1,), (0,)))


def slide_masks(land, row_labels, col_labels, cells):
    for block in range(8):
        line = land[block, 3 * cells : 3 * cells + 1, :].astype(F32)
        col_labels[:, block * cells : (block + 1) * cells] = line
        row_labels[block * cells : (block + 1) * cells, :] = jnp.broadcast_to(line, (cells, cells)).T


ORDER = (
    (BOTTLENECK_,), (FEED_, 0), (FEED_, 1), (FEED_, 2), (FEED_, 3), (NORM2_,), (ATT_,), (GOUT_,),
    (MASKS_,), (BRANCH_,), (X_, DOWN0_), (RELAY_, TWO_), (X_, DOWN1_), (ROWS_, 0), (ROWS_, 1),
    (LATS_,), (LATENT_,), (BASE_,), (ATTENDED_,), (ROWS_, 2), (ROWS_, 3), (BACK_,), (Z_, DOWN0_),
    (RELAY_, LATENT_), (RELAY_, BASE_), (X_, HIDDEN0_), (F_, DOWN0_), (Z_, DOWN1_), (IN_,), (NORM1_,),
    (QKV_,), (SMALL_,), (RELAY_, LATENT_), (RELAY_, BASE_), (RELAY_, ATTENDED_), (X_, HIDDEN1_),
    (X_, PANEL_), (X_, QUERY_), (X_, KEY_), (X_, VALUE_), (X_, MEAN_), (X_, LOGVAR_),
    (X_, DECODER_), (X_, OUTPUT_), (F_, DOWN1_), (SUMS_,), (Z_, HIDDEN0_), (S_, DOWN0_),
    (Z_, PANEL_), (S_, DOWN1_), (F_, HIDDEN0_), (F_, PANEL_), (Z_, HIDDEN1_), (Z_, QUERY_),
    (Z_, KEY_), (Z_, VALUE_), (PANEL_,), (Z_, MEAN_), (Z_, LOGVAR_), (Z_, DECODER_),
    (RELAY_, PANEL_), (Z_, OUTPUT_), (S_, HIDDEN0_), (F_, HIDDEN1_), (F_, QUERY_), (F_, KEY_),
    (F_, VALUE_), (RELAY_, PANEL_), (F_, MEAN_), (F_, LOGVAR_), (F_, DECODER_), (F_, OUTPUT_),
    (RELAY_, PANEL_), (S_, HIDDEN1_), (S_, QUERY_), (S_, KEY_), (S_, VALUE_), (S_, MEAN_),
    (S_, LOGVAR_), (S_, DECODER_), (S_, OUTPUT_), (S2_, DECODER_), (S2_, DOWN0_), (S2_, DOWN1_),
    (S2_, MEAN_), (S2_, LOGVAR_), (S2_, HIDDEN0_), (S2_, OUTPUT_), (S2_, HIDDEN1_), (S2_, QUERY_),
    (S2_, KEY_), (S2_, VALUE_), (DONE_,), (RELAY_, PANEL_), (S2_, DECODER_), (S2_, DOWN0_),
    (S2_, DOWN1_), (S2_, MEAN_), (S2_, LOGVAR_), (S2_, HIDDEN0_), (S2_, OUTPUT_), (S2_, HIDDEN1_),
    (S2_, QUERY_), (S2_, KEY_), (S2_, VALUE_),
)


def layer_kernel(
    ids_ref, counts_ref, library_ref, positions_ref, freqs_ref, labels_ref, noise_ref, source_ref, gain_one, shift_one,
    gain_two, shift_two, hidden_bias, down_bias, centres_ref, weight_ref, floor_ref,
    table_hbm, wq_hbm, wk_hbm, wv_hbm, wo_hbm, wh_hbm, wd_hbm, wm_hbm, wl_hbm, wdec_hbm,
    decoded_out, kl_out, panel_out, query_out, key_out, value_out, output_out, hidden_out, down_out, mean_out, logvar_out,
    decoder_out, small_out,
    slots, wo, wm, wl, wdec, part, panel_land, qkv_send, land, att_send_fwd, att_land_fwd, row_labels, col_labels,
    act_parts, final, kl_own, kl_slides, kl_sum, kl_blks, start, middle, inner_sums, mean_part, logvar_part, glatent, whole,
    quarters, base_all, latent_all, branch_all, gmean, glogvar, gmean_all, glogvar_all, ginner, ginner_all, gout, gout_all,
    gmiddle, gqkv_all, genc_all, att_send, att_land, dqkv, dqkv_land, dk_sum, dv_sum, grad_qkv, encoded, small, small_land,
    small_own, small_slides, load_sem, send_sem, recv_sem, *unit_refs,
):
    slide, blk = lax.axis_index("slide"), lax.axis_index("blk")
    cells, width = counts_ref.shape
    inner, latents, per = inner_sums.shape[1], mean_part.shape[1], width // 8
    loads = {}
    loaded = set()

    def load(name, source, target):
        loads[name] = pltpu.make_async_copy(source, target, load_sem.at[len(loads)])
        loads[name].start()

    def have(*names):
        for name in names:
            if name not in loaded:
                loaded.add(name)
                loads[name].wait()

    def load_quarter(name, which, wide, tall):
        columns = pl.ds(which * width if isinstance(which, int) else pl.multiple_of(which * width, 128), width)
        load((WH_, *name), wh_hbm.at[:, columns], slots.at[wide])
        load((WD_, *name), wd_hbm.at[columns, :], slots.at[tall])

    load(T0_, table_hbm.at[pl.ds(0, width)], slots.at[0])
    load(T1_, table_hbm.at[pl.ds(width, width)], slots.at[1])
    load(WQ_, wq_hbm, slots.at[2])
    load(WK_, wk_hbm, slots.at[3])
    load(WO_, wo_hbm, wo)
    load(WM_, wm_hbm, wm)
    load(WL_, wl_hbm, wl)
    load(WDEC_, wdec_hbm, wdec)
    greet(slide, blk, SLIDE_PEERS + BLK_PEERS)
    links = Links(slide, blk, send_sem, recv_sem)

    def column(line):
        return jnp.broadcast_to(line, (line.shape[1], line.shape[1])).T[:, 0:1]

    genes = ids_ref.shape[1]
    table_rows, block_rows = 2 * width, genes // 64
    first = (blk * table_rows).astype(F32)
    have(T0_, T1_)
    for side in range(2):
        ids = ids_ref[:, pl.ds(pl.multiple_of(slide * (genes // 4) + side * 128, 128), 128)].astype(F32)
        places = lax.broadcasted_iota(jnp.int32, (128, table_rows), 1).astype(F32) + first
        selector = (places == column(ids)).astype(F32).astype(BF16)
        rows = jnp.dot(selector[:, 0:width], slots[0], preferred_element_type=F32) + jnp.dot(
            selector[:, width:], slots[1], preferred_element_type=F32
        )
        part[side] = rows.astype(BF16).reshape(8, block_rows, width)
    load(WV_, wv_hbm, slots.at[0])
    part_copies = [
        [links.send(part.at[side, flipped(blk, far)], panel_land.at[side, far], 0, far) for far in (6, 4, 2, 7, 5, 3, 1)]
        for side in range(2)
    ]
    scale = column(10000.0 / library_ref[...].astype(F32))
    express = jnp.log(1.0 + counts_ref[...].astype(F32) * scale).astype(BF16)
    whole[0:cells, 0:width] = express
    quarter = width // 4
    for axis in range(2):
        angle = column(positions_ref[axis : axis + 1, :].astype(F32)) * freqs_ref[...]
        start[:, 2 * axis * quarter : (2 * axis + 1) * quarter] = jnp.sin(angle)
        start[:, (2 * axis + 1) * quarter : (2 * axis + 2) * quarter] = jnp.cos(angle)

    def panel_rows(far_slide, far_blk, side):
        first_gene = (far_slide * 2 + side) * 8 * block_rows + far_blk * block_rows
        return panel_out.at[pl.ds(pl.multiple_of(first_gene, 16), block_rows)]

    row_spreads = []
    for side in range(2):
        total = part[side, blk].astype(F32)
        for place, far in enumerate((6, 4, 2, 7, 5, 3, 1)):
            part_copies[side][place].wait_recv()
            total = total + panel_land[side, far].astype(F32)
        own_rows = panel_rows(slide, blk, side)
        own_rows[...] = total.astype(BF16)
        row_spreads.append(spread_everywhere(links, lambda far_slide, far_blk, side=side: panel_rows(far_slide, far_blk, side)))
        next(row_spreads[side])
        if side:
            next(row_spreads[1])
            next(row_spreads[0])
        else:
            next(row_spreads[0])
    next(row_spreads[1])
    next(row_spreads[0])
    next(row_spreads[1])
    next(row_spreads[0])
    next(row_spreads[1])
    panel_copies = list(links.copies)
    send_express = across(links, whole, pl.ds(0, width), cells)
    next(send_express)

    def source_part(which):
        return source_ref.at[:, pl.ds(pl.multiple_of(which * quarter, 128), quarter)]

    def source_slot(place):
        return quarters.at[pl.ds(place * cells, cells), pl.ds(inner // 4, quarter)]

    source_copies = [links.send(source_part(flipped(slide, far)), source_slot(far), far, 0) for far in (2, 3, 1)]
    source_slot(0)[...] = source_part(slide)[...]

    hidden_start = start[...] + jnp.dot(express, panel_out[...], preferred_element_type=F32)
    start[...] = hidden_start
    normed = (norm_parts(hidden_start)[0] * gain_one[...] + shift_one[...]).astype(BF16)
    whole[0:cells, width : 2 * width] = normed
    qkv_send[:, 3 * cells :, :] = jnp.broadcast_to(labels_ref[...].astype(F32).astype(BF16).reshape(1, 1, cells), (8, 16, per))
    have(WQ_, WK_, WV_)
    load((WH_, 0), wh_hbm.at[:, pl.ds(0, width)], slots.at[1])

    along_x, along_z = blk % 2, blk // 2
    qkv_copies = []
    for far in (3, 2, 1, 0):
        pair = flipped(along_z, far)
        columns = pl.ds(pl.multiple_of(pair * 2 * per, 128), 2 * per)
        for number, weight in enumerate((slots.at[2], slots.at[3], slots.at[0])):
            product = jnp.dot(normed, weight[:, columns], preferred_element_type=F32).astype(BF16)
            for side in range(2):
                qkv_send[pair * 2 + side, number * cells : (number + 1) * cells, :] = product[:, side * per : (side + 1) * per]
        for side in (1, 0):
            if far or side:
                target = flipped(pair * 2 + along_x, side)
                qkv_copies.append(links.send(qkv_send.at[target], land.at[blk], 0, 2 * far + side))
    land[blk] = qkv_send[blk]
    load((WD_, 0), wd_hbm.at[pl.ds(0, width), :], slots.at[2])
    load_quarter((1,), 1, 3, 0)
    next(send_express)
    send_normed = across(links, whole, pl.ds(width, width), cells)
    next(send_normed)
    for copy in panel_copies:
        links.drain(copy)
    for copy in qkv_copies:
        copy.wait_recv()

    slide_masks(land, row_labels, col_labels, cells)
    key = land[:, cells : 2 * cells, :].reshape(8 * cells, per)
    value = land[:, 2 * cells : 3 * cells, :].reshape(8 * cells, per)
    att_copies = []
    for far in (3, 2, 1, 0):
        pair = flipped(along_z, far)
        query = land[pl.ds(pair * 2, 2), 0:cells, :].reshape(2 * cells, per)
        same_slide = row_labels[pl.ds(pl.multiple_of(pair * 2 * cells, 128), 2 * cells), 0:1] == col_labels[...]
        lane = lax.broadcasted_iota(jnp.int32, query.shape, 1)
        out = None
        for head in range(per // HEAD_DIM):
            mine = lane // HEAD_DIM == head
            shifted, inverse = head_scores(jnp.where(mine, query, 0) * HEAD_SCALE, key, same_slide)
            part = jnp.dot((shifted * inverse).astype(BF16), value, preferred_element_type=F32)
            out = part if out is None else jnp.where(mine, part, out)
        att_send_fwd[pl.ds(pair * 2, 2)] = out.astype(BF16).reshape(2, cells, per)
        for side in (1, 0):
            if far or side:
                target = flipped(pair * 2 + along_x, side)
                att_copies.append(links.send(att_send_fwd.at[target], att_land_fwd.at[blk], 0, 2 * far + side))
    att_land_fwd[blk] = att_send_fwd[blk]
    next(send_normed)
    for copy in att_copies:
        copy.wait_recv()
    for block in range(8):
        whole[0:cells, 2 * width + block * per : 2 * width + (block + 1) * per] = att_land_fwd[block]

    have(WO_)
    hidden_middle = start[...] + jnp.dot(
        whole[0:cells, 2 * width : 3 * width], wo[...], preferred_element_type=F32
    )
    middle[...] = hidden_middle
    normed_two = (norm_parts(hidden_middle)[0] * gain_two[...] + shift_two[...]).astype(BF16)
    whole[0:cells, 3 * width :] = normed_two
    send_two = across(links, whole, pl.ds(3 * width, width), cells)
    next(send_two)
    final[...] = hidden_middle + down_bias[...]
    chunk = inner // 8

    act_copies = []
    for which in range(4):
        wide, tall = ((1, 2), (3, 0))[which % 2]
        have((WH_, which), (WD_, which))

        def feed_on(j, carry, which=which, wide=wide, tall=tall):
            near = pl.ds(pl.multiple_of(j * chunk, 128), chunk)
            where = pl.ds(pl.multiple_of(which * width + j * chunk, 128), chunk)
            inner_sum = jnp.dot(whole[0:cells, 3 * width :], slots[wide, :, near], preferred_element_type=F32) + hidden_bias[:, where]
            inner_sums[:, where] = inner_sum
            act = gelu_tanh(inner_sum).astype(BF16)
            place = pl.ds(pl.multiple_of((which * 2 + j) * (chunk // 4), 128), chunk // 4)
            for block in range(4):
                act_parts[block, :, place] = act[:, block * (chunk // 4) : (block + 1) * (chunk // 4)]
            final[...] += jnp.dot(act, slots[tall, near, :], preferred_element_type=F32)
            return carry

        lax.fori_loop(0, 2, feed_on, 0)
        place = pl.ds(which * (chunk // 2), chunk // 2)
        for far in (2, 3, 1):
            act_copies.append(
                links.send(
                    act_parts.at[flipped(slide, far), :, place], quarters.at[pl.ds(far * cells, cells), place], far, 0
                )
            )
        if which < 2:
            load_quarter((which + 2,), which + 2, wide, tall)
        else:
            load_quarter((B_, which), flipped(slide, which), wide, tall)
    quarters[0:cells, 0 : inner // 4] = act_parts[slide]
    base = final[...].astype(BF16)
    base_all[0:cells, :] = base
    have(WM_, WL_, WDEC_)
    mean_lat = jnp.dot(base, wm[...], preferred_element_type=F32)
    log_var = jnp.dot(base, wl[...], preferred_element_type=F32)
    mean_part[...] = mean_lat
    logvar_part[...] = log_var
    centres = centres_ref[...]
    resp, mixed = mixture(mean_lat, centres)
    mixed_square = exact_dot(resp, centres * centres, ((1,), (0,)))
    kl_cell = 0.5 * (
        jnp.exp(log_var) - 1.0 - log_var + mean_lat * mean_lat - 2.0 * mean_lat * mixed + mixed_square
    )
    kl_line = jnp.sum(kl_cell, axis=0, keepdims=True)
    kl_own[...] = jnp.zeros_like(kl_own)
    for block in range(latents // 128):
        kl_own[block : block + 1, :] = kl_line[:, block * 128 : (block + 1) * 128]
    kl_copies = [links.send(kl_own, kl_slides.at[slide], far, 0) for far in (2, 3, 1)]
    kl_slides[slide] = kl_own[...]
    latent = (mean_lat + jnp.exp(0.5 * log_var) * noise_ref[...]).astype(BF16)
    rows = latents // 8
    for side in range(2):
        for step in range(4):
            place = (step * 2 + side) * rows
            latent_all[0:cells, (side * 4 + step) * rows : (side * 4 + step + 1) * rows] = latent[:, place : place + rows]
    flows = {}
    decoded_out[...] = jnp.dot(latent, wdec[...], preferred_element_type=F32)
    for copy in kl_copies:
        copy.wait_recv()
    kl_sum[...] = (kl_slides[0] + kl_slides[1]) + (kl_slides[2] + kl_slides[3])
    kl_copies = [links.send(kl_sum, kl_blks.at[blk], 0, far) for far in (6, 4, 2, 7, 5, 3, 1)]
    kl_blks[blk] = kl_sum[...]
    glatent[...] = dot_nt(source_ref[...], wdec[...])
    for copy in kl_copies:
        copy.wait_recv()
    kl_total = kl_blks[0]
    for block in range(1, 8):
        kl_total = kl_total + kl_blks[block]
    kl_out[...] = kl_total
    flows[ACT_], flows[SOURCE_] = act_copies, source_copies
    flows[EXPRESS_], flows[NORMED_], flows[TWO_] = send_express, send_normed, send_two

    def lanes(ref, which, size):
        return ref.at[:, pl.ds(pl.multiple_of(which * size, 128), size)]

    def swap(ref, size, target):
        copies = []
        for far in (2, 3, 1):
            copies.append(links.send(lanes(ref, flipped(slide, far), size), target.at[far], far, 0))
        target[0] = lanes(ref, slide, size)[...]
        return copies

    waited = set()

    def arrived(*names):
        for name in names:
            if name not in waited:
                waited.add(name)
                for copy in flows[name]:
                    copy.wait_recv()

    def start_latent():
        flows[LATENT_] = across(links, latent_all, pl.ds(0, latents), cells)
        next(flows[LATENT_])

    def start_attended():
        flows[ATTENDED_] = across(links, whole, pl.ds(2 * width, width), cells)
        next(flows[ATTENDED_])

    def start_base():
        flows[BASE_] = across(links, base_all, pl.ds(0, width), cells)
        next(flows[BASE_])

    def relay(name):
        next(flows[name])

    small[...] = jnp.zeros_like(small)

    def bottleneck():
        kl_mean = jnp.concatenate([kl_out[block : block + 1, :] for block in range(latents // 128)], axis=1) / (32 * cells)
        grad_kl = weight_ref[0, 0] * (kl_mean > floor_ref[...]).astype(F32)
        mean_lat, log_var, centres = mean_part[...], logvar_part[...], centres_ref[...]
        grad_latent = glatent[...]
        resp, mixed = mixture(mean_lat, centres)
        weighted = mean_lat * grad_kl
        half_square = exact_dot(jnp.broadcast_to(0.5 * grad_kl, (8, latents)), centres * centres, ((1,), (1,)))[0:1]
        grad_resp = half_square - exact_dot(weighted, centres, ((1,), (1,)))
        grad_logits = resp * (grad_resp - jnp.sum(resp * grad_resp, axis=1, keepdims=True)) / math.sqrt(latents)
        grad_mean = grad_latent + grad_kl * (mean_lat - mixed) + exact_dot(grad_logits, centres, ((1,), (0,)))
        grad_logvar = grad_latent * (0.5 * jnp.exp(0.5 * log_var) * noise_ref[...]) + 0.5 * grad_kl * (jnp.exp(log_var) - 1.0)
        gmean[...] = grad_mean.astype(BF16)
        glogvar[...] = grad_logvar.astype(BF16)
        have(WM_, WL_)
        grad_final = dot_nt(gmean[...], wm[...]) + dot_nt(glogvar[...], wl[...])
        gmiddle[...] = grad_final
        branch_all[0] = grad_final.astype(BF16)
        flows[FAR_] = [links.send(branch_all.at[0], branch_all.at[2], 2, 0)]
        flows[NEAR_] = [links.send(branch_all.at[0], branch_all.at[1], 1, 0)]
        ones = jnp.ones((cells, 128), F32)
        logit_sum = exact_dot(grad_logits, ones, ((0,), (0,)))[:, 0:1]
        resp_sum = exact_dot(resp, ones, ((0,), (0,)))[:, 0:1]
        centres_grad = (
            exact_dot(grad_logits, mean_lat, ((0,), (0,)))
            - logit_sum * centres
            - exact_dot(resp, weighted, ((0,), (0,)))
            + resp_sum * grad_kl * centres
        )
        count = centres.shape[0]
        for block in range(8):
            small[block, 16 : 16 + count, 0 : latents // 8] = centres_grad[:, block * (latents // 8) : (block + 1) * (latents // 8)]
        bias_line = jnp.sum(branch_all[0].astype(F32), axis=0, keepdims=True)
        for block in range(8):
            small[block, 8:9, :] = bias_line[:, block * 128 : (block + 1) * 128]


    def swap_latents():
        flows[GMEAN_] = swap(gmean, latents // 4, gmean_all)
        flows[GLOGVAR_] = swap(glogvar, latents // 4, glogvar_all)

    def branch_on():
        arrived(FAR_)
        flows[NEAR_].append(links.send(branch_all.at[2], branch_all.at[3], 1, 0))

    width_at = {EXPRESS_: 0, ONE_: width, ATTENDED_: 2 * width, TWO_: 3 * width}

    def of_whole(name):
        def left(column):
            return whole[:, pl.ds(width_at[name] + column, 128)]

        return left

    def of_base(column):
        return base_all[:, pl.ds(column, 128)]

    def of_latent(column):
        return latent_all[:, pl.ds(column, 128)]

    def of_act(column):
        return quarters[:, pl.ds(column, 128)]

    def flat(ref, start=None, size=None):
        def right():
            block = ref[...] if start is None else ref[:, :, start : start + size]
            return block.reshape(4 * cells, block.shape[-1])

        return right

    def source_all():
        return quarters[:, inner // 4 :]

    half_w, half_i = width // 2, inner // 8
    operands = {
        DECODER_: (of_latent, source_all),
        DOWN0_: (of_act, flat(branch_all, 0, half_w)),
        DOWN1_: (of_act, flat(branch_all, half_w, half_w)),
        MEAN_: (of_base, flat(gmean_all)),
        LOGVAR_: (of_base, flat(glogvar_all)),
        HIDDEN0_: (of_whole(TWO_), flat(ginner_all, 0, half_i)),
        HIDDEN1_: (of_whole(TWO_), flat(ginner_all, half_i, half_i)),
        OUTPUT_: (of_whole(ATTENDED_), flat(gout_all)),
        PANEL_: (of_whole(EXPRESS_), flat(genc_all)),
        QUERY_: (of_whole(ONE_), flat(gqkv_all.at[0])),
        KEY_: (of_whole(ONE_), flat(gqkv_all.at[1])),
        VALUE_: (of_whole(ONE_), flat(gqkv_all.at[2])),
    }
    units = {}
    for number, (name, rows, columns, dense) in enumerate(reductions_of(cells, width, inner, latents)):
        left, right = operands[name]
        units[name] = (ReductionAlongZ if name in Z_FIRST else Reduction)(
            links, left, right, rows, columns, dense, unit_refs[3 * number : 3 * number + 3]
        )

    result_slots = {
        DECODER_: lambda place: lanes(decoder_out, place, width // 4),
        DOWN0_: lambda place: down_out.at[pl.ds(pl.multiple_of(place * (inner // 32), inner // 32), inner // 32), pl.ds(0, half_w)],
        DOWN1_: lambda place: down_out.at[pl.ds(pl.multiple_of(place * (inner // 32), inner // 32), inner // 32), pl.ds(half_w, half_w)],
        MEAN_: lambda place: lanes(mean_out, place, latents // 4),
        LOGVAR_: lambda place: lanes(logvar_out, place, latents // 4),
        HIDDEN0_: lambda place: hidden_out.at[:, pl.ds(pl.multiple_of(place * (inner // 4), 128), half_i)],
        HIDDEN1_: lambda place: hidden_out.at[:, pl.ds(pl.multiple_of(place * (inner // 4) + half_i, 128), half_i)],
        OUTPUT_: lambda place: lanes(output_out, place, width // 4),
        QUERY_: lambda place: lanes(query_out, place, width // 4),
        KEY_: lambda place: lanes(key_out, place, width // 4),
        VALUE_: lambda place: lanes(value_out, place, width // 4),
    }
    spreads = {}

    def spread(name):
        spreads[name] = spread_slide(links, result_slots[name], units[name].total())
        next(spreads[name])

    chunk = inner // 8
    encoded[...] = jnp.zeros_like(encoded)

    def feed_back(turn):
        far = (2, 3, 1, 0)[turn]
        wide, tall = ((1, 2), (3, 0))[turn % 2]
        have((WD_, B_, far), (WH_, B_, far))
        which = flipped(slide, far)

        def feed(j, carry, wide=wide, tall=tall, which=which):
            near = pl.ds(pl.multiple_of(j * chunk, 128), chunk)
            where = pl.ds(pl.multiple_of(which * (inner // 4) + j * chunk, 128), chunk)
            values = inner_sums[:, where]
            squared = values * values
            bent = jnp.tanh(0.7978845608028654 * (values + 0.044715 * squared * values))
            slope = 0.5 * (1.0 + bent) + 0.5 * values * (1.0 - bent * bent) * (
                0.7978845608028654 * (1.0 + 3 * 0.044715 * squared)
            )
            grad = (dot_nt(branch_all[0], slots[tall, near, :]) * slope).astype(BF16)
            ginner[:, where] = grad
            line = jnp.sum(grad.astype(F32), axis=0, keepdims=True)
            for block in range(chunk // 128):
                small[which * 2 + j, 4 + block : 5 + block, :] = line[:, block * 128 : (block + 1) * 128]
            encoded[...] += dot_nt(grad, slots[wide, :, near])
            return carry

        lax.fori_loop(0, 2, feed, 0)
        if far:
            flows[INNER_] = flows.get(INNER_, []) + [
                links.send(lanes(ginner, which, inner // 4), ginner_all.at[far], far, 0)
            ]
        else:
            ginner_all[0] = lanes(ginner, slide, inner // 4)[...]
        if turn < 2:
            load_quarter((B_, (1, 0)[turn]), flipped(slide, (1, 0)[turn]), wide, tall)
        if turn == 3:
            for number, (name, source) in enumerate(((WQ_, wq_hbm), (WK_, wk_hbm), (WV_, wv_hbm))):
                load((B_, name), source, slots.at[number])

    wq, wk, wv = slots.at[0], slots.at[1], slots.at[2]

    def norm_two():
        grad_hidden, gain_grad, shift_grad = norm_back(middle[...], gain_two[...], encoded[...])
        for block in range(8):
            small[block, 2:3, :] = gain_grad[:, block * 128 : (block + 1) * 128]
            small[block, 3:4, :] = shift_grad[:, block * 128 : (block + 1) * 128]
        gmiddle[...] += grad_hidden
        gout[...] = gmiddle[...].astype(BF16)

    def att_out():
        have(WO_)

        def att_block(target, store):
            rows = wo[pl.ds(pl.multiple_of(target * per, per), per), :]
            store(dot_nt(gout[...], rows).astype(BF16))

        att_copies = flows[ATT_] = []
        for far in (6, 4, 2, 7, 5, 3, 1):
            target = flipped(blk, far)

            def keep(block, far=far):
                att_send[far] = block

            att_block(target, keep)
            att_copies.append(links.send(att_send.at[far], att_land.at[blk], 0, far))

        def keep_own(block):
            att_land[blk] = block

        att_block(blk, keep_own)

    def swap_out():
        flows[GOUT_] = swap(gout, width // 4, gout_all)

    def masks():
        dk_sum[...] = jnp.zeros_like(dk_sum)
        dv_sum[...] = jnp.zeros_like(dv_sum)

    scale = HEAD_DIM**-0.5
    rows = 2 * cells

    def rows_back(i):
        arrived(ATT_)
        where = pl.ds(pl.multiple_of(i * rows, rows), rows)
        same_slide = row_labels[where, 0:1] == col_labels[...]
        query = land[pl.ds(2 * i, 2), 0:cells, :].reshape(rows, per)
        grad = att_land[pl.ds(2 * i, 2)].reshape(rows, per)
        key = land[:, cells : 2 * cells, :].reshape(8 * cells, per)
        value = land[:, 2 * cells : 3 * cells, :].reshape(8 * cells, per)
        lane = lax.broadcasted_iota(jnp.int32, query.shape, 1)
        grad_query = None
        for head in range(per // HEAD_DIM):
            mine = lane // HEAD_DIM == head
            own_query = jnp.where(mine, query, 0) * HEAD_SCALE
            own_grad = jnp.where(mine, grad, 0)
            shifted, inverse = head_scores(own_query, key, same_slide)
            shares = shifted * inverse
            grad_shares = dot_nt(own_grad, value)
            inner_dot = jnp.sum(shares * grad_shares, axis=1, keepdims=True)
            grad_scores = (shares * (grad_shares - inner_dot)).astype(BF16)
            part = jnp.dot(grad_scores, key, preferred_element_type=F32)
            grad_query = part if grad_query is None else jnp.where(mine, part, grad_query)
            dk_sum[...] += dot_tn(grad_scores, own_query)
            dv_sum[...] += dot_tn(shares.astype(BF16), own_grad)
        dqkv[pl.ds(2 * i, 2), 0:cells, :] = (grad_query * scale).astype(BF16).reshape(2, cells, per)

    def back_out():
        dqkv[:, cells : 2 * cells, :] = dk_sum[...].astype(BF16).reshape(8, cells, per)
        dqkv[:, 2 * cells :, :] = dv_sum[...].astype(BF16).reshape(8, cells, per)
        back_copies = flows[BACK_] = []
        for far in (6, 4, 2, 7, 5, 3, 1):
            back_copies.append(links.send(dqkv.at[flipped(blk, far)], dqkv_land.at[blk], 0, far))
        dqkv_land[blk] = dqkv[blk]

    def back_in():
        arrived(BACK_)
        have((B_, WQ_), (B_, WK_), (B_, WV_))
        for part in range(3):
            for block in range(8):
                grad_qkv[part, :, block * per : (block + 1) * per] = dqkv_land[block, part * cells : (part + 1) * cells, :]


    def swap_qkv():
        for part in range(3):
            flows[(QKV_, part)] = swap(grad_qkv.at[part], width // 4, gqkv_all.at[part])

    def norm_input(i, carry):
        where = pl.ds(pl.multiple_of(i * 256, 256), 256)
        encoded_sum = (
            dot_nt(grad_qkv[0], wq[where, :]) + dot_nt(grad_qkv[1], wk[where, :]) + dot_nt(grad_qkv[2], wv[where, :])
        )
        encoded[:, where] = encoded_sum
        return carry

    def norm_one():
        lax.fori_loop(0, width // 256, norm_input, 0)
        grad_hidden, gain_grad, shift_grad = norm_back(start[...], gain_one[...], encoded[...])
        grad_qkv[3] = (gmiddle[...] + grad_hidden).astype(BF16)
        flows[GENC_] = swap(grad_qkv.at[3], width // 4, genc_all)
        for block in range(8):
            small[block, 0:1, :] = gain_grad[:, block * 128 : (block + 1) * 128]
            small[block, 1:2, :] = shift_grad[:, block * 128 : (block + 1) * 128]

    def small_out_blk():
        flows[SMALL_] = [links.send(small.at[flipped(blk, far)], small_land.at[blk], 0, far) for far in range(1, 8)]
        small_land[blk] = small[blk]

    def small_out_slide():
        arrived(SMALL_)
        small_sum = small_land[0]
        for block in range(1, 8):
            small_sum = small_sum + small_land[block]
        small_own[...] = small_sum
        flows[SUMS_] = [links.send(small_own, small_slides.at[slide], far, 0) for far in (2, 3, 1)]
        small_slides[slide] = small_sum

    def small_done():
        arrived(SUMS_)
        small_out[...] = (small_slides[0] + small_slides[1]) + (small_slides[2] + small_slides[3])

    panel_slot = lambda far_slide, far_blk: panel_out.at[
        pl.ds(pl.multiple_of(far_blk * (width // 8), 128), width // 8),
        pl.ds(pl.multiple_of(far_slide * (width // 4), 128), width // 4),
    ]
    needs = {
        DECODER_: (SOURCE_,), DOWN0_: (ACT_, NEAR_), DOWN1_: (ACT_, NEAR_), MEAN_: (GMEAN_,), LOGVAR_: (GLOGVAR_,),
        HIDDEN0_: (INNER_,), HIDDEN1_: (INNER_,), OUTPUT_: (GOUT_,), PANEL_: (GENC_,), QUERY_: ((QKV_, 0),),
        KEY_: ((QKV_, 1),), VALUE_: ((QKV_, 2),),
    }

    def along(name):
        arrived(*needs[name])
        held = {HIDDEN0_: TWO_, HIDDEN1_: TWO_, OUTPUT_: ATTENDED_, PANEL_: EXPRESS_}
        held = held.get(name, NORMED_ if name in (QUERY_, KEY_, VALUE_) else None)
        if held and held not in waited:
            waited.add(held)
            next(flows[held])
        units[name].send_x()

    def panel_out_start():
        own_slot = panel_slot(slide, blk)
        own_slot[...] = units[PANEL_].total()
        flows[PANEL_] = spread_everywhere(links, panel_slot)
        next(flows[PANEL_])

    def spread_on(name):
        next(spreads[name])

    steps = {
        LATENT_: start_latent, ATTENDED_: start_attended, BASE_: start_base, RELAY_: relay, BOTTLENECK_: bottleneck, LATS_: swap_latents,
        BRANCH_: branch_on, FEED_: feed_back, NORM2_: norm_two, ATT_: att_out, GOUT_: swap_out, MASKS_: masks,
        ROWS_: rows_back, BACK_: back_out, IN_: back_in, QKV_: swap_qkv, NORM1_: norm_one, SMALL_: small_out_blk,
        SUMS_: small_out_slide, DONE_: small_done, X_: along, Z_: lambda name: units[name].send_z(),
        F_: lambda name: units[name].send_far(), S_: spread, S2_: spread_on, PANEL_: panel_out_start,
    }
    for step in ORDER:
        steps[step[0]](*step[1:])
    links.finish()


def layer(inputs, weights, cells, width, inner, latents):
    per = width // 8
    small_rows = 32
    shape = jax.ShapeDtypeStruct
    unit_scratch = []
    for _, rows, columns, _ in reductions_of(cells, width, inner, latents):
        unit_scratch += [pltpu.VMEM((4 * rows, columns), BF16)] * 2 + [pltpu.VMEM((3, rows, columns), BF16)]
    copies = 352
    vmem, left = pl.BlockSpec(memory_space=pltpu.VMEM), pl.BlockSpec(memory_space=pl.ANY)
    outs = (
        shape((cells, width), F32),
        shape((8, 128), F32),
        shape((width, width), BF16),
        shape((per, width), BF16),
        shape((per, width), BF16),
        shape((per, width), BF16),
        shape((per, width), BF16),
        shape((per, inner), BF16),
        shape((inner // 8, width), BF16),
        shape((per, latents), BF16),
        shape((per, latents), BF16),
        shape((latents // 8, width), BF16),
        shape((small_rows, 128), F32),
    )
    scratch = [
        ((4, width, width), BF16),
        ((width, width), BF16),
        ((width, latents), BF16),
        ((width, latents), BF16),
        ((latents, width), BF16),
        ((2, 8, width // 64, width), BF16),
        ((2, 8, width // 64, width), BF16),
        ((8, 3 * cells + 16, per), BF16),
        ((8, 3 * cells + 16, per), BF16),
        ((8, cells, per), BF16),
        ((8, cells, per), BF16),
        ((8 * cells, cells), F32),
        ((1, 8 * cells), F32),
        ((4, cells, inner // 4), BF16),
        ((cells, width), F32),
        ((8, 128), F32),
        ((4, 8, 128), F32),
        ((8, 128), F32),
        ((8, 8, 128), F32),
        ((cells, width), F32),
        ((cells, width), F32),
        ((cells, inner), F32),
        ((cells, latents), F32),
        ((cells, latents), F32),
        ((cells, latents), F32),
        ((4 * cells, 4 * width), BF16),
        ((4 * cells, inner // 4 + width // 4), BF16),
        ((4 * cells, width), BF16),
        ((4 * cells, latents), BF16),
        ((4, cells, width), BF16),
        ((cells, latents), BF16),
        ((cells, latents), BF16),
        ((4, cells, latents // 4), BF16),
        ((4, cells, latents // 4), BF16),
        ((cells, inner), BF16),
        ((4, cells, inner // 4), BF16),
        ((cells, width), BF16),
        ((4, cells, width // 4), BF16),
        ((cells, width), F32),
        ((3, 4, cells, width // 4), BF16),
        ((4, cells, width // 4), BF16),
        ((8, cells, per), BF16),
        ((8, cells, per), BF16),
        ((8, 3 * cells, per), BF16),
        ((8, 3 * cells, per), BF16),
        ((8 * cells, per), F32),
        ((8 * cells, per), F32),
        ((4, cells, width), BF16),
        ((cells, width), F32),
        ((8, small_rows, 128), F32),
        ((8, small_rows, 128), F32),
        ((small_rows, 128), F32),
        ((4, small_rows, 128), F32),
    ]
    return pl.pallas_call(
        layer_kernel,
        out_shape=outs,
        in_specs=[vmem] * len(inputs) + [left] * len(weights),
        out_specs=[vmem] * len(outs),
        scratch_shapes=[pltpu.VMEM(*item) for item in scratch]
        + [
            pltpu.SemaphoreType.DMA((28,)),
            pltpu.SemaphoreType.DMA((copies,)),
            pltpu.SemaphoreType.DMA((copies,)),
        ]
        + unit_scratch,
        compiler_params=pltpu.CompilerParams(
            collective_id=1, has_side_effects=True, vmem_limit_bytes=63 << 20
        ),
        name="layer",
    )(*inputs, *weights)


def finish_kernel(ids_ref, panel_ref, small_ref, kl_ref, weight_ref, floor_ref, *refs):
    count = (len(refs) - 9) // 2
    table_out, grads, outs, tiny = refs[count], refs[:count], refs[count + 1 : 2 * count + 1], refs[2 * count + 1 :]
    rows = table_out.shape[0]
    first = (lax.axis_index("blk") * pl.num_programs(0) + pl.program_id(0)) * rows
    row_ids = first + lax.broadcasted_iota(jnp.int32, (rows, ids_ref.shape[1]), 0)
    spread = (row_ids == ids_ref[...]).astype(F32).astype(BF16)
    table_out[...] = jnp.dot(spread, panel_ref[...], preferred_element_type=F32)
    for grad, out in zip(grads, outs):
        out[...] = grad[...].astype(F32)

    @pl.when(pl.program_id(0) == 0)
    def _():
        start = 0
        for out in tiny[:6]:
            out[...] = small_ref[start : start + out.shape[0], :]
            start += out.shape[0]
        centres = tiny[6]
        centres[...] = small_ref[16 : 16 + centres.shape[0], 0 : centres.shape[1]]
        total = jnp.zeros((1, 128), F32)
        for block in range(floor_ref.shape[1] // 128):
            lanes = slice(block * 128, (block + 1) * 128)
            total = total + jnp.maximum(kl_ref[block : block + 1, :] / weight_ref[0, 1], floor_ref[:, lanes])
        tiny[7][...] = weight_ref[0, 0] * (jnp.sum(total, axis=1, keepdims=True) / floor_ref.shape[1])


def finish(gene_ids, panel, grads, small, kl_total, weight, floor, table_rows, centres_shape, bias_rows, rows=1024):
    genes, width = panel.shape
    steps = table_rows // rows
    shape = jax.ShapeDtypeStruct
    tiny = [(1, 128)] * 4 + [(bias_rows, 128), (1, 128), centres_shape, (1, 1)]

    def cut(grad):
        if grad.shape[0] // steps % 16 == 0:
            return pl.BlockSpec((grad.shape[0] // steps, grad.shape[1]), lambda i: (i, 0))
        return pl.BlockSpec((grad.shape[0], grad.shape[1] // steps), lambda i: (0, i))

    def whole(size):
        return pl.BlockSpec(size, lambda i: (0, 0))

    return pl.pallas_call(
        finish_kernel,
        grid=(steps,),
        out_shape=[shape((table_rows, width), F32)] + [shape(grad.shape, F32) for grad in grads] + [shape(size, F32) for size in tiny],
        in_specs=[
            whole((1, genes)), whole(panel.shape), whole(small.shape), whole(kl_total.shape),
            pl.BlockSpec(memory_space=pltpu.SMEM), whole(floor.shape),
        ]
        + [cut(grad) for grad in grads],
        out_specs=[pl.BlockSpec((rows, width), lambda i: (i, 0))] + [cut(grad) for grad in grads] + [whole(size) for size in tiny],
        compiler_params=pltpu.CompilerParams(vmem_limit_bytes=62 << 20),
        name="finish",
    )(gene_ids, panel, small, kl_total, weight, floor, *grads)


def on_device_fast(
    counts,
    library,
    gene_ids,
    positions,
    slide_of_cell,
    latent_noise,
    decoded_grad,
    gene_table,
    first_gain,
    first_shift,
    query_weight,
    key_weight,
    value_weight,
    output_weight,
    second_gain,
    second_shift,
    hidden_weight,
    hidden_bias,
    down_weight,
    down_bias,
    mean_weight,
    logvar_weight,
    component_means,
    decoder_weight,
    divergence_weight,
    free_floor,
):
    cells = counts.shape[1]
    width = gene_table.shape[1]
    latents = mean_weight.shape[1]
    inner = hidden_weight.shape[1]
    table_rows = gene_table.shape[0]
    quarter = width // 4
    freqs = np.exp(-math.log(10000.0) * np.arange(quarter, dtype=np.float32) / quarter).astype(np.float32)
    (
        decoded, kl_total, panel_sum, query_grad, key_grad, value_grad, output_grad, hidden_grad, down_grad, mean_grad,
        logvar_grad, decoder_grad, small,
    ) = layer(
        (
            gene_ids[None], counts[0], library, positions[0], freqs[None], slide_of_cell, latent_noise[0], decoded_grad[0],
            first_gain[None], first_shift[None], second_gain[None], second_shift[None], hidden_bias[None],
            down_bias[None], component_means, divergence_weight[None], free_floor[None],
        ),
        (
            gene_table, query_weight, key_weight, value_weight, output_weight, hidden_weight, down_weight, mean_weight,
            logvar_weight, decoder_weight,
        ),
        cells, width, inner, latents,
    )
    (
        table_grad, query_grad, key_grad, value_grad, output_grad, hidden_grad, down_grad, mean_grad, logvar_grad,
        decoder_grad, gain_one, shift_one, gain_two, shift_two, hidden_small, down_small, centres_grad, divergence,
    ) = finish(
        gene_ids[None], panel_sum,
        (
            query_grad, key_grad, value_grad, output_grad, hidden_grad, down_grad, mean_grad, logvar_grad,
            decoder_grad,
        ),
        small, kl_total, jnp.stack([divergence_weight[0], jnp.float32(32 * cells)])[None], free_floor[None], table_rows,
        (component_means.shape[0], latents // 8), inner // 8 // 128,
    )
    return (
        decoded[None],
        divergence.reshape(1),
        table_grad,
        gain_one.reshape(-1),
        shift_one.reshape(-1),
        query_grad,
        key_grad,
        value_grad,
        output_grad,
        gain_two.reshape(-1),
        shift_two.reshape(-1),
        hidden_grad,
        hidden_small.reshape(-1),
        down_grad,
        down_small.reshape(-1),
        mean_grad,
        logvar_grad,
        centres_grad,
        decoder_grad,
    )


def solution(mesh):
    placed = (
        P("slide", "blk", None),
        P("slide", "blk"),
        P(),
        P("slide", None, "blk"),
        P("slide", "blk"),
        P("slide", "blk", None),
        P("slide", "blk", None),
        P("blk", None),
        P(),
        P(),
        P(),
        P(),
        P(),
        P(),
        P(),
        P(),
        P(),
        P(),
        P(),
        P(),
        P(),
        P(),
        P(),
        P(),
        P(),
        P(),
    )
    return jax.shard_map(
        on_device_fast if fits(mesh) else on_device_general,
        mesh=mesh,
        in_specs=placed,
        out_specs=(
            P("slide", "blk", None),
            P(),
            P("blk", None),
            P("blk"),
            P("blk"),
            P("blk", None),
            P("blk", None),
            P("blk", None),
            P("blk", None),
            P("blk"),
            P("blk"),
            P("blk", None),
            P("blk"),
            P("blk", None),
            P("blk"),
            P("blk", None),
            P("blk", None),
            P(None, "blk"),
            P("blk", None),
        ),
        check_vma=False,
    )
```
